128 devices in a mesh: dp: 16 (over z_lo, x, core), seq: 8 (over y, z_hi).
Axes of the slice: x: 4, y: 4, z: 4 (z_hi: 2, z_lo: 2; z = z_hi * 2 + z_lo), core: 2. Of those that a mesh axis runs over, the one named last changes fastest.
Arguments:
- tokens: bfloat16 [1024, 16, 2048], P('seq', 'dp'), may hold values from -6 to 6
- cotangent: bfloat16 [1024, 16, 2048], P('seq', 'dp'), may hold values from -6 to 6
- w_qkv: bfloat16 [2048, 3, 2048], P(None, None, 'seq'), may hold values from -0.125 to 0.125
- w_out: bfloat16 [2048, 2048], P('seq'), may hold values from -4 to 4
- w_gate_up: bfloat16 [2048, 2, 5461], P('seq'), may hold values from -0.125 to 0.125
- w_down: bfloat16 [2048, 5461], P('seq'), may hold values from -0.4375 to 0.4375
- attn_gain: float32 [2048], replicated, may hold values from 0.5 to 1.5
- attn_bias: float32 [2048], replicated, may hold values from -1 to 1
- ffn_gain: float32 [2048], replicated, may hold values from 0.5 to 1.5
- ffn_bias: float32 [2048], replicated, may hold values from -1 to 1
- prefix_len: int32 [16], P('dp'), may hold values from 1 to 1024
- clusters: int32 [16], replicated, may hold values from 0 to 15
Outputs:
- output: bfloat16 [1024, 16, 2048], P('seq', 'dp')
- input_grad: float32 [1024, 16, 2048], P('seq', 'dp')
- grad_qkv: float32 [2048, 3, 2048], P(None, None, 'seq')
- grad_out: float32 [2048, 2048], P('seq')
- grad_gate_up: float32 [2048, 2, 5461], P('seq')
- grad_down: float32 [2048, 5461], P('seq')
- grad_attn_gain: float32 [2048], P('seq')
- grad_attn_bias: float32 [2048], P('seq')
- grad_ffn_gain: float32 [2048], P('seq')
- grad_ffn_bias: float32 [2048], P('seq')
The draws below stay inside these ranges and needn't reach their ends.
All inputs are finite; a program needn't handle non-finite values.
Results may differ from the reference program's by a relative error of at most 0.03.
Values may be sent and summed in bfloat16 or wider, within the bound.
A program may use at most 192 MiB of HBM per device.

```python
import math
import jax
import jax.numpy as jnp
import numpy as np
from jax import lax

D = 2048
HEADS = 16
HEAD_DIM = 128
FF = 5461
LEN = 1024
SEQS = 16


def with_ends(entries, rng, low, high):
    extent = entries.shape
    place = [jax.random.randint(jax.random.fold_in(rng, axis), (), 0, extent[axis]) for axis in range(len(extent))]
    entries = entries.at[tuple(place)].set(low)
    longest = extent.index(max(extent))
    place[longest] = (place[longest] + 1) % extent[longest]
    return entries.at[tuple(place)].set(high)


def block_levels(key, dims, split, least, high):
    loudness, own = 1.0, jax.random.fold_in(key, 6)
    for dim, parts in split:
        draws = jnp.exp(jax.random.uniform(jax.random.fold_in(own, dim), (parts,), jnp.float32, least / len(split), high / len(split)))
        loudness = loudness * jnp.repeat(draws, dims[dim] // parts).reshape([-1 if axis == dim else 1 for axis in range(len(dims))])
    return loudness


def rank_bounds(amount, slope):
    weights = [(1 << 20) // math.isqrt(grade ** slope) + 1 for grade in range(1, amount + 1)]
    deviation = 1 + sum(weights) // (1 << 30)
    return np.cumsum(np.array([max(1, weight // deviation) for weight in weights]))


def ranked_ids(stream_key, shape, count, skew):
    table = rank_bounds(count, skew)
    pick = jax.random.randint(jax.random.fold_in(stream_key, 1), shape, 0, int(table[count - 1]))
    grade = jnp.searchsorted(jnp.asarray(table, jnp.int32), pick, side="right")
    return jax.random.permutation(jax.random.fold_in(stream_key, 2), count)[grade].astype(jnp.int32)


def noise(rng, dims, deviation, limit, split=(), kind=jnp.bfloat16):
    drawn = deviation * jax.random.normal(rng, dims, jnp.float32)
    if split:
        drawn = drawn * block_levels(rng, dims, split, -0.22, 0.18)
    return jnp.clip(drawn, -limit, limit).astype(kind)


def setup_inputs(seed: int = 0) -> dict:
    key_list = jax.random.split(jax.random.key(seed), 13)
    return {
        "tokens": noise(key_list[0], (LEN, SEQS, D), 1.0, 6.0, ((0, 8), (1, 16))),
        "cotangent": noise(key_list[1], (LEN, SEQS, D), 1.0, 6.0, ((0, 8), (1, 16))),
        "w_qkv": noise(key_list[2], (D, 3, D), D ** -0.5, 0.125, ((2, 8),)),
        "w_out": noise(key_list[3], (D, D), (max(1, D // LEN)) ** -0.5, 4.0, ((0, 8),)),
        "w_gate_up": noise(key_list[4], (D, 2, FF), D ** -0.5, 0.125, ((0, 8),)),
        "w_down": noise(key_list[5], (D, FF), (max(1, FF // 30)) ** -0.5, 0.4375, ((0, 8),)),
        "attn_gain": jnp.clip(1.0 + 0.1 * jax.random.normal(key_list[6], (D,), jnp.float32), 0.5, 1.5),
        "attn_bias": noise(key_list[7], (D,), 0.2, 1.0, (), jnp.float32),
        "ffn_gain": jnp.clip(1.0 + 0.1 * jax.random.normal(key_list[8], (D,), jnp.float32), 0.5, 1.5),
        "ffn_bias": noise(key_list[9], (D,), 0.2, 1.0, (), jnp.float32),
        "prefix_len": with_ends(jax.random.randint(key_list[10], (SEQS,), 1, LEN + 1), jax.random.fold_in(key_list[10], 1), 1, LEN).astype(jnp.int32),
        "clusters": with_ends(ranked_ids(key_list[11], (SEQS,), SEQS, 2), jax.random.fold_in(key_list[11], 3), 0, SEQS - 1).astype(jnp.int32),
    }


deep_alpha = 48.0 ** 0.25
norm_eps = 1e-05
rotary_base = 10000.0
highest = lax.Precision.HIGHEST

@jax.custom_vjp
def low(v):
    return lax.optimization_barrier(v.astype(jnp.bfloat16)).astype(jnp.float32)

@jax.custom_vjp
def low_back(v):
    return v

def low_keep(v):
    return (low(v), None)

def low_pass(kept, grad):
    return (grad,)

def back_keep(v):
    return (v, None)

def back_low(kept, grad):
    return (low(grad),)
low.defvjp(low_keep, low_pass)
low_back.defvjp(back_keep, back_low)

def rotary_tables(length, head_width):
    half_width = head_width // 2
    position = jnp.arange(length, dtype=jnp.float32)
    inverse = rotary_base ** (-jnp.arange(half_width, dtype=jnp.float32) * 2.0 / head_width)
    angles = position[:, None] * inverse[None, :]
    cosine_table = jnp.cos(angles)
    sine_table = jnp.sin(angles)
    return (jnp.concatenate([cosine_table, cosine_table], axis=1), jnp.concatenate([sine_table, sine_table], axis=1))

def rotate(values_in, cosine_table, sine_table):
    half_width = values_in.shape[-1] // 2
    turned = jnp.concatenate([-values_in[..., half_width:], values_in[..., :half_width]], axis=-1)
    return values_in * cosine_table + turned * sine_table

def layer_norm(row_total, gain, bias):
    center = row_total - lax.optimization_barrier(jnp.mean(row_total, axis=-1, keepdims=True))
    spread = lax.optimization_barrier(jnp.mean(center * center, axis=-1, keepdims=True))
    return center * lax.rsqrt(spread + norm_eps) * gain + bias

def attend(queries, key_rows, value_rows, prefix):
    head_count, length, depth = queries.shape
    block_rows = min(512, length)
    num_blocks = length // block_rows
    positions = jnp.arange(length, dtype=jnp.int32)
    starts = jnp.arange(num_blocks, dtype=jnp.int32) * block_rows
    query_blocks = queries.reshape(head_count, num_blocks, block_rows, depth).transpose(1, 0, 2, 3)

    @jax.checkpoint
    def one_block(block_item):
        query_block, first_row = block_item
        scores = low_back(jnp.einsum('hqe,hke->hqk', query_block, key_rows, precision=highest))
        row_pos = first_row + jnp.arange(block_rows, dtype=jnp.int32)
        visible = (positions[None, :] < prefix) | (positions[None, :] <= row_pos[:, None])
        scores = jnp.where(visible[None], scores, -1e+30)
        row_peak = lax.optimization_barrier(jnp.max(scores, axis=-1, keepdims=True))
        exponent = jnp.exp(scores - row_peak)
        weights_low = low(exponent / lax.optimization_barrier(jnp.sum(exponent, axis=-1, keepdims=True)))
        return jnp.einsum('hqk,hke->hqe', weights_low, value_rows, precision=highest)
    block_outputs = lax.map(one_block, (query_blocks, starts))
    return block_outputs.transpose(1, 0, 2, 3).reshape(head_count, length, depth)

def layer(seq_in, weights, prefix, cosine_table, sine_table):
    w_qkv, w_out, w_gate_up, w_down, attn_gain, attn_bias, ffn_gain, ffn_bias = weights
    length = seq_in.shape[0]
    score_scale = HEAD_DIM ** (-0.5)
    project = low_back(jnp.einsum('td,dch->tch', seq_in, w_qkv, precision=highest))
    heads_split = project.reshape(length, 3, HEADS, HEAD_DIM)
    queries = low(rotate(heads_split[:, 0], cosine_table, sine_table) * score_scale)
    key_rows = low(rotate(heads_split[:, 1], cosine_table, sine_table))
    value_rows = low(heads_split[:, 2])
    mixed_heads = attend(queries.transpose(1, 0, 2), key_rows.transpose(1, 0, 2), value_rows.transpose(1, 0, 2), prefix)
    heads_out = low(low_back(mixed_heads.transpose(1, 0, 2).reshape(length, D)))
    attended = low_back(jnp.dot(heads_out, w_out, precision=highest))
    normed = layer_norm(deep_alpha * seq_in + attended, attn_gain, attn_bias)
    gate_up = low_back(jnp.einsum('td,dcf->tcf', low(normed), w_gate_up, precision=highest))
    hidden = low(jax.nn.gelu(gate_up[:, 0], approximate=False) * gate_up[:, 1])
    branch = low_back(jnp.einsum('tf,df->td', hidden, w_down, precision=highest))
    return layer_norm(deep_alpha * normed + branch, ffn_gain, ffn_bias)

def reference(tokens, cotangent, w_qkv, w_out, w_gate_up, w_down, attn_gain, attn_bias, ffn_gain, ffn_bias, prefix_len, clusters):
    same_cluster = (clusters[:, None] == clusters[None, :]).astype(jnp.float32)
    seq_weight = 1.0 / lax.optimization_barrier(jnp.sum(same_cluster, axis=1))
    params = (w_qkv.astype(jnp.float32), w_out.astype(jnp.float32), w_gate_up.astype(jnp.float32), w_down.astype(jnp.float32), attn_gain, attn_bias, ffn_gain, ffn_bias)
    cosine_table, sine_table = rotary_tables(LEN, HEAD_DIM)
    cosine_wide = cosine_table[:, None, :]
    sine_wide = sine_table[:, None, :]

    def one_sequence(totals, block_item):
        seq_tokens, seq_cot, prefix, weight = block_item

        def forward(seq_in, weights):
            return layer(seq_in, weights, prefix, cosine_wide, sine_wide)
        result, backward = jax.vjp(forward, seq_tokens.astype(jnp.float32), params)
        grad_in, grad_params = backward(seq_cot.astype(jnp.float32) * weight)
        totals = tuple((total_now + grad_now for total_now, grad_now in zip(totals, grad_params)))
        return (totals, (result.astype(jnp.bfloat16), grad_in))
    zero_grads = tuple((jnp.zeros_like(param) for param in params))
    totals, (outputs, input_grads) = lax.scan(one_sequence, zero_grads, (tokens.transpose(1, 0, 2), cotangent.transpose(1, 0, 2), prefix_len, seq_weight))
    return (outputs.transpose(1, 0, 2), input_grads.transpose(1, 0, 2), totals[0], totals[1], totals[2], totals[3], totals[4], totals[5], totals[6], totals[7])
```

```python
import functools

import jax
import jax.numpy as jnp
import numpy as np
from jax import lax
from jax.experimental import pallas as pl
from jax.experimental.pallas import tpu as pltpu
from jax.sharding import PartitionSpec as P

MESH = pl.DeviceIdType.MESH
F32, BF16 = jnp.float32, jnp.bfloat16
HEAD_DIM = 128
ROWS = 128
WIDE = 2048
COLS = 768
LEN = 1024
VMEM_BYTES = 60 * 1024 * 1024
deep_alpha = 48.0**0.25
norm_eps = 1e-05
rotary_base = 10000.0

ORDER = (0, 1, 2, 3, 4, 5, 6, 7)


def rotary_tables(length, head_width):
    half_width = head_width // 2
    position = np.arange(length, dtype=np.float64)
    inverse = rotary_base ** (-np.arange(half_width, dtype=np.float64) * 2.0 / head_width)
    angles = position[:, None] * inverse[None, :]
    cosine_table = np.cos(angles)
    sine_table = np.sin(angles)
    return (
        np.concatenate([cosine_table, cosine_table], axis=1).astype(np.float32),
        np.concatenate([-sine_table, sine_table], axis=1).astype(np.float32),
    )


class Links:
    def __init__(self, send, recv):
        self.send, self.recv, self.count = send, recv, 0
        dp, seq = lax.axis_index("dp"), lax.axis_index("seq")
        y, z_hi = seq // 2, seq % 2
        self.y, self.z_hi = y, z_hi
        self.up = (dp, lax.rem(y + 1, 4) * 2 + z_hi)
        self.down = (dp, lax.rem(y + 3, 4) * 2 + z_hi)
        self.across = (dp, y * 2 + 1 - z_hi)

    def barrier(self):
        gate = pltpu.get_barrier_semaphore()
        for where in (self.up, self.down, self.across):
            pl.semaphore_signal(gate, inc=1, device_id=where, device_id_type=MESH)
        pl.semaphore_wait(gate, 3)

    def start(self, src, dst, where):
        copy = pltpu.make_async_remote_copy(
            src_ref=src,
            dst_ref=dst,
            send_sem=self.send.at[self.count],
            recv_sem=self.recv.at[self.count],
            device_id=where,
            device_id_type=MESH,
        )
        self.count += 1
        copy.start()
        return copy

    def first_row(self, slot):
        step = (0, 3, 1, 2)[slot % 4]
        half = self.z_hi if slot < 4 else 1 - self.z_hi
        return pl.multiple_of((lax.rem(self.y + step, 4) * 2 + half) * ROWS, ROWS)


A, B = pl.ds(0, 80), pl.ds(80, 48)
A0, A1 = pl.ds(0, 48), pl.ds(48, 32)
B0, B1 = pl.ds(80, 16), pl.ds(96, 32)
GATHER_COPIES = 22
SCATTER_COPIES = 19


def gather(links, buf, work):
    go, up, down, across = links.start, links.up, links.down, links.across
    sent = []

    def send(src, dst, where):
        copy = go(buf.at[src[0], src[1]], buf.at[dst, src[1]], where)
        sent.append(copy)
        return copy

    u_a = send((0, A), 1, up)
    d_a = send((0, A), 2, down)
    z_a = send((0, A), 4, across)
    u_b = send((0, B), 1, up)
    d_b = send((0, B), 2, down)
    z_b = send((0, B), 4, across)
    u_a.wait_recv()
    u_a2 = send((1, A0), 3, up)
    d_a.wait_recv()
    d_a2 = send((2, A1), 3, down)
    z_a.wait_recv()
    u_p = send((4, A), 5, up)
    d_p = send((4, A), 6, down)
    u_b.wait_recv()
    z_b1 = send((1, B), 5, across)
    u_b2 = send((1, B0), 3, up)
    d_b.wait_recv()
    z_b2 = send((2, B), 6, across)
    d_b2 = send((2, B1), 3, down)
    work((0, 1))
    u_a2.wait_recv()
    d_a2.wait_recv()
    u_p.wait_recv()
    u_p2 = send((5, A0), 7, up)
    d_p.wait_recv()
    d_p2 = send((6, A1), 7, down)
    u_b2.wait_recv()
    z_b3 = send((3, B0), 7, across)
    d_b2.wait_recv()
    z_b4 = send((3, B1), 7, across)
    work((2, 3))
    z_b.wait_recv()
    z_b1.wait_recv()
    work((4, 5))
    z_b2.wait_recv()
    u_p2.wait_recv()
    d_p2.wait_recv()
    z_b3.wait_recv()
    z_b4.wait_recv()
    work((6, 7))
    for copy in sent:
        copy.wait_send()


def add_into(target, at, other, other_at):
    target[at] = (target[at].astype(F32) + other[other_at].astype(F32)).astype(BF16)


SCATTER_SCRATCH = (
    pltpu.VMEM((8, ROWS, WIDE), BF16),
    pltpu.VMEM((4, 48, WIDE), BF16),
    pltpu.VMEM((48, WIDE), BF16),
    pltpu.VMEM((2, 48, WIDE), BF16),
    pltpu.VMEM((2, 80, WIDE), BF16),
    pltpu.VMEM((2, 2, 80, WIDE), BF16),
    pltpu.VMEM((80, WIDE), BF16),
)


def scatter(links, bufs, compute, total):
    sums, from_z, b_far, b_near, a_far, a_near, a_z = bufs
    go, up, down, across = links.start, links.up, links.down, links.across
    sent = []

    def send(src, dst, where):
        copy = go(src, dst, where)
        sent.append(copy)
        return copy

    def far_a(o):
        half = o // 4
        return (
            send(sums.at[o + 3, A0], a_far.at[half, pl.ds(0, 48)], up),
            send(sums.at[o + 3, A1], a_far.at[half, pl.ds(48, 32)], down),
        )

    def near_a(o, far):
        half = o // 4
        far[0].wait_recv()
        sums[o + 2, 0:48] = (
            sums[o + 2, 0:48].astype(F32) + a_far[half, 0:48].astype(F32)
        ).astype(BF16)
        one = send(sums.at[o + 2, A], a_near.at[half, 0], up)
        far[1].wait_recv()
        sums[o + 1, 48:80] = (
            sums[o + 1, 48:80].astype(F32) + a_far[half, 48:80].astype(F32)
        ).astype(BF16)
        two = send(sums.at[o + 1, A], a_near.at[half, 1], down)
        return one, two

    def cross_b(j):
        return send(sums.at[4 + j, B], from_z.at[j], across)

    def take_b(j, copy):
        copy.wait_recv()
        sums[j, 80:128] = (sums[j, 80:128].astype(F32) + from_z[j].astype(F32)).astype(BF16)

    compute((7, 3))
    z3 = cross_b(3)
    far_other = far_a(4)
    far_own = far_a(0)
    compute((5, 6))
    z1 = cross_b(1)
    z2 = cross_b(2)
    compute((1, 2))
    take_b(3, z3)
    far_b = (
        send(sums.at[3, B0], b_far.at[pl.ds(0, 16)], up),
        send(sums.at[3, B1], b_far.at[pl.ds(16, 32)], down),
    )
    near_other = near_a(4, far_other)
    compute((4, 0))
    z0 = cross_b(0)
    near_own = near_a(0, far_own)
    for copy in near_other:
        copy.wait_recv()
    sums[4, 0:80] = (
        sums[4, 0:80].astype(F32) + a_near[1, 0].astype(F32) + a_near[1, 1].astype(F32)
    ).astype(BF16)
    z_a = send(sums.at[4, A], a_z, across)
    take_b(2, z2)
    far_b[0].wait_recv()
    sums[2, 80:96] = (sums[2, 80:96].astype(F32) + b_far[0:16].astype(F32)).astype(BF16)
    near_b0 = send(sums.at[2, B], b_near.at[0], up)
    take_b(1, z1)
    far_b[1].wait_recv()
    sums[1, 96:128] = (sums[1, 96:128].astype(F32) + b_far[16:48].astype(F32)).astype(BF16)
    near_b1 = send(sums.at[1, B], b_near.at[1], down)
    z0.wait_recv()
    near_b0.wait_recv()
    near_b1.wait_recv()
    total[80:128] = (
        sums[0, 80:128].astype(F32)
        + from_z[0].astype(F32)
        + b_near[0].astype(F32)
        + b_near[1].astype(F32)
    )
    for copy in near_own:
        copy.wait_recv()
    z_a.wait_recv()
    total[0:80] = (
        sums[0, 0:80].astype(F32)
        + a_near[0, 0].astype(F32)
        + a_near[0, 1].astype(F32)
        + a_z[...].astype(F32)
    )
    for copy in sent:
        copy.wait_send()


def dot(a, b):
    return jnp.dot(a, b, preferred_element_type=F32)


def dot_t(a, b):
    return lax.dot_general(a, b, (((1,), (1,)), ((), ())), preferred_element_type=F32)


def dot_rows(a, b):
    return lax.dot_general(a, b, (((0,), (0,)), ((), ())), preferred_element_type=F32)


def pair_of(ref, pair):
    return jnp.concatenate([ref[pair[0]], ref[pair[1]]], axis=0)


def by_chunks(body):
    def step(i, carry):
        body(pl.ds(pl.multiple_of(i * 16, 16), 16))
        return carry

    lax.fori_loop(0, ROWS // 16, step, 0)


def norm_parts(row_total):
    center = row_total - jnp.mean(row_total, axis=-1, keepdims=True)
    spread = jnp.mean(center * center, axis=-1, keepdims=True)
    inverse = lax.rsqrt(spread + norm_eps)
    return center * inverse, inverse


def norm_backward(grad_result, unit, inverse, gain):
    grad_unit = grad_result * gain
    return inverse * (
        grad_unit
        - jnp.mean(grad_unit, axis=-1, keepdims=True)
        - unit * jnp.mean(grad_unit * unit, axis=-1, keepdims=True)
    )


def rows8(values):
    return values[0:8] + values[8:16]


def call(body, name, ident, outs, operands, spaces, scratch, copies, flops=0):
    vmem = pl.BlockSpec(memory_space=pltpu.VMEM)
    kinds = {"v": vmem, "s": pl.BlockSpec(memory_space=pltpu.SMEM), "h": pl.BlockSpec(memory_space=pl.ANY)}
    sems = [pltpu.SemaphoreType.DMA((copies,)), pltpu.SemaphoreType.DMA((copies,))]
    return pl.pallas_call(
        body,
        name=name,
        out_shape=tuple(jax.ShapeDtypeStruct(s, d) for s, d in outs),
        in_specs=[kinds[k] for k in spaces],
        out_specs=tuple(vmem for _ in outs),
        scratch_shapes=[*scratch, *sems],
        compiler_params=pltpu.CompilerParams(
            collective_id=ident, has_side_effects=True, vmem_limit_bytes=VMEM_BYTES
        ),
        cost_estimate=pl.CostEstimate(flops=flops, bytes_accessed=20_000_000, transcendentals=0),
    )(*operands)


def project_kernel(x_ref, w_ref, cos_ref, sin_ref, all_ref, q_ref, k_ref, v_ref, send, recv):
    links = Links(send, recv)
    all_ref[0] = x_ref[...]
    links.barrier()

    def work(pair):
        rows = pair_of(all_ref, pair)
        for part, out in enumerate((q_ref, k_ref, v_ref)):
            result = dot(rows, w_ref[:, part * 256 : part * 256 + 256])
            for i, slot in enumerate(pair):
                at = pl.ds(links.first_row(slot), ROWS)
                piece = result[i * ROWS : (i + 1) * ROWS]
                if part == 2:
                    out[at] = piece.astype(BF16)
                    continue
                cosine, sine = cos_ref[at], sin_ref[at]
                for head in range(2):
                    lanes = slice(head * 128, head * 128 + 128)
                    turned = piece[:, lanes] * cosine + pltpu.roll(piece[:, lanes], 64, 1) * sine
                    if part == 0:
                        turned = turned * HEAD_DIM**-0.5
                    out[at, lanes] = turned.astype(BF16)

    gather(links, all_ref, work)


def attend_kernel(prefix_ref, q_ref, k_ref, v_ref, out_ref, lse_ref):
    block = q_ref.shape[0]
    first = pl.program_id(1) * block
    scores = dot_t(k_ref[...], q_ref[...])
    key = lax.broadcasted_iota(jnp.int32, scores.shape, 0)
    query = lax.broadcasted_iota(jnp.int32, (1, block), 1) + first
    limit = jnp.maximum(query, prefix_ref[0] - 1)
    scores = jnp.where(key <= limit, scores, -1e30)
    peak = jnp.max(scores, axis=0, keepdims=True)
    exponent = jnp.exp(scores - peak)
    total = jnp.sum(exponent, axis=0, keepdims=True)
    weights = (exponent * (1.0 / total)).astype(BF16)
    out_ref[...] = dot_rows(weights, v_ref[...]).astype(BF16)
    lse_ref[0] = peak + jnp.log(total)


def attend(prefix, q, k, v):
    block = 512
    return pl.pallas_call(
        attend_kernel,
        name="attend",
        grid=(2, LEN // block),
        in_specs=[
            pl.BlockSpec(memory_space=pltpu.SMEM),
            pl.BlockSpec((block, 128), lambda h, b: (b, h)),
            pl.BlockSpec((LEN, 128), lambda h, b: (0, h)),
            pl.BlockSpec((LEN, 128), lambda h, b: (0, h)),
        ],
        out_specs=(
            pl.BlockSpec((block, 128), lambda h, b: (b, h)),
            pl.BlockSpec((1, 1, block), lambda h, b: (h, 0, b)),
        ),
        out_shape=(
            jax.ShapeDtypeStruct((LEN, 256), BF16),
            jax.ShapeDtypeStruct((2, 1, LEN), F32),
        ),
        compiler_params=pltpu.CompilerParams(vmem_limit_bytes=VMEM_BYTES),
    )(prefix, q, k, v)


def attend_back_kernel(
    prefix_ref, q_ref, k_ref, v_ref, g_ref, lse_ref, cos_ref, sin_ref, cosq_ref, sinq_ref,
    dq_ref, dk_ref, dv_ref, dk_sum, dv_sum
):
    block = q_ref.shape[0]
    step = pl.program_id(1)
    scores = dot_t(k_ref[...], q_ref[...])
    key = lax.broadcasted_iota(jnp.int32, scores.shape, 0)
    query = lax.broadcasted_iota(jnp.int32, (1, block), 1) + step * block
    limit = jnp.maximum(query, prefix_ref[0] - 1)
    weights = jnp.where(key <= limit, jnp.exp(scores - lse_ref[0]), 0.0)
    grad_weights = dot_t(v_ref[...], g_ref[...])
    inner = jnp.sum(weights * grad_weights, axis=0, keepdims=True)
    grad_scores = (weights * (grad_weights - inner)).astype(BF16)
    d_query = dot_rows(grad_scores, k_ref[...]) * HEAD_DIM**-0.5
    dq_ref[...] = (d_query * cosq_ref[...] - pltpu.roll(d_query, 64, 1) * sinq_ref[...]).astype(BF16)
    d_key = dot(grad_scores, q_ref[...])
    d_value = dot(weights.astype(BF16), g_ref[...])

    @pl.when(step == 0)
    def _():
        dk_sum[...] = d_key
        dv_sum[...] = d_value

    @pl.when(step > 0)
    def _():
        dk_sum[...] += d_key
        dv_sum[...] += d_value

    @pl.when(step == pl.num_programs(1) - 1)
    def _():
        total = dk_sum[...]
        dk_ref[...] = (total * cos_ref[...] - pltpu.roll(total, 64, 1) * sin_ref[...]).astype(BF16)
        dv_ref[...] = dv_sum[...].astype(BF16)


def attend_back(prefix, q, k, v, g, lse, cosine, sine):
    block = 512
    part = pl.BlockSpec((block, 128), lambda h, b: (b, h))
    whole = pl.BlockSpec((LEN, 128), lambda h, b: (0, h))
    table = pl.BlockSpec((LEN, 128), lambda h, b: (0, 0))
    table_part = pl.BlockSpec((block, 128), lambda h, b: (b, 0))
    return pl.pallas_call(
        attend_back_kernel,
        name="attend_back",
        grid=(2, LEN // block),
        in_specs=[
            pl.BlockSpec(memory_space=pltpu.SMEM), part, whole, whole, part,
            pl.BlockSpec((1, 1, block), lambda h, b: (h, 0, b)),
            table, table, table_part, table_part,
        ],
        out_specs=(part, whole, whole),
        out_shape=tuple(jax.ShapeDtypeStruct((LEN, 256), BF16) for _ in range(3)),
        scratch_shapes=[pltpu.VMEM((LEN, 128), F32), pltpu.VMEM((LEN, 128), F32)],
        compiler_params=pltpu.CompilerParams(vmem_limit_bytes=VMEM_BYTES),
    )(prefix, q, k, v, g, lse, cosine, sine, cosine, sine)


def attended_kernel(
    heads_ref, w_ref, x_ref, gain_ref, bias_ref, normed_ref, unit_ref, inverse_ref, total, *rest
):
    bufs, (send, recv) = rest[:7], rest[7:]
    links = Links(send, recv)
    links.barrier()

    def compute(pair):
        rows = jnp.concatenate([heads_ref[pl.ds(links.first_row(s), ROWS)] for s in pair], axis=0)
        result = dot(rows, w_ref[...]).astype(BF16)
        for i, slot in enumerate(pair):
            bufs[0][slot] = result[i * ROWS : (i + 1) * ROWS]

    scatter(links, bufs, compute, total)

    def finish(at):
        unit, inverse = norm_parts(deep_alpha * x_ref[at].astype(F32) + total[at])
        unit_ref[at] = unit
        inverse_ref[at] = jnp.broadcast_to(inverse, (16, 128))
        normed_ref[at] = unit * gain_ref[...] + bias_ref[...]

    by_chunks(finish)


def load_weights(w_hbm, w_vmem, sem, parts):
    copies = [
        pltpu.make_async_copy(
            w_hbm.at[d, pl.ds(0, parts)], w_vmem.at[:, :, pl.ds(d * 16, 16)], sem.at[d]
        )
        for d in range(16)
    ]
    for copy in copies:
        copy.start()
    return copies


def feed_kernel(
    normed_ref, cot_ref, weight_ref, w_hbm, gain_ref, bias_ref,
    out_ref, all_ref, hidden_ref, gz_all_ref, ggu_ref, gz_ref, vec_ref,
    w, act, slope, total, w_sem, *rest,
):
    bufs, (send, recv) = rest[:7], rest[7:]
    links = Links(send, recv)
    loads = load_weights(w_hbm, w, w_sem, 3)

    def to_low(at):
        all_ref[0, at] = normed_ref[at].astype(BF16)

    by_chunks(to_low)
    links.barrier()
    for copy in loads:
        copy.wait()

    def forward(pair):
        rows = pair_of(all_ref, pair)
        for c in range(0, COLS, 256):
            cols = slice(c, c + 256)
            gate = dot(rows, w[0, :, :, cols].reshape(WIDE, 256))
            up = dot(rows, w[1, :, :, cols].reshape(WIDE, 256))
            bell = 0.5 + 0.5 * lax.erf(gate * np.float32(np.sqrt(0.5)))
            gelu = gate * bell
            turn = bell + gate * (jnp.exp(-0.5 * gate * gate) * np.float32(1.0 / np.sqrt(2.0 * np.pi)))
            hidden = (gelu * up).astype(BF16)
            turn = turn * up
            for i, slot in enumerate(pair):
                part = slice(i * ROWS, (i + 1) * ROWS)
                act[slot, :, cols] = gelu[part]
                slope[slot, :, cols] = turn[part]
                hidden_ref[slot, :, cols] = hidden[part]

    gather(links, all_ref, forward)

    def compute(pair):
        rows = pair_of(hidden_ref, pair)
        for d in range(8):
            result = dot_t(rows, w[2, d]).astype(BF16)
            for i, slot in enumerate(pair):
                bufs[0][slot, :, d * 256 : d * 256 + 256] = result[i * ROWS : (i + 1) * ROWS]

    scatter(links, bufs, compute, total)
    vec_ref[...] = jnp.zeros_like(vec_ref)

    def finish(at):
        unit, inverse = norm_parts(deep_alpha * normed_ref[at] + total[at])
        out_ref[at] = (unit * gain_ref[...] + bias_ref[...]).astype(BF16)
        grad = cot_ref[at].astype(F32) * weight_ref[0]
        grad_z = norm_backward(grad, unit, inverse, gain_ref[...])
        gz_ref[at] = grad_z
        gz_all_ref[0, at] = grad_z.astype(BF16)
        vec_ref[0] += rows8(grad * unit)
        vec_ref[1] += rows8(grad)

    by_chunks(finish)

    def backward(pair):
        rows = pair_of(gz_all_ref, pair)
        for c in range(0, COLS, 256):
            cols = slice(c, c + 256)
            grad_hidden = dot(rows, w[2, :, :, cols].reshape(WIDE, 256))
            for i, slot in enumerate(pair):
                part = grad_hidden[i * ROWS : (i + 1) * ROWS]
                ggu_ref[slot, :, cols] = (part * slope[slot, :, cols]).astype(BF16)
                ggu_ref[slot, :, COLS + c : COLS + c + 256] = (part * act[slot, :, cols]).astype(BF16)

    gather(links, gz_all_ref, backward)


def feed_back_kernel(
    ggu_ref, gz_ref, w_hbm, unit_ref, inverse_ref, gain_ref, w_out_ref,
    gz1_ref, all_ref, grad_heads_ref, vec_ref,
    w, total, w_sem, *rest,
):
    bufs, (send, recv) = rest[:7], rest[7:]
    links = Links(send, recv)
    loads = load_weights(w_hbm, w, w_sem, 2)
    links.barrier()
    for copy in loads:
        copy.wait()

    def compute(pair):
        rows = pair_of(ggu_ref, pair)
        for d in range(8):
            result = dot_t(rows[:, :COLS], w[0, d]) + dot_t(rows[:, COLS:], w[1, d])
            result = result.astype(BF16)
            for i, slot in enumerate(pair):
                bufs[0][slot, :, d * 256 : d * 256 + 256] = result[i * ROWS : (i + 1) * ROWS]

    scatter(links, bufs, compute, total)
    vec_ref[...] = jnp.zeros_like(vec_ref)

    def finish(at):
        grad = deep_alpha * gz_ref[at] + total[at]
        unit = unit_ref[at]
        grad_z = norm_backward(grad, unit, inverse_ref[at][:, 0:1], gain_ref[...])
        gz1_ref[at] = grad_z
        all_ref[0, at] = grad_z.astype(BF16)
        vec_ref[0] += rows8(grad * unit)
        vec_ref[1] += rows8(grad)

    by_chunks(finish)

    def work(pair):
        result = dot_t(pair_of(all_ref, pair), w_out_ref[...]).astype(BF16)
        for i, slot in enumerate(pair):
            grad_heads_ref[pl.ds(links.first_row(slot), ROWS)] = result[i * ROWS : (i + 1) * ROWS]

    gather(links, all_ref, work)


def input_kernel(dq_ref, dk_ref, dv_ref, w_ref, gz1_ref, out_ref, total, *rest):
    bufs, (send, recv) = rest[:7], rest[7:]
    links = Links(send, recv)
    links.barrier()

    def compute(pair):
        result = 0.0
        for part, ref in enumerate((dq_ref, dk_ref, dv_ref)):
            rows = jnp.concatenate([ref[pl.ds(links.first_row(s), ROWS)] for s in pair], axis=0)
            result = result + dot_t(rows, w_ref[:, part * 256 : part * 256 + 256])
        result = result.astype(BF16)
        for i, slot in enumerate(pair):
            bufs[0][slot] = result[i * ROWS : (i + 1) * ROWS]

    scatter(links, bufs, compute, total)

    def finish(at):
        out_ref[at] = deep_alpha * gz1_ref[at] + total[at]

    by_chunks(finish)


def feed_weight_kernel(normed_ref, gz_ref, ggu_ref, hidden_ref, out_ref):
    gate_up = dot_rows(normed_ref[...], ggu_ref[...]).astype(BF16)
    down = dot_rows(gz_ref[...], hidden_ref[...]).astype(BF16)
    out_ref[:, 0, 0] = gate_up[:, :COLS].reshape(16, 16, COLS)
    out_ref[:, 1, 0] = gate_up[:, COLS:].reshape(16, 16, COLS)
    out_ref[:, 2, 0] = down.reshape(16, 16, COLS)


def feed_weights(normed_all, gz_all, ggu, hidden):
    flat = lambda v: v.reshape(LEN, v.shape[-1])
    lhs = pl.BlockSpec((LEN, 256), lambda s: (0, s))
    return pl.pallas_call(
        feed_weight_kernel,
        name="feed_weights",
        grid=(8,),
        in_specs=[
            lhs,
            lhs,
            pl.BlockSpec((LEN, 2 * COLS), lambda s: (0, 0)),
            pl.BlockSpec((LEN, COLS), lambda s: (0, 0)),
        ],
        out_specs=pl.BlockSpec((16, 3, 1, 16, COLS), lambda s: (0, 0, s, 0, 0)),
        out_shape=jax.ShapeDtypeStruct((16, 3, 8, 16, COLS), BF16),
        compiler_params=pltpu.CompilerParams(vmem_limit_bytes=VMEM_BYTES),
    )(flat(normed_all), flat(gz_all), flat(ggu), flat(hidden))


def in_order(values):
    seq = lax.axis_index("seq")
    y, z_hi = seq // 2, seq % 2
    place = jnp.array([0, 2, 3, 1], jnp.int32)
    position = jnp.arange(8, dtype=jnp.int32)
    slot = (position % 2 ^ z_hi) * 4 + place[(position // 2 - y) % 4]
    return jnp.take(values, slot, axis=0)


def on_device(
    tokens, cotangent, w_qkv, w_out, w_gate_up, w_down,
    attn_gain, attn_bias, ffn_gain, ffn_bias, prefix_len, clusters,
):
    x = tokens.reshape(ROWS, WIDE)
    cot = cotangent.reshape(ROWS, WIDE)
    dp = lax.axis_index("dp")
    own_id = lax.dynamic_slice_in_dim(clusters, dp, 1)
    seq_weight = 1.0 / jnp.sum((own_id[:, None] == clusters[None, :]).astype(F32), axis=1)
    cosine, sine = (jnp.asarray(t) for t in rotary_tables(LEN, HEAD_DIM))
    row = lambda v: v.reshape(1, WIDE)
    ff_total = w_down.shape[1]
    pad = 8 * COLS - ff_total

    own_rows = lax.dynamic_slice_in_dim(w_gate_up, dp * 16, 16, axis=0)
    own_down = lax.dynamic_slice_in_dim(w_down, dp * 16, 16, axis=0)
    piece = jnp.concatenate([own_rows.transpose(1, 0, 2), own_down[None]], axis=0)
    piece = jnp.pad(piece, ((0, 0), (0, 0), (0, pad))).reshape(3, 16, 8, COLS).transpose(2, 0, 1, 3)
    piece = lax.all_to_all(piece, "seq", split_axis=0, concat_axis=0, tiled=True)
    piece = piece.transpose(1, 0, 2, 3)
    ffn_w = lax.all_gather(piece, "dp", axis=0)

    w_in = w_qkv.reshape(WIDE, 768)
    tokens_all, q, k, v = call(
        project_kernel, "project", 0,
        [((8, ROWS, WIDE), BF16)] + [((LEN, 256), BF16)] * 3,
        (x, w_in, cosine, sine), "vvvv", (), GATHER_COPIES, 2 * LEN * WIDE * 768,
    )
    heads_out, lse = attend(prefix_len, q, k, v)
    normed, unit_one, inverse_one = call(
        attended_kernel, "attended", 1,
        [((ROWS, WIDE), F32), ((ROWS, WIDE), F32), ((ROWS, 128), F32)],
        (heads_out, w_out, x, row(attn_gain), row(attn_bias)), "vvvvv",
        (pltpu.VMEM((ROWS, WIDE), F32), *SCATTER_SCRATCH), SCATTER_COPIES, 2 * LEN * WIDE * 256,
    )
    weight_scratch = lambda n: pltpu.VMEM((n, 8, 256, COLS), BF16)
    output, normed_all, hidden, gz_all, ggu, grad_z2, ffn_vec = call(
        feed_kernel, "feed", 2,
        [
            ((ROWS, WIDE), BF16), ((8, ROWS, WIDE), BF16), ((8, ROWS, COLS), BF16),
            ((8, ROWS, WIDE), BF16), ((8, ROWS, 2 * COLS), BF16), ((ROWS, WIDE), F32),
            ((2, 8, WIDE), F32),
        ],
        (normed, cot, seq_weight, ffn_w, row(ffn_gain), row(ffn_bias)), "vvshvv",
        (
            weight_scratch(3), pltpu.VMEM((8, ROWS, COLS), F32), pltpu.VMEM((8, ROWS, COLS), F32),
            pltpu.VMEM((ROWS, WIDE), F32), pltpu.SemaphoreType.DMA((16,)), *SCATTER_SCRATCH,
        ),
        2 * GATHER_COPIES + SCATTER_COPIES, 2 * LEN * WIDE * COLS * 4,
    )
    ffn_grad = feed_weights(normed_all, gz_all, ggu, hidden)
    ffn_part = lax.psum_scatter(ffn_grad, "dp", scatter_dimension=0, tiled=False)
    grad_z1, gz1_all, grad_heads, attn_vec = call(
        feed_back_kernel, "feed_back", 3,
        [((ROWS, WIDE), F32), ((8, ROWS, WIDE), BF16), ((LEN, 256), BF16), ((2, 8, WIDE), F32)],
        (ggu, grad_z2, ffn_w, unit_one, inverse_one, row(attn_gain), w_out), "vvhvvvv",
        (
            weight_scratch(2), pltpu.VMEM((ROWS, WIDE), F32), pltpu.SemaphoreType.DMA((16,)),
            *SCATTER_SCRATCH,
        ),
        GATHER_COPIES + SCATTER_COPIES, 2 * LEN * WIDE * COLS * 2,
    )
    dq, dk, dv = attend_back(prefix_len, q, k, v, grad_heads, lse, cosine, sine)
    (input_grad,) = call(
        input_kernel, "input", 4, [((ROWS, WIDE), F32)],
        (dq, dk, dv, w_in, grad_z1), "vvvvv",
        (pltpu.VMEM((ROWS, WIDE), F32), *SCATTER_SCRATCH), SCATTER_COPIES, 2 * LEN * WIDE * 768,
    )

    tokens_rows = in_order(tokens_all).reshape(LEN, WIDE)
    gz1_rows = in_order(gz1_all).reshape(LEN, WIDE)
    grad_project = jnp.concatenate([dq, dk, dv], axis=1)
    qkv_grad = jnp.einsum("td,tc->dc", tokens_rows, grad_project, preferred_element_type=F32)
    out_grad = jnp.einsum("th,td->hd", heads_out, gz1_rows, preferred_element_type=F32)
    vec = jnp.concatenate([attn_vec.sum(1), ffn_vec.sum(1)], axis=0)
    vec = lax.psum_scatter(vec, "seq", scatter_dimension=1, tiled=True)
    vec = lax.psum(vec, "dp")

    def over_dp(value):
        part = lax.psum_scatter(value.astype(BF16), "dp", scatter_dimension=0, tiled=True)
        return lax.all_gather(part, "dp", axis=0, tiled=True).astype(F32)

    grad_qkv = over_dp(qkv_grad).reshape(WIDE, 3, 256)
    grad_out = over_dp(out_grad)

    ffn_part = ffn_part.transpose(1, 0, 2, 3)
    ffn_part = lax.all_to_all(ffn_part, "seq", split_axis=0, concat_axis=0, tiled=True)
    ffn_whole = lax.all_gather(ffn_part, "dp", axis=0)
    ffn_whole = ffn_whole.transpose(0, 3, 2, 1, 4).reshape(256, 3, 8 * COLS)[:, :, :ff_total]
    ffn_whole = ffn_whole.astype(F32)
    return (
        output.reshape(tokens.shape),
        input_grad.reshape(tokens.shape),
        grad_qkv,
        grad_out,
        ffn_whole[:, :2],
        ffn_whole[:, 2],
        vec[0],
        vec[1],
        vec[2],
        vec[3],
    )


def solution(mesh):
    return jax.shard_map(
        on_device,
        mesh=mesh,
        in_specs=(
            P("seq", "dp", None), P("seq", "dp", None), P(None, None, "seq"), P("seq", None),
            P("seq", None, None), P("seq", None), P(), P(), P(), P(), P("dp"), P(),
        ),
        out_specs=(
            P("seq", "dp", None), P("seq", "dp", None), P(None, None, "seq"), P("seq", None),
            P("seq", None, None), P("seq", None), P("seq"), P("seq"), P("seq"), P("seq"),
        ),
        check_vma=False,
    )
```

```python
import functools

import jax
import jax.numpy as jnp
import numpy as np
from jax import lax
from jax.experimental import pallas as pl
from jax.experimental.pallas import tpu as pltpu
from jax.sharding import PartitionSpec as P

MESH = pl.DeviceIdType.MESH
F32, BF16 = jnp.float32, jnp.bfloat16
HEAD_DIM = 128
ROWS = 128
WIDE = 2048
COLS = 768
LEN = 1024
VMEM_BYTES = 60 * 1024 * 1024
deep_alpha = 48.0**0.25
norm_eps = 1e-05
rotary_base = 10000.0


def rotary_tables(length, head_width):
    half_width = head_width // 2
    position = np.arange(length, dtype=np.float64)
    inverse = rotary_base ** (-np.arange(half_width, dtype=np.float64) * 2.0 / head_width)
    angles = position[:, None] * inverse[None, :]
    cosine_table = np.cos(angles)
    sine_table = np.sin(angles)
    return (
        np.concatenate([cosine_table, cosine_table], axis=1).astype(np.float32),
        np.concatenate([-sine_table, sine_table], axis=1).astype(np.float32),
    )


FF = 704
PART = 176


class Links:
    def __init__(self, send, recv):
        self.send, self.recv, self.count = send, recv, 0
        dp, seq = lax.axis_index("dp"), lax.axis_index("seq")
        y, z_hi = seq // 2, lax.rem(seq, 2)
        z_lo, x, core = dp // 8, lax.rem(dp // 2, 4), lax.rem(dp, 2)
        self.y, self.z_hi, self.z_lo, self.x, self.core = y, z_hi, z_lo, x, core
        self.z = z_hi * 2 + z_lo

    def to(self, x=0, y=0, z=0, sibling=False):
        z_hi, z_lo = self.z_at(z)
        x, y = lax.rem(self.x + x, 4), lax.rem(self.y + y, 4)
        core = 1 - self.core if sibling else self.core
        return (z_lo * 8 + x * 2 + core, y * 2 + z_hi)

    def z_at(self, offset):
        z = lax.rem(self.z + offset, 4)
        return z // 2, lax.rem(z, 2)

    def part(self, offset):
        return pl.ds(pl.multiple_of(lax.rem(self.x + offset, 4) * PART, 16), PART)

    def barrier(self, *where):
        gate = pltpu.get_barrier_semaphore()
        for device in where:
            pl.semaphore_signal(gate, inc=1, device_id=device, device_id_type=MESH)
        pl.semaphore_wait(gate, len(where))

    def start(self, src, dst, where):
        copy = pltpu.make_async_remote_copy(
            src_ref=src,
            dst_ref=dst,
            send_sem=self.send.at[self.count],
            recv_sem=self.recv.at[self.count],
            device_id=where,
            device_id_type=MESH,
        )
        self.count += 1
        copy.start()
        return copy

    def first_row(self, slot):
        step = (0, 3, 1, 2)[slot % 4]
        half = self.z_hi if slot < 4 else 1 - self.z_hi
        return pl.multiple_of((lax.rem(self.y + step, 4) * 2 + half) * ROWS, ROWS)


def together(*tasks):
    due = [[next(task), i, task] for i, task in enumerate(tasks)]
    while due:
        due.sort(key=lambda entry: entry[:2])
        try:
            due[0][0] = next(due[0][2])
        except StopIteration:
            due.pop(0)


def received(*copies):
    for copy in copies:
        copy.wait_recv()


def sent(copies):
    for copy in copies:
        copy.wait_send()


H0, H1 = pl.ds(0, 64), pl.ds(64, 64)


def gather(links, buf, work):
    up, down, across = links.to(y=1), links.to(y=3), links.to(z=2)
    copies = []

    def send(slot, rows, dst, where):
        copies.append(links.start(buf.at[slot, rows], buf.at[dst, rows], where))
        return copies[-1]

    u0, d1 = send(0, H0, 1, up), send(0, H1, 2, down)
    z0, z1 = send(0, H0, 4, across), send(0, H1, 4, across)
    u1, d0 = send(0, H1, 1, up), send(0, H0, 2, down)
    yield 6
    received(u0)
    fu = send(1, H0, 3, up)
    received(d1)
    fd = send(2, H1, 3, down)
    yield 12
    received(z0)
    pu0 = send(4, H0, 5, up)
    received(z1)
    pd1 = send(4, H1, 6, down)
    pu1, pd0 = send(4, H1, 5, up), send(4, H0, 6, down)
    received(u1, d0)
    work((0, 1))
    yield 19
    received(fu, fd)
    work((2, 3))
    yield 24
    received(pu0)
    gu = send(5, H0, 7, up)
    received(pd1)
    gd = send(6, H1, 7, down)
    yield 29
    received(pu1, pd0)
    work((4, 5))
    yield 36
    received(gu, gd)
    work((6, 7))
    sent(copies)


def gather_near(links, buf, work):
    up, down, side = links.to(y=1), links.to(y=3), links.to(sibling=True)
    copies = []

    def send(slot, rows, dst, where):
        copies.append(links.start(buf.at[slot, rows], buf.at[dst, rows], where))
        return copies[-1]

    every = pl.ds(0, ROWS)
    u0, d1 = send(0, H0, 1, up), send(0, H1, 2, down)
    u1, d0 = send(0, H1, 1, up), send(0, H0, 2, down)
    s0 = send(0, every, 4, side)
    yield 1
    received(s0)
    work((0, 4))
    yield 6
    received(u0)
    fu = send(1, H0, 3, up)
    received(d1)
    fd = send(2, H1, 3, down)
    yield 11
    received(u1)
    s1 = send(1, every, 5, side)
    received(d0)
    s2 = send(2, every, 6, side)
    work((1, 2))
    yield 13
    received(s1, s2)
    work((5, 6))
    yield 17
    received(fu)
    s30 = send(3, H0, 7, side)
    received(fd)
    s31 = send(3, H1, 7, side)
    yield 18
    received(s30, s31)
    work((3, 7))
    sent(copies)


A, B = pl.ds(0, 80), pl.ds(80, 48)
A0, A1 = pl.ds(0, 48), pl.ds(48, 32)
B0, B1 = pl.ds(80, 16), pl.ds(96, 32)
SCATTER_SCRATCH = (
    pltpu.VMEM((8, ROWS, WIDE), BF16),
    pltpu.VMEM((4, 48, WIDE), BF16),
    pltpu.VMEM((48, WIDE), BF16),
    pltpu.VMEM((2, 48, WIDE), BF16),
    pltpu.VMEM((2, 80, WIDE), BF16),
    pltpu.VMEM((2, 2, 80, WIDE), BF16),
    pltpu.VMEM((80, WIDE), BF16),
)


def add_rows(target, slot, rows, *others):
    value = target[slot, rows].astype(F32)
    for other in others:
        value = value + other.astype(F32)
    target[slot, rows] = value.astype(BF16)


def scatter(links, bufs, compute, total):
    sums, from_z, b_far, b_near, a_far, a_near, a_z = bufs
    up, down, across = links.to(y=1), links.to(y=3), links.to(z=2)
    copies = []

    def send(src, dst, where):
        copies.append(links.start(src, dst, where))
        return copies[-1]

    def far_a(o):
        half = o // 4
        return (
            send(sums.at[o + 3, A0], a_far.at[half, pl.ds(0, 48)], up),
            send(sums.at[o + 3, A1], a_far.at[half, pl.ds(48, 32)], down),
        )

    def near_a(o, far):
        half = o // 4
        received(far[0])
        add_rows(sums, o + 2, A0, a_far[half, 0:48])
        one = send(sums.at[o + 2, A], a_near.at[half, 0], up)
        received(far[1])
        add_rows(sums, o + 1, A1, a_far[half, 48:80])
        return one, send(sums.at[o + 1, A], a_near.at[half, 1], down)

    def cross_b(j):
        return send(sums.at[4 + j, B], from_z.at[j], across)

    compute((7, 3))
    z3 = cross_b(3)
    far_other = far_a(4)
    far_own = far_a(0)
    compute((5, 6))
    z1, z2 = cross_b(1), cross_b(2)
    compute((1, 2))
    yield 8
    received(z3)
    add_rows(sums, 3, B, from_z[3])
    far_b = (
        send(sums.at[3, B0], b_far.at[pl.ds(0, 16)], up),
        send(sums.at[3, B1], b_far.at[pl.ds(16, 32)], down),
    )
    near_other = near_a(4, far_other)
    compute((4, 0))
    z0 = cross_b(0)
    yield 12
    near_own = near_a(0, far_own)
    yield 18
    received(*near_other)
    add_rows(sums, 4, A, a_near[1, 0], a_near[1, 1])
    z_a = send(sums.at[4, A], a_z, across)
    yield 20
    received(z2)
    add_rows(sums, 2, B, from_z[2])
    received(far_b[0])
    add_rows(sums, 2, B0, b_far[0:16])
    near_b0 = send(sums.at[2, B], b_near.at[0], up)
    received(z1)
    add_rows(sums, 1, B, from_z[1])
    received(far_b[1])
    add_rows(sums, 1, B1, b_far[16:48])
    near_b1 = send(sums.at[1, B], b_near.at[1], down)
    yield 27
    received(z0, near_b0, near_b1)
    total[80:128] = (
        sums[0, B].astype(F32)
        + from_z[0].astype(F32)
        + b_near[0].astype(F32)
        + b_near[1].astype(F32)
    )
    received(*near_own)
    yield 30
    received(z_a)
    total[0:80] = (
        sums[0, A].astype(F32)
        + a_near[0, 0].astype(F32)
        + a_near[0, 1].astype(F32)
        + a_z[...].astype(F32)
    )
    sent(copies)


NEAR_SCRATCH = (
    pltpu.VMEM((8, ROWS, WIDE), BF16),
    pltpu.VMEM((4, ROWS, WIDE), BF16),
    pltpu.VMEM((ROWS, WIDE), BF16),
    pltpu.VMEM((2, ROWS, WIDE), BF16),
)


def scatter_near(links, bufs, compute, total):
    sums, from_side, far, near = bufs
    up, down, side = links.to(y=1), links.to(y=3), links.to(sibling=True)
    copies = []

    def send(src, dst, where):
        copies.append(links.start(src, dst, where))
        return copies[-1]

    every = pl.ds(0, ROWS)
    compute((7, 3))
    s3 = send(sums.at[7], from_side.at[3], side)
    compute((5, 6))
    s1 = send(sums.at[5], from_side.at[1], side)
    s2 = send(sums.at[6], from_side.at[2], side)
    received(s3)
    add_rows(sums, 3, every, from_side[3])
    fu = send(sums.at[3, H0], far.at[H0], up)
    fd = send(sums.at[3, H1], far.at[H1], down)
    compute((1, 2))
    received(s1, s2)
    add_rows(sums, 2, every, from_side[2])
    nu1 = send(sums.at[2, H1], near.at[0, H1], up)
    add_rows(sums, 1, every, from_side[1])
    nd0 = send(sums.at[1, H0], near.at[1, H0], down)
    compute((4, 0))
    s0 = send(sums.at[4], from_side.at[0], side)
    yield 8
    received(fu)
    add_rows(sums, 2, H0, far[0:64])
    nu0 = send(sums.at[2, H0], near.at[0, H0], up)
    received(fd)
    add_rows(sums, 1, H1, far[64:128])
    nd1 = send(sums.at[1, H1], near.at[1, H1], down)
    yield 17
    received(s0, nu1, nd0, nu0, nd1)
    total[...] = (
        sums[0].astype(F32)
        + from_side[0].astype(F32)
        + near[0].astype(F32)
        + near[1].astype(F32)
    )
    sent(copies)


Y0, Y1 = pl.ds(0, 2), pl.ds(2, 2)
GU = pl.ds(0, 2)


def spread(links, piece, w, local):
    xp, xm, zp, zm = links.to(x=1), links.to(x=3), links.to(z=1), links.to(z=3)
    copies = []

    def at(k, z, x, y=pl.ds(0, 4)):
        z_hi, z_lo = links.z_at(z)
        return w.at[k, z_hi, y, z_lo, links.part(x)]

    def send(ref, where):
        copies.append(links.start(ref, ref, where))
        return copies[-1]

    def own():
        return w.at[:, links.z_hi, links.y, links.z_lo, links.part(0)]

    keep = pltpu.make_async_copy(piece.at[links.y], own(), local)
    keep.start()
    first = []
    for step in (2, 1, 3):
        copies.append(
            links.start(piece.at[lax.rem(links.y + step, 4)], own(), links.to(y=step))
        )
        first.append(copies[-1])
    yield 9
    keep.wait()
    received(*first)
    zu, zd = send(at(GU, 0, 0), zp), send(at(GU, 0, 0), zm)
    du, dd = send(at(2, 0, 0), xp), send(at(2, 0, 0), xm)
    gx = [(send(at(GU, 0, 0), xp), send(at(GU, 0, 0), xm))]
    dz = [(send(at(2, 0, 0), zp), send(at(2, 0, 0), zm))]
    yield 16
    received(du)
    fdu = send(at(2, 0, 3, Y0), xp)
    dz.append((send(at(2, 0, 3), zp), send(at(2, 0, 3), zm)))
    received(dd)
    fdd = send(at(2, 0, 1, Y1), xm)
    dz.append((send(at(2, 0, 1), zp), send(at(2, 0, 1), zm)))
    yield 20
    received(zu)
    fzu = send(at(0, 3, 0), zp)
    gx.append((send(at(GU, 3, 0), xp), send(at(GU, 3, 0), xm)))
    received(zd)
    fzd = send(at(1, 1, 0), zm)
    gx.append((send(at(GU, 1, 0), xp), send(at(GU, 1, 0), xm)))
    yield 25
    received(*gx[0])
    gf = [(send(at(0, 0, 3), xp), send(at(1, 0, 1), xm))]
    yield 28
    received(*dz[0])
    df = [(send(at(2, 3, 0, Y0), zp), send(at(2, 1, 0, Y1), zm))]
    received(fdu, fdd)
    dz.append((send(at(2, 0, 2), zp), send(at(2, 0, 2), zm)))
    yield 30
    received(fzu, fzd)
    gx.append((send(at(GU, 2, 0), xp), send(at(GU, 2, 0), xm)))
    yield 35
    received(*gx[1])
    gf.append((send(at(0, 3, 3), xp), send(at(1, 3, 1), xm)))
    received(*dz[1])
    df.append((send(at(2, 3, 3, Y0), zp), send(at(2, 1, 3, Y1), zm)))
    yield 42
    received(*gx[2])
    gf.append((send(at(0, 1, 3), xp), send(at(1, 1, 1), xm)))
    received(*dz[2])
    df.append((send(at(2, 3, 1, Y0), zp), send(at(2, 1, 1, Y1), zm)))
    yield 48
    received(*dz[3])
    df.append((send(at(2, 3, 2, Y0), zp), send(at(2, 1, 2, Y1), zm)))
    received(*gx[3])
    gf.append((send(at(0, 2, 3), xp), send(at(1, 2, 1), xm)))
    yield 60
    for pair in gf + df:
        received(*pair)
    sent(copies)


BLOCKS = pltpu.VMEM((2, 2, 4, 2, PART, 128), BF16)
REDUCE_SCRATCH = (
    pltpu.VMEM((3, 2, 4, 2, FF, 128), BF16),
    BLOCKS,
    pltpu.VMEM((2, 2, 2, 4, 2, PART, 128), BF16),
    pltpu.VMEM((2, 4, PART, 128), BF16),
    pltpu.VMEM((2, 2, 4, PART, 128), BF16),
    pltpu.VMEM((4, FF, 128), BF16),
    pltpu.VMEM((2, 4, FF, 128), BF16),
    pltpu.VMEM((4, PART, 128), BF16),
    pltpu.VMEM((2, 4, PART, 128), BF16),
)


def accumulate(count, target, *others):
    def step(i, carry):
        ref = target(i)
        value = ref[...].astype(F32)
        for other in others:
            value = value + other(i)[...].astype(F32)
        ref[...] = value.astype(BF16)
        return carry

    lax.fori_loop(0, count, step, 0)


def reduce(links, bufs, shard):
    g, fx, nx, fz, nz, fz2, nz2, fx2, nx2 = bufs
    xp, xm, zp, zm = links.to(x=1), links.to(x=3), links.to(z=1), links.to(z=3)
    copies = []
    every = pl.ds(0, 4)

    def send(src, dst, where):
        copies.append(links.start(src, dst, where))
        return copies[-1]

    def along_x(k, x):
        return g.at[k, :, :, :, links.part(x)]

    def block_x(k, x):
        return lambda i: g.at[k, i // 8, lax.rem(i // 2, 4), lax.rem(i, 2), links.part(x)]

    def plain(ref):
        return lambda i: ref.at[i // 8, lax.rem(i // 2, 4), lax.rem(i, 2)]

    def along_z(k, z, y=every, rows=pl.ds(0, FF)):
        z_hi, z_lo = links.z_at(z)
        return g.at[k, z_hi, y, z_lo, rows]

    def block_z(k, z, rows, first=0):
        z_hi, z_lo = links.z_at(z)
        return lambda i: g.at[k, z_hi, i + first, z_lo, rows]

    def shift(ref, first=0):
        return lambda i: ref.at[i + first]

    here = links.part(0)
    whole = pl.ds(0, FF)
    c1, c2 = send(along_x(0, 2), fx.at[0], xp), send(along_x(1, 2), fx.at[1], xm)
    e1 = send(along_z(2, 2, Y0), fz2.at[Y0], zp)
    e2 = send(along_z(2, 2, Y1), fz2.at[Y1], zm)
    c3, c4 = send(along_x(1, 1), nx.at[0, 1], xp), send(along_x(0, 3), nx.at[1, 0], xm)
    e3 = send(along_z(2, 1, Y1), nz2.at[0, Y1], zp)
    e4 = send(along_z(2, 3, Y0), nz2.at[1, Y0], zm)
    yield 9
    received(e1)
    accumulate(2, block_z(2, 1, whole), shift(fz2))
    e5 = send(along_z(2, 1, Y0), nz2.at[0, Y0], zp)
    received(e2)
    accumulate(2, block_z(2, 3, whole, 2), shift(fz2, 2))
    e6 = send(along_z(2, 3, Y1), nz2.at[1, Y1], zm)
    yield 17
    received(c1)
    accumulate(16, block_x(0, 1), plain(fx.at[0]))
    c5 = send(along_x(0, 1), nx.at[0, 0], xp)
    received(c2)
    accumulate(16, block_x(1, 3), plain(fx.at[1]))
    c6 = send(along_x(1, 3), nx.at[1, 1], xm)
    yield 26
    received(e3, e4, e5, e6)
    accumulate(4, block_z(2, 0, whole), shift(nz2.at[0]), shift(nz2.at[1]))
    d1 = send(along_z(2, 0, Y0, links.part(2)), fx2.at[Y0], xp)
    d2 = send(along_z(2, 0, Y1, links.part(2)), fx2.at[Y1], xm)
    d3 = send(along_z(2, 0, Y1, links.part(1)), nx2.at[0, Y1], xp)
    d4 = send(along_z(2, 0, Y0, links.part(3)), nx2.at[1, Y0], xm)
    yield 46
    received(c3, c4, c5, c6)
    for k in range(2):
        accumulate(16, block_x(k, 0), plain(nx.at[0, k]), plain(nx.at[1, k]))
    f1 = send(along_z(0, 2, every, here), fz.at[0], zp)
    f2 = send(along_z(1, 2, every, here), fz.at[1], zm)
    f3 = send(along_z(1, 1, every, here), nz.at[0, 1], zp)
    f4 = send(along_z(0, 3, every, here), nz.at[1, 0], zm)
    received(d1)
    accumulate(2, block_z(2, 0, links.part(1)), shift(fx2))
    d5 = send(along_z(2, 0, Y0, links.part(1)), nx2.at[0, Y0], xp)
    received(d2)
    accumulate(2, block_z(2, 0, links.part(3), 2), shift(fx2, 2))
    d6 = send(along_z(2, 0, Y1, links.part(3)), nx2.at[1, Y1], xm)
    yield 52
    received(f1)
    accumulate(4, block_z(0, 1, here), shift(fz.at[0]))
    f5 = send(along_z(0, 1, every, here), nz.at[0, 0], zp)
    received(f2)
    accumulate(4, block_z(1, 3, here), shift(fz.at[1]))
    f6 = send(along_z(1, 3, every, here), nz.at[1, 1], zm)
    yield 58
    received(d3, d4, d5, d6)
    accumulate(4, block_z(2, 0, here), shift(nx2.at[0]), shift(nx2.at[1]))
    received(f3, f4, f5, f6)
    for k in range(2):
        accumulate(4, block_z(k, 0, here), shift(nz.at[0, k]), shift(nz.at[1, k]))
    for k in range(3):
        shard[k] = along_z(k, 0, every, here)[...]
    sent(copies)


def regather(links, at, half, times):
    xp, xm, side = links.to(x=1), links.to(x=3), links.to(sibling=True)
    beside = (lax.rem(lax.axis_index("dp") + 8, 16), lax.axis_index("seq"))
    copies, sides = [], []

    def send(ref, where):
        copies.append(links.start(ref, ref, where))
        return copies[-1]

    def share(ref):
        sides.append(send(ref, side))

    z = send(at(0, 0), beside)
    near = [(send(at(0, 0), xp), send(at(0, 0), xm))]
    share(at(0, 0))
    yield times[0]
    received(z)
    near.append((send(at(1, 0), xp), send(at(1, 0), xm)))
    share(at(1, 0))
    for i in range(2):
        yield times[1 + 2 * i]
        received(near[i][0])
        far_up = send(half(at(i, 3), 0), xp)
        share(at(i, 3))
        received(near[i][1])
        far_down = send(half(at(i, 1), 1), xm)
        share(at(i, 1))
        yield times[2 + 2 * i]
        received(far_up, far_down)
        share(at(i, 2))
    received(*sides)
    sent(copies)


def collect(links, shard, out, local, late):
    copies = []

    def own(y):
        return out.at[:, y, links.core, links.z_lo, links.part(0)]

    keep = pltpu.make_async_copy(shard.at[:, links.y], own(links.y), local)
    keep.start()
    for step in (2, 1, 3):
        there = lax.rem(links.y + step, 4)
        copies.append(links.start(shard.at[:, there], own(links.y), links.to(y=step)))
    yield 7
    keep.wait()
    received(*copies)

    def at(z, x):
        return out.at[:, :, links.core, lax.rem(links.z_lo + z, 2), links.part(x)]

    def half(ref, i):
        return ref.at[:, pl.ds(2 * i, 2)]

    yield from regather(links, at, half, [t + late for t in (12, 18, 24, 32, 45)])
    sent(copies)


SHARE_SCRATCH = (
    pltpu.VMEM((2, 2, 4, 512, 256), BF16),
    pltpu.VMEM((2, 4, 512, 256), BF16),
    pltpu.VMEM((2, 512, 256), BF16),
    pltpu.VMEM((2, 2, 512, 256), BF16),
    pltpu.VMEM((512, 256), BF16),
)


def share(links, bufs, out, late):
    q, from_side, far, near, from_z = bufs
    xp, xm, side = links.to(x=1), links.to(x=3), links.to(sibling=True)
    beside = (lax.rem(lax.axis_index("dp") + 8, 16), lax.axis_index("seq"))
    core, z_lo = links.core, links.z_lo
    copies = []

    def send(src, dst, where):
        copies.append(links.start(src, dst, where))
        return copies[-1]

    def there(x):
        return lax.rem(links.x + x, 4)

    def rows(ref):
        return lambda i: ref.at[pl.ds(pl.multiple_of(i * 64, 64), 64)]

    s = send(q.at[1 - core], from_side, side)
    yield late
    received(s)
    for z in range(2):
        for x in range(4):
            accumulate(8, rows(q.at[core, z, x]), rows(from_side.at[z, x]))
    a1, a2 = send(q.at[core, 0, there(2)], far.at[0], xp), send(q.at[core, 1, there(2)], far.at[1], xm)
    a3 = send(q.at[core, 1, there(1)], near.at[0, 1], xp)
    a4 = send(q.at[core, 0, there(3)], near.at[1, 0], xm)
    yield late + 8
    received(a1)
    accumulate(8, rows(q.at[core, 0, there(1)]), rows(far.at[0]))
    a5 = send(q.at[core, 0, there(1)], near.at[0, 0], xp)
    received(a2)
    accumulate(8, rows(q.at[core, 1, there(3)]), rows(far.at[1]))
    a6 = send(q.at[core, 1, there(3)], near.at[1, 1], xm)
    yield late + 20
    received(a3, a4, a5, a6)
    for z in range(2):
        accumulate(8, rows(q.at[core, z, there(0)]), rows(near.at[0, z]), rows(near.at[1, z]))
    b = send(q.at[core, 1 - z_lo, there(0)], from_z, beside)
    yield late + 26
    received(b)

    def finish(i, carry):
        at = pl.ds(pl.multiple_of(i * 64, 64), 64)
        value = q[core, z_lo, links.x, at].astype(F32) + from_z[at].astype(F32)
        out[core, z_lo, links.x, at] = value.astype(BF16)
        return carry

    lax.fori_loop(0, 8, finish, 0)

    def at(z, x):
        return out.at[core, lax.rem(z_lo + z, 2), there(x)]

    def half(ref, i):
        return ref.at[pl.ds(256 * i, 256)]

    yield from regather(links, at, half, [t + late for t in (33, 36, 42, 46, 54)])
    sent(copies)


def agree(links, vec, bufs):
    y, x = links.y, links.x
    copies = []
    steps = (
        links.to(sibling=True),
        links.to(y=1 + 2 * lax.rem(y, 2)),
        links.to(y=2),
        links.to(z=2),
        links.to(x=1 + 2 * lax.rem(x, 2)),
        links.to(x=2),
        (lax.rem(lax.axis_index("dp") + 8, 16), lax.axis_index("seq")),
    )
    held, got = bufs
    held[0] = vec[...]
    for i, where in enumerate(steps):
        copies.append(links.start(held.at[i], got.at[i], where))
        yield 6 + 6 * i
        received(copies[-1])
        if i < len(steps) - 1:
            held[i + 1] = held[i] + got[i]
        else:
            vec[...] = held[i] + got[i]
    sent(copies)


def dot(a, b):
    return jnp.dot(a, b, preferred_element_type=F32)


def dot_t(a, b):
    return lax.dot_general(a, b, (((1,), (1,)), ((), ())), preferred_element_type=F32)


def dot_rows(a, b):
    return lax.dot_general(a, b, (((0,), (0,)), ((), ())), preferred_element_type=F32)


def pair_of(ref, pair):
    return jnp.concatenate([ref[pair[0]], ref[pair[1]]], axis=0)


def by_chunks(body):
    def step(i, carry):
        body(pl.ds(pl.multiple_of(i * 16, 16), 16))
        return carry

    lax.fori_loop(0, ROWS // 16, step, 0)


def norm_parts(row_total):
    center = row_total - jnp.mean(row_total, axis=-1, keepdims=True)
    spread = jnp.mean(center * center, axis=-1, keepdims=True)
    inverse = lax.rsqrt(spread + norm_eps)
    return center * inverse, inverse


def norm_backward(grad_result, unit, inverse, gain):
    grad_unit = grad_result * gain
    return inverse * (
        grad_unit
        - jnp.mean(grad_unit, axis=-1, keepdims=True)
        - unit * jnp.mean(grad_unit * unit, axis=-1, keepdims=True)
    )


def rows8(values):
    return values[0:8] + values[8:16]


VMEM = pl.BlockSpec(memory_space=pltpu.VMEM)
HBM = pl.BlockSpec(memory_space=pl.ANY)
SMEM = pl.BlockSpec(memory_space=pltpu.SMEM)
KINDS = {"v": VMEM, "s": SMEM, "h": HBM}


def call(body, name, ident, outs, operands, spaces, scratch, copies, flops=0):
    sems = [pltpu.SemaphoreType.DMA((copies,)), pltpu.SemaphoreType.DMA((copies,))]
    return pl.pallas_call(
        body,
        name=name,
        out_shape=tuple(jax.ShapeDtypeStruct(s, d) for s, d, _ in outs),
        in_specs=[KINDS[k] for k in spaces],
        out_specs=tuple(KINDS[k] for _, _, k in outs),
        scratch_shapes=[*scratch, *sems],
        compiler_params=pltpu.CompilerParams(
            collective_id=ident, has_side_effects=True, vmem_limit_bytes=VMEM_BYTES
        ),
        cost_estimate=pl.CostEstimate(flops=flops, bytes_accessed=20_000_000, transcendentals=0),
    )(*operands)


def piece_kernel(place_ref, gate_up_ref, down_ref, out_ref):
    chunk = (pl.program_id(0) * 2 + place_ref[0]) * 4 + place_ref[1]
    total = place_ref[3]
    row = lax.broadcasted_iota(jnp.int32, (PART, 128), 0) + chunk * PART
    inside = row < total
    both = gate_up_ref[...].astype(F32)
    out_ref[0, 0] = jnp.where(inside, both[:, 0], 0.0).astype(BF16)
    out_ref[0, 1] = jnp.where(inside, both[:, 1], 0.0).astype(BF16)
    out_ref[0, 2] = jnp.where(inside, down_ref[...].astype(F32), 0.0).astype(BF16)


def piece_of(gate_up, down, place):
    def chunk(y, place):
        return (y * 2 + place[0]) * 4 + place[1]

    return pl.pallas_call(
        piece_kernel,
        name="piece",
        grid_spec=pltpu.PrefetchScalarGridSpec(
            num_scalar_prefetch=1,
            grid=(4,),
            in_specs=[
                pl.BlockSpec((PART, 2, 128), lambda y, p: (chunk(y, p), 0, p[2])),
                pl.BlockSpec((PART, 128), lambda y, p: (chunk(y, p), p[2])),
            ],
            out_specs=pl.BlockSpec((1, 3, PART, 128), lambda y, p: (y, 0, 0, 0)),
        ),
        out_shape=jax.ShapeDtypeStruct((4, 3, PART, 128), BF16),
    )(place, gate_up, down)


def project_kernel(
    x_ref, w_ref, cos_ref, sin_ref, piece_ref, all_ref, q_ref, k_ref, v_ref, w_all_ref, local, send, recv
):
    links = Links(send, recv)
    all_ref[0] = x_ref[...]
    to = links.to
    links.barrier(to(y=1), to(y=3), to(z=2), to(y=2), to(x=1), to(x=3), to(z=1), to(z=3))

    def work(pair):
        rows = pair_of(all_ref, pair)
        for part, out in enumerate((q_ref, k_ref, v_ref)):
            result = dot(rows, w_ref[part])
            for i, slot in enumerate(pair):
                at = pl.ds(links.first_row(slot), ROWS)
                piece = result[i * ROWS : (i + 1) * ROWS]
                if part == 2:
                    out[at] = piece.astype(BF16)
                    continue
                cosine, sine = cos_ref[at], sin_ref[at]
                for head in range(2):
                    lanes = slice(head * 128, head * 128 + 128)
                    turned = piece[:, lanes] * cosine + pltpu.roll(piece[:, lanes], 64, 1) * sine
                    if part == 0:
                        turned = turned * HEAD_DIM**-0.5
                    out[at, lanes] = turned.astype(BF16)

    together(gather(links, all_ref, work), spread(links, piece_ref, w_all_ref, local))


def attend_kernel(prefix_ref, q_ref, k_ref, v_ref, out_ref, lse_ref):
    block = q_ref.shape[0]
    first = pl.program_id(1) * block
    scores = dot_t(k_ref[...], q_ref[...])
    key = lax.broadcasted_iota(jnp.int32, scores.shape, 0)
    query = lax.broadcasted_iota(jnp.int32, (1, block), 1) + first
    limit = jnp.maximum(query, prefix_ref[0] - 1)
    scores = jnp.where(key <= limit, scores, -1e30)
    peak = jnp.max(scores, axis=0, keepdims=True)
    exponent = jnp.exp(scores - peak)
    total = jnp.sum(exponent, axis=0, keepdims=True)
    weights = (exponent * (1.0 / total)).astype(BF16)
    out_ref[...] = dot_rows(weights, v_ref[...]).astype(BF16)
    lse_ref[0] = peak + jnp.log(total)


def attend(prefix, q, k, v):
    block = 512
    return pl.pallas_call(
        attend_kernel,
        name="attend",
        grid=(2, LEN // block),
        in_specs=[
            SMEM,
            pl.BlockSpec((block, 128), lambda h, b: (b, h)),
            pl.BlockSpec((LEN, 128), lambda h, b: (0, h)),
            pl.BlockSpec((LEN, 128), lambda h, b: (0, h)),
        ],
        out_specs=(
            pl.BlockSpec((block, 128), lambda h, b: (b, h)),
            pl.BlockSpec((1, 1, block), lambda h, b: (h, 0, b)),
        ),
        out_shape=(
            jax.ShapeDtypeStruct((LEN, 256), BF16),
            jax.ShapeDtypeStruct((2, 1, LEN), F32),
        ),
        compiler_params=pltpu.CompilerParams(vmem_limit_bytes=VMEM_BYTES),
    )(prefix, q, k, v)


def attend_back_kernel(
    prefix_ref, q_ref, k_ref, v_ref, g_ref, lse_ref, cos_ref, sin_ref, cosq_ref, sinq_ref,
    dq_ref, dk_ref, dv_ref, dk_sum, dv_sum
):
    block = q_ref.shape[0]
    step = pl.program_id(1)
    scores = dot_t(k_ref[...], q_ref[...])
    key = lax.broadcasted_iota(jnp.int32, scores.shape, 0)
    query = lax.broadcasted_iota(jnp.int32, (1, block), 1) + step * block
    limit = jnp.maximum(query, prefix_ref[0] - 1)
    weights = jnp.where(key <= limit, jnp.exp(scores - lse_ref[0]), 0.0)
    grad_weights = dot_t(v_ref[...], g_ref[...])
    inner = jnp.sum(weights * grad_weights, axis=0, keepdims=True)
    grad_scores = (weights * (grad_weights - inner)).astype(BF16)
    d_query = dot_rows(grad_scores, k_ref[...]) * HEAD_DIM**-0.5
    dq_ref[...] = (d_query * cosq_ref[...] - pltpu.roll(d_query, 64, 1) * sinq_ref[...]).astype(BF16)
    d_key = dot(grad_scores, q_ref[...])
    d_value = dot(weights.astype(BF16), g_ref[...])

    @pl.when(step == 0)
    def _():
        dk_sum[...] = d_key
        dv_sum[...] = d_value

    @pl.when(step > 0)
    def _():
        dk_sum[...] += d_key
        dv_sum[...] += d_value

    @pl.when(step == pl.num_programs(1) - 1)
    def _():
        total = dk_sum[...]
        dk_ref[...] = (total * cos_ref[...] - pltpu.roll(total, 64, 1) * sin_ref[...]).astype(BF16)
        dv_ref[...] = dv_sum[...].astype(BF16)


def attend_back(prefix, q, k, v, g, lse, cosine, sine):
    block = 512
    part = pl.BlockSpec((block, 128), lambda h, b: (b, h))
    whole = pl.BlockSpec((LEN, 128), lambda h, b: (0, h))
    table = pl.BlockSpec((LEN, 128), lambda h, b: (0, 0))
    table_part = pl.BlockSpec((block, 128), lambda h, b: (b, 0))
    return pl.pallas_call(
        attend_back_kernel,
        name="attend_back",
        grid=(2, LEN // block),
        in_specs=[
            SMEM, part, whole, whole, part,
            pl.BlockSpec((1, 1, block), lambda h, b: (h, 0, b)),
            table, table, table_part, table_part,
        ],
        out_specs=(part, whole, whole),
        out_shape=tuple(jax.ShapeDtypeStruct((LEN, 256), BF16) for _ in range(3)),
        scratch_shapes=[pltpu.VMEM((LEN, 128), F32), pltpu.VMEM((LEN, 128), F32)],
        compiler_params=pltpu.CompilerParams(vmem_limit_bytes=VMEM_BYTES),
    )(prefix, q, k, v, g, lse, cosine, sine, cosine, sine)


def attended_kernel(
    heads_ref, w_ref, x_ref, gain_ref, bias_ref, normed_ref, unit_ref, inverse_ref, total, *rest
):
    bufs, (send, recv) = rest[:7], rest[7:]
    links = Links(send, recv)
    links.barrier(links.to(y=1), links.to(y=3), links.to(z=2))

    def compute(pair):
        rows = jnp.concatenate([heads_ref[pl.ds(links.first_row(s), ROWS)] for s in pair], axis=0)
        result = dot(rows, w_ref[...]).astype(BF16)
        for i, slot in enumerate(pair):
            bufs[0][slot] = result[i * ROWS : (i + 1) * ROWS]

    together(scatter(links, bufs, compute, total))

    def finish(at):
        unit, inverse = norm_parts(deep_alpha * x_ref[at].astype(F32) + total[at])
        unit_ref[at] = unit
        inverse_ref[at] = jnp.broadcast_to(inverse, (16, 128))
        normed_ref[at] = unit * gain_ref[...] + bias_ref[...]

    by_chunks(finish)


def load_weights(w_hbm, w, sem, parts):
    copies = []
    for k in range(parts):
        for i in range(16):
            src = w_hbm.at[k, lax.rem(i // 2, 2), i // 4, lax.rem(i, 2)]
            copies.append(
                pltpu.make_async_copy(src, w.at[k, pl.ds(0, FF), pl.ds(i * 128, 128)], sem.at[k, i])
            )
    for copy in copies:
        copy.start()
    for k in range(parts):
        w[k, FF:COLS] = jnp.zeros((COLS - FF, WIDE), BF16)
    return copies


def feed_kernel(
    normed_ref, cot_ref, weight_ref, w_hbm, gain_ref, bias_ref,
    out_ref, all_ref, gz_all_ref, act_ref, gz_ref, vec_ref,
    w, gelu_ref, slope, total, w_sem, *rest,
):
    bufs, (send, recv) = rest[:4], rest[4:]
    links = Links(send, recv)
    loads = load_weights(w_hbm, w, w_sem, 3)

    def to_low(at):
        all_ref[0, at] = normed_ref[at].astype(BF16)

    by_chunks(to_low)
    links.barrier(links.to(y=1), links.to(y=3), links.to(sibling=True))
    for copy in loads:
        copy.wait()

    def forward(pair):
        rows = pair_of(all_ref, pair)
        for c in range(0, COLS, 256):
            cols = slice(c, c + 256)
            gate = dot_t(rows, w[0, cols])
            up = dot_t(rows, w[1, cols])
            bell = 0.5 + 0.5 * lax.erf(gate * np.float32(np.sqrt(0.5)))
            gelu = gate * bell
            turn = bell + gate * (jnp.exp(-0.5 * gate * gate) * np.float32(1.0 / np.sqrt(2.0 * np.pi)))
            hidden = (gelu * up).astype(BF16)
            turn = turn * up
            for i, slot in enumerate(pair):
                part = slice(i * ROWS, (i + 1) * ROWS)
                gelu_ref[slot, :, cols] = gelu[part]
                slope[slot, :, cols] = turn[part]
                act_ref[slot, :, 2 * COLS + c : 2 * COLS + c + 256] = hidden[part]

    together(gather_near(links, all_ref, forward))

    def compute(pair):
        rows = jnp.concatenate([act_ref[slot, :, 2 * COLS :] for slot in pair], axis=0)
        for d in range(0, WIDE, 512):
            result = dot(rows, w[2, :, d : d + 512]).astype(BF16)
            for i, slot in enumerate(pair):
                bufs[0][slot, :, d : d + 512] = result[i * ROWS : (i + 1) * ROWS]

    together(scatter_near(links, bufs, compute, total))
    vec_ref[...] = jnp.zeros_like(vec_ref)

    def finish(at):
        unit, inverse = norm_parts(deep_alpha * normed_ref[at] + total[at])
        out_ref[at] = (unit * gain_ref[...] + bias_ref[...]).astype(BF16)
        grad = cot_ref[at].astype(F32) * weight_ref[0]
        grad_z = norm_backward(grad, unit, inverse, gain_ref[...])
        gz_ref[at] = grad_z
        gz_all_ref[0, at] = grad_z.astype(BF16)
        vec_ref[0] += rows8(grad * unit)
        vec_ref[1] += rows8(grad)

    by_chunks(finish)

    def backward(pair):
        rows = pair_of(gz_all_ref, pair)
        for c in range(0, COLS, 256):
            cols = slice(c, c + 256)
            grad_hidden = dot_t(rows, w[2, cols])
            for i, slot in enumerate(pair):
                part = grad_hidden[i * ROWS : (i + 1) * ROWS]
                act_ref[slot, :, cols] = (part * slope[slot, :, cols]).astype(BF16)
                act_ref[slot, :, COLS + c : COLS + c + 256] = (part * gelu_ref[slot, :, cols]).astype(BF16)

    together(gather_near(links, gz_all_ref, backward))


def feed_back_kernel(
    act_ref, gz_ref, w_hbm, g_hbm, unit_ref, inverse_ref, gain_ref, w_out_ref,
    gz1_ref, all_ref, grad_heads_ref, vec_ref, shard_ref,
    w, total, w_sem, g_sem, *rest,
):
    bufs, more, (send, recv) = rest[:4], rest[4:13], rest[13:]
    links = Links(send, recv)
    loads = load_weights(w_hbm, w, w_sem, 2)
    for k in range(3):
        for i in range(16):
            dst = more[0].at[k, lax.rem(i // 2, 2), i // 4, lax.rem(i, 2)]
            src = g_hbm.at[k, pl.ds(0, FF), pl.ds(i * 128, 128)]
            loads.append(pltpu.make_async_copy(src, dst, g_sem.at[k, i]))
            loads[-1].start()
    to = links.to
    links.barrier(
        to(y=1), to(y=3), to(z=2), to(x=1), to(x=3), to(z=1), to(z=3), to(sibling=True)
    )
    for copy in loads:
        copy.wait()

    def compute(pair):
        rows = jnp.concatenate([act_ref[slot, :, : 2 * COLS] for slot in pair], axis=0)
        for d in range(0, WIDE, 512):
            cols = slice(d, d + 512)
            result = dot(rows[:, :COLS], w[0, :, cols]) + dot(rows[:, COLS:], w[1, :, cols])
            result = result.astype(BF16)
            for i, slot in enumerate(pair):
                bufs[0][slot, :, cols] = result[i * ROWS : (i + 1) * ROWS]

    def finish(at):
        grad = deep_alpha * gz_ref[at] + total[at]
        unit = unit_ref[at]
        grad_z = norm_backward(grad, unit, inverse_ref[at][:, 0:1], gain_ref[...])
        gz1_ref[at] = grad_z
        all_ref[0, at] = grad_z.astype(BF16)
        vec_ref[0] += rows8(grad * unit)
        vec_ref[1] += rows8(grad)

    def work(pair):
        result = dot_t(pair_of(all_ref, pair), w_out_ref[...]).astype(BF16)
        for i, slot in enumerate(pair):
            grad_heads_ref[pl.ds(links.first_row(slot), ROWS)] = result[i * ROWS : (i + 1) * ROWS]

    def chain():
        yield from scatter_near(links, bufs, compute, total)
        vec_ref[...] = jnp.zeros_like(vec_ref)
        by_chunks(finish)
        for time in gather(links, all_ref, work):
            yield time + 22

    together(reduce(links, more, shard_ref), chain())


def input_kernel(
    dq_ref, dk_ref, dv_ref, w_ref, gz1_ref, tokens_ref, heads_ref, gz_all_ref, shard_ref, vec_in_ref,
    out_ref, q_out_ref, vec_ref, feed_ref,
    total, grads, heads, held, got, local, *rest,
):
    bufs, more, (send, recv) = rest[:7], rest[7:12], rest[12:]
    links = Links(send, recv)
    to = links.to
    beside = (lax.rem(lax.axis_index("dp") + 8, 16), lax.axis_index("seq"))
    links.barrier(
        to(y=1), to(y=2), to(y=3), to(z=2), to(x=1), to(x=2), to(x=3), to(sibling=True), beside
    )
    for slot in range(8):
        at = pl.ds(links.first_row(slot), ROWS)
        heads[slot] = heads_ref[at]
        for part, ref in enumerate((dq_ref, dk_ref, dv_ref)):
            grads[slot, :, part * 256 : part * 256 + 256] = ref[at]
    vec_ref[...] = vec_in_ref[...]

    def compute(pair):
        rows = pair_of(grads, pair)
        result = 0.0
        for part in range(3):
            result = result + dot_t(rows[:, part * 256 : part * 256 + 256], w_ref[part])
        result = result.astype(BF16)
        for i, slot in enumerate(pair):
            bufs[0][slot] = result[i * ROWS : (i + 1) * ROWS]

    def qkv():
        flat = more[0]
        right = grads[...].reshape(LEN, 768)
        for d in range(8):
            left = tokens_ref[:, :, d * 256 : d * 256 + 256].reshape(LEN, 256)
            result = dot_rows(left, right).astype(BF16)
            for part in range(3):
                chunk = part * 4 + d // 2
                flat[chunk // 8, chunk // 4 % 2, chunk % 4, d % 2 * 256 : d % 2 * 256 + 256] = result[
                    :, part * 256 : part * 256 + 256
                ]
        result = dot_rows(heads[...].reshape(LEN, 256), gz_all_ref[...].reshape(LEN, WIDE)).astype(BF16)
        for d in range(8):
            chunk = 12 + d // 2
            flat[chunk // 8, chunk // 4 % 2, chunk % 4, d % 2 * 256 : d % 2 * 256 + 256] = result[
                :, d * 256 : d * 256 + 256
            ]

    def shared():
        yield 9
        qkv()
        yield from share(links, more, q_out_ref, 16)

    together(
        collect(links, shard_ref, feed_ref, local, 0),
        scatter(links, bufs, compute, total),
        shared(),
        agree(links, vec_ref, (held, got)),
    )

    def finish(at):
        out_ref[at] = deep_alpha * gz1_ref[at] + total[at]

    by_chunks(finish)


def feed_weight_kernel(act_ref, normed_ref, gz_ref, out_ref):
    @pl.when(pl.program_id(0) < 6)
    def _():
        out_ref[0] = dot_rows(act_ref[...], normed_ref[...]).astype(BF16)

    @pl.when(pl.program_id(0) >= 6)
    def _():
        out_ref[0] = dot_rows(act_ref[...], gz_ref[...]).astype(BF16)


def feed_weights(act, normed_all, gz_all):
    flat = lambda v: v.reshape(LEN, v.shape[-1])
    return pl.pallas_call(
        feed_weight_kernel,
        name="feed_weights",
        grid=(9,),
        in_specs=[pl.BlockSpec((LEN, 256), lambda i: (0, i)), VMEM, VMEM],
        out_specs=pl.BlockSpec((1, 256, WIDE), lambda i: (i // 3, i % 3, 0)),
        out_shape=jax.ShapeDtypeStruct((3, COLS, WIDE), BF16),
        compiler_params=pltpu.CompilerParams(vmem_limit_bytes=VMEM_BYTES),
    )(flat(act), flat(normed_all), flat(gz_all))


def feed_out_kernel(feed_ref, gate_up_ref, down_ref):
    for z in range(2):
        lanes = slice(z * 128, z * 128 + 128)
        gate_up_ref[:, 0, lanes] = feed_ref[0, 0, 0, z].astype(F32)
        gate_up_ref[:, 1, lanes] = feed_ref[1, 0, 0, z].astype(F32)
        down_ref[:, lanes] = feed_ref[2, 0, 0, z].astype(F32)


def feed_out(feed, total):
    return pl.pallas_call(
        feed_out_kernel,
        name="feed_out",
        grid=(8,),
        in_specs=[pl.BlockSpec((3, 1, 1, 2, FF, 128), lambda i: (0, i // 2, i % 2, 0, 0, 0))],
        out_specs=(
            pl.BlockSpec((FF, 2, 256), lambda i: (i, 0, 0)),
            pl.BlockSpec((FF, 256), lambda i: (i, 0)),
        ),
        out_shape=(
            jax.ShapeDtypeStruct((total, 2, 256), F32),
            jax.ShapeDtypeStruct((total, 256), F32),
        ),
        compiler_params=pltpu.CompilerParams(vmem_limit_bytes=VMEM_BYTES),
    )(feed)


def on_device(
    tokens, cotangent, w_qkv, w_out, w_gate_up, w_down,
    attn_gain, attn_bias, ffn_gain, ffn_bias, prefix_len, clusters,
):
    x = tokens.reshape(ROWS, WIDE)
    cot = cotangent.reshape(ROWS, WIDE)
    dp, seq = lax.axis_index("dp"), lax.axis_index("seq")
    own_id = lax.dynamic_slice_in_dim(clusters, dp, 1)
    seq_weight = 1.0 / jnp.sum((own_id[:, None] == clusters[None, :]).astype(F32), axis=1)
    cosine, sine = (jnp.asarray(t) for t in rotary_tables(LEN, HEAD_DIM))
    row = lambda v: v.reshape(1, WIDE)
    ff_total = w_down.shape[1]
    place = jnp.stack([dp % 2, dp // 2 % 4, dp // 8, jnp.int32(ff_total)]).astype(jnp.int32)
    piece = piece_of(w_gate_up.transpose(2, 1, 0), w_down.T, place)
    w_in = w_qkv.transpose(1, 0, 2)
    low, full = BF16, F32
    blocks = (8, ROWS, WIDE)

    tokens_all, q, k, v, ffn_w = call(
        project_kernel, "project", 0,
        [(blocks, low, "v")] + [((LEN, 256), low, "v")] * 3 + [((3, 2, 4, 2, FF, 128), low, "h")],
        (x, w_in, cosine, sine, piece), "vvvvv", (pltpu.SemaphoreType.DMA,), 67,
        2 * LEN * WIDE * 768,
    )
    heads_out, lse = attend(prefix_len, q, k, v)
    normed, unit_one, inverse_one = call(
        attended_kernel, "attended", 1,
        [((ROWS, WIDE), full, "v"), ((ROWS, WIDE), full, "v"), ((ROWS, 128), full, "v")],
        (heads_out, w_out, x, row(attn_gain), row(attn_bias)), "vvvvv",
        (pltpu.VMEM((ROWS, WIDE), F32), *SCATTER_SCRATCH), 19, 2 * LEN * WIDE * 256,
    )
    output, normed_all, gz_all, act, grad_z2, ffn_vec = call(
        feed_kernel, "feed", 2,
        [
            ((ROWS, WIDE), low, "v"), (blocks, low, "v"), (blocks, low, "v"),
            ((8, ROWS, 3 * COLS), low, "v"), ((ROWS, WIDE), full, "v"), ((2, 8, WIDE), full, "v"),
        ],
        (normed, cot, seq_weight, ffn_w, row(ffn_gain), row(ffn_bias)), "vvshvv",
        (
            pltpu.VMEM((3, COLS, WIDE), BF16), pltpu.VMEM((8, ROWS, COLS), F32),
            pltpu.VMEM((8, ROWS, COLS), F32), pltpu.VMEM((ROWS, WIDE), F32),
            pltpu.SemaphoreType.DMA((3, 16)), *NEAR_SCRATCH,
        ),
        34, 2 * LEN * WIDE * COLS * 4,
    )
    ffn_grad = feed_weights(act, normed_all, gz_all)
    grad_z1, gz1_all, grad_heads, attn_vec, shard = call(
        feed_back_kernel, "feed_back", 3,
        [
            ((ROWS, WIDE), full, "v"), (blocks, low, "v"), ((LEN, 256), low, "v"),
            ((2, 8, WIDE), full, "v"), ((3, 4, PART, 128), low, "v"),
        ],
        (act, grad_z2, ffn_w, ffn_grad, unit_one, inverse_one, row(attn_gain), w_out), "vvhhvvvv",
        (
            pltpu.VMEM((2, COLS, WIDE), BF16), pltpu.VMEM((ROWS, WIDE), F32),
            pltpu.SemaphoreType.DMA((2, 16)), pltpu.SemaphoreType.DMA((3, 16)),
            *NEAR_SCRATCH, *REDUCE_SCRATCH,
        ),
        52, 2 * LEN * WIDE * COLS * 2,
    )
    dq, dk, dv = attend_back(prefix_len, q, k, v, grad_heads, lse, cosine, sine)
    vec = jnp.concatenate([attn_vec.sum(1), ffn_vec.sum(1), jnp.zeros((4, WIDE), F32)], axis=0)
    steps = pltpu.VMEM((7, 8, WIDE), F32)
    input_grad, qkv_out, vec, ffn_whole = call(
        input_kernel, "input", 4,
        [
            ((ROWS, WIDE), full, "v"), ((2, 2, 4, 512, 256), low, "v"), ((8, WIDE), full, "v"),
            ((3, 4, 2, 2, FF, 128), low, "h"),
        ],
        (dq, dk, dv, w_in, grad_z1, tokens_all, heads_out, gz1_all, shard, vec), "vvvvvvvvvv",
        (
            pltpu.VMEM((ROWS, WIDE), F32), pltpu.VMEM((8, ROWS, 768), BF16),
            pltpu.VMEM((8, ROWS, 256), BF16), steps, steps, pltpu.SemaphoreType.DMA,
            *SCATTER_SCRATCH, *SHARE_SCRATCH,
        ),
        77, 2 * LEN * WIDE * 768,
    )
    grad_gate_up, grad_down = feed_out(ffn_whole, ff_total)
    qkv_out = qkv_out.reshape(8192, 256).astype(F32)
    grad_qkv = qkv_out[:6144].reshape(3, WIDE, 256).transpose(1, 0, 2)
    grad_out = qkv_out[6144:].reshape(8, 256, 256).transpose(1, 0, 2).reshape(256, WIDE)
    own = lax.dynamic_slice_in_dim(vec, seq * 256, 256, axis=1)
    return (
        output.reshape(tokens.shape),
        input_grad.reshape(tokens.shape),
        grad_qkv,
        grad_out,
        grad_gate_up.transpose(2, 1, 0),
        grad_down.T,
        own[0],
        own[1],
        own[2],
        own[3],
    )


def solution(mesh):
    return jax.shard_map(
        on_device,
        mesh=mesh,
        in_specs=(
            P("seq", "dp", None), P("seq", "dp", None), P(None, None, "seq"), P("seq", None),
            P("seq", None, None), P("seq", None), P(), P(), P(), P(), P("dp"), P(),
        ),
        out_specs=(
            P("seq", "dp", None), P("seq", "dp", None), P(None, None, "seq"), P("seq", None),
            P("seq", None, None), P("seq", None), P("seq"), P("seq"), P("seq"), P("seq"),
        ),
        check_vma=False,
    )
```

```python
import functools

import jax
import jax.numpy as jnp
import numpy as np
from jax import lax
from jax.experimental import pallas as pl
from jax.experimental.pallas import tpu as pltpu
from jax.sharding import PartitionSpec as P

MESH = pl.DeviceIdType.MESH
F32, BF16 = jnp.float32, jnp.bfloat16
HEAD_DIM = 128
ROWS = 128
WIDE = 2048
COLS = 768
LEN = 1024
VMEM_BYTES = 60 * 1024 * 1024
deep_alpha = 48.0**0.25
norm_eps = 1e-05
rotary_base = 10000.0


def rotary_tables(length, head_width):
    half_width = head_width // 2
    position = np.arange(length, dtype=np.float64)
    inverse = rotary_base ** (-np.arange(half_width, dtype=np.float64) * 2.0 / head_width)
    angles = position[:, None] * inverse[None, :]
    cosine_table = np.cos(angles)
    sine_table = np.sin(angles)
    return (
        np.concatenate([cosine_table, cosine_table], axis=1).astype(np.float32),
        np.concatenate([-sine_table, sine_table], axis=1).astype(np.float32),
    )


FF = 704
PART = 176


class Links:
    def __init__(self, send, recv):
        self.send, self.recv, self.count = send, recv, 0
        dp, seq = lax.axis_index("dp"), lax.axis_index("seq")
        y, z_hi = seq // 2, lax.rem(seq, 2)
        z_lo, x, core = dp // 8, lax.rem(dp // 2, 4), lax.rem(dp, 2)
        self.y, self.z_hi, self.z_lo, self.x, self.core = y, z_hi, z_lo, x, core
        self.z = z_hi * 2 + z_lo

    def to(self, x=0, y=0, z=0, sibling=False):
        z_hi, z_lo = self.z_at(z)
        x, y = lax.rem(self.x + x, 4), lax.rem(self.y + y, 4)
        core = 1 - self.core if sibling else self.core
        return (z_lo * 8 + x * 2 + core, y * 2 + z_hi)

    def z_at(self, offset):
        z = lax.rem(self.z + offset, 4)
        return z // 2, lax.rem(z, 2)

    def part(self, offset):
        return pl.ds(pl.multiple_of(lax.rem(self.x + offset, 4) * PART, 16), PART)

    def barrier(self, *where):
        gate = pltpu.get_barrier_semaphore()
        for device in where:
            pl.semaphore_signal(gate, inc=1, device_id=device, device_id_type=MESH)
        pl.semaphore_wait(gate, len(where))

    def start(self, src, dst, where):
        copy = pltpu.make_async_remote_copy(
            src_ref=src,
            dst_ref=dst,
            send_sem=self.send.at[self.count],
            recv_sem=self.recv.at[self.count],
            device_id=where,
            device_id_type=MESH,
        )
        self.count += 1
        copy.start()
        return copy

    def first_row(self, slot):
        step = (0, 3, 1, 2)[slot % 4]
        half = self.z_hi if slot < 4 else 1 - self.z_hi
        return pl.multiple_of((lax.rem(self.y + step, 4) * 2 + half) * ROWS, ROWS)


def together(*tasks):
    due = [[next(task), i, task] for i, task in enumerate(tasks)]
    while due:
        due.sort(key=lambda entry: entry[:2])
        try:
            due[0][0] = next(due[0][2])
        except StopIteration:
            due.pop(0)


def received(*copies):
    for copy in copies:
        copy.wait_recv()


def sent(copies):
    for copy in copies:
        copy.wait_send()


H0, H1 = pl.ds(0, 64), pl.ds(64, 64)


def gather(links, buf, work):
    up, down, across = links.to(y=1), links.to(y=3), links.to(z=2)
    copies = []

    def send(slot, rows, dst, where):
        copies.append(links.start(buf.at[slot, rows], buf.at[dst, rows], where))
        return copies[-1]

    u0, d1 = send(0, H0, 1, up), send(0, H1, 2, down)
    z0, z1 = send(0, H0, 4, across), send(0, H1, 4, across)
    u1, d0 = send(0, H1, 1, up), send(0, H0, 2, down)
    yield 6
    received(u0)
    fu = send(1, H0, 3, up)
    received(d1)
    fd = send(2, H1, 3, down)
    yield 12
    received(z0)
    pu0 = send(4, H0, 5, up)
    received(z1)
    pd1 = send(4, H1, 6, down)
    pu1, pd0 = send(4, H1, 5, up), send(4, H0, 6, down)
    received(u1, d0)
    work((0, 1))
    yield 19
    received(fu, fd)
    work((2, 3))
    yield 24
    received(pu0)
    gu = send(5, H0, 7, up)
    received(pd1)
    gd = send(6, H1, 7, down)
    yield 29
    received(pu1, pd0)
    work((4, 5))
    yield 36
    received(gu, gd)
    work((6, 7))
    sent(copies)


def gather_near(links, buf, work):
    up, down, side = links.to(y=1), links.to(y=3), links.to(sibling=True)
    copies = []

    def send(slot, rows, dst, where):
        copies.append(links.start(buf.at[slot, rows], buf.at[dst, rows], where))
        return copies[-1]

    every = pl.ds(0, ROWS)
    u0, d1 = send(0, H0, 1, up), send(0, H1, 2, down)
    u1, d0 = send(0, H1, 1, up), send(0, H0, 2, down)
    s0 = send(0, every, 4, side)
    yield 1
    received(s0)
    work((0, 4))
    yield 6
    received(u0)
    fu = send(1, H0, 3, up)
    received(d1)
    fd = send(2, H1, 3, down)
    yield 11
    received(u1)
    s1 = send(1, every, 5, side)
    received(d0)
    s2 = send(2, every, 6, side)
    work((1, 2))
    yield 13
    received(s1, s2)
    work((5, 6))
    yield 17
    received(fu)
    s30 = send(3, H0, 7, side)
    received(fd)
    s31 = send(3, H1, 7, side)
    yield 18
    received(s30, s31)
    work((3, 7))
    sent(copies)


A, B = pl.ds(0, 80), pl.ds(80, 48)
A0, A1 = pl.ds(0, 48), pl.ds(48, 32)
B0, B1 = pl.ds(80, 16), pl.ds(96, 32)
SCATTER_SCRATCH = (
    pltpu.VMEM((8, ROWS, WIDE), BF16),
    pltpu.VMEM((4, 48, WIDE), BF16),
    pltpu.VMEM((48, WIDE), BF16),
    pltpu.VMEM((2, 48, WIDE), BF16),
    pltpu.VMEM((2, 80, WIDE), BF16),
    pltpu.VMEM((2, 2, 80, WIDE), BF16),
    pltpu.VMEM((80, WIDE), BF16),
)


def add_rows(target, slot, rows, *others):
    value = target[slot, rows].astype(F32)
    for other in others:
        value = value + other.astype(F32)
    target[slot, rows] = value.astype(BF16)


def scatter(links, bufs, compute, total):
    sums, from_z, b_far, b_near, a_far, a_near, a_z = bufs
    up, down, across = links.to(y=1), links.to(y=3), links.to(z=2)
    copies = []

    def send(src, dst, where):
        copies.append(links.start(src, dst, where))
        return copies[-1]

    def far_a(o):
        half = o // 4
        return (
            send(sums.at[o + 3, A0], a_far.at[half, pl.ds(0, 48)], up),
            send(sums.at[o + 3, A1], a_far.at[half, pl.ds(48, 32)], down),
        )

    def near_a(o, far):
        half = o // 4
        received(far[0])
        add_rows(sums, o + 2, A0, a_far[half, 0:48])
        one = send(sums.at[o + 2, A], a_near.at[half, 0], up)
        received(far[1])
        add_rows(sums, o + 1, A1, a_far[half, 48:80])
        return one, send(sums.at[o + 1, A], a_near.at[half, 1], down)

    def cross_b(j):
        return send(sums.at[4 + j, B], from_z.at[j], across)

    compute((7, 3))
    z3 = cross_b(3)
    far_other = far_a(4)
    far_own = far_a(0)
    compute((5, 6))
    z1, z2 = cross_b(1), cross_b(2)
    compute((1, 2))
    yield 8
    received(z3)
    add_rows(sums, 3, B, from_z[3])
    far_b = (
        send(sums.at[3, B0], b_far.at[pl.ds(0, 16)], up),
        send(sums.at[3, B1], b_far.at[pl.ds(16, 32)], down),
    )
    near_other = near_a(4, far_other)
    compute((4, 0))
    z0 = cross_b(0)
    yield 12
    near_own = near_a(0, far_own)
    yield 18
    received(*near_other)
    add_rows(sums, 4, A, a_near[1, 0], a_near[1, 1])
    z_a = send(sums.at[4, A], a_z, across)
    yield 20
    received(z2)
    add_rows(sums, 2, B, from_z[2])
    received(far_b[0])
    add_rows(sums, 2, B0, b_far[0:16])
    near_b0 = send(sums.at[2, B], b_near.at[0], up)
    received(z1)
    add_rows(sums, 1, B, from_z[1])
    received(far_b[1])
    add_rows(sums, 1, B1, b_far[16:48])
    near_b1 = send(sums.at[1, B], b_near.at[1], down)
    yield 27
    received(z0, near_b0, near_b1)
    total[80:128] = (
        sums[0, B].astype(F32)
        + from_z[0].astype(F32)
        + b_near[0].astype(F32)
        + b_near[1].astype(F32)
    )
    received(*near_own)
    yield 30
    received(z_a)
    total[0:80] = (
        sums[0, A].astype(F32)
        + a_near[0, 0].astype(F32)
        + a_near[0, 1].astype(F32)
        + a_z[...].astype(F32)
    )
    sent(copies)


NEAR_SCRATCH = (
    pltpu.VMEM((8, ROWS, WIDE), BF16),
    pltpu.VMEM((4, ROWS, WIDE), BF16),
    pltpu.VMEM((ROWS, WIDE), BF16),
    pltpu.VMEM((2, ROWS, WIDE), BF16),
)


def scatter_near(links, bufs, compute, total):
    sums, from_side, far, near = bufs
    up, down, side = links.to(y=1), links.to(y=3), links.to(sibling=True)
    copies = []

    def send(src, dst, where):
        copies.append(links.start(src, dst, where))
        return copies[-1]

    every = pl.ds(0, ROWS)
    compute((7, 3))
    s3 = send(sums.at[7], from_side.at[3], side)
    compute((5, 6))
    s1 = send(sums.at[5], from_side.at[1], side)
    s2 = send(sums.at[6], from_side.at[2], side)
    received(s3)
    add_rows(sums, 3, every, from_side[3])
    fu = send(sums.at[3, H0], far.at[H0], up)
    fd = send(sums.at[3, H1], far.at[H1], down)
    compute((1, 2))
    received(s1, s2)
    add_rows(sums, 2, every, from_side[2])
    nu1 = send(sums.at[2, H1], near.at[0, H1], up)
    add_rows(sums, 1, every, from_side[1])
    nd0 = send(sums.at[1, H0], near.at[1, H0], down)
    compute((4, 0))
    s0 = send(sums.at[4], from_side.at[0], side)
    yield 8
    received(fu)
    add_rows(sums, 2, H0, far[0:64])
    nu0 = send(sums.at[2, H0], near.at[0, H0], up)
    received(fd)
    add_rows(sums, 1, H1, far[64:128])
    nd1 = send(sums.at[1, H1], near.at[1, H1], down)
    yield 17
    received(s0, nu1, nd0, nu0, nd1)
    total[...] = (
        sums[0].astype(F32)
        + from_side[0].astype(F32)
        + near[0].astype(F32)
        + near[1].astype(F32)
    )
    sent(copies)


Y0, Y1 = pl.ds(0, 2), pl.ds(2, 2)
GU = pl.ds(0, 2)


def two_rings(links, at, first, second, times):
    up, down = first
    right, left = second
    copies = []

    def send(ref, where):
        copies.append(links.start(ref, ref, where))
        return copies[-1]

    def both(a):
        return send(at(a, 0), right), send(at(a, 0), left)

    def onward(a):
        return send(at(a, 3, Y0), right), send(at(a, 1, Y1), left)

    u, d = send(at(0, 0), up), send(at(0, 0), down)
    near = [both(0)]
    yield times[0]
    received(u)
    fu = send(at(3, 0, Y0), up)
    near.append(both(3))
    received(d)
    fd = send(at(1, 0, Y1), down)
    near.append(both(1))
    yield times[1]
    received(*near[0])
    far = [*onward(0)]
    received(fu, fd)
    near.append(both(2))
    for i, a in enumerate((3, 1, 2)):
        yield times[2 + i]
        received(*near[1 + i])
        far += onward(a)
    yield times[5]
    received(*far)
    sent(copies)


def across_y(links, piece, own, local):
    keep = pltpu.make_async_copy(piece(links.y), own(), local)
    keep.start()
    copies = []
    for step in (2, 1, 3):
        there = lax.rem(links.y + step, 4)
        copies.append(links.start(piece(there), own(), links.to(y=step)))
    return keep, copies


def spread(links, piece, w, matrices, local):
    along_x = (links.to(x=1), links.to(x=3))
    along_z = (links.to(z=1), links.to(z=3))
    every = pl.ds(0, 4)

    def place(k, z, x, y):
        z_hi, z_lo = links.z_at(z)
        return w.at[k, z_hi, y, z_lo, links.part(x)]

    def own():
        return w.at[:, links.z_hi, links.y, links.z_lo, links.part(0)]

    keep, copies = across_y(links, lambda y: piece.at[y, matrices], own, local)
    yield 8
    keep.wait()
    received(*copies)
    count = matrices.size
    rings = [
        two_rings(
            links, lambda a, b, y=every: place(0, a, b, y), along_z, along_x, (14, 19, 24, 29, 34, 39)
        )
    ]
    if count == 2:
        rings.append(
            two_rings(
                links, lambda a, b, y=every: place(1, b, a, y), along_x, along_z, (15, 23, 29, 34, 39, 44)
            )
        )
    due = [[next(ring), i, ring] for i, ring in enumerate(rings)]
    while due:
        due.sort(key=lambda entry: entry[:2])
        yield due[0][0]
        try:
            due[0][0] = next(due[0][2])
        except StopIteration:
            due.pop(0)
    sent(copies)


BLOCKS = pltpu.VMEM((2, 2, 4, 2, PART, 128), BF16)
REDUCE_SCRATCH = (
    pltpu.VMEM((3, 2, 4, 2, FF, 128), BF16),
    BLOCKS,
    pltpu.VMEM((2, 2, 2, 4, 2, PART, 128), BF16),
    pltpu.VMEM((2, 4, PART, 128), BF16),
    pltpu.VMEM((2, 2, 4, PART, 128), BF16),
    pltpu.VMEM((4, FF, 128), BF16),
    pltpu.VMEM((2, 4, FF, 128), BF16),
    pltpu.VMEM((4, PART, 128), BF16),
    pltpu.VMEM((2, 4, PART, 128), BF16),
)


def accumulate(count, target, *others):
    def step(i, carry):
        ref = target(i)
        value = ref[...].astype(F32)
        for other in others:
            value = value + other(i)[...].astype(F32)
        ref[...] = value.astype(BF16)
        return carry

    lax.fori_loop(0, count, step, 0)


def reduce(links, bufs, make, shard):
    g, fx, nx, fz, nz, fz2, nz2, fx2, nx2 = bufs
    xp, xm, zp, zm = links.to(x=1), links.to(x=3), links.to(z=1), links.to(z=3)
    copies = []
    every = pl.ds(0, 4)

    def send(src, dst, where):
        copies.append(links.start(src, dst, where))
        return copies[-1]

    def along_x(k, x):
        return g.at[k, :, :, :, links.part(x)]

    def block_x(k, x):
        return lambda i: g.at[k, i // 8, lax.rem(i // 2, 4), lax.rem(i, 2), links.part(x)]

    def plain(ref):
        return lambda i: ref.at[i // 8, lax.rem(i // 2, 4), lax.rem(i, 2)]

    def along_z(k, z, y=every, rows=pl.ds(0, FF)):
        z_hi, z_lo = links.z_at(z)
        return g.at[k, z_hi, y, z_lo, rows]

    def block_z(k, z, rows, first=0):
        z_hi, z_lo = links.z_at(z)
        return lambda i: g.at[k, z_hi, i + first, z_lo, rows]

    def shift(ref, first=0):
        return lambda i: ref.at[i + first]

    here = links.part(0)
    whole = pl.ds(0, FF)
    yield from make(0)
    c1, c4 = send(along_x(0, 2), fx.at[0], xp), send(along_x(0, 3), nx.at[1, 0], xm)
    yield from make(1)
    c2, c3 = send(along_x(1, 2), fx.at[1], xm), send(along_x(1, 1), nx.at[0, 1], xp)
    yield from make(2)
    e1 = send(along_z(2, 2, Y0), fz2.at[Y0], zp)
    e2 = send(along_z(2, 2, Y1), fz2.at[Y1], zm)
    e3 = send(along_z(2, 1, Y1), nz2.at[0, Y1], zp)
    e4 = send(along_z(2, 3, Y0), nz2.at[1, Y0], zm)
    yield 31
    received(c1)
    accumulate(16, block_x(0, 1), plain(fx.at[0]))
    c5 = send(along_x(0, 1), nx.at[0, 0], xp)
    yield 36
    received(e1)
    accumulate(2, block_z(2, 1, whole), shift(fz2))
    e5 = send(along_z(2, 1, Y0), nz2.at[0, Y0], zp)
    received(e2)
    accumulate(2, block_z(2, 3, whole, 2), shift(fz2, 2))
    e6 = send(along_z(2, 3, Y1), nz2.at[1, Y1], zm)
    yield 42
    received(c2)
    accumulate(16, block_x(1, 3), plain(fx.at[1]))
    c6 = send(along_x(1, 3), nx.at[1, 1], xm)
    yield 53
    received(e3, e4, e5, e6)
    accumulate(4, block_z(2, 0, whole), shift(nz2.at[0]), shift(nz2.at[1]))
    d1 = send(along_z(2, 0, Y0, links.part(2)), fx2.at[Y0], xp)
    d2 = send(along_z(2, 0, Y1, links.part(2)), fx2.at[Y1], xm)
    d3 = send(along_z(2, 0, Y1, links.part(1)), nx2.at[0, Y1], xp)
    d4 = send(along_z(2, 0, Y0, links.part(3)), nx2.at[1, Y0], xm)
    yield 62
    received(c3, c4, c5, c6)
    for k in range(2):
        accumulate(16, block_x(k, 0), plain(nx.at[0, k]), plain(nx.at[1, k]))
    f1 = send(along_z(0, 2, every, here), fz.at[0], zp)
    f2 = send(along_z(1, 2, every, here), fz.at[1], zm)
    f3 = send(along_z(1, 1, every, here), nz.at[0, 1], zp)
    f4 = send(along_z(0, 3, every, here), nz.at[1, 0], zm)
    received(d1)
    accumulate(2, block_z(2, 0, links.part(1)), shift(fx2))
    d5 = send(along_z(2, 0, Y0, links.part(1)), nx2.at[0, Y0], xp)
    received(d2)
    accumulate(2, block_z(2, 0, links.part(3), 2), shift(fx2, 2))
    d6 = send(along_z(2, 0, Y1, links.part(3)), nx2.at[1, Y1], xm)
    yield 68
    received(f1)
    accumulate(4, block_z(0, 1, here), shift(fz.at[0]))
    f5 = send(along_z(0, 1, every, here), nz.at[0, 0], zp)
    received(f2)
    accumulate(4, block_z(1, 3, here), shift(fz.at[1]))
    f6 = send(along_z(1, 3, every, here), nz.at[1, 1], zm)
    yield 75
    received(d3, d4, d5, d6)
    accumulate(4, block_z(2, 0, here), shift(nx2.at[0]), shift(nx2.at[1]))
    received(f3, f4, f5, f6)
    for k in range(2):
        accumulate(4, block_z(k, 0, here), shift(nz.at[0, k]), shift(nz.at[1, k]))
    for k in range(3):
        shard[k] = along_z(k, 0, every, here)[...]
    sent(copies)


def regather(links, at, half, times):
    xp, xm, side = links.to(x=1), links.to(x=3), links.to(sibling=True)
    beside = (lax.rem(lax.axis_index("dp") + 8, 16), lax.axis_index("seq"))
    copies, sides = [], []

    def send(ref, where):
        copies.append(links.start(ref, ref, where))
        return copies[-1]

    def share(ref):
        sides.append(send(ref, side))

    z = send(at(0, 0), beside)
    near = [(send(at(0, 0), xp), send(at(0, 0), xm))]
    share(at(0, 0))
    yield times[0]
    received(z)
    near.append((send(at(1, 0), xp), send(at(1, 0), xm)))
    share(at(1, 0))
    for i in range(2):
        yield times[1 + 2 * i]
        received(near[i][0])
        far_up = send(half(at(i, 3), 0), xp)
        share(at(i, 3))
        received(near[i][1])
        far_down = send(half(at(i, 1), 1), xm)
        share(at(i, 1))
        yield times[2 + 2 * i]
        received(far_up, far_down)
        share(at(i, 2))
    received(*sides)
    sent(copies)


def collect(links, shard, out, local, late):
    copies = []

    def own(y):
        return out.at[:, y, links.core, links.z_lo, links.part(0)]

    keep = pltpu.make_async_copy(shard.at[:, links.y], own(links.y), local)
    keep.start()
    for step in (2, 1, 3):
        there = lax.rem(links.y + step, 4)
        copies.append(links.start(shard.at[:, there], own(links.y), links.to(y=step)))
    yield 7
    keep.wait()
    received(*copies)

    def at(z, x):
        return out.at[:, :, links.core, lax.rem(links.z_lo + z, 2), links.part(x)]

    def half(ref, i):
        return ref.at[:, pl.ds(2 * i, 2)]

    yield from regather(links, at, half, [t + late for t in (12, 18, 24, 32, 45)])
    sent(copies)


SHARE_SCRATCH = (
    pltpu.VMEM((2, 2, 4, 512, 256), BF16),
    pltpu.VMEM((2, 4, 512, 256), BF16),
    pltpu.VMEM((2, 512, 256), BF16),
    pltpu.VMEM((2, 2, 512, 256), BF16),
    pltpu.VMEM((512, 256), BF16),
)


def share(links, bufs, out, late):
    q, from_side, far, near, from_z = bufs
    xp, xm, side = links.to(x=1), links.to(x=3), links.to(sibling=True)
    beside = (lax.rem(lax.axis_index("dp") + 8, 16), lax.axis_index("seq"))
    core, z_lo = links.core, links.z_lo
    copies = []

    def send(src, dst, where):
        copies.append(links.start(src, dst, where))
        return copies[-1]

    def there(x):
        return lax.rem(links.x + x, 4)

    def rows(ref):
        return lambda i: ref.at[pl.ds(pl.multiple_of(i * 64, 64), 64)]

    s = send(q.at[1 - core], from_side, side)
    yield late
    received(s)
    for z in range(2):
        for x in range(4):
            accumulate(8, rows(q.at[core, z, x]), rows(from_side.at[z, x]))
    a1, a2 = send(q.at[core, 0, there(2)], far.at[0], xp), send(q.at[core, 1, there(2)], far.at[1], xm)
    a3 = send(q.at[core, 1, there(1)], near.at[0, 1], xp)
    a4 = send(q.at[core, 0, there(3)], near.at[1, 0], xm)
    yield late + 8
    received(a1)
    accumulate(8, rows(q.at[core, 0, there(1)]), rows(far.at[0]))
    a5 = send(q.at[core, 0, there(1)], near.at[0, 0], xp)
    received(a2)
    accumulate(8, rows(q.at[core, 1, there(3)]), rows(far.at[1]))
    a6 = send(q.at[core, 1, there(3)], near.at[1, 1], xm)
    yield late + 20
    received(a3, a4, a5, a6)
    for z in range(2):
        accumulate(8, rows(q.at[core, z, there(0)]), rows(near.at[0, z]), rows(near.at[1, z]))
    b = send(q.at[core, 1 - z_lo, there(0)], from_z, beside)
    yield late + 26
    received(b)

    def finish(i, carry):
        at = pl.ds(pl.multiple_of(i * 64, 64), 64)
        value = q[core, z_lo, links.x, at].astype(F32) + from_z[at].astype(F32)
        out[core, z_lo, links.x, at] = value.astype(BF16)
        return carry

    lax.fori_loop(0, 8, finish, 0)

    def at(z, x):
        return out.at[core, lax.rem(z_lo + z, 2), there(x)]

    def half(ref, i):
        return ref.at[pl.ds(256 * i, 256)]

    yield from regather(links, at, half, [t + late for t in (33, 36, 42, 46, 54)])
    sent(copies)


def agree(links, vec, bufs):
    y, x = links.y, links.x
    copies = []
    steps = (
        links.to(sibling=True),
        links.to(y=1 + 2 * lax.rem(y, 2)),
        links.to(y=2),
        links.to(z=2),
        links.to(x=1 + 2 * lax.rem(x, 2)),
        links.to(x=2),
        (lax.rem(lax.axis_index("dp") + 8, 16), lax.axis_index("seq")),
    )
    held, got = bufs
    held[0] = vec[...]
    for i, where in enumerate(steps):
        copies.append(links.start(held.at[i], got.at[i], where))
        yield 6 + 6 * i
        received(copies[-1])
        if i < len(steps) - 1:
            held[i + 1] = held[i] + got[i]
        else:
            vec[...] = held[i] + got[i]
    sent(copies)


def dot(a, b):
    return jnp.dot(a, b, preferred_element_type=F32)


def dot_t(a, b):
    return lax.dot_general(a, b, (((1,), (1,)), ((), ())), preferred_element_type=F32)


def dot_rows(a, b):
    return lax.dot_general(a, b, (((0,), (0,)), ((), ())), preferred_element_type=F32)


def pair_of(ref, pair):
    return jnp.concatenate([ref[pair[0]], ref[pair[1]]], axis=0)


def by_chunks(body):
    def step(i, carry):
        body(pl.ds(pl.multiple_of(i * 16, 16), 16))
        return carry

    lax.fori_loop(0, ROWS // 16, step, 0)


def norm_parts(row_total):
    center = row_total - jnp.mean(row_total, axis=-1, keepdims=True)
    spread = jnp.mean(center * center, axis=-1, keepdims=True)
    inverse = lax.rsqrt(spread + norm_eps)
    return center * inverse, inverse


def norm_backward(grad_result, unit, inverse, gain):
    grad_unit = grad_result * gain
    return inverse * (
        grad_unit
        - jnp.mean(grad_unit, axis=-1, keepdims=True)
        - unit * jnp.mean(grad_unit * unit, axis=-1, keepdims=True)
    )


def rows8(values):
    return values[0:8] + values[8:16]


VMEM = pl.BlockSpec(memory_space=pltpu.VMEM)
HBM = pl.BlockSpec(memory_space=pl.ANY)
SMEM = pl.BlockSpec(memory_space=pltpu.SMEM)
KINDS = {"v": VMEM, "s": SMEM, "h": HBM}


def call(body, name, ident, outs, operands, spaces, scratch, copies, flops=0):
    sems = [pltpu.SemaphoreType.DMA((copies,)), pltpu.SemaphoreType.DMA((copies,))]
    return pl.pallas_call(
        body,
        name=name,
        out_shape=tuple(jax.ShapeDtypeStruct(s, d) for s, d, _ in outs),
        in_specs=[KINDS[k] for k in spaces],
        out_specs=tuple(KINDS[k] for _, _, k in outs),
        scratch_shapes=[*scratch, *sems],
        compiler_params=pltpu.CompilerParams(
            collective_id=ident, has_side_effects=True, vmem_limit_bytes=VMEM_BYTES
        ),
        cost_estimate=pl.CostEstimate(flops=flops, bytes_accessed=20_000_000, transcendentals=0),
    )(*operands)


def piece_kernel(place_ref, gate_up_ref, down_ref, out_ref):
    chunk = (pl.program_id(0) * 2 + place_ref[0]) * 4 + place_ref[1]
    total = place_ref[3]
    row = lax.broadcasted_iota(jnp.int32, (PART, 128), 0) + chunk * PART
    inside = row < total
    both = gate_up_ref[...].astype(F32)
    out_ref[0, 0] = jnp.where(inside, both[:, 0], 0.0).astype(BF16)
    out_ref[0, 1] = jnp.where(inside, both[:, 1], 0.0).astype(BF16)
    out_ref[0, 2] = jnp.where(inside, down_ref[...].astype(F32), 0.0).astype(BF16)


def piece_of(gate_up, down, place):
    def chunk(y, place):
        return (y * 2 + place[0]) * 4 + place[1]

    return pl.pallas_call(
        piece_kernel,
        name="piece",
        grid_spec=pltpu.PrefetchScalarGridSpec(
            num_scalar_prefetch=1,
            grid=(4,),
            in_specs=[
                pl.BlockSpec((PART, 2, 128), lambda y, p: (chunk(y, p), 0, p[2])),
                pl.BlockSpec((PART, 128), lambda y, p: (chunk(y, p), p[2])),
            ],
            out_specs=pl.BlockSpec((1, 3, PART, 128), lambda y, p: (y, 0, 0, 0)),
        ),
        out_shape=jax.ShapeDtypeStruct((4, 3, PART, 128), BF16),
    )(place, gate_up, down)


def project_kernel(
    x_ref, w_ref, cos_ref, sin_ref, piece_ref, out_ref, q_ref, k_ref, v_ref, w_all_ref,
    all_ref, local, out_sem, send, recv,
):
    links = Links(send, recv)
    all_ref[0] = x_ref[...]
    to = links.to
    links.barrier(to(y=1), to(y=3), to(z=2), to(y=2), to(x=1), to(x=3), to(z=1), to(z=3))

    def work(pair):
        rows = pair_of(all_ref, pair)
        for part, out in enumerate((q_ref, k_ref, v_ref)):
            result = dot(rows, w_ref[part])
            for i, slot in enumerate(pair):
                at = pl.ds(links.first_row(slot), ROWS)
                piece = result[i * ROWS : (i + 1) * ROWS]
                if part == 2:
                    out[at] = piece.astype(BF16)
                    continue
                cosine, sine = cos_ref[at], sin_ref[at]
                for head in range(2):
                    lanes = slice(head * 128, head * 128 + 128)
                    turned = piece[:, lanes] * cosine + pltpu.roll(piece[:, lanes], 64, 1) * sine
                    if part == 0:
                        turned = turned * HEAD_DIM**-0.5
                    out[at, lanes] = turned.astype(BF16)

    written = pltpu.make_async_copy(all_ref, out_ref, out_sem)

    def tokens():
        yield from gather(links, all_ref, work)
        written.start()

    together(tokens(), spread(links, piece_ref, w_all_ref, GU, local))
    written.wait()


def attend_kernel(prefix_ref, q_ref, k_ref, v_ref, out_ref, lse_ref):
    block = q_ref.shape[0]
    first = pl.program_id(1) * block
    scores = dot_t(k_ref[...], q_ref[...])
    key = lax.broadcasted_iota(jnp.int32, scores.shape, 0)
    query = lax.broadcasted_iota(jnp.int32, (1, block), 1) + first
    limit = jnp.maximum(query, prefix_ref[0] - 1)
    scores = jnp.where(key <= limit, scores, -1e30)
    peak = jnp.max(scores, axis=0, keepdims=True)
    exponent = jnp.exp(scores - peak)
    total = jnp.sum(exponent, axis=0, keepdims=True)
    weights = (exponent * (1.0 / total)).astype(BF16)
    out_ref[...] = dot_rows(weights, v_ref[...]).astype(BF16)
    lse_ref[0] = peak + jnp.log(total)


def attend(prefix, q, k, v):
    block = 512
    return pl.pallas_call(
        attend_kernel,
        name="attend",
        grid=(2, LEN // block),
        in_specs=[
            SMEM,
            pl.BlockSpec((block, 128), lambda h, b: (b, h)),
            pl.BlockSpec((LEN, 128), lambda h, b: (0, h)),
            pl.BlockSpec((LEN, 128), lambda h, b: (0, h)),
        ],
        out_specs=(
            pl.BlockSpec((block, 128), lambda h, b: (b, h)),
            pl.BlockSpec((1, 1, block), lambda h, b: (h, 0, b)),
        ),
        out_shape=(
            jax.ShapeDtypeStruct((LEN, 256), BF16),
            jax.ShapeDtypeStruct((2, 1, LEN), F32),
        ),
        compiler_params=pltpu.CompilerParams(vmem_limit_bytes=VMEM_BYTES),
    )(prefix, q, k, v)


def attended_kernel(
    heads_ref, w_ref, x_ref, gain_ref, bias_ref, piece_ref, normed_ref, unit_ref, inverse_ref, w_all_ref,
    total, local, *rest,
):
    bufs, (send, recv) = rest[:7], rest[7:]
    links = Links(send, recv)
    to = links.to
    links.barrier(to(y=1), to(y=3), to(z=2), to(y=2), to(x=1), to(x=3), to(z=1), to(z=3))

    def compute(pair):
        rows = jnp.concatenate([heads_ref[pl.ds(links.first_row(s), ROWS)] for s in pair], axis=0)
        result = dot(rows, w_ref[...]).astype(BF16)
        for i, slot in enumerate(pair):
            bufs[0][slot] = result[i * ROWS : (i + 1) * ROWS]

    def finish(at):
        unit, inverse = norm_parts(deep_alpha * x_ref[at].astype(F32) + total[at])
        unit_ref[at] = unit
        inverse_ref[at] = jnp.broadcast_to(inverse, (16, 128))
        normed_ref[at] = unit * gain_ref[...] + bias_ref[...]

    def chain():
        yield from scatter(links, bufs, compute, total)
        by_chunks(finish)

    together(chain(), spread(links, piece_ref, w_all_ref, pl.ds(2, 1), local))


class Loads:
    def __init__(self):
        self.copies = []

    def start(self, src, dst, sem):
        copy = pltpu.make_async_copy(src, dst, sem)
        copy.start()
        self.copies.append(copy)

    def wait(self):
        while self.copies:
            self.copies.pop().wait()


def load_weights(w_hbm, w, sem, first, parts):
    loads = Loads()
    for k in range(parts):
        for i in range(16):
            src = w_hbm.at[k, lax.rem(i // 2, 2), i // 4, lax.rem(i, 2)]
            loads.start(src, w.at[first + k, pl.ds(0, FF), pl.ds(i * 128, 128)], sem.at[first + k, i])
    for k in range(parts):
        w[first + k, FF:COLS] = jnp.zeros((COLS - FF, WIDE), BF16)
    return loads


def feed_kernel(
    clusters_ref, normed_ref, cot_ref, gu_hbm, down_hbm, gain_ref, bias_ref,
    out_ref, all_out, gz_all_out, act_out, gz_ref, vec_ref,
    w, all_ref, gz_all_ref, act_ref, gelu_ref, slope, total, w_sem, out_sem, *rest,
):
    bufs, (send, recv) = rest[:4], rest[4:]
    links = Links(send, recv)

    def to_low(at):
        all_ref[0, at] = normed_ref[at].astype(BF16)

    by_chunks(to_low)
    load_gu = load_weights(gu_hbm, w, w_sem, 0, 2)
    load_down = load_weights(down_hbm, w, w_sem, 2, 1)
    links.barrier(links.to(y=1), links.to(y=3), links.to(sibling=True))
    written = Loads()

    def forward(pair):
        load_gu.wait()
        rows = pair_of(all_ref, pair)
        for c in range(0, COLS, 256):
            cols = slice(c, c + 256)
            gate = dot_t(rows, w[0, cols])
            up = dot_t(rows, w[1, cols])
            bell = 0.5 + 0.5 * lax.erf(gate * np.float32(np.sqrt(0.5)))
            gelu = gate * bell
            turn = bell + gate * (jnp.exp(-0.5 * gate * gate) * np.float32(1.0 / np.sqrt(2.0 * np.pi)))
            hidden = (gelu * up).astype(BF16)
            turn = turn * up
            for i, slot in enumerate(pair):
                part = slice(i * ROWS, (i + 1) * ROWS)
                gelu_ref[slot, :, cols] = gelu[part]
                slope[slot, :, cols] = turn[part]
                act_ref[slot, :, 2 * COLS + c : 2 * COLS + c + 256] = hidden[part]

    together(gather_near(links, all_ref, forward))
    written.start(all_ref, all_out, out_sem.at[8])

    def compute(pair):
        load_down.wait()
        rows = jnp.concatenate([act_ref[slot, :, 2 * COLS :] for slot in pair], axis=0)
        for d in range(0, WIDE, 512):
            result = dot(rows, w[2, :, d : d + 512]).astype(BF16)
            for i, slot in enumerate(pair):
                bufs[0][slot, :, d : d + 512] = result[i * ROWS : (i + 1) * ROWS]

    together(scatter_near(links, bufs, compute, total))
    vec_ref[...] = jnp.zeros_like(vec_ref)
    own, same = clusters_ref[lax.axis_index("dp")], np.float32(0.0)
    for i in range(clusters_ref.shape[0]):
        same = same + jnp.where(clusters_ref[i] == own, np.float32(1.0), np.float32(0.0))
    seq_weight = 1.0 / jnp.full((1, WIDE), same, F32)

    def finish(at):
        unit, inverse = norm_parts(deep_alpha * normed_ref[at] + total[at])
        out_ref[at] = (unit * gain_ref[...] + bias_ref[...]).astype(BF16)
        grad = cot_ref[at].astype(F32) * seq_weight
        grad_z = norm_backward(grad, unit, inverse, gain_ref[...])
        gz_ref[at] = grad_z
        gz_all_ref[0, at] = grad_z.astype(BF16)
        vec_ref[0] += rows8(grad * unit)
        vec_ref[1] += rows8(grad)

    by_chunks(finish)

    def backward(pair):
        rows = pair_of(gz_all_ref, pair)
        for c in range(0, COLS, 256):
            cols = slice(c, c + 256)
            grad_hidden = dot_t(rows, w[2, cols])
            for i, slot in enumerate(pair):
                part = grad_hidden[i * ROWS : (i + 1) * ROWS]
                act_ref[slot, :, cols] = (part * slope[slot, :, cols]).astype(BF16)
                act_ref[slot, :, COLS + c : COLS + c + 256] = (part * gelu_ref[slot, :, cols]).astype(BF16)
        for slot in pair:
            written.start(act_ref.at[slot], act_out.at[slot], out_sem.at[slot])

    together(gather_near(links, gz_all_ref, backward))
    written.start(gz_all_ref, gz_all_out, out_sem.at[9])
    written.wait()


def feed_back_kernel(
    act_hbm, gz_ref, w_hbm, normed_hbm, gz_all_hbm, unit_ref, inverse_ref, gain_ref, w_out_ref,
    gz1_ref, all_out, grad_heads_ref, vec_ref, shard_ref,
    act_ref, rows_ref, all_ref, w, total, w_sem, sem, *rest,
):
    bufs, more, (send, recv) = rest[:4], rest[4:13], rest[13:]
    links = Links(send, recv)
    load_act, load_rows = Loads(), Loads()
    load_act.start(act_hbm, act_ref, sem.at[0])
    load_w = load_weights(w_hbm, w, w_sem, 0, 2)
    load_rows.start(normed_hbm, rows_ref, sem.at[1])
    to = links.to
    links.barrier(
        to(y=1), to(y=3), to(z=2), to(x=1), to(x=3), to(z=1), to(z=3), to(sibling=True)
    )
    load_act.wait()
    load_w.wait()

    def compute(pair):
        rows = jnp.concatenate([act_ref[slot, :, : 2 * COLS] for slot in pair], axis=0)
        for d in range(0, WIDE, 512):
            cols = slice(d, d + 512)
            result = dot(rows[:, :COLS], w[0, :, cols]) + dot(rows[:, COLS:], w[1, :, cols])
            result = result.astype(BF16)
            for i, slot in enumerate(pair):
                bufs[0][slot, :, cols] = result[i * ROWS : (i + 1) * ROWS]

    def finish(at):
        grad = deep_alpha * gz_ref[at] + total[at]
        unit = unit_ref[at]
        grad_z = norm_backward(grad, unit, inverse_ref[at][:, 0:1], gain_ref[...])
        gz1_ref[at] = grad_z
        all_ref[0, at] = grad_z.astype(BF16)
        vec_ref[0] += rows8(grad * unit)
        vec_ref[1] += rows8(grad)

    def work(pair):
        result = dot_t(pair_of(all_ref, pair), w_out_ref[...]).astype(BF16)
        for i, slot in enumerate(pair):
            grad_heads_ref[pl.ds(links.first_row(slot), ROWS)] = result[i * ROWS : (i + 1) * ROWS]

    written = Loads()

    def chain():
        yield from scatter_near(links, bufs, compute, total)
        vec_ref[...] = jnp.zeros_like(vec_ref)
        by_chunks(finish)
        for time in gather(links, all_ref, work):
            yield time + 24
        written.start(all_ref, all_out, sem.at[3])

    g = more[0]

    def make(k):
        load_rows.wait()
        for c in range(0, COLS, 256):
            left = act_ref[:, :, k * COLS + c : k * COLS + c + 256].reshape(LEN, 256)
            height = min(256, FF - c)
            for d in range(0, WIDE, 512):
                right = rows_ref[:, :, d : d + 512].reshape(LEN, 512)
                result = dot_rows(left, right)[:height].astype(BF16)
                for i in range(4):
                    at = d // 128 + i
                    g[k, at // 2 % 2, at // 4, at % 2, c : c + height] = result[:, i * 128 : i * 128 + 128]
            if k == 1 and c == 512:
                load_rows.start(gz_all_hbm, rows_ref, sem.at[2])
            yield 8 + 6 * k + c // 128

    together(chain(), reduce(links, more, make, shard_ref))
    written.wait()


def input_kernel(
    prefix_ref, q_ref, k_ref, v_ref, g_ref, lse_ref, cos_ref, sin_ref,
    w_hbm, gz1_ref, tokens_hbm, heads_ref, gz_all_hbm, shard_ref, vec_in_ref,
    out_ref, q_out_ref, vec_ref, feed_ref,
    total, w_ref, tokens_ref, gz_all_ref, back, grads, heads, key_sum, value_sum, held, got, local, sem, *rest,
):
    bufs, more, (send, recv) = rest[:7], rest[7:12], rest[12:]
    links = Links(send, recv)
    to = links.to
    loads = Loads()
    loads.start(w_hbm, w_ref, sem.at[0])
    loads.start(tokens_hbm, tokens_ref, sem.at[1])
    loads.start(gz_all_hbm, gz_all_ref, sem.at[2])
    beside = (lax.rem(lax.axis_index("dp") + 8, 16), lax.axis_index("seq"))
    links.barrier(
        to(y=1), to(y=2), to(y=3), to(z=2), to(x=1), to(x=2), to(x=3), to(sibling=True), beside
    )
    vec_ref[...] = vec_in_ref[...]
    block = 512

    def attend_back():
        for head in range(2):
            lanes = slice(head * 128, head * 128 + 128)
            for first in range(0, LEN, block):
                at = slice(first, first + block)
                query, grad = q_ref[at, lanes], g_ref[at, lanes]
                scores = dot_t(k_ref[:, lanes], query)
                key = lax.broadcasted_iota(jnp.int32, scores.shape, 0)
                limit = lax.broadcasted_iota(jnp.int32, (1, block), 1) + first
                limit = jnp.maximum(limit, prefix_ref[0] - 1)
                weights = jnp.where(key <= limit, jnp.exp(scores - lse_ref[head, :, at]), 0.0)
                grad_weights = dot_t(v_ref[:, lanes], grad)
                inner = jnp.sum(weights * grad_weights, axis=0, keepdims=True)
                grad_scores = (weights * (grad_weights - inner)).astype(BF16)
                turned = dot_rows(grad_scores, k_ref[:, lanes]) * HEAD_DIM**-0.5
                turned = turned * cos_ref[at] - pltpu.roll(turned, 64, 1) * sin_ref[at]
                back[at, lanes] = turned.astype(BF16)
                grad_key = dot(grad_scores, query)
                grad_value = dot(weights.astype(BF16), grad)
                if first == 0:
                    key_sum[...] = grad_key
                    value_sum[...] = grad_value
                else:
                    key_sum[...] += grad_key
                    value_sum[...] += grad_value
                yield 4 * head + first // 200
            turned = key_sum[...]
            turned = turned * cos_ref[...] - pltpu.roll(turned, 64, 1) * sin_ref[...]
            back[:, 256 + head * 128 : 384 + head * 128] = turned.astype(BF16)
            back[:, 512 + head * 128 : 640 + head * 128] = value_sum[...].astype(BF16)

    def compute(pair):
        rows = pair_of(grads, pair)
        result = 0.0
        for part in range(3):
            result = result + dot_t(rows[:, part * 256 : part * 256 + 256], w_ref[part])
        result = result.astype(BF16)
        for i, slot in enumerate(pair):
            bufs[0][slot] = result[i * ROWS : (i + 1) * ROWS]

    def finish(at):
        value = deep_alpha * gz1_ref[at] + total[at]
        for lane in range(WIDE // 128):
            out_ref[at, lane] = value[:, lane * 128 : lane * 128 + 128]

    def chain():
        yield from attend_back()
        for slot in range(8):
            at = pl.ds(links.first_row(slot), ROWS)
            heads[slot] = heads_ref[at]
            grads[slot] = back[at]
        loads.wait()
        for time in scatter(links, bufs, compute, total):
            yield time + 14
        by_chunks(finish)

    def qkv():
        flat = more[0]
        right = grads[...].reshape(LEN, 768)
        for d in range(8):
            left = tokens_ref[:, :, d * 256 : d * 256 + 256].reshape(LEN, 256)
            result = dot_rows(left, right).astype(BF16)
            for part in range(3):
                chunk = part * 4 + d // 2
                flat[chunk // 8, chunk // 4 % 2, chunk % 4, d % 2 * 256 : d % 2 * 256 + 256] = result[
                    :, part * 256 : part * 256 + 256
                ]
        result = dot_rows(heads[...].reshape(LEN, 256), gz_all_ref[...].reshape(LEN, WIDE)).astype(BF16)
        for d in range(8):
            chunk = 12 + d // 2
            flat[chunk // 8, chunk // 4 % 2, chunk % 4, d % 2 * 256 : d % 2 * 256 + 256] = result[
                :, d * 256 : d * 256 + 256
            ]

    def shared():
        yield 18
        qkv()
        yield from share(links, more, q_out_ref, 31)

    together(
        collect(links, shard_ref, feed_ref, local, 0),
        chain(),
        shared(),
        agree(links, vec_ref, (held, got)),
    )


def outputs_kernel(feed_ref, qkv_ref, out_ref, gate_up_ref, down_ref, grad_qkv_ref, grad_out_ref):
    for z in range(2):
        lanes = slice(z * 128, z * 128 + 128)
        gate_up_ref[:, 0, lanes] = feed_ref[0, 0, 0, z].astype(F32)
        gate_up_ref[:, 1, lanes] = feed_ref[1, 0, 0, z].astype(F32)
        down_ref[:, lanes] = feed_ref[2, 0, 0, z].astype(F32)
    grad_qkv_ref[...] = qkv_ref[...].astype(F32)
    grad_out_ref[...] = out_ref[...].astype(F32)


def outputs(feed, attention, total):
    return pl.pallas_call(
        outputs_kernel,
        name="outputs",
        grid=(8,),
        in_specs=[
            pl.BlockSpec((3, 1, 1, 2, FF, 128), lambda i: (0, i // 2, i % 2, 0, 0, 0)),
            pl.BlockSpec((768, 256), lambda i: (i, 0)),
            pl.BlockSpec((256, 256), lambda i: (24 + i, 0)),
        ],
        out_specs=(
            pl.BlockSpec((FF, 2, 256), lambda i: (i, 0, 0)),
            pl.BlockSpec((FF, 256), lambda i: (i, 0)),
            pl.BlockSpec((768, 256), lambda i: (i, 0)),
            pl.BlockSpec((256, 256), lambda i: (0, i)),
        ),
        out_shape=(
            jax.ShapeDtypeStruct((total, 2, 256), F32),
            jax.ShapeDtypeStruct((total, 256), F32),
            jax.ShapeDtypeStruct((6144, 256), F32),
            jax.ShapeDtypeStruct((256, WIDE), F32),
        ),
        compiler_params=pltpu.CompilerParams(vmem_limit_bytes=VMEM_BYTES),
    )(feed, attention, attention)


def on_device(
    tokens, cotangent, w_qkv, w_out, w_gate_up, w_down,
    attn_gain, attn_bias, ffn_gain, ffn_bias, prefix_len, clusters,
):
    x = tokens.reshape(ROWS, WIDE)
    cot = cotangent.reshape(ROWS, WIDE)
    dp, seq = lax.axis_index("dp"), lax.axis_index("seq")
    cosine, sine = (jnp.asarray(t) for t in rotary_tables(LEN, HEAD_DIM))
    row = lambda v: v.reshape(1, WIDE)
    ff_total = w_down.shape[1]
    place = jnp.stack([dp % 2, dp // 2 % 4, dp // 8, jnp.int32(ff_total)]).astype(jnp.int32)
    piece = piece_of(w_gate_up.transpose(2, 1, 0), w_down.T, place)
    w_in = w_qkv.transpose(1, 0, 2)
    low, full = BF16, F32
    blocks = (8, ROWS, WIDE)
    one = pltpu.SemaphoreType.DMA
    some = lambda *n: pltpu.SemaphoreType.DMA(n)
    rows_f32 = pltpu.VMEM((ROWS, WIDE), F32)
    blocks_low = pltpu.VMEM(blocks, BF16)

    tokens_all, q, k, v, w_gu = call(
        project_kernel, "project", 0,
        [(blocks, low, "h")] + [((LEN, 256), low, "v")] * 3 + [((2, 2, 4, 2, FF, 128), low, "h")],
        (x, w_in, cosine, sine, piece), "vvvvv", (blocks_low, one, one), 60,
        2 * LEN * WIDE * 768,
    )
    heads_out, lse = attend(prefix_len, q, k, v)
    normed, unit_one, inverse_one, w_dn = call(
        attended_kernel, "attended", 1,
        [
            ((ROWS, WIDE), full, "v"), ((ROWS, WIDE), full, "v"), ((ROWS, 128), full, "v"),
            ((1, 2, 4, 2, FF, 128), low, "h"),
        ],
        (heads_out, w_out, x, row(attn_gain), row(attn_bias), piece), "vvvvvv",
        (rows_f32, one, *SCATTER_SCRATCH), 42, 2 * LEN * WIDE * 256,
    )
    output, normed_all, gz_all, act, grad_z2, ffn_vec = call(
        feed_kernel, "feed", 2,
        [
            ((ROWS, WIDE), low, "v"), (blocks, low, "h"), (blocks, low, "h"),
            ((8, ROWS, 3 * COLS), low, "h"), ((ROWS, WIDE), full, "v"), ((2, 8, WIDE), full, "v"),
        ],
        (clusters, normed, cot, w_gu, w_dn, row(ffn_gain), row(ffn_bias)), "svvhhvv",
        (
            pltpu.VMEM((3, COLS, WIDE), BF16), blocks_low, blocks_low,
            pltpu.VMEM((8, ROWS, 3 * COLS), BF16), pltpu.VMEM((8, ROWS, COLS), F32),
            pltpu.VMEM((8, ROWS, COLS), F32), rows_f32, some(3, 16), some(10), *NEAR_SCRATCH,
        ),
        34, 2 * LEN * WIDE * COLS * 4,
    )
    grad_z1, gz1_all, grad_heads, attn_vec, shard = call(
        feed_back_kernel, "feed_back", 3,
        [
            ((ROWS, WIDE), full, "v"), (blocks, low, "h"), ((LEN, 256), low, "v"),
            ((2, 8, WIDE), full, "v"), ((3, 4, PART, 128), low, "v"),
        ],
        (act, grad_z2, w_gu, normed_all, gz_all, unit_one, inverse_one, row(attn_gain), w_out),
        "hvhhhvvvv",
        (
            pltpu.VMEM((8, ROWS, 3 * COLS), BF16), blocks_low, blocks_low,
            pltpu.VMEM((2, COLS, WIDE), BF16), rows_f32, some(2, 16), some(4),
            *NEAR_SCRATCH, *REDUCE_SCRATCH,
        ),
        52, 2 * LEN * WIDE * COLS * 5,
    )
    vec = jnp.concatenate([attn_vec.sum(1), ffn_vec.sum(1), jnp.zeros((4, WIDE), F32)], axis=0)
    steps = pltpu.VMEM((7, 8, WIDE), F32)
    head_sum = pltpu.VMEM((LEN, 128), F32)
    input_grad, attention, vec, ffn_whole = call(
        input_kernel, "input", 4,
        [
            ((ROWS, WIDE // 128, 128), full, "v"), ((2, 2, 4, 512, 256), low, "v"), ((8, WIDE), full, "v"),
            ((3, 4, 2, 2, FF, 128), low, "h"),
        ],
        (
            prefix_len, q, k, v, grad_heads, lse, cosine, sine,
            w_in, grad_z1, tokens_all, heads_out, gz1_all, shard, vec,
        ),
        "svvvvvvvhvhvhvv",
        (
            rows_f32, pltpu.VMEM((3, WIDE, 256), BF16), blocks_low, blocks_low,
            pltpu.VMEM((LEN, 768), BF16), pltpu.VMEM((8, ROWS, 768), BF16),
            pltpu.VMEM((8, ROWS, 256), BF16), head_sum, head_sum, steps, steps, one, some(3),
            *SCATTER_SCRATCH, *SHARE_SCRATCH,
        ),
        77, 2 * LEN * WIDE * 768,
    )
    grad_gate_up, grad_down, grad_qkv, grad_out = outputs(
        ffn_whole, attention.reshape(8192, 256), ff_total
    )
    own = lax.dynamic_slice_in_dim(vec, seq * 256, 256, axis=1)
    return (
        output.reshape(tokens.shape),
        input_grad.reshape(tokens.shape),
        grad_qkv.reshape(3, WIDE, 256).transpose(1, 0, 2),
        grad_out,
        grad_gate_up.transpose(2, 1, 0),
        grad_down.T,
        own[0],
        own[1],
        own[2],
        own[3],
    )


def solution(mesh):
    return jax.shard_map(
        on_device,
        mesh=mesh,
        in_specs=(
            P("seq", "dp", None), P("seq", "dp", None), P(None, None, "seq"), P("seq", None),
            P("seq", None, None), P("seq", None), P(), P(), P(), P(), P("dp"), P(),
        ),
        out_specs=(
            P("seq", "dp", None), P("seq", "dp", None), P(None, None, "seq"), P("seq", None),
            P("seq", None, None), P("seq", None), P("seq"), P("seq"), P("seq"), P("seq"),
        ),
        check_vma=False,
    )
```

```python
import functools

import jax
import jax.numpy as jnp
import numpy as np
from jax import lax
from jax.experimental import pallas as pl
from jax.experimental.pallas import tpu as pltpu
from jax.sharding import PartitionSpec as P

MESH = pl.DeviceIdType.MESH
F32, BF16 = jnp.float32, jnp.bfloat16
HEAD_DIM = 128
ROWS = 128
WIDE = 2048
COLS = 768
LEN = 1024
VMEM_BYTES = 60 * 1024 * 1024
deep_alpha = 48.0**0.25
norm_eps = 1e-05
rotary_base = 10000.0


def rotary_tables(length, head_width):
    half_width = head_width // 2
    position = np.arange(length, dtype=np.float64)
    inverse = rotary_base ** (-np.arange(half_width, dtype=np.float64) * 2.0 / head_width)
    angles = position[:, None] * inverse[None, :]
    cosine_table = np.cos(angles)
    sine_table = np.sin(angles)
    return (
        np.concatenate([cosine_table, cosine_table], axis=1).astype(np.float32),
        np.concatenate([-sine_table, sine_table], axis=1).astype(np.float32),
    )


FF = 704
PART = 176


class Links:
    def __init__(self, send, recv):
        self.send, self.recv, self.count = send, recv, 0
        dp, seq = lax.axis_index("dp"), lax.axis_index("seq")
        y, z_hi = seq // 2, lax.rem(seq, 2)
        z_lo, x, core = dp // 8, lax.rem(dp // 2, 4), lax.rem(dp, 2)
        self.y, self.z_hi, self.z_lo, self.x, self.core = y, z_hi, z_lo, x, core
        self.z = z_hi * 2 + z_lo

    def to(self, x=0, y=0, z=0, sibling=False):
        z_hi, z_lo = self.z_at(z)
        x, y = lax.rem(self.x + x, 4), lax.rem(self.y + y, 4)
        core = 1 - self.core if sibling else self.core
        return (z_lo * 8 + x * 2 + core, y * 2 + z_hi)

    def beside(self):
        return (lax.rem(lax.axis_index("dp") + 8, 16), lax.axis_index("seq"))

    def z_at(self, offset):
        z = lax.rem(self.z + offset, 4)
        return z // 2, lax.rem(z, 2)

    def part(self, offset):
        return pl.ds(pl.multiple_of(lax.rem(self.x + offset, 4) * PART, 16), PART)

    def barrier(self, *where):
        gate = pltpu.get_barrier_semaphore()
        for device in where:
            pl.semaphore_signal(gate, inc=1, device_id=device, device_id_type=MESH)
        pl.semaphore_wait(gate, len(where))

    def start(self, src, dst, where):
        assert self.count < self.send.shape[0]
        copy = pltpu.make_async_remote_copy(
            src_ref=src,
            dst_ref=dst,
            send_sem=self.send.at[self.count],
            recv_sem=self.recv.at[self.count],
            device_id=where,
            device_id_type=MESH,
        )
        self.count += 1
        copy.start()
        return copy

    def first_row(self, slot):
        step = (0, 3, 1, 2)[slot % 4]
        half = self.z_hi if slot < 4 else 1 - self.z_hi
        return pl.multiple_of((lax.rem(self.y + step, 4) * 2 + half) * ROWS, ROWS)


class Once:
    def __init__(self, *copies):
        self.copies = list(copies)

    def wait_recv(self):
        while self.copies:
            self.copies.pop().wait_recv()


class Mark:
    done = False


class Local:
    def __init__(self, src, dst, sem):
        self.copy = pltpu.make_async_copy(src, dst, sem)
        self.copy.start()

    def wait_recv(self):
        self.copy.wait()


def together(order, *tasks):
    tasks = list(tasks)
    for task in tasks:
        next(task)
    left = len(tasks)
    for which in order:
        try:
            next(tasks[which])
        except StopIteration:
            left -= 1
    assert left == 0


def alone(task):
    for _ in task:
        pass


def received(*copies):
    for copy in copies:
        copy.wait_recv()


def sent(copies):
    for copy in copies:
        copy.wait_send()


H0, H1 = pl.ds(0, 64), pl.ds(64, 64)


def gather(links, buf, work):
    up, down, across = links.to(y=1), links.to(y=3), links.to(z=2)
    copies = []

    def send(slot, rows, dst, where):
        copies.append(links.start(buf.at[slot, rows], buf.at[dst, rows], where))
        return copies[-1]

    u0, d1 = send(0, H0, 1, up), send(0, H1, 2, down)
    z0, z1 = send(0, H0, 4, across), send(0, H1, 4, across)
    u1, d0 = send(0, H1, 1, up), send(0, H0, 2, down)
    yield u0, d1
    received(u0)
    fu = send(1, H0, 3, up)
    received(d1)
    fd = send(2, H1, 3, down)
    yield z0, z1
    received(z0)
    pu0 = send(4, H0, 5, up)
    received(z1)
    pd1 = send(4, H1, 6, down)
    pu1, pd0 = send(4, H1, 5, up), send(4, H0, 6, down)
    yield u1, d0
    received(u1, d0)
    work((0, 1))
    yield fu, fd
    received(fu, fd)
    work((2, 3))
    yield pu0, pd1
    received(pu0)
    gu = send(5, H0, 7, up)
    received(pd1)
    gd = send(6, H1, 7, down)
    yield pu1, pd0
    received(pu1, pd0)
    work((4, 5))
    yield gu, gd
    received(gu, gd)
    work((6, 7))
    sent(copies)


def gather_near(links, buf, work):
    up, down, side = links.to(y=1), links.to(y=3), links.to(sibling=True)
    copies = []

    def send(slot, rows, dst, where):
        copies.append(links.start(buf.at[slot, rows], buf.at[dst, rows], where))
        return copies[-1]

    every = pl.ds(0, ROWS)
    u0, d1 = send(0, H0, 1, up), send(0, H1, 2, down)
    u1, d0 = send(0, H1, 1, up), send(0, H0, 2, down)
    s0 = send(0, every, 4, side)
    yield 1
    received(s0)
    work((0, 4))
    yield 6
    received(u0)
    fu = send(1, H0, 3, up)
    received(d1)
    fd = send(2, H1, 3, down)
    yield 11
    received(u1)
    s1 = send(1, every, 5, side)
    received(d0)
    s2 = send(2, every, 6, side)
    work((1, 2))
    yield 13
    received(s1, s2)
    work((5, 6))
    yield 17
    received(fu)
    s30 = send(3, H0, 7, side)
    received(fd)
    s31 = send(3, H1, 7, side)
    yield 18
    received(s30, s31)
    work((3, 7))
    sent(copies)


A, B = pl.ds(0, 80), pl.ds(80, 48)
A0, A1 = pl.ds(0, 48), pl.ds(48, 32)
B0, B1 = pl.ds(80, 16), pl.ds(96, 32)
SCATTER_SCRATCH = (
    pltpu.VMEM((8, ROWS, WIDE), BF16),
    pltpu.VMEM((4, 48, WIDE), BF16),
    pltpu.VMEM((48, WIDE), BF16),
    pltpu.VMEM((2, 48, WIDE), BF16),
    pltpu.VMEM((2, 80, WIDE), BF16),
    pltpu.VMEM((2, 2, 80, WIDE), BF16),
    pltpu.VMEM((80, WIDE), BF16),
)


def add_rows(target, slot, rows, *others):
    value = target[slot, rows].astype(F32)
    for other in others:
        value = value + other.astype(F32)
    target[slot, rows] = value.astype(BF16)


def scatter(links, bufs, compute, total):
    sums, from_z, b_far, b_near, a_far, a_near, a_z = bufs
    up, down, across = links.to(y=1), links.to(y=3), links.to(z=2)
    copies = []

    def send(src, dst, where):
        copies.append(links.start(src, dst, where))
        return copies[-1]

    def far_a(o):
        half = o // 4
        return (
            send(sums.at[o + 3, A0], a_far.at[half, pl.ds(0, 48)], up),
            send(sums.at[o + 3, A1], a_far.at[half, pl.ds(48, 32)], down),
        )

    def near_a(o, far):
        half = o // 4
        received(far[0])
        add_rows(sums, o + 2, A0, a_far[half, 0:48])
        one = send(sums.at[o + 2, A], a_near.at[half, 0], up)
        received(far[1])
        add_rows(sums, o + 1, A1, a_far[half, 48:80])
        return one, send(sums.at[o + 1, A], a_near.at[half, 1], down)

    def cross_b(j):
        return send(sums.at[4 + j, B], from_z.at[j], across)

    compute((7, 3))
    z3 = cross_b(3)
    far_other = far_a(4)
    far_own = far_a(0)
    compute((5, 6))
    z1, z2 = cross_b(1), cross_b(2)
    compute((1, 2))
    yield far_other
    near_other = near_a(4, far_other)
    compute((4, 0))
    z0 = cross_b(0)
    yield (z3,)
    received(z3)
    add_rows(sums, 3, B, from_z[3])
    far_b = (
        send(sums.at[3, B0], b_far.at[pl.ds(0, 16)], up),
        send(sums.at[3, B1], b_far.at[pl.ds(16, 32)], down),
    )
    yield far_own
    near_own = near_a(0, far_own)
    yield z1, z2
    received(z2)
    add_rows(sums, 2, B, from_z[2])
    received(z1)
    add_rows(sums, 1, B, from_z[1])
    yield far_b
    received(far_b[0])
    add_rows(sums, 2, B0, b_far[0:16])
    near_b0 = send(sums.at[2, B], b_near.at[0], up)
    received(far_b[1])
    add_rows(sums, 1, B1, b_far[16:48])
    near_b1 = send(sums.at[1, B], b_near.at[1], down)
    yield near_other
    received(*near_other)
    add_rows(sums, 4, A, a_near[1, 0], a_near[1, 1])
    z_a = send(sums.at[4, A], a_z, across)
    yield z0, near_b0, near_b1
    received(z0, near_b0, near_b1)
    total[80:128] = (
        sums[0, B].astype(F32)
        + from_z[0].astype(F32)
        + b_near[0].astype(F32)
        + b_near[1].astype(F32)
    )
    yield (z_a, *near_own)
    received(*near_own)
    received(z_a)
    total[0:80] = (
        sums[0, A].astype(F32)
        + a_near[0, 0].astype(F32)
        + a_near[0, 1].astype(F32)
        + a_z[...].astype(F32)
    )
    sent(copies)


NEAR_SCRATCH = (
    pltpu.VMEM((8, ROWS, WIDE), BF16),
    pltpu.VMEM((4, ROWS, WIDE), BF16),
    pltpu.VMEM((ROWS, WIDE), BF16),
    pltpu.VMEM((2, ROWS, WIDE), BF16),
)


def scatter_near(links, bufs, compute, total):
    sums, from_side, far, near = bufs
    up, down, side = links.to(y=1), links.to(y=3), links.to(sibling=True)
    copies = []

    def send(src, dst, where):
        copies.append(links.start(src, dst, where))
        return copies[-1]

    every = pl.ds(0, ROWS)
    compute((7, 3))
    s3 = send(sums.at[7], from_side.at[3], side)
    compute((5, 6))
    s1 = send(sums.at[5], from_side.at[1], side)
    s2 = send(sums.at[6], from_side.at[2], side)
    received(s3)
    add_rows(sums, 3, every, from_side[3])
    fu = send(sums.at[3, H0], far.at[H0], up)
    fd = send(sums.at[3, H1], far.at[H1], down)
    compute((1, 2))
    received(s1, s2)
    add_rows(sums, 2, every, from_side[2])
    nu1 = send(sums.at[2, H1], near.at[0, H1], up)
    add_rows(sums, 1, every, from_side[1])
    nd0 = send(sums.at[1, H0], near.at[1, H0], down)
    compute((4, 0))
    s0 = send(sums.at[4], from_side.at[0], side)
    yield fu, fd
    received(fu)
    add_rows(sums, 2, H0, far[0:64])
    nu0 = send(sums.at[2, H0], near.at[0, H0], up)
    received(fd)
    add_rows(sums, 1, H1, far[64:128])
    nd1 = send(sums.at[1, H1], near.at[1, H1], down)
    yield s0, nu1, nd0, nu0, nd1
    received(s0, nu1, nd0, nu0, nd1)
    total[...] = (
        sums[0].astype(F32)
        + from_side[0].astype(F32)
        + near[0].astype(F32)
        + near[1].astype(F32)
    )
    sent(copies)


Y0, Y1 = pl.ds(0, 2), pl.ds(2, 2)
GU = pl.ds(0, 2)


def across_y(links, piece, own, local):
    copies = []
    for step in (2, 1, 3):
        there = lax.rem(links.y + step, 4)
        copies.append(links.start(piece(there), own(), links.to(y=step)))
    keep = Local(piece(links.y), own(), local)
    return Once(keep, *copies), copies


def ring_gather(links, arrived, at, first, second):
    up, down = first
    right, left = second
    copies = []

    def send(ref, where):
        copies.append(links.start(ref, ref, where))
        return copies[-1]

    def both(a):
        return send(at(a, 0), right), send(at(a, 0), left)

    def onward(a):
        return send(at(a, 3, Y0), right), send(at(a, 1, Y1), left)

    yield (arrived,)
    received(arrived)
    u, d = send(at(0, 0), up), send(at(0, 0), down)
    near = [both(0)]
    yield u, d
    received(u)
    fu = send(at(3, 0, Y0), up)
    received(d)
    fd = send(at(1, 0, Y1), down)
    near.append(both(3))
    near.append(both(1))
    yield near[0]
    received(*near[0])
    far = [*onward(0)]
    yield fu, fd
    received(fu, fd)
    near.append(both(2))
    for i, a in enumerate((3, 1, 2)):
        yield near[1 + i]
        received(*near[1 + i])
        far += onward(a)
    yield far
    received(*far)
    sent(copies)


def spread(links, piece, w, matrices, local):
    along_x = (links.to(x=1), links.to(x=3))
    along_z = (links.to(z=1), links.to(z=3))
    every = pl.ds(0, 4)

    def place(k, z, x, y):
        z_hi, z_lo = links.z_at(z)
        return w.at[k, z_hi, y, z_lo, links.part(x)]

    def own():
        return w.at[:, links.z_hi, links.y, links.z_lo, links.part(0)]

    arrived, copies = across_y(links, lambda y: piece.at[y, matrices], own, local)

    def one():
        yield from ring_gather(links, arrived, lambda a, b, y=every: place(0, a, b, y), along_z, along_x)
        sent(copies)

    def two():
        yield from ring_gather(links, arrived, lambda a, b, y=every: place(1, b, a, y), along_x, along_z)

    return (one(),) if matrices.size == 1 else (one(), two())


def ring_scratch(*block):
    return [pltpu.VMEM(block, BF16), pltpu.VMEM((2, *block), BF16)]


REDUCE_SCRATCH = (
    pltpu.VMEM((3, 4, 2, 2, FF, 128), BF16),
    *ring_scratch(4, 2, 2, PART, 128), *ring_scratch(4, PART, 128),
    *ring_scratch(4, 2, 2, PART, 128), *ring_scratch(4, PART, 128),
    *ring_scratch(4, FF, 128), *ring_scratch(4, PART, 128),
)


def accumulate(count, target, *others):
    def step(i, carry):
        ref = target(i)
        value = ref[...].astype(F32)
        for other in others:
            value = value + other(i)[...].astype(F32)
        ref[...] = value.astype(BF16)
        return carry

    lax.fori_loop(0, count, step, 0)


def ring_reduce(links, at, blocks, ring, far, near, devices):
    up, down = devices
    copies = []
    every = pl.ds(0, 4)

    def send(src, dst, where):
        copies.append(links.start(src, dst, where))
        return copies[-1]

    half = ring // 2
    fu, fd = send(at(2, Y0), far.at[Y0], up), send(at(2, Y1), far.at[Y1], down)
    nu, nd = send(at(1, Y1), near.at[0, Y1], up), send(at(3, Y0), near.at[1, Y0], down)
    yield fu, fd
    received(fu)
    accumulate(half, lambda i: blocks(at(1, every), i), lambda i: blocks(far, i))
    mu = send(at(1, Y0), near.at[0, Y0], up)
    received(fd)
    accumulate(half, lambda i: blocks(at(3, every), i + half), lambda i: blocks(far, i + half))
    md = send(at(3, Y1), near.at[1, Y1], down)
    yield nu, nd, mu, md
    received(nu, nd, mu, md)
    accumulate(
        ring, lambda i: blocks(at(0, every), i), lambda i: blocks(near.at[0], i), lambda i: blocks(near.at[1], i)
    )
    sent(copies)


def reduce(links, bufs, make, shard):
    g = bufs[0]
    along_x = (links.to(x=1), links.to(x=3))
    along_z = (links.to(z=1), links.to(z=3))
    made = [Mark(), Mark()]

    def one(k, x_first):
        far, near, far2, near2 = bufs[1 + 4 * k : 5 + 4 * k]
        z_hi, z_lo = links.z_at(0)

        def along_z_at(a, y):
            hi, lo = links.z_at(a)
            return g.at[k, y, hi, lo]

        def along_x_at(a, y):
            return g.at[k, y, :, :, links.part(a)]

        def rest_z(a, y):
            hi, lo = links.z_at(a)
            return g.at[k, y, hi, lo, links.part(0)]

        def rest_x(a, y):
            return g.at[k, y, z_hi, z_lo, links.part(a)]

        def four(ref, i):
            return ref.at[i // 4, lax.rem(i // 2, 2), lax.rem(i, 2)]

        def plain(ref, i):
            return ref.at[i]

        if k:
            yield (made[k - 1],)
        yield from make(k)
        if k < 2:
            made[k].done = True
        if x_first:
            yield from ring_reduce(links, along_x_at, four, 16, far, near, along_x)
            yield from ring_reduce(links, rest_z, plain, 4, far2, near2, along_z)
        else:
            yield from ring_reduce(links, along_z_at, plain, 4, far, near, along_z)
            yield from ring_reduce(links, rest_x, plain, 4, far2, near2, along_x)
        shard[k] = g[k, :, z_hi, z_lo, links.part(0)]

    return one(0, True), one(1, True), one(2, False)


def regather(links, at, half):
    xp, xm, side = links.to(x=1), links.to(x=3), links.to(sibling=True)
    beside = links.beside()
    copies, sides = [], []

    def send(ref, where):
        copies.append(links.start(ref, ref, where))
        return copies[-1]

    def share(ref):
        sides.append(send(ref, side))

    z = send(at(0, 0), beside)
    near = [(send(at(0, 0), xp), send(at(0, 0), xm))]
    share(at(0, 0))
    yield (z,)
    received(z)
    near.append((send(at(1, 0), xp), send(at(1, 0), xm)))
    share(at(1, 0))
    far = []
    for i in range(2):
        yield near[i]
        received(near[i][0])
        far_up = send(half(at(i, 3), 0), xp)
        received(near[i][1])
        far.append((far_up, send(half(at(i, 1), 1), xm)))
        share(at(i, 3))
        share(at(i, 1))
    for i in range(2):
        yield far[i]
        received(*far[i])
        share(at(i, 2))
    yield sides
    received(*sides)
    sent(copies)


def collect(links, shard, out, local):
    def own():
        return out.at[:, links.y, links.core, links.z_lo, links.part(0)]

    arrived, copies = across_y(links, lambda y: shard.at[:, y], own, local)
    yield (arrived,)
    received(arrived)

    def at(z, x):
        return out.at[:, :, links.core, lax.rem(links.z_lo + z, 2), links.part(x)]

    def half(ref, i):
        return ref.at[:, pl.ds(2 * i, 2)]

    yield from regather(links, at, half)
    sent(copies)


def share_scratch(rows, lanes):
    return [
        pltpu.VMEM((2, 2, 4, rows, lanes), BF16),
        pltpu.VMEM((2, 4, rows, lanes), BF16),
        pltpu.VMEM((2, rows, lanes), BF16),
        pltpu.VMEM((2, 2, rows, lanes), BF16),
        pltpu.VMEM((rows, lanes), BF16),
    ]


def share(links, bufs, out):
    q, from_side, far, near, from_z = bufs
    xp, xm, side = links.to(x=1), links.to(x=3), links.to(sibling=True)
    beside = links.beside()
    core, z_lo = links.core, links.z_lo
    count = q.shape[3]
    copies = []

    def send(src, dst, where):
        copies.append(links.start(src, dst, where))
        return copies[-1]

    def there(x):
        return lax.rem(links.x + x, 4)

    def rows(ref):
        return lambda i: ref.at[pl.ds(pl.multiple_of(i * 64, 64), 64)]

    def add(target, *others):
        accumulate(count // 64, rows(target), *(rows(other) for other in others))

    s = send(q.at[1 - core], from_side, side)
    yield (s,)
    received(s)
    for x in (2, 1, 3, 0):
        for z in range(2):
            add(q.at[core, z, there(x)], from_side.at[z, there(x)])
        if x == 2:
            fu, fd = send(q.at[core, 0, there(2)], far.at[0], xp), send(q.at[core, 1, there(2)], far.at[1], xm)
    nu = send(q.at[core, 1, there(1)], near.at[0, 1], xp)
    nd = send(q.at[core, 0, there(3)], near.at[1, 0], xm)
    yield fu, fd
    received(fu)
    add(q.at[core, 0, there(1)], far.at[0])
    mu = send(q.at[core, 0, there(1)], near.at[0, 0], xp)
    received(fd)
    add(q.at[core, 1, there(3)], far.at[1])
    md = send(q.at[core, 1, there(3)], near.at[1, 1], xm)
    yield nu, nd, mu, md
    received(nu, nd, mu, md)
    for z in range(2):
        add(q.at[core, z, there(0)], near.at[0, z], near.at[1, z])
    b = send(q.at[core, 1 - z_lo, there(0)], from_z, beside)
    yield (b,)
    received(b)

    def finish(i, carry):
        at = pl.ds(pl.multiple_of(i * 64, 64), 64)
        value = q[core, z_lo, links.x, at].astype(F32) + from_z[at].astype(F32)
        out[core, z_lo, links.x, at] = value.astype(BF16)
        return carry

    lax.fori_loop(0, count // 64, finish, 0)

    def at(z, x):
        return out.at[core, lax.rem(z_lo + z, 2), there(x)]

    def half(ref, i):
        return ref.at[pl.ds(count // 2 * i, count // 2)]

    yield from regather(links, at, half)
    sent(copies)


def agree(links, vec, bufs):
    y, x = links.y, links.x
    copies = []
    steps = (
        links.to(sibling=True),
        links.to(y=1 + 2 * lax.rem(y, 2)),
        links.to(y=2),
        links.to(z=2),
        links.to(x=1 + 2 * lax.rem(x, 2)),
        links.to(x=2),
        links.beside(),
    )
    held, got = bufs
    held[0] = vec[...]
    for i, where in enumerate(steps):
        copies.append(links.start(held.at[i], got.at[i], where))
        yield (copies[-1],)
        received(copies[-1])
        if i < len(steps) - 1:
            held[i + 1] = held[i] + got[i]
        else:
            vec[...] = held[i] + got[i]
    sent(copies)


def dot(a, b):
    return jnp.dot(a, b, preferred_element_type=F32)


def dot_t(a, b):
    return lax.dot_general(a, b, (((1,), (1,)), ((), ())), preferred_element_type=F32)


def dot_rows(a, b):
    return lax.dot_general(a, b, (((0,), (0,)), ((), ())), preferred_element_type=F32)


def pair_of(ref, pair):
    return jnp.concatenate([ref[pair[0]], ref[pair[1]]], axis=0)


def by_chunks(body):
    def step(i, carry):
        body(pl.ds(pl.multiple_of(i * 16, 16), 16))
        return carry

    lax.fori_loop(0, ROWS // 16, step, 0)


def norm_parts(row_total):
    center = row_total - jnp.mean(row_total, axis=-1, keepdims=True)
    spread = jnp.mean(center * center, axis=-1, keepdims=True)
    inverse = lax.rsqrt(spread + norm_eps)
    return center * inverse, inverse


def norm_backward(grad_result, unit, inverse, gain):
    grad_unit = grad_result * gain
    return inverse * (
        grad_unit
        - jnp.mean(grad_unit, axis=-1, keepdims=True)
        - unit * jnp.mean(grad_unit * unit, axis=-1, keepdims=True)
    )


def rows8(values):
    return values[0:8] + values[8:16]


VMEM = pl.BlockSpec(memory_space=pltpu.VMEM)
HBM = pl.BlockSpec(memory_space=pl.ANY)
SMEM = pl.BlockSpec(memory_space=pltpu.SMEM)
KINDS = {"v": VMEM, "s": SMEM, "h": HBM}


def call(body, name, ident, outs, operands, spaces, scratch, copies, flops=0):
    sems = [pltpu.SemaphoreType.DMA((copies,)), pltpu.SemaphoreType.DMA((copies,))]
    return pl.pallas_call(
        body,
        name=name,
        out_shape=tuple(jax.ShapeDtypeStruct(s, d) for s, d, _ in outs),
        in_specs=[KINDS[k] for k in spaces],
        out_specs=tuple(KINDS[k] for _, _, k in outs),
        scratch_shapes=[*scratch, *sems],
        compiler_params=pltpu.CompilerParams(
            collective_id=ident, has_side_effects=True, vmem_limit_bytes=VMEM_BYTES
        ),
        cost_estimate=pl.CostEstimate(flops=flops, bytes_accessed=20_000_000, transcendentals=0),
    )(*operands)


PROJECT = (1, 2, 0, 0, 1, 2, 1, 0, 2, 1, 1, 0, 1, 0, 2, 2, 2, 0, 1, 2, 0, 1, 2)
ATTENDED = (1, 0, 0, 0, 0, 1, 1, 0, 0, 1, 1, 1, 0, 0, 1, 1)
FEED_BACK = (1, 1, 2, 2, 2, 3, 3, 3, 0, 1, 0, 3, 2, 0, 0, 0, 0, 1, 3, 1, 0, 2, 3, 1, 0, 2, 3, 0, 2)
INPUT = (2, 1, 0, 5, 2, 1, 2, 3, 3, 5, 2, 3, 0, 2, 0, 3, 2, 4, 4, 2, 5, 1, 4, 0, 2, 2, 2, 0, 3, 2, 2, 4, 5, 1, 3, 0, 0, 4, 2, 2, 1, 5, 3, 1, 3, 4, 1, 5, 3, 4, 3, 5, 1, 4, 1, 3, 3, 4, 1, 4, 4, 4)


def piece_kernel(place_ref, gate_up_ref, down_ref, out_ref):
    chunk = (pl.program_id(0) * 2 + place_ref[0]) * 4 + place_ref[1]
    total = place_ref[3]
    row = lax.broadcasted_iota(jnp.int32, (PART, 128), 0) + chunk * PART
    inside = row < total
    both = gate_up_ref[...].astype(F32)
    out_ref[0, 0] = jnp.where(inside, both[:, 0], 0.0).astype(BF16)
    out_ref[0, 1] = jnp.where(inside, both[:, 1], 0.0).astype(BF16)
    out_ref[0, 2] = jnp.where(inside, down_ref[...].astype(F32), 0.0).astype(BF16)


def piece_of(gate_up, down, place):
    def chunk(y, place):
        return (y * 2 + place[0]) * 4 + place[1]

    return pl.pallas_call(
        piece_kernel,
        name="piece",
        grid_spec=pltpu.PrefetchScalarGridSpec(
            num_scalar_prefetch=1,
            grid=(4,),
            in_specs=[
                pl.BlockSpec((PART, 2, 128), lambda y, p: (chunk(y, p), 0, p[2])),
                pl.BlockSpec((PART, 128), lambda y, p: (chunk(y, p), p[2])),
            ],
            out_specs=pl.BlockSpec((1, 3, PART, 128), lambda y, p: (y, 0, 0, 0)),
        ),
        out_shape=jax.ShapeDtypeStruct((4, 3, PART, 128), BF16),
    )(place, gate_up, down)


def project_kernel(
    x_ref, w_ref, cos_ref, sin_ref, piece_ref, out_ref, q_ref, k_ref, v_ref, w_all_ref,
    all_ref, local, out_sem, send, recv,
):
    links = Links(send, recv)
    all_ref[0] = x_ref[...]
    to = links.to
    links.barrier(to(y=1), to(y=3), to(z=2), to(y=2), to(x=1), to(x=3), to(z=1), to(z=3))

    def work(pair):
        rows = pair_of(all_ref, pair)
        for part, out in enumerate((q_ref, k_ref, v_ref)):
            result = dot(rows, w_ref[part])
            for i, slot in enumerate(pair):
                at = pl.ds(links.first_row(slot), ROWS)
                piece = result[i * ROWS : (i + 1) * ROWS]
                if part == 2:
                    out[at] = piece.astype(BF16)
                    continue
                cosine, sine = cos_ref[at], sin_ref[at]
                for head in range(2):
                    lanes = slice(head * 128, head * 128 + 128)
                    turned = piece[:, lanes] * cosine + pltpu.roll(piece[:, lanes], 64, 1) * sine
                    if part == 0:
                        turned = turned * HEAD_DIM**-0.5
                    out[at, lanes] = turned.astype(BF16)

    written = pltpu.make_async_copy(all_ref, out_ref, out_sem)

    def tokens():
        yield from gather(links, all_ref, work)
        written.start()

    together(PROJECT, tokens(), *spread(links, piece_ref, w_all_ref, GU, local))
    written.wait()


def attend_kernel(prefix_ref, q_ref, k_ref, v_ref, out_ref, lse_ref):
    block = q_ref.shape[0]
    first = pl.program_id(1) * block
    scores = dot_t(k_ref[...], q_ref[...])
    key = lax.broadcasted_iota(jnp.int32, scores.shape, 0)
    query = lax.broadcasted_iota(jnp.int32, (1, block), 1) + first
    limit = jnp.maximum(query, prefix_ref[0] - 1)
    scores = jnp.where(key <= limit, scores, -1e30)
    peak = jnp.max(scores, axis=0, keepdims=True)
    exponent = jnp.exp(scores - peak)
    total = jnp.sum(exponent, axis=0, keepdims=True)
    weights = (exponent * (1.0 / total)).astype(BF16)
    out_ref[...] = dot_rows(weights, v_ref[...]).astype(BF16)
    lse_ref[0] = peak + jnp.log(total)


def attend(prefix, q, k, v):
    block = 512
    return pl.pallas_call(
        attend_kernel,
        name="attend",
        grid=(2, LEN // block),
        in_specs=[
            SMEM,
            pl.BlockSpec((block, 128), lambda h, b: (b, h)),
            pl.BlockSpec((LEN, 128), lambda h, b: (0, h)),
            pl.BlockSpec((LEN, 128), lambda h, b: (0, h)),
        ],
        out_specs=(
            pl.BlockSpec((block, 128), lambda h, b: (b, h)),
            pl.BlockSpec((1, 1, block), lambda h, b: (h, 0, b)),
        ),
        out_shape=(
            jax.ShapeDtypeStruct((LEN, 256), BF16),
            jax.ShapeDtypeStruct((2, 1, LEN), F32),
        ),
        compiler_params=pltpu.CompilerParams(vmem_limit_bytes=VMEM_BYTES),
    )(prefix, q, k, v)


def attended_kernel(
    heads_ref, w_ref, x_ref, gain_ref, bias_ref, piece_ref, normed_ref, unit_ref, inverse_ref, w_all_ref,
    total, local, *rest,
):
    bufs, (send, recv) = rest[:7], rest[7:]
    links = Links(send, recv)
    to = links.to
    links.barrier(to(y=1), to(y=3), to(z=2), to(y=2), to(x=1), to(x=3), to(z=1), to(z=3))

    def compute(pair):
        rows = jnp.concatenate([heads_ref[pl.ds(links.first_row(s), ROWS)] for s in pair], axis=0)
        result = dot(rows, w_ref[...]).astype(BF16)
        for i, slot in enumerate(pair):
            bufs[0][slot] = result[i * ROWS : (i + 1) * ROWS]

    def finish(at):
        unit, inverse = norm_parts(deep_alpha * x_ref[at].astype(F32) + total[at])
        unit_ref[at] = unit
        inverse_ref[at] = jnp.broadcast_to(inverse, (16, 128))
        normed_ref[at] = unit * gain_ref[...] + bias_ref[...]

    def chain():
        yield from scatter(links, bufs, compute, total)
        by_chunks(finish)

    together(ATTENDED, chain(), *spread(links, piece_ref, w_all_ref, pl.ds(2, 1), local))


class Loads:
    def __init__(self):
        self.copies = []

    def start(self, src, dst, sem):
        copy = pltpu.make_async_copy(src, dst, sem)
        copy.start()
        self.copies.append(copy)

    def wait(self):
        while self.copies:
            self.copies.pop().wait()


def load_weights(w_hbm, w, sem, first, parts):
    loads = Loads()
    for k in range(parts):
        for i in range(16):
            src = w_hbm.at[k, lax.rem(i // 2, 2), i // 4, lax.rem(i, 2)]
            loads.start(src, w.at[first + k, pl.ds(0, FF), pl.ds(i * 128, 128)], sem.at[first + k, i])
    for k in range(parts):
        w[first + k, FF:COLS] = jnp.zeros((COLS - FF, WIDE), BF16)
    return loads


def feed_kernel(
    clusters_ref, normed_ref, cot_ref, gu_hbm, down_hbm, gain_ref, bias_ref,
    out_ref, all_out, gz_all_out, act_out, gz_ref, vec_ref,
    w, all_ref, gz_all_ref, act_ref, gelu_ref, slope, total, w_sem, out_sem, *rest,
):
    bufs, (send, recv) = rest[:4], rest[4:]
    links = Links(send, recv)

    def to_low(at):
        all_ref[0, at] = normed_ref[at].astype(BF16)

    by_chunks(to_low)
    load_gu = load_weights(gu_hbm, w, w_sem, 0, 2)
    load_down = load_weights(down_hbm, w, w_sem, 2, 1)
    links.barrier(links.to(y=1), links.to(y=3), links.to(sibling=True))
    written = Loads()

    def forward(pair):
        load_gu.wait()
        rows = pair_of(all_ref, pair)
        for c in range(0, COLS, 256):
            cols = slice(c, c + 256)
            gate = dot_t(rows, w[0, cols])
            up = dot_t(rows, w[1, cols])
            bell = 0.5 + 0.5 * lax.erf(gate * np.float32(np.sqrt(0.5)))
            gelu = gate * bell
            turn = bell + gate * (jnp.exp(-0.5 * gate * gate) * np.float32(1.0 / np.sqrt(2.0 * np.pi)))
            hidden = (gelu * up).astype(BF16)
            turn = turn * up
            for i, slot in enumerate(pair):
                part = slice(i * ROWS, (i + 1) * ROWS)
                gelu_ref[slot, :, cols] = gelu[part]
                slope[slot, :, cols] = turn[part]
                act_ref[slot, :, 2 * COLS + c : 2 * COLS + c + 256] = hidden[part]

    alone(gather_near(links, all_ref, forward))
    written.start(all_ref, all_out, out_sem.at[8])

    def compute(pair):
        load_down.wait()
        rows = jnp.concatenate([act_ref[slot, :, 2 * COLS :] for slot in pair], axis=0)
        for d in range(0, WIDE, 512):
            result = dot(rows, w[2, :, d : d + 512]).astype(BF16)
            for i, slot in enumerate(pair):
                bufs[0][slot, :, d : d + 512] = result[i * ROWS : (i + 1) * ROWS]

    alone(scatter_near(links, bufs, compute, total))
    vec_ref[...] = jnp.zeros_like(vec_ref)
    own, same = clusters_ref[lax.axis_index("dp")], np.float32(0.0)
    for i in range(clusters_ref.shape[0]):
        same = same + jnp.where(clusters_ref[i] == own, np.float32(1.0), np.float32(0.0))
    seq_weight = 1.0 / jnp.full((1, WIDE), same, F32)

    def finish(at):
        unit, inverse = norm_parts(deep_alpha * normed_ref[at] + total[at])
        out_ref[at] = (unit * gain_ref[...] + bias_ref[...]).astype(BF16)
        grad = cot_ref[at].astype(F32) * seq_weight
        grad_z = norm_backward(grad, unit, inverse, gain_ref[...])
        gz_ref[at] = grad_z
        gz_all_ref[0, at] = grad_z.astype(BF16)
        vec_ref[0] += rows8(grad * unit)
        vec_ref[1] += rows8(grad)

    by_chunks(finish)

    def backward(pair):
        rows = pair_of(gz_all_ref, pair)
        for c in range(0, COLS, 256):
            cols = slice(c, c + 256)
            grad_hidden = dot_t(rows, w[2, cols])
            for i, slot in enumerate(pair):
                part = grad_hidden[i * ROWS : (i + 1) * ROWS]
                act_ref[slot, :, cols] = (part * slope[slot, :, cols]).astype(BF16)
                act_ref[slot, :, COLS + c : COLS + c + 256] = (part * gelu_ref[slot, :, cols]).astype(BF16)
        for slot in pair:
            written.start(act_ref.at[slot], act_out.at[slot], out_sem.at[slot])

    alone(gather_near(links, gz_all_ref, backward))
    written.start(gz_all_ref, gz_all_out, out_sem.at[9])
    written.wait()


def feed_back_kernel(
    act_hbm, gz_ref, w_hbm, normed_hbm, gz_all_hbm, unit_ref, inverse_ref, gain_ref, w_out_ref,
    gz1_ref, all_out, grad_heads_ref, vec_ref, shard_ref,
    act_ref, rows_ref, all_ref, w, total, w_sem, sem, *rest,
):
    bufs, more, (send, recv) = rest[:4], rest[4:17], rest[17:]
    links = Links(send, recv)
    load_act, load_rows = Loads(), Loads()
    load_act.start(act_hbm, act_ref, sem.at[0])
    load_w = load_weights(w_hbm, w, w_sem, 0, 2)
    load_rows.start(normed_hbm, rows_ref, sem.at[1])
    to = links.to
    links.barrier(
        to(y=1), to(y=3), to(z=2), to(x=1), to(x=3), to(z=1), to(z=3), to(sibling=True)
    )
    load_act.wait()
    load_w.wait()

    def compute(pair):
        rows = jnp.concatenate([act_ref[slot, :, : 2 * COLS] for slot in pair], axis=0)
        for d in range(0, WIDE, 512):
            cols = slice(d, d + 512)
            result = dot(rows[:, :COLS], w[0, :, cols]) + dot(rows[:, COLS:], w[1, :, cols])
            result = result.astype(BF16)
            for i, slot in enumerate(pair):
                bufs[0][slot, :, cols] = result[i * ROWS : (i + 1) * ROWS]

    def finish(at):
        grad = deep_alpha * gz_ref[at] + total[at]
        unit = unit_ref[at]
        grad_z = norm_backward(grad, unit, inverse_ref[at][:, 0:1], gain_ref[...])
        gz1_ref[at] = grad_z
        all_ref[0, at] = grad_z.astype(BF16)
        vec_ref[0] += rows8(grad * unit)
        vec_ref[1] += rows8(grad)

    def work(pair):
        result = dot_t(pair_of(all_ref, pair), w_out_ref[...]).astype(BF16)
        for i, slot in enumerate(pair):
            grad_heads_ref[pl.ds(links.first_row(slot), ROWS)] = result[i * ROWS : (i + 1) * ROWS]

    written = Loads()

    def chain():
        yield from scatter_near(links, bufs, compute, total)
        vec_ref[...] = jnp.zeros_like(vec_ref)
        by_chunks(finish)
        yield from gather(links, all_ref, work)
        written.start(all_ref, all_out, sem.at[3])

    g = more[0]

    def make(k):
        load_rows.wait()
        for c in range(0, COLS, 256):
            left = act_ref[:, :, k * COLS + c : k * COLS + c + 256].reshape(LEN, 256)
            height = min(256, FF - c)
            for d in range(0, WIDE, 512):
                right = rows_ref[:, :, d : d + 512].reshape(LEN, 512)
                result = dot_rows(left, right)[:height].astype(BF16)
                for i in range(4):
                    at = d // 128 + i
                    g[k, at // 4, at // 2 % 2, at % 2, c : c + height] = result[:, i * 128 : i * 128 + 128]
            if k == 1 and c == 512:
                load_rows.start(gz_all_hbm, rows_ref, sem.at[2])
            if c < 512:
                yield ()

    together(FEED_BACK, chain(), *reduce(links, more, make, shard_ref))
    written.wait()


def input_kernel(
    prefix_ref, q_ref, k_ref, v_ref, g_ref, lse_ref, cos_ref, sin_ref,
    w_hbm, gz1_ref, tokens_hbm, heads_ref, gz_all_hbm, shard_ref, vec_in_ref,
    out_ref, one_ref, two_ref, whole_ref, vec_ref, feed_ref,
    total, w_ref, tokens_ref, gz_all_ref, grads, heads, key_sum, value_sum, held, got, local, sem, *rest,
):
    bufs, more, (send, recv) = rest[:7], rest[7:22], rest[22:]
    links = Links(send, recv)
    to = links.to
    load_gz, load_tokens, load_w = Loads(), Loads(), Loads()
    load_gz.start(gz_all_hbm, gz_all_ref, sem.at[2])
    load_tokens.start(tokens_hbm, tokens_ref, sem.at[1])
    load_w.start(w_hbm, w_ref, sem.at[0])
    links.barrier(
        to(y=1), to(y=2), to(y=3), to(z=2), to(x=1), to(x=2), to(x=3), to(sibling=True), links.beside()
    )
    vec_ref[...] = vec_in_ref[...]
    block = 512
    ready = [Mark(), Mark(), Mark()]

    def attend_back(head):
        lanes = slice(head * 128, head * 128 + 128)

        def keep(part, first, value):
            for i in range(value.shape[0] // ROWS):
                seq = first // ROWS + i
                d = lax.rem(seq // 2 + 4 - links.y, 4)
                slot = 2 * d - d * (d - 1) // 2 - d * (d - 1) * (d - 2) // 3
                slot = slot + 4 * lax.rem(links.z_hi + seq, 2)
                at = head * 384 + part * 128
                grads[slot, :, at : at + 128] = value[i * ROWS : (i + 1) * ROWS].astype(BF16)

        for first in range(0, LEN, block):
            at = slice(first, first + block)
            query, grad = q_ref[at, lanes], g_ref[at, lanes]
            scores = dot_t(k_ref[:, lanes], query)
            key = lax.broadcasted_iota(jnp.int32, scores.shape, 0)
            limit = lax.broadcasted_iota(jnp.int32, (1, block), 1) + first
            limit = jnp.maximum(limit, prefix_ref[0] - 1)
            weights = jnp.where(key <= limit, jnp.exp(scores - lse_ref[head, :, at]), 0.0)
            grad_weights = dot_t(v_ref[:, lanes], grad)
            inner = jnp.sum(weights * grad_weights, axis=0, keepdims=True)
            grad_scores = (weights * (grad_weights - inner)).astype(BF16)
            turned = dot_rows(grad_scores, k_ref[:, lanes]) * HEAD_DIM**-0.5
            keep(0, first, turned * cos_ref[at] - pltpu.roll(turned, 64, 1) * sin_ref[at])
            grad_key = dot(grad_scores, query)
            grad_value = dot(weights.astype(BF16), grad)
            if first == 0:
                key_sum[...] = grad_key
                value_sum[...] = grad_value
            else:
                key_sum[...] += grad_key
                value_sum[...] += grad_value
            yield ()
        turned = key_sum[...]
        keep(1, 0, turned * cos_ref[...] - pltpu.roll(turned, 64, 1) * sin_ref[...])
        keep(2, 0, value_sum[...])

    def compute(pair):
        load_w.wait()
        rows = pair_of(grads, pair)
        result = 0.0
        for part in range(3):
            for head in range(2):
                at = head * 384 + part * 128
                result = result + dot_t(rows[:, at : at + 128], w_ref[part, :, head * 128 : head * 128 + 128])
        result = result.astype(BF16)
        for i, slot in enumerate(pair):
            bufs[0][slot] = result[i * ROWS : (i + 1) * ROWS]

    def finish(at):
        value = deep_alpha * gz1_ref[at] + total[at]
        for lane in range(WIDE // 128):
            out_ref[at, lane] = value[:, lane * 128 : lane * 128 + 128]

    def chain():
        yield (ready[2],)
        for head in range(2):
            yield from attend_back(head)
            ready[head].done = True
            if head == 0:
                yield ()
        yield from scatter(links, bufs, compute, total)
        by_chunks(finish)

    def qkv(head):
        flat = more[5 * head]
        yield (ready[head],)
        load_tokens.wait()
        right = grads[:, :, head * 384 : head * 384 + 384].reshape(LEN, 384)
        for d in range(8):
            left = tokens_ref[:, :, d * 256 : d * 256 + 256].reshape(LEN, 256)
            result = dot_rows(left, right).astype(BF16)
            for part in range(3):
                for i in range(2):
                    row = part * WIDE + d * 256 + i * 128
                    chunk, at = row // 384, row % 384
                    flat[chunk // 8, chunk // 4 % 2, chunk % 4, at : at + 128] = result[
                        i * 128 : i * 128 + 128, part * 128 : part * 128 + 128
                    ]
            if d == 3:
                yield ()

    def first_shared():
        for slot in range(8):
            heads[slot] = heads_ref[pl.ds(links.first_row(slot), ROWS)]
        load_gz.wait()
        left = heads[...].reshape(LEN, 256)
        for d in range(0, WIDE, 512):
            result = dot_rows(left, gz_all_ref[:, :, d : d + 512].reshape(LEN, 512)).astype(BF16)
            for i in range(4):
                lane = d // 128 + i
                for j in range(2):
                    chunk = lane // 2 * 2 + j
                    more[10][chunk // 8, chunk // 4 % 2, chunk % 4, :, lane % 2 * 128 : lane % 2 * 128 + 128] = result[
                        j * 128 : j * 128 + 128, i * 128 : i * 128 + 128
                    ]
        ready[2].done = True
        yield from share(links, more[10:15], whole_ref)

    def shared(head):
        yield from qkv(head)
        yield from share(links, more[5 * head : 5 * head + 5], (one_ref, two_ref)[head])

    together(
        INPUT,
        collect(links, shard_ref, feed_ref, local),
        first_shared(),
        chain(),
        shared(0),
        shared(1),
        agree(links, vec_ref, (held, got)),
    )


def outputs_kernel(feed_ref, one_ref, two_ref, out_ref, gate_up_ref, down_ref, grad_qkv_ref, grad_out_ref):
    for z in range(2):
        lanes = slice(z * 128, z * 128 + 128)
        gate_up_ref[:, 0, lanes] = feed_ref[0, 0, 0, z].astype(F32)
        gate_up_ref[:, 1, lanes] = feed_ref[1, 0, 0, z].astype(F32)
        down_ref[:, lanes] = feed_ref[2, 0, 0, z].astype(F32)
    grad_qkv_ref[:, 0:128] = one_ref[...].astype(F32)
    grad_qkv_ref[:, 128:256] = two_ref[...].astype(F32)
    grad_out_ref[...] = out_ref[...].astype(F32)


def outputs(feed, one, two, out, total):
    return pl.pallas_call(
        outputs_kernel,
        name="outputs",
        grid=(8,),
        in_specs=[
            pl.BlockSpec((3, 1, 1, 2, FF, 128), lambda i: (0, i // 2, i % 2, 0, 0, 0)),
            pl.BlockSpec((768, 128), lambda i: (i, 0)),
            pl.BlockSpec((768, 128), lambda i: (i, 0)),
            pl.BlockSpec((256, 256), lambda i: (i, 0)),
        ],
        out_specs=(
            pl.BlockSpec((FF, 2, 256), lambda i: (i, 0, 0)),
            pl.BlockSpec((FF, 256), lambda i: (i, 0)),
            pl.BlockSpec((768, 256), lambda i: (i, 0)),
            pl.BlockSpec((256, 256), lambda i: (0, i)),
        ),
        out_shape=(
            jax.ShapeDtypeStruct((total, 2, 256), F32),
            jax.ShapeDtypeStruct((total, 256), F32),
            jax.ShapeDtypeStruct((6144, 256), F32),
            jax.ShapeDtypeStruct((256, WIDE), F32),
        ),
        compiler_params=pltpu.CompilerParams(vmem_limit_bytes=VMEM_BYTES),
    )(feed, one, two, out)


def on_device(
    tokens, cotangent, w_qkv, w_out, w_gate_up, w_down,
    attn_gain, attn_bias, ffn_gain, ffn_bias, prefix_len, clusters,
):
    x = tokens.reshape(ROWS, WIDE)
    cot = cotangent.reshape(ROWS, WIDE)
    dp, seq = lax.axis_index("dp"), lax.axis_index("seq")
    cosine, sine = (jnp.asarray(t) for t in rotary_tables(LEN, HEAD_DIM))
    row = lambda v: v.reshape(1, WIDE)
    ff_total = w_down.shape[1]
    place = jnp.stack([dp % 2, dp // 2 % 4, dp // 8, jnp.int32(ff_total)]).astype(jnp.int32)
    piece = piece_of(w_gate_up.transpose(2, 1, 0), w_down.T, place)
    w_in = w_qkv.transpose(1, 0, 2)
    low, full = BF16, F32
    blocks = (8, ROWS, WIDE)
    one = pltpu.SemaphoreType.DMA
    some = lambda *n: pltpu.SemaphoreType.DMA(n)
    rows_f32 = pltpu.VMEM((ROWS, WIDE), F32)
    blocks_low = pltpu.VMEM(blocks, BF16)

    tokens_all, q, k, v, w_gu = call(
        project_kernel, "project", 0,
        [(blocks, low, "h")] + [((LEN, 256), low, "v")] * 3 + [((2, 2, 4, 2, FF, 128), low, "h")],
        (x, w_in, cosine, sine, piece), "vvvvv", (blocks_low, one, one), 60,
        2 * LEN * WIDE * 768,
    )
    heads_out, lse = attend(prefix_len, q, k, v)
    normed, unit_one, inverse_one, w_dn = call(
        attended_kernel, "attended", 1,
        [
            ((ROWS, WIDE), full, "v"), ((ROWS, WIDE), full, "v"), ((ROWS, 128), full, "v"),
            ((1, 2, 4, 2, FF, 128), low, "h"),
        ],
        (heads_out, w_out, x, row(attn_gain), row(attn_bias), piece), "vvvvvv",
        (rows_f32, one, *SCATTER_SCRATCH), 42, 2 * LEN * WIDE * 256,
    )
    output, normed_all, gz_all, act, grad_z2, ffn_vec = call(
        feed_kernel, "feed", 2,
        [
            ((ROWS, WIDE), low, "v"), (blocks, low, "h"), (blocks, low, "h"),
            ((8, ROWS, 3 * COLS), low, "h"), ((ROWS, WIDE), full, "v"), ((2, 8, WIDE), full, "v"),
        ],
        (clusters, normed, cot, w_gu, w_dn, row(ffn_gain), row(ffn_bias)), "svvhhvv",
        (
            pltpu.VMEM((3, COLS, WIDE), BF16), blocks_low, blocks_low,
            pltpu.VMEM((8, ROWS, 3 * COLS), BF16), pltpu.VMEM((8, ROWS, COLS), F32),
            pltpu.VMEM((8, ROWS, COLS), F32), rows_f32, some(3, 16), some(10), *NEAR_SCRATCH,
        ),
        34, 2 * LEN * WIDE * COLS * 4,
    )
    grad_z1, gz1_all, grad_heads, attn_vec, shard = call(
        feed_back_kernel, "feed_back", 3,
        [
            ((ROWS, WIDE), full, "v"), (blocks, low, "h"), ((LEN, 256), low, "v"),
            ((2, 8, WIDE), full, "v"), ((3, 4, PART, 128), low, "v"),
        ],
        (act, grad_z2, w_gu, normed_all, gz_all, unit_one, inverse_one, row(attn_gain), w_out),
        "hvhhhvvvv",
        (
            pltpu.VMEM((8, ROWS, 3 * COLS), BF16), blocks_low, blocks_low,
            pltpu.VMEM((2, COLS, WIDE), BF16), rows_f32, some(2, 16), some(4),
            *NEAR_SCRATCH, *REDUCE_SCRATCH,
        ),
        60, 2 * LEN * WIDE * COLS * 5,
    )
    vec = jnp.concatenate([attn_vec.sum(1), ffn_vec.sum(1), jnp.zeros((4, WIDE), F32)], axis=0)
    steps = pltpu.VMEM((7, 8, WIDE), F32)
    head_sum = pltpu.VMEM((LEN, 128), F32)
    input_grad, one, two, out_whole, vec, ffn_whole = call(
        input_kernel, "input", 4,
        [
            ((ROWS, WIDE // 128, 128), full, "v"), ((2, 2, 4, 384, 128), low, "v"),
            ((2, 2, 4, 384, 128), low, "v"), ((2, 2, 4, 128, 256), low, "v"), ((8, WIDE), full, "v"),
            ((3, 4, 2, 2, FF, 128), low, "h"),
        ],
        (
            prefix_len, q, k, v, grad_heads, lse, cosine, sine,
            w_in, grad_z1, tokens_all, heads_out, gz1_all, shard, vec,
        ),
        "svvvvvvvhvhvhvv",
        (
            rows_f32, pltpu.VMEM((3, WIDE, 256), BF16), blocks_low, blocks_low,
            pltpu.VMEM((8, ROWS, 768), BF16), pltpu.VMEM((8, ROWS, 256), BF16),
            head_sum, head_sum, steps, steps, pltpu.SemaphoreType.DMA, some(3),
            *SCATTER_SCRATCH, *share_scratch(384, 128), *share_scratch(384, 128), *share_scratch(128, 256),
        ),
        130, 2 * LEN * WIDE * 768,
    )
    grad_gate_up, grad_down, grad_qkv, grad_out = outputs(
        ffn_whole, one.reshape(6144, 128), two.reshape(6144, 128), out_whole.reshape(2048, 256), ff_total
    )
    own = lax.dynamic_slice_in_dim(vec, seq * 256, 256, axis=1)
    return (
        output.reshape(tokens.shape),
        input_grad.reshape(tokens.shape),
        grad_qkv.reshape(3, WIDE, 256).transpose(1, 0, 2),
        grad_out,
        grad_gate_up.transpose(2, 1, 0),
        grad_down.T,
        own[0],
        own[1],
        own[2],
        own[3],
    )


def solution(mesh):
    return jax.shard_map(
        on_device,
        mesh=mesh,
        in_specs=(
            P("seq", "dp", None), P("seq", "dp", None), P(None, None, "seq"), P("seq", None),
            P("seq", None, None), P("seq", None), P(), P(), P(), P(), P("dp"), P(),
        ),
        out_specs=(
            P("seq", "dp", None), P("seq", "dp", None), P(None, None, "seq"), P("seq", None),
            P("seq", None, None), P("seq", None), P("seq"), P("seq"), P("seq"), P("seq"),
        ),
        check_vma=False,
    )
```

```python
import functools

import jax
import jax.numpy as jnp
import numpy as np
from jax import lax
from jax.experimental import pallas as pl
from jax.experimental.pallas import tpu as pltpu
from jax.sharding import PartitionSpec as P

MESH = pl.DeviceIdType.MESH
F32, BF16 = jnp.float32, jnp.bfloat16
HEAD_DIM = 128
ROWS = 128
WIDE = 2048
COLS = 768
LEN = 1024
VMEM_BYTES = 60 * 1024 * 1024
deep_alpha = 48.0**0.25
norm_eps = 1e-05
rotary_base = 10000.0


def rotary_tables(length, head_width):
    half_width = head_width // 2
    position = np.arange(length, dtype=np.float64)
    inverse = rotary_base ** (-np.arange(half_width, dtype=np.float64) * 2.0 / head_width)
    angles = position[:, None] * inverse[None, :]
    cosine_table = np.cos(angles)
    sine_table = np.sin(angles)
    return (
        np.concatenate([cosine_table, cosine_table], axis=1).astype(np.float32),
        np.concatenate([-sine_table, sine_table], axis=1).astype(np.float32),
    )


FF = 704
PART = 176


class Links:
    def __init__(self, send, recv):
        self.send, self.recv, self.count = send, recv, 0
        dp, seq = lax.axis_index("dp"), lax.axis_index("seq")
        y, z_hi = seq // 2, lax.rem(seq, 2)
        z_lo, x, core = dp // 8, lax.rem(dp // 2, 4), lax.rem(dp, 2)
        self.y, self.z_hi, self.z_lo, self.x, self.core = y, z_hi, z_lo, x, core
        self.z = z_hi * 2 + z_lo

    def to(self, x=0, y=0, z=0, sibling=False):
        z_hi, z_lo = self.z_at(z)
        x, y = lax.rem(self.x + x, 4), lax.rem(self.y + y, 4)
        core = 1 - self.core if sibling else self.core
        return (z_lo * 8 + x * 2 + core, y * 2 + z_hi)

    def beside(self):
        return (lax.rem(lax.axis_index("dp") + 8, 16), lax.axis_index("seq"))

    def z_at(self, offset):
        z = lax.rem(self.z + offset, 4)
        return z // 2, lax.rem(z, 2)

    def part(self, offset):
        return pl.ds(pl.multiple_of(lax.rem(self.x + offset, 4) * PART, 16), PART)

    def barrier(self, *where):
        gate = pltpu.get_barrier_semaphore()
        for device in where:
            pl.semaphore_signal(gate, inc=1, device_id=device, device_id_type=MESH)
        pl.semaphore_wait(gate, len(where))

    def start(self, src, dst, where):
        assert self.count < self.send.shape[0]
        copy = pltpu.make_async_remote_copy(
            src_ref=src,
            dst_ref=dst,
            send_sem=self.send.at[self.count],
            recv_sem=self.recv.at[self.count],
            device_id=where,
            device_id_type=MESH,
        )
        self.count += 1
        copy.start()
        return copy

    def first_row(self, slot):
        step = (0, 3, 1, 2)[slot % 4]
        half = self.z_hi if slot < 4 else 1 - self.z_hi
        return pl.multiple_of((lax.rem(self.y + step, 4) * 2 + half) * ROWS, ROWS)


class Once:
    def __init__(self, *copies):
        self.copies = list(copies)

    def wait_recv(self):
        while self.copies:
            self.copies.pop().wait_recv()


class Mark:
    done = False


class Local:
    def __init__(self, src, dst, sem):
        self.copy = pltpu.make_async_copy(src, dst, sem)
        self.copy.start()

    def wait_recv(self):
        self.copy.wait()


def together(order, *tasks):
    tasks = list(tasks)
    for task in tasks:
        next(task)
    left = len(tasks)
    for which in order:
        try:
            next(tasks[which])
        except StopIteration:
            left -= 1
    assert left == 0


def alone(task):
    for _ in task:
        pass


def received(*copies):
    for copy in copies:
        copy.wait_recv()


def sent(copies):
    for copy in copies:
        copy.wait_send()


H0, H1 = pl.ds(0, 64), pl.ds(64, 64)


def gather(links, buf, work):
    up, down, across = links.to(y=1), links.to(y=3), links.to(z=2)
    copies = []

    def send(slot, rows, dst, where):
        copies.append(links.start(buf.at[slot, rows], buf.at[dst, rows], where))
        return copies[-1]

    u0, d1 = send(0, H0, 1, up), send(0, H1, 2, down)
    z0, z1 = send(0, H0, 4, across), send(0, H1, 4, across)
    u1, d0 = send(0, H1, 1, up), send(0, H0, 2, down)
    yield u0, d1
    received(u0)
    fu = send(1, H0, 3, up)
    received(d1)
    fd = send(2, H1, 3, down)
    yield z0, z1
    received(z0)
    pu0 = send(4, H0, 5, up)
    received(z1)
    pd1 = send(4, H1, 6, down)
    pu1, pd0 = send(4, H1, 5, up), send(4, H0, 6, down)
    yield u1, d0
    received(u1, d0)
    work((0, 1))
    yield fu, fd
    received(fu, fd)
    work((2, 3))
    yield pu0, pd1
    received(pu0)
    gu = send(5, H0, 7, up)
    received(pd1)
    gd = send(6, H1, 7, down)
    yield pu1, pd0
    received(pu1, pd0)
    work((4, 5))
    yield gu, gd
    received(gu, gd)
    work((6, 7))
    sent(copies)


def gather_near(links, buf, work):
    up, down, side = links.to(y=1), links.to(y=3), links.to(sibling=True)
    copies = []

    def send(slot, rows, dst, where):
        copies.append(links.start(buf.at[slot, rows], buf.at[dst, rows], where))
        return copies[-1]

    every = pl.ds(0, ROWS)
    u0, d1 = send(0, H0, 1, up), send(0, H1, 2, down)
    u1, d0 = send(0, H1, 1, up), send(0, H0, 2, down)
    s0 = send(0, every, 4, side)
    yield 1
    received(s0)
    work((0, 4))
    yield 6
    received(u0)
    fu = send(1, H0, 3, up)
    received(d1)
    fd = send(2, H1, 3, down)
    yield 11
    received(u1)
    s1 = send(1, every, 5, side)
    received(d0)
    s2 = send(2, every, 6, side)
    work((1, 2))
    yield 13
    received(s1, s2)
    work((5, 6))
    yield 17
    received(fu)
    s30 = send(3, H0, 7, side)
    received(fd)
    s31 = send(3, H1, 7, side)
    yield 18
    received(s30, s31)
    work((3, 7))
    sent(copies)


A, B = pl.ds(0, 80), pl.ds(80, 48)
A0, A1 = pl.ds(0, 48), pl.ds(48, 32)
B0, B1 = pl.ds(80, 16), pl.ds(96, 32)
SCATTER_SCRATCH = (
    pltpu.VMEM((8, ROWS, WIDE), BF16),
    pltpu.VMEM((4, 48, WIDE), BF16),
    pltpu.VMEM((48, WIDE), BF16),
    pltpu.VMEM((2, 48, WIDE), BF16),
    pltpu.VMEM((2, 80, WIDE), BF16),
    pltpu.VMEM((2, 2, 80, WIDE), BF16),
    pltpu.VMEM((80, WIDE), BF16),
)


def add_rows(target, slot, rows, *others):
    value = target[slot, rows].astype(F32)
    for other in others:
        value = value + other.astype(F32)
    target[slot, rows] = value.astype(BF16)


def scatter(links, bufs, compute, total):
    sums, from_z, b_far, b_near, a_far, a_near, a_z = bufs
    up, down, across = links.to(y=1), links.to(y=3), links.to(z=2)
    copies = []

    def send(src, dst, where):
        copies.append(links.start(src, dst, where))
        return copies[-1]

    def far_a(o):
        half = o // 4
        return (
            send(sums.at[o + 3, A0], a_far.at[half, pl.ds(0, 48)], up),
            send(sums.at[o + 3, A1], a_far.at[half, pl.ds(48, 32)], down),
        )

    def near_a(o, far):
        half = o // 4
        received(far[0])
        add_rows(sums, o + 2, A0, a_far[half, 0:48])
        one = send(sums.at[o + 2, A], a_near.at[half, 0], up)
        received(far[1])
        add_rows(sums, o + 1, A1, a_far[half, 48:80])
        return one, send(sums.at[o + 1, A], a_near.at[half, 1], down)

    def cross_b(j):
        return send(sums.at[4 + j, B], from_z.at[j], across)

    compute((7, 3))
    z3 = cross_b(3)
    far_other = far_a(4)
    far_own = far_a(0)
    yield ()
    compute((5, 1))
    z1 = cross_b(1)
    yield ()
    compute((6, 2))
    z2 = cross_b(2)
    yield far_other
    near_other = near_a(4, far_other)
    compute((4, 0))
    z0 = cross_b(0)
    yield (z3,)
    received(z3)
    add_rows(sums, 3, B, from_z[3])
    far_b = (
        send(sums.at[3, B0], b_far.at[pl.ds(0, 16)], up),
        send(sums.at[3, B1], b_far.at[pl.ds(16, 32)], down),
    )
    yield far_own
    near_own = near_a(0, far_own)
    yield z1, z2
    received(z2)
    add_rows(sums, 2, B, from_z[2])
    received(z1)
    add_rows(sums, 1, B, from_z[1])
    yield far_b
    received(far_b[0])
    add_rows(sums, 2, B0, b_far[0:16])
    near_b0 = send(sums.at[2, B], b_near.at[0], up)
    received(far_b[1])
    add_rows(sums, 1, B1, b_far[16:48])
    near_b1 = send(sums.at[1, B], b_near.at[1], down)
    yield near_other
    received(*near_other)
    add_rows(sums, 4, A, a_near[1, 0], a_near[1, 1])
    z_a = send(sums.at[4, A], a_z, across)
    yield z0, near_b0, near_b1
    received(z0, near_b0, near_b1)
    total[80:128] = (
        sums[0, B].astype(F32)
        + from_z[0].astype(F32)
        + b_near[0].astype(F32)
        + b_near[1].astype(F32)
    )
    yield (z_a, *near_own)
    received(*near_own)
    received(z_a)
    total[0:80] = (
        sums[0, A].astype(F32)
        + a_near[0, 0].astype(F32)
        + a_near[0, 1].astype(F32)
        + a_z[...].astype(F32)
    )
    sent(copies)


NEAR_SCRATCH = (
    pltpu.VMEM((8, ROWS, WIDE), BF16),
    pltpu.VMEM((4, ROWS, WIDE), BF16),
    pltpu.VMEM((ROWS, WIDE), BF16),
    pltpu.VMEM((2, ROWS, WIDE), BF16),
)


def scatter_near(links, bufs, compute, total):
    sums, from_side, far, near = bufs
    up, down, side = links.to(y=1), links.to(y=3), links.to(sibling=True)
    copies = []

    def send(src, dst, where):
        copies.append(links.start(src, dst, where))
        return copies[-1]

    every = pl.ds(0, ROWS)
    compute((7, 3))
    s3 = send(sums.at[7], from_side.at[3], side)
    compute((5, 6))
    s1 = send(sums.at[5], from_side.at[1], side)
    s2 = send(sums.at[6], from_side.at[2], side)
    received(s3)
    add_rows(sums, 3, every, from_side[3])
    fu = send(sums.at[3, H0], far.at[H0], up)
    fd = send(sums.at[3, H1], far.at[H1], down)
    compute((1, 2))
    received(s1, s2)
    add_rows(sums, 2, every, from_side[2])
    nu1 = send(sums.at[2, H1], near.at[0, H1], up)
    add_rows(sums, 1, every, from_side[1])
    nd0 = send(sums.at[1, H0], near.at[1, H0], down)
    compute((4, 0))
    s0 = send(sums.at[4], from_side.at[0], side)
    yield fu, fd
    received(fu)
    add_rows(sums, 2, H0, far[0:64])
    nu0 = send(sums.at[2, H0], near.at[0, H0], up)
    received(fd)
    add_rows(sums, 1, H1, far[64:128])
    nd1 = send(sums.at[1, H1], near.at[1, H1], down)
    yield s0, nu1, nd0, nu0, nd1
    received(s0, nu1, nd0, nu0, nd1)
    total[...] = (
        sums[0].astype(F32)
        + from_side[0].astype(F32)
        + near[0].astype(F32)
        + near[1].astype(F32)
    )
    sent(copies)


Y0, Y1 = pl.ds(0, 2), pl.ds(2, 2)
GU = pl.ds(0, 2)


def across_y(links, piece, own, local):
    copies = []
    for step in (2, 1, 3):
        there = lax.rem(links.y + step, 4)
        copies.append(links.start(piece(there), own(), links.to(y=step)))
    keep = Local(piece(links.y), own(), local)
    return Once(keep, *copies), copies


def ring_gather(links, arrived, at, first, second, whole=True):
    up, down = first
    right, left = second
    copies = []

    def send(ref, where):
        copies.append(links.start(ref, ref, where))
        return copies[-1]

    def both(a):
        return send(at(a, 0), right), send(at(a, 0), left)

    def onward(a):
        return [send(at(a, 3, Y0), right), send(at(a, 1, Y1), left)] if whole else []

    yield (arrived,)
    received(arrived)
    u, d = send(at(0, 0), up), send(at(0, 0), down)
    near = [both(0)]
    yield u, d
    received(u)
    fu = send(at(3, 0, Y0), up)
    received(d)
    fd = send(at(1, 0, Y1), down)
    near.append(both(3))
    near.append(both(1))
    yield near[0]
    received(*near[0])
    far = onward(0)
    yield fu, fd
    received(fu, fd)
    near.append(both(2))
    for i, a in enumerate((3, 1, 2)):
        yield near[1 + i]
        received(*near[1 + i])
        far += onward(a)
    yield far
    received(*far)
    sent(copies)


def spread(links, piece, w, matrices, local):
    along_x = (links.to(x=1), links.to(x=3))
    along_z = (links.to(z=1), links.to(z=3))
    every = pl.ds(0, 4)

    def place(k, z, x, y):
        z_hi, z_lo = links.z_at(z)
        return w.at[k, z_hi, y, z_lo, links.part(x)]

    def own():
        return w.at[:, links.z_hi, links.y, links.z_lo, links.part(0)]

    arrived, copies = across_y(links, lambda y: piece.at[y, matrices], own, local)

    def one():
        yield from ring_gather(
            links, arrived, lambda a, b, y=every: place(0, a, b, y), along_z, along_x, matrices.size == 2
        )
        sent(copies)

    def two():
        yield from ring_gather(links, arrived, lambda a, b, y=every: place(1, b, a, y), along_x, along_z)

    return (one(),) if matrices.size == 1 else (one(), two())


def ring_scratch(*block):
    return [pltpu.VMEM(block, BF16), pltpu.VMEM((2, *block), BF16)]


REDUCE_SCRATCH = (
    pltpu.VMEM((3, 4, 2, 2, FF, 128), BF16),
    *ring_scratch(4, 2, 2, PART, 128), *ring_scratch(4, PART, 128),
    *ring_scratch(4, 2, 2, PART, 128), *ring_scratch(4, PART, 128),
    *ring_scratch(4, FF, 128), *ring_scratch(4, PART, 128),
)


def accumulate(count, target, *others):
    def step(i, carry):
        ref = target(i)
        value = ref[...].astype(F32)
        for other in others:
            value = value + other(i)[...].astype(F32)
        ref[...] = value.astype(BF16)
        return carry

    lax.fori_loop(0, count, step, 0)


def ring_reduce(links, at, blocks, ring, far, near, devices):
    up, down = devices
    copies = []
    every = pl.ds(0, 4)

    def send(src, dst, where):
        copies.append(links.start(src, dst, where))
        return copies[-1]

    half = ring // 2
    fu, fd = send(at(2, Y0), far.at[Y0], up), send(at(2, Y1), far.at[Y1], down)
    nu, nd = send(at(1, Y1), near.at[0, Y1], up), send(at(3, Y0), near.at[1, Y0], down)
    yield fu, fd
    received(fu)
    accumulate(half, lambda i: blocks(at(1, every), i), lambda i: blocks(far, i))
    mu = send(at(1, Y0), near.at[0, Y0], up)
    received(fd)
    accumulate(half, lambda i: blocks(at(3, every), i + half), lambda i: blocks(far, i + half))
    md = send(at(3, Y1), near.at[1, Y1], down)
    yield nu, nd, mu, md
    received(nu, nd, mu, md)
    accumulate(
        ring, lambda i: blocks(at(0, every), i), lambda i: blocks(near.at[0], i), lambda i: blocks(near.at[1], i)
    )
    sent(copies)


def reduce(links, bufs, make, shard):
    g = bufs[0]
    along_x = (links.to(x=1), links.to(x=3))
    along_z = (links.to(z=1), links.to(z=3))
    made = [Mark(), Mark()]

    def one(k, x_first):
        far, near, far2, near2 = bufs[1 + 4 * k : 5 + 4 * k]
        z_hi, z_lo = links.z_at(0)

        def along_z_at(a, y):
            hi, lo = links.z_at(a)
            return g.at[k, y, hi, lo]

        def along_x_at(a, y):
            return g.at[k, y, :, :, links.part(a)]

        def rest_z(a, y):
            hi, lo = links.z_at(a)
            return g.at[k, y, hi, lo, links.part(0)]

        def rest_x(a, y):
            return g.at[k, y, z_hi, z_lo, links.part(a)]

        def four(ref, i):
            return ref.at[i // 4, lax.rem(i // 2, 2), lax.rem(i, 2)]

        def plain(ref, i):
            return ref.at[i]

        if k:
            yield (made[k - 1],)
        yield from make(k)
        if k < 2:
            made[k].done = True
        if x_first:
            yield from ring_reduce(links, along_x_at, four, 16, far, near, along_x)
            yield from ring_reduce(links, rest_z, plain, 4, far2, near2, along_z)
        else:
            yield from ring_reduce(links, along_z_at, plain, 4, far, near, along_z)
            yield from ring_reduce(links, rest_x, plain, 4, far2, near2, along_x)
        shard[k] = g[k, :, z_hi, z_lo, links.part(0)]

    return one(0, True), one(1, True), one(2, False)


def regather(links, at, half):
    xp, xm, side = links.to(x=1), links.to(x=3), links.to(sibling=True)
    beside = links.beside()
    copies, sides = [], []

    def send(ref, where):
        copies.append(links.start(ref, ref, where))
        return copies[-1]

    def share(ref):
        sides.append(send(ref, side))

    z = send(at(0, 0), beside)
    near = [(send(at(0, 0), xp), send(at(0, 0), xm))]
    share(at(0, 0))
    yield (z,)
    received(z)
    near.append((send(at(1, 0), xp), send(at(1, 0), xm)))
    share(at(1, 0))
    far = []
    for i in range(2):
        yield near[i]
        received(near[i][0])
        far_up = send(half(at(i, 3), 0), xp)
        received(near[i][1])
        far.append((far_up, send(half(at(i, 1), 1), xm)))
        share(at(i, 3))
        share(at(i, 1))
    for i in range(2):
        yield far[i]
        received(*far[i])
        share(at(i, 2))
    yield sides
    received(*sides)
    sent(copies)


def collect(links, shard, out, local):
    def own():
        return out.at[:, links.y, links.core, links.z_lo, links.part(0)]

    arrived, copies = across_y(links, lambda y: shard.at[:, y], own, local)
    yield (arrived,)
    received(arrived)

    def at(z, x):
        return out.at[:, :, links.core, lax.rem(links.z_lo + z, 2), links.part(x)]

    def half(ref, i):
        return ref.at[:, pl.ds(2 * i, 2)]

    yield from regather(links, at, half)
    sent(copies)


def share_scratch(rows, lanes):
    return [
        pltpu.VMEM((2, 2, 4, rows, lanes), BF16),
        pltpu.VMEM((2, 4, rows, lanes), BF16),
        pltpu.VMEM((2, rows, lanes), BF16),
        pltpu.VMEM((2, 2, rows, lanes), BF16),
        pltpu.VMEM((rows, lanes), BF16),
    ]


def share(links, bufs, out):
    q, from_side, far, near, from_z = bufs
    xp, xm, side = links.to(x=1), links.to(x=3), links.to(sibling=True)
    beside = links.beside()
    core, z_lo = links.core, links.z_lo
    count = q.shape[3]
    copies = []

    def send(src, dst, where):
        copies.append(links.start(src, dst, where))
        return copies[-1]

    def there(x):
        return lax.rem(links.x + x, 4)

    def rows(ref):
        return lambda i: ref.at[pl.ds(pl.multiple_of(i * 64, 64), 64)]

    def add(target, *others):
        accumulate(count // 64, rows(target), *(rows(other) for other in others))

    s = send(q.at[1 - core], from_side, side)
    yield (s,)
    received(s)
    for x in (2, 1, 3, 0):
        for z in range(2):
            add(q.at[core, z, there(x)], from_side.at[z, there(x)])
        if x == 2:
            fu, fd = send(q.at[core, 0, there(2)], far.at[0], xp), send(q.at[core, 1, there(2)], far.at[1], xm)
    nu = send(q.at[core, 1, there(1)], near.at[0, 1], xp)
    nd = send(q.at[core, 0, there(3)], near.at[1, 0], xm)
    yield fu, fd
    received(fu)
    add(q.at[core, 0, there(1)], far.at[0])
    mu = send(q.at[core, 0, there(1)], near.at[0, 0], xp)
    received(fd)
    add(q.at[core, 1, there(3)], far.at[1])
    md = send(q.at[core, 1, there(3)], near.at[1, 1], xm)
    yield nu, nd, mu, md
    received(nu, nd, mu, md)
    for z in range(2):
        add(q.at[core, z, there(0)], near.at[0, z], near.at[1, z])
    b = send(q.at[core, 1 - z_lo, there(0)], from_z, beside)
    yield (b,)
    received(b)

    def finish(i, carry):
        at = pl.ds(pl.multiple_of(i * 64, 64), 64)
        value = q[core, z_lo, links.x, at].astype(F32) + from_z[at].astype(F32)
        out[core, z_lo, links.x, at] = value.astype(BF16)
        return carry

    lax.fori_loop(0, count // 64, finish, 0)

    def at(z, x):
        return out.at[core, lax.rem(z_lo + z, 2), there(x)]

    def half(ref, i):
        return ref.at[pl.ds(count // 2 * i, count // 2)]

    yield from regather(links, at, half)
    sent(copies)


def agree(links, vec, bufs):
    y, x = links.y, links.x
    copies = []
    steps = (
        links.to(sibling=True),
        links.to(y=1 + 2 * lax.rem(y, 2)),
        links.to(y=2),
        links.to(z=2),
        links.to(x=1 + 2 * lax.rem(x, 2)),
        links.to(x=2),
        links.beside(),
    )
    held, got = bufs
    held[0] = vec[...]
    for i, where in enumerate(steps):
        copies.append(links.start(held.at[i], got.at[i], where))
        yield (copies[-1],)
        received(copies[-1])
        if i < len(steps) - 1:
            held[i + 1] = held[i] + got[i]
        else:
            vec[...] = held[i] + got[i]
    sent(copies)


def dot(a, b):
    return jnp.dot(a, b, preferred_element_type=F32)


def dot_t(a, b):
    return lax.dot_general(a, b, (((1,), (1,)), ((), ())), preferred_element_type=F32)


def dot_rows(a, b):
    return lax.dot_general(a, b, (((0,), (0,)), ((), ())), preferred_element_type=F32)


def pair_of(ref, pair):
    return jnp.concatenate([ref[pair[0]], ref[pair[1]]], axis=0)


def by_chunks(body):
    def step(i, carry):
        body(pl.ds(pl.multiple_of(i * 16, 16), 16))
        return carry

    lax.fori_loop(0, ROWS // 16, step, 0)


def norm_parts(row_total):
    center = row_total - jnp.mean(row_total, axis=-1, keepdims=True)
    spread = jnp.mean(center * center, axis=-1, keepdims=True)
    inverse = lax.rsqrt(spread + norm_eps)
    return center * inverse, inverse


def norm_backward(grad_result, unit, inverse, gain):
    grad_unit = grad_result * gain
    return inverse * (
        grad_unit
        - jnp.mean(grad_unit, axis=-1, keepdims=True)
        - unit * jnp.mean(grad_unit * unit, axis=-1, keepdims=True)
    )


def rows8(values):
    return values[0:8] + values[8:16]


VMEM = pl.BlockSpec(memory_space=pltpu.VMEM)
HBM = pl.BlockSpec(memory_space=pl.ANY)
SMEM = pl.BlockSpec(memory_space=pltpu.SMEM)
KINDS = {"v": VMEM, "s": SMEM, "h": HBM}


def call(body, name, ident, outs, operands, spaces, scratch, copies, flops=0):
    sems = [pltpu.SemaphoreType.DMA((copies,)), pltpu.SemaphoreType.DMA((copies,))]
    return pl.pallas_call(
        body,
        name=name,
        out_shape=tuple(jax.ShapeDtypeStruct(s, d) for s, d, _ in outs),
        in_specs=[KINDS[k] for k in spaces],
        out_specs=tuple(KINDS[k] for _, _, k in outs),
        scratch_shapes=[*scratch, *sems],
        compiler_params=pltpu.CompilerParams(
            collective_id=ident, has_side_effects=True, vmem_limit_bytes=VMEM_BYTES
        ),
        cost_estimate=pl.CostEstimate(flops=flops, bytes_accessed=20_000_000, transcendentals=0),
    )(*operands)


PROJECT = (1, 2, 0, 0, 1, 2, 1, 0, 2, 1, 1, 0, 1, 0, 2, 2, 2, 0, 1, 2, 0, 1, 2)
ATTENDED = (0, 0, 1, 0, 0, 0, 0, 1, 1, 0, 0, 1, 1, 1, 0, 0, 1, 1)
FEED_BACK = (1, 1, 2, 2, 2, 3, 3, 3, 0, 1, 0, 3, 2, 0, 0, 0, 0, 1, 3, 1, 0, 2, 3, 1, 0, 2, 3, 0, 2)
INPUT = (2, 1, 0, 2, 1, 2, 2, 2, 2, 0, 4, 0, 4, 2, 2, 4, 5, 2, 1, 2, 2, 3, 0, 3, 2, 5, 0, 3, 4, 2, 2, 1, 0, 5, 0, 3, 1, 2, 2, 4, 5, 1, 3, 4, 1, 5, 1, 3, 4, 4, 1, 1, 5, 3, 3, 4, 5, 4, 3, 3, 4, 4, 3, 3)


def piece_kernel(place_ref, gate_up_ref, down_ref, out_ref):
    chunk = (pl.program_id(0) * 2 + place_ref[0]) * 4 + place_ref[1]
    total = place_ref[3]
    row = lax.broadcasted_iota(jnp.int32, (PART, 128), 0) + chunk * PART
    inside = row < total
    both = gate_up_ref[...].astype(F32)
    out_ref[0, 0] = jnp.where(inside, both[:, 0], 0.0).astype(BF16)
    out_ref[0, 1] = jnp.where(inside, both[:, 1], 0.0).astype(BF16)
    out_ref[0, 2] = jnp.where(inside, down_ref[...].astype(F32), 0.0).astype(BF16)


def piece_of(gate_up, down, place):
    def chunk(y, place):
        return (y * 2 + place[0]) * 4 + place[1]

    return pl.pallas_call(
        piece_kernel,
        name="piece",
        grid_spec=pltpu.PrefetchScalarGridSpec(
            num_scalar_prefetch=1,
            grid=(4,),
            in_specs=[
                pl.BlockSpec((PART, 2, 128), lambda y, p: (chunk(y, p), 0, p[2])),
                pl.BlockSpec((PART, 128), lambda y, p: (chunk(y, p), p[2])),
            ],
            out_specs=pl.BlockSpec((1, 3, PART, 128), lambda y, p: (y, 0, 0, 0)),
        ),
        out_shape=jax.ShapeDtypeStruct((4, 3, PART, 128), BF16),
    )(place, gate_up, down)


def project_kernel(
    x_ref, w_ref, cos_ref, sin_ref, piece_ref, out_ref, q_ref, k_ref, v_ref, w_all_ref,
    all_ref, local, out_sem, send, recv,
):
    links = Links(send, recv)
    all_ref[0] = x_ref[...]
    to = links.to
    links.barrier(to(y=1), to(y=3), to(z=2), to(y=2), to(x=1), to(x=3), to(z=1), to(z=3))

    def work(pair):
        rows = pair_of(all_ref, pair)
        for part, out in enumerate((q_ref, k_ref, v_ref)):
            result = dot(rows, w_ref[part])
            for i, slot in enumerate(pair):
                at = pl.ds(links.first_row(slot), ROWS)
                piece = result[i * ROWS : (i + 1) * ROWS]
                if part == 2:
                    out[at] = piece.astype(BF16)
                    continue
                cosine, sine = cos_ref[at], sin_ref[at]
                for head in range(2):
                    lanes = slice(head * 128, head * 128 + 128)
                    turned = piece[:, lanes] * cosine + pltpu.roll(piece[:, lanes], 64, 1) * sine
                    if part == 0:
                        turned = turned * HEAD_DIM**-0.5
                    out[at, lanes] = turned.astype(BF16)

    written = pltpu.make_async_copy(all_ref, out_ref, out_sem)

    def tokens():
        yield from gather(links, all_ref, work)
        written.start()

    together(PROJECT, tokens(), *spread(links, piece_ref, w_all_ref, GU, local))
    written.wait()


def attended_kernel(
    prefix_ref, q_ref, k_ref, v_ref, w_ref, x_ref, gain_ref, bias_ref, piece_ref,
    heads_ref, lse_ref, normed_ref, unit_ref, inverse_ref, w_all_ref, total, local, *rest,
):
    bufs, (send, recv) = rest[:7], rest[7:]
    links = Links(send, recv)
    to = links.to
    links.barrier(to(y=1), to(y=3), to(z=2), to(y=2), to(x=1), to(x=3), to(z=1), to(z=3))

    def attend(first, block):
        at = pl.ds(first, block)
        for head in range(2):
            lanes = slice(head * 128, head * 128 + 128)
            scores = dot_t(k_ref[:, lanes], q_ref[at, lanes])
            key = lax.broadcasted_iota(jnp.int32, scores.shape, 0)
            limit = lax.broadcasted_iota(jnp.int32, (1, block), 1) + first
            limit = jnp.maximum(limit, prefix_ref[0] - 1)
            scores = jnp.where(key <= limit, scores, -1e30)
            peak = jnp.max(scores, axis=0, keepdims=True)
            exponent = jnp.exp(scores - peak)
            total = jnp.sum(exponent, axis=0, keepdims=True)
            weights = (exponent * (1.0 / total)).astype(BF16)
            heads_ref[at, lanes] = dot_rows(weights, v_ref[:, lanes]).astype(BF16)
            lse_ref[head, :, at] = peak + jnp.log(total)

    def compute(pair):
        step = (0, 3, 1, 2)[pair[1]]
        attend(pl.multiple_of(lax.rem(links.y + step, 4) * 2 * ROWS, 2 * ROWS), 2 * ROWS)
        rows = jnp.concatenate([heads_ref[pl.ds(links.first_row(s), ROWS)] for s in pair], axis=0)
        result = dot(rows, w_ref[...]).astype(BF16)
        for i, slot in enumerate(pair):
            bufs[0][slot] = result[i * ROWS : (i + 1) * ROWS]

    def finish(at):
        unit, inverse = norm_parts(deep_alpha * x_ref[at].astype(F32) + total[at])
        unit_ref[at] = unit
        inverse_ref[at] = jnp.broadcast_to(inverse, (16, 128))
        normed_ref[at] = unit * gain_ref[...] + bias_ref[...]

    def chain():
        yield from scatter(links, bufs, compute, total)
        by_chunks(finish)

    together(ATTENDED, chain(), *spread(links, piece_ref, w_all_ref, pl.ds(2, 1), local))


class Loads:
    def __init__(self):
        self.copies = []

    def start(self, src, dst, sem):
        copy = pltpu.make_async_copy(src, dst, sem)
        copy.start()
        self.copies.append(copy)

    def wait(self):
        while self.copies:
            self.copies.pop().wait()


def load_weights(w_hbm, w, sem, parts):
    loads = Loads()
    for k in range(parts):
        for i in range(16):
            src = w_hbm.at[k, lax.rem(i // 2, 2), i // 4, lax.rem(i, 2)]
            loads.start(src, w.at[k, pl.ds(0, FF), pl.ds(i * 128, 128)], sem.at[k, i])
    for k in range(parts):
        w[k, FF:COLS] = jnp.zeros((COLS - FF, WIDE), BF16)
    return loads


def load_down(links, w_hbm, w, sem):
    loads, copies = Loads(), []
    for i in range(16):
        lanes = pl.ds(i * 128, 128)
        at = w_hbm.at[0, lax.rem(i // 2, 2), i // 4, lax.rem(i, 2)]
        step, where = (3, links.to(x=1)) if i // 4 < 2 else (1, links.to(x=3))
        rows = links.part(step)
        copies.append(links.start(at.at[rows], w.at[rows, lanes], where))
        for j, step in enumerate((0, 1, 3)):
            rows = links.part(step)
            loads.start(at.at[rows], w.at[rows, lanes], sem.at[j, i])
    w[FF:COLS] = jnp.zeros((COLS - FF, WIDE), BF16)
    return loads, copies


def feed_kernel(
    clusters_ref, normed_ref, cot_ref, gu_hbm, down_hbm, gain_ref, bias_ref,
    out_ref, all_out, gz_all_out, act_out, gz_ref, vec_ref,
    w, down, all_ref, gz_all_ref, act_ref, gelu_ref, slope, total, w_sem, down_sem, out_sem, *rest,
):
    bufs, (send, recv) = rest[:4], rest[4:]
    links = Links(send, recv)

    def to_low(at):
        all_ref[0, at] = normed_ref[at].astype(BF16)

    by_chunks(to_low)
    load_gu = load_weights(gu_hbm, w, w_sem, 2)
    to = links.to
    links.barrier(to(y=1), to(y=3), to(x=1), to(x=3), to(sibling=True))
    written = Loads()

    def forward(pair):
        load_gu.wait()
        rows = pair_of(all_ref, pair)
        for c in range(0, COLS, 256):
            cols = slice(c, c + 256)
            gate = dot_t(rows, w[0, cols])
            up = dot_t(rows, w[1, cols])
            bell = 0.5 + 0.5 * lax.erf(gate * np.float32(np.sqrt(0.5)))
            gelu = gate * bell
            turn = bell + gate * (jnp.exp(-0.5 * gate * gate) * np.float32(1.0 / np.sqrt(2.0 * np.pi)))
            hidden = (gelu * up).astype(BF16)
            turn = turn * up
            for i, slot in enumerate(pair):
                part = slice(i * ROWS, (i + 1) * ROWS)
                gelu_ref[slot, :, cols] = gelu[part]
                slope[slot, :, cols] = turn[part]
                act_ref[slot, :, 2 * COLS + c : 2 * COLS + c + 256] = hidden[part]

    gathering = gather_near(links, all_ref, forward)
    next(gathering)
    down_here, down_far = load_down(links, down_hbm, down, down_sem)
    alone(gathering)
    written.start(all_ref, all_out, out_sem.at[8])

    def compute(pair):
        rows = jnp.concatenate([act_ref[slot, :, 2 * COLS :] for slot in pair], axis=0)
        for d in range(0, WIDE, 512):
            result = dot(rows, down[:, d : d + 512]).astype(BF16)
            for i, slot in enumerate(pair):
                bufs[0][slot, :, d : d + 512] = result[i * ROWS : (i + 1) * ROWS]

    down_here.wait()
    received(*down_far)
    alone(scatter_near(links, bufs, compute, total))
    sent(down_far)
    vec_ref[...] = jnp.zeros_like(vec_ref)
    own, same = clusters_ref[lax.axis_index("dp")], np.float32(0.0)
    for i in range(clusters_ref.shape[0]):
        same = same + jnp.where(clusters_ref[i] == own, np.float32(1.0), np.float32(0.0))
    seq_weight = 1.0 / jnp.full((1, WIDE), same, F32)

    def finish(at):
        unit, inverse = norm_parts(deep_alpha * normed_ref[at] + total[at])
        out_ref[at] = (unit * gain_ref[...] + bias_ref[...]).astype(BF16)
        grad = cot_ref[at].astype(F32) * seq_weight
        grad_z = norm_backward(grad, unit, inverse, gain_ref[...])
        gz_ref[at] = grad_z
        gz_all_ref[0, at] = grad_z.astype(BF16)
        vec_ref[0] += rows8(grad * unit)
        vec_ref[1] += rows8(grad)

    by_chunks(finish)

    def backward(pair):
        rows = pair_of(gz_all_ref, pair)
        for c in range(0, COLS, 256):
            cols = slice(c, c + 256)
            grad_hidden = dot_t(rows, down[cols])
            for i, slot in enumerate(pair):
                part = grad_hidden[i * ROWS : (i + 1) * ROWS]
                act_ref[slot, :, cols] = (part * slope[slot, :, cols]).astype(BF16)
                act_ref[slot, :, COLS + c : COLS + c + 256] = (part * gelu_ref[slot, :, cols]).astype(BF16)
        for slot in pair:
            written.start(act_ref.at[slot], act_out.at[slot], out_sem.at[slot])

    alone(gather_near(links, gz_all_ref, backward))
    written.start(gz_all_ref, gz_all_out, out_sem.at[9])
    written.wait()


def feed_back_kernel(
    act_hbm, gz_ref, w_hbm, normed_hbm, gz_all_hbm, unit_ref, inverse_ref, gain_ref, w_out_ref,
    gz1_ref, all_out, grad_heads_ref, vec_ref, shard_ref,
    act_ref, rows_ref, all_ref, w, total, w_sem, sem, *rest,
):
    bufs, more, (send, recv) = rest[:4], rest[4:17], rest[17:]
    links = Links(send, recv)
    load_act, load_rows = Loads(), Loads()
    load_act.start(act_hbm, act_ref, sem.at[0])
    load_w = load_weights(w_hbm, w, w_sem, 2)
    load_rows.start(normed_hbm, rows_ref, sem.at[1])
    to = links.to
    links.barrier(
        to(y=1), to(y=3), to(z=2), to(x=1), to(x=3), to(z=1), to(z=3), to(sibling=True)
    )
    load_act.wait()
    load_w.wait()

    def compute(pair):
        rows = jnp.concatenate([act_ref[slot, :, : 2 * COLS] for slot in pair], axis=0)
        for d in range(0, WIDE, 512):
            cols = slice(d, d + 512)
            result = dot(rows[:, :COLS], w[0, :, cols]) + dot(rows[:, COLS:], w[1, :, cols])
            result = result.astype(BF16)
            for i, slot in enumerate(pair):
                bufs[0][slot, :, cols] = result[i * ROWS : (i + 1) * ROWS]

    def finish(at):
        grad = deep_alpha * gz_ref[at] + total[at]
        unit = unit_ref[at]
        grad_z = norm_backward(grad, unit, inverse_ref[at][:, 0:1], gain_ref[...])
        gz1_ref[at] = grad_z
        all_ref[0, at] = grad_z.astype(BF16)
        vec_ref[0] += rows8(grad * unit)
        vec_ref[1] += rows8(grad)

    def work(pair):
        result = dot_t(pair_of(all_ref, pair), w_out_ref[...]).astype(BF16)
        for i, slot in enumerate(pair):
            grad_heads_ref[pl.ds(links.first_row(slot), ROWS)] = result[i * ROWS : (i + 1) * ROWS]

    written = Loads()

    def chain():
        yield from scatter_near(links, bufs, compute, total)
        vec_ref[...] = jnp.zeros_like(vec_ref)
        by_chunks(finish)
        yield from gather(links, all_ref, work)
        written.start(all_ref, all_out, sem.at[3])

    g = more[0]

    def make(k):
        load_rows.wait()
        for c in range(0, COLS, 256):
            left = act_ref[:, :, k * COLS + c : k * COLS + c + 256].reshape(LEN, 256)
            height = min(256, FF - c)
            for d in range(0, WIDE, 512):
                right = rows_ref[:, :, d : d + 512].reshape(LEN, 512)
                result = dot_rows(left, right)[:height].astype(BF16)
                for i in range(4):
                    at = d // 128 + i
                    g[k, at // 4, at // 2 % 2, at % 2, c : c + height] = result[:, i * 128 : i * 128 + 128]
            if k == 1 and c == 512:
                load_rows.start(gz_all_hbm, rows_ref, sem.at[2])
            if c < 512:
                yield ()

    together(FEED_BACK, chain(), *reduce(links, more, make, shard_ref))
    written.wait()


def input_kernel(
    prefix_ref, q_ref, k_ref, v_ref, g_ref, lse_ref, cos_ref, sin_ref,
    w_hbm, gz1_ref, tokens_hbm, heads_ref, gz_all_hbm, shard_ref, attn_vec_ref, feed_vec_ref,
    out_ref, one_ref, two_ref, whole_ref, own_ref, feed_ref,
    total, vec_ref, w_ref, tokens_ref, gz_all_ref, grads, heads, key_sum, value_sum, held, got, local, sem, *rest,
):
    bufs, more, (send, recv) = rest[:7], rest[7:22], rest[22:]
    links = Links(send, recv)
    to = links.to
    load_gz, load_tokens, load_w = Loads(), Loads(), Loads()
    load_gz.start(gz_all_hbm, gz_all_ref, sem.at[2])
    load_tokens.start(tokens_hbm, tokens_ref, sem.at[1])
    load_w.start(w_hbm, w_ref, sem.at[0])
    links.barrier(
        to(y=1), to(y=2), to(y=3), to(z=2), to(x=1), to(x=2), to(x=3), to(sibling=True), links.beside()
    )
    for i, ref in enumerate((attn_vec_ref, feed_vec_ref)):
        for j in range(2):
            vec_ref[2 * i + j : 2 * i + j + 1] = jnp.sum(ref[j], axis=0, keepdims=True)
    vec_ref[4:8] = jnp.zeros((4, WIDE), F32)
    block = 512
    ready = [Mark(), Mark(), Mark()]

    def attend_back(head):
        lanes = slice(head * 128, head * 128 + 128)

        def keep(part, first, value):
            for i in range(value.shape[0] // ROWS):
                seq = first // ROWS + i
                d = lax.rem(seq // 2 + 4 - links.y, 4)
                slot = 2 * d - d * (d - 1) // 2 - d * (d - 1) * (d - 2) // 3
                slot = slot + 4 * lax.rem(links.z_hi + seq, 2)
                at = head * 384 + part * 128
                grads[slot, :, at : at + 128] = value[i * ROWS : (i + 1) * ROWS].astype(BF16)

        for first in range(0, LEN, block):
            at = slice(first, first + block)
            query, grad = q_ref[at, lanes], g_ref[at, lanes]
            scores = dot_t(k_ref[:, lanes], query)
            key = lax.broadcasted_iota(jnp.int32, scores.shape, 0)
            limit = lax.broadcasted_iota(jnp.int32, (1, block), 1) + first
            limit = jnp.maximum(limit, prefix_ref[0] - 1)
            weights = jnp.where(key <= limit, jnp.exp(scores - lse_ref[head, :, at]), 0.0)
            grad_weights = dot_t(v_ref[:, lanes], grad)
            inner = jnp.sum(weights * grad_weights, axis=0, keepdims=True)
            grad_scores = (weights * (grad_weights - inner)).astype(BF16)
            turned = dot_rows(grad_scores, k_ref[:, lanes]) * HEAD_DIM**-0.5
            keep(0, first, turned * cos_ref[at] - pltpu.roll(turned, 64, 1) * sin_ref[at])
            grad_key = dot(grad_scores, query)
            grad_value = dot(weights.astype(BF16), grad)
            if first == 0:
                key_sum[...] = grad_key
                value_sum[...] = grad_value
            else:
                key_sum[...] += grad_key
                value_sum[...] += grad_value
            yield ()
        turned = key_sum[...]
        keep(1, 0, turned * cos_ref[...] - pltpu.roll(turned, 64, 1) * sin_ref[...])
        keep(2, 0, value_sum[...])

    def compute(pair):
        load_w.wait()
        rows = pair_of(grads, pair)
        result = 0.0
        for part in range(3):
            for head in range(2):
                at = head * 384 + part * 128
                result = result + dot_t(rows[:, at : at + 128], w_ref[part, :, head * 128 : head * 128 + 128])
        result = result.astype(BF16)
        for i, slot in enumerate(pair):
            bufs[0][slot] = result[i * ROWS : (i + 1) * ROWS]

    def finish(at):
        value = deep_alpha * gz1_ref[at] + total[at]
        for lane in range(WIDE // 128):
            out_ref[at, lane] = value[:, lane * 128 : lane * 128 + 128]

    def chain():
        yield (ready[2],)
        for head in range(2):
            yield from attend_back(head)
            ready[head].done = True
            if head == 0:
                yield ()
        yield from scatter(links, bufs, compute, total)
        by_chunks(finish)

    def qkv(head):
        flat = more[5 * head]
        yield (ready[head],)
        load_tokens.wait()
        right = grads[:, :, head * 384 : head * 384 + 384].reshape(LEN, 384)
        for d in range(8):
            left = tokens_ref[:, :, d * 256 : d * 256 + 256].reshape(LEN, 256)
            result = dot_rows(left, right).astype(BF16)
            for part in range(3):
                for i in range(2):
                    row = part * WIDE + d * 256 + i * 128
                    chunk, at = row // 384, row % 384
                    flat[chunk // 8, chunk // 4 % 2, chunk % 4, at : at + 128] = result[
                        i * 128 : i * 128 + 128, part * 128 : part * 128 + 128
                    ]
            if d == 3:
                yield ()

    def first_shared():
        for slot in range(8):
            heads[slot] = heads_ref[pl.ds(links.first_row(slot), ROWS)]
        load_gz.wait()
        left = heads[...].reshape(LEN, 256)
        for d in range(0, WIDE, 512):
            result = dot_rows(left, gz_all_ref[:, :, d : d + 512].reshape(LEN, 512)).astype(BF16)
            for i in range(4):
                lane = d // 128 + i
                for j in range(2):
                    chunk = lane // 2 * 2 + j
                    more[10][chunk // 8, chunk // 4 % 2, chunk % 4, :, lane % 2 * 128 : lane % 2 * 128 + 128] = result[
                        j * 128 : j * 128 + 128, i * 128 : i * 128 + 128
                    ]
        ready[2].done = True
        yield from share(links, more[10:15], whole_ref)

    def shared(head):
        yield from qkv(head)
        yield from share(links, more[5 * head : 5 * head + 5], (one_ref, two_ref)[head])

    together(
        INPUT,
        collect(links, shard_ref, feed_ref, local),
        first_shared(),
        chain(),
        shared(0),
        shared(1),
        agree(links, vec_ref, (held, got)),
    )
    own_ref[...] = vec_ref[:, pl.ds(pl.multiple_of(lax.axis_index("seq") * 256, 256), 256)]


def outputs_kernel(
    feed_ref, one_ref, two_ref, out_ref, vec_ref, output_ref, input_ref,
    gate_up_ref, down_ref, grad_qkv_ref, grad_out_ref, v0_ref, v1_ref, v2_ref, v3_ref, output_out, input_out,
):
    for z in range(2):
        lanes = slice(z * 128, z * 128 + 128)
        gate_up_ref[:, 0, lanes] = feed_ref[0, 0, 0, z].astype(F32)
        gate_up_ref[:, 1, lanes] = feed_ref[1, 0, 0, z].astype(F32)
        down_ref[:, lanes] = feed_ref[2, 0, 0, z].astype(F32)
    grad_qkv_ref[:, 0:128] = one_ref[...].astype(F32)
    grad_qkv_ref[:, 128:256] = two_ref[...].astype(F32)
    grad_out_ref[...] = out_ref[...].astype(F32)
    for i, ref in enumerate((v0_ref, v1_ref, v2_ref, v3_ref)):
        ref[...] = vec_ref[i : i + 1]
    output_out[...] = output_ref[...]
    input_out[...] = input_ref[...]


def outputs(feed, one, two, out, vec, output, input_grad, total):
    half = FF // 2
    vec_part = pl.BlockSpec((1, 256), lambda i: (0, 0))
    output_part = pl.BlockSpec((ROWS // 8, WIDE), lambda i: (i // 2, 0))
    input_part = pl.BlockSpec((ROWS // 16, WIDE // 128, 128), lambda i: (i, 0, 0))
    return pl.pallas_call(
        outputs_kernel,
        name="outputs",
        grid=(16,),
        in_specs=[
            pl.BlockSpec((3, 1, 1, 2, half, 128), lambda i: (0, i // 4, i // 2 % 2, 0, i % 2, 0)),
            pl.BlockSpec((384, 128), lambda i: (i, 0)),
            pl.BlockSpec((384, 128), lambda i: (i, 0)),
            pl.BlockSpec((128, 256), lambda i: (i, 0)),
            pl.BlockSpec((8, 256), lambda i: (0, 0)),
            output_part,
            input_part,
        ],
        out_specs=(
            pl.BlockSpec((half, 2, 256), lambda i: (i, 0, 0)),
            pl.BlockSpec((half, 256), lambda i: (i, 0)),
            pl.BlockSpec((384, 256), lambda i: (i, 0)),
            pl.BlockSpec((128, 256), lambda i: (i % 2, i // 2)),
            vec_part, vec_part, vec_part, vec_part,
            output_part,
            input_part,
        ),
        out_shape=(
            jax.ShapeDtypeStruct((total, 2, 256), F32),
            jax.ShapeDtypeStruct((total, 256), F32),
            jax.ShapeDtypeStruct((6144, 256), F32),
            jax.ShapeDtypeStruct((256, WIDE), F32),
            *(jax.ShapeDtypeStruct((1, 256), F32) for _ in range(4)),
            jax.ShapeDtypeStruct(output.shape, BF16),
            jax.ShapeDtypeStruct(input_grad.shape, F32),
        ),
        compiler_params=pltpu.CompilerParams(vmem_limit_bytes=VMEM_BYTES),
    )(feed, one, two, out, vec, output, input_grad)


def on_device(
    tokens, cotangent, w_qkv, w_out, w_gate_up, w_down,
    attn_gain, attn_bias, ffn_gain, ffn_bias, prefix_len, clusters,
):
    x = tokens.reshape(ROWS, WIDE)
    cot = cotangent.reshape(ROWS, WIDE)
    dp = lax.axis_index("dp")
    cosine, sine = (jnp.asarray(t) for t in rotary_tables(LEN, HEAD_DIM))
    row = lambda v: v.reshape(1, WIDE)
    ff_total = w_down.shape[1]
    place = jnp.stack([dp % 2, dp // 2 % 4, dp // 8, jnp.int32(ff_total)]).astype(jnp.int32)
    piece = piece_of(w_gate_up.transpose(2, 1, 0), w_down.T, place)
    w_in = w_qkv.transpose(1, 0, 2)
    low, full = BF16, F32
    blocks = (8, ROWS, WIDE)
    one = pltpu.SemaphoreType.DMA
    some = lambda *n: pltpu.SemaphoreType.DMA(n)
    rows_f32 = pltpu.VMEM((ROWS, WIDE), F32)
    blocks_low = pltpu.VMEM(blocks, BF16)

    tokens_all, q, k, v, w_gu = call(
        project_kernel, "project", 0,
        [(blocks, low, "h")] + [((LEN, 256), low, "v")] * 3 + [((2, 2, 4, 2, FF, 128), low, "h")],
        (x, w_in, cosine, sine, piece), "vvvvv", (blocks_low, one, one), 60,
        2 * LEN * WIDE * 768,
    )
    heads_out, lse, normed, unit_one, inverse_one, w_dn = call(
        attended_kernel, "attended", 1,
        [
            ((LEN, 256), low, "v"), ((2, 1, LEN), full, "v"),
            ((ROWS, WIDE), full, "v"), ((ROWS, WIDE), full, "v"), ((ROWS, 128), full, "v"),
            ((1, 2, 4, 2, FF, 128), low, "h"),
        ],
        (prefix_len, q, k, v, w_out, x, row(attn_gain), row(attn_bias), piece), "svvvvvvvv",
        (rows_f32, one, *SCATTER_SCRATCH), 42, 2 * LEN * WIDE * 256,
    )
    output, normed_all, gz_all, act, grad_z2, ffn_vec = call(
        feed_kernel, "feed", 2,
        [
            ((ROWS, WIDE), low, "v"), (blocks, low, "h"), (blocks, low, "h"),
            ((8, ROWS, 3 * COLS), low, "h"), ((ROWS, WIDE), full, "v"), ((2, 8, WIDE), full, "v"),
        ],
        (clusters, normed, cot, w_gu, w_dn, row(ffn_gain), row(ffn_bias)), "svvhhvv",
        (
            pltpu.VMEM((2, COLS, WIDE), BF16), pltpu.VMEM((COLS, WIDE), BF16), blocks_low, blocks_low,
            pltpu.VMEM((8, ROWS, 3 * COLS), BF16), pltpu.VMEM((8, ROWS, COLS), F32),
            pltpu.VMEM((8, ROWS, COLS), F32), rows_f32, some(2, 16), some(3, 16), some(10), *NEAR_SCRATCH,
        ),
        48, 2 * LEN * WIDE * COLS * 4,
    )
    grad_z1, gz1_all, grad_heads, attn_vec, shard = call(
        feed_back_kernel, "feed_back", 3,
        [
            ((ROWS, WIDE), full, "v"), (blocks, low, "h"), ((LEN, 256), low, "v"),
            ((2, 8, WIDE), full, "v"), ((3, 4, PART, 128), low, "v"),
        ],
        (act, grad_z2, w_gu, normed_all, gz_all, unit_one, inverse_one, row(attn_gain), w_out),
        "hvhhhvvvv",
        (
            pltpu.VMEM((8, ROWS, 3 * COLS), BF16), blocks_low, blocks_low,
            pltpu.VMEM((2, COLS, WIDE), BF16), rows_f32, some(2, 16), some(4),
            *NEAR_SCRATCH, *REDUCE_SCRATCH,
        ),
        60, 2 * LEN * WIDE * COLS * 5,
    )
    steps = pltpu.VMEM((7, 8, WIDE), F32)
    head_sum = pltpu.VMEM((LEN, 128), F32)
    input_grad, one, two, out_whole, vec, ffn_whole = call(
        input_kernel, "input", 4,
        [
            ((ROWS, WIDE // 128, 128), full, "v"), ((2, 2, 4, 384, 128), low, "v"),
            ((2, 2, 4, 384, 128), low, "v"), ((2, 2, 4, 128, 256), low, "v"), ((8, 256), full, "v"),
            ((3, 4, 2, 2, FF, 128), low, "h"),
        ],
        (
            prefix_len, q, k, v, grad_heads, lse, cosine, sine,
            w_in, grad_z1, tokens_all, heads_out, gz1_all, shard, attn_vec, ffn_vec,
        ),
        "svvvvvvvhvhvhvvv",
        (
            rows_f32, pltpu.VMEM((8, WIDE), F32), pltpu.VMEM((3, WIDE, 256), BF16), blocks_low, blocks_low,
            pltpu.VMEM((8, ROWS, 768), BF16), pltpu.VMEM((8, ROWS, 256), BF16),
            head_sum, head_sum, steps, steps, pltpu.SemaphoreType.DMA, some(3),
            *SCATTER_SCRATCH, *share_scratch(384, 128), *share_scratch(384, 128), *share_scratch(128, 256),
        ),
        130, 2 * LEN * WIDE * 768,
    )
    grad_gate_up, grad_down, grad_qkv, grad_out, *vecs, output, input_grad = outputs(
        ffn_whole, one.reshape(6144, 128), two.reshape(6144, 128), out_whole.reshape(2048, 256),
        vec, output, input_grad, ff_total,
    )
    return (
        output.reshape(tokens.shape),
        input_grad.reshape(tokens.shape),
        grad_qkv.reshape(3, WIDE, 256).transpose(1, 0, 2),
        grad_out,
        grad_gate_up.transpose(2, 1, 0),
        grad_down.T,
        *(v.reshape(256) for v in vecs),
    )


def solution(mesh):
    return jax.shard_map(
        on_device,
        mesh=mesh,
        in_specs=(
            P("seq", "dp", None), P("seq", "dp", None), P(None, None, "seq"), P("seq", None),
            P("seq", None, None), P("seq", None), P(), P(), P(), P(), P("dp"), P(),
        ),
        out_specs=(
            P("seq", "dp", None), P("seq", "dp", None), P(None, None, "seq"), P("seq", None),
            P("seq", None, None), P("seq", None), P("seq"), P("seq"), P("seq"), P("seq"),
        ),
        check_vma=False,
    )
```

```python
import functools

import jax
import jax.numpy as jnp
import numpy as np
from jax import lax
from jax.experimental import pallas as pl
from jax.experimental.pallas import tpu as pltpu
from jax.sharding import PartitionSpec as P

MESH = pl.DeviceIdType.MESH
F32, BF16 = jnp.float32, jnp.bfloat16
HEAD_DIM = 128
ROWS = 128
WIDE = 2048
COLS = 768
LEN = 1024
VMEM_BYTES = 60 * 1024 * 1024
deep_alpha = 48.0**0.25
norm_eps = 1e-05
rotary_base = 10000.0


def rotary_tables(length, head_width):
    half_width = head_width // 2
    position = np.arange(length, dtype=np.float64)
    inverse = rotary_base ** (-np.arange(half_width, dtype=np.float64) * 2.0 / head_width)
    angles = position[:, None] * inverse[None, :]
    cosine_table = np.cos(angles)
    sine_table = np.sin(angles)
    return (
        np.concatenate([cosine_table, cosine_table], axis=1).astype(np.float32),
        np.concatenate([-sine_table, sine_table], axis=1).astype(np.float32),
    )


FF = 704
PART = 176


class Links:
    def __init__(self, send, recv):
        self.send, self.recv, self.count = send, recv, 0
        dp, seq = lax.axis_index("dp"), lax.axis_index("seq")
        y, z_hi = seq // 2, lax.rem(seq, 2)
        z_lo, x, core = dp // 8, lax.rem(dp // 2, 4), lax.rem(dp, 2)
        self.y, self.z_hi, self.z_lo, self.x, self.core = y, z_hi, z_lo, x, core
        self.z = z_hi * 2 + z_lo

    def to(self, x=0, y=0, z=0, sibling=False):
        z_hi, z_lo = self.z_at(z)
        x, y = lax.rem(self.x + x, 4), lax.rem(self.y + y, 4)
        core = 1 - self.core if sibling else self.core
        return (z_lo * 8 + x * 2 + core, y * 2 + z_hi)

    def beside(self):
        return (lax.rem(lax.axis_index("dp") + 8, 16), lax.axis_index("seq"))

    def z_at(self, offset):
        z = lax.rem(self.z + offset, 4)
        return z // 2, lax.rem(z, 2)

    def part(self, offset):
        return pl.ds(pl.multiple_of(lax.rem(self.x + offset, 4) * PART, 16), PART)

    def barrier(self, *where):
        gate = pltpu.get_barrier_semaphore()
        for device in where:
            pl.semaphore_signal(gate, inc=1, device_id=device, device_id_type=MESH)
        pl.semaphore_wait(gate, len(where))

    def start(self, src, dst, where):
        assert self.count < self.send.shape[0]
        copy = pltpu.make_async_remote_copy(
            src_ref=src,
            dst_ref=dst,
            send_sem=self.send.at[self.count],
            recv_sem=self.recv.at[self.count],
            device_id=where,
            device_id_type=MESH,
        )
        self.count += 1
        copy.start()
        return copy

    def first_row(self, slot):
        step = (0, 3, 1, 2)[slot % 4]
        half = self.z_hi if slot < 4 else 1 - self.z_hi
        return pl.multiple_of((lax.rem(self.y + step, 4) * 2 + half) * ROWS, ROWS)


class Once:
    def __init__(self, *copies):
        self.copies = list(copies)

    def wait_recv(self):
        while self.copies:
            self.copies.pop().wait_recv()


class Mark:
    done = False


class Local:
    def __init__(self, src, dst, sem):
        self.copy = pltpu.make_async_copy(src, dst, sem)
        self.copy.start()

    def wait_recv(self):
        self.copy.wait()


def together(order, *tasks):
    tasks = list(tasks)
    for task in tasks:
        next(task)
    left = len(tasks)
    for which in order:
        try:
            next(tasks[which])
        except StopIteration:
            left -= 1
    assert left == 0


def alone(task):
    for _ in task:
        pass


def received(*copies):
    for copy in copies:
        copy.wait_recv()


def sent(copies):
    for copy in copies:
        copy.wait_send()


def gather(links, buf, work, first=0, rows=ROWS):
    up, down, across = links.to(y=1), links.to(y=3), links.to(z=2)
    h0, h1 = pl.ds(first, rows // 2), pl.ds(first + rows // 2, rows // 2)
    copies = []

    def send(slot, at, dst, where):
        copies.append(links.start(buf.at[slot, at], buf.at[dst, at], where))
        return copies[-1]

    u0, d1 = send(0, h0, 1, up), send(0, h1, 2, down)
    z0, z1 = send(0, h0, 4, across), send(0, h1, 4, across)
    u1, d0 = send(0, h1, 1, up), send(0, h0, 2, down)
    yield u0, d1
    received(u0)
    fu = send(1, h0, 3, up)
    received(d1)
    fd = send(2, h1, 3, down)
    yield z0, z1
    received(z0)
    pu0 = send(4, h0, 5, up)
    received(z1)
    pd1 = send(4, h1, 6, down)
    pu1, pd0 = send(4, h1, 5, up), send(4, h0, 6, down)
    yield u1, d0
    received(u1, d0)
    work((0, 1))
    yield fu, fd
    received(fu, fd)
    work((2, 3))
    yield pu0, pd1
    received(pu0)
    gu = send(5, h0, 7, up)
    received(pd1)
    gd = send(6, h1, 7, down)
    yield pu1, pd0
    received(pu1, pd0)
    work((4, 5))
    yield gu, gd
    received(gu, gd)
    work((6, 7))
    sent(copies)


def when_whole(work, times):
    seen = {}

    def count(pair):
        seen[pair] = seen.get(pair, 0) + 1
        if seen[pair] == times:
            work(pair)

    return count


def gather_near(links, buf, work, first=0, rows=ROWS):
    up, down, side = links.to(y=1), links.to(y=3), links.to(sibling=True)
    every = pl.ds(first, rows)
    h0, h1 = pl.ds(first, rows // 2), pl.ds(first + rows // 2, rows // 2)
    copies = []

    def send(slot, at, dst, where):
        copies.append(links.start(buf.at[slot, at], buf.at[dst, at], where))
        return copies[-1]

    u0, d1 = send(0, h0, 1, up), send(0, h1, 2, down)
    u1, d0 = send(0, h1, 1, up), send(0, h0, 2, down)
    s0 = send(0, every, 4, side)
    yield (s0,)
    received(s0)
    work((0, 4))
    yield u0, d1
    received(u0)
    fu = send(1, h0, 3, up)
    received(d1)
    fd = send(2, h1, 3, down)
    yield u1, d0
    received(u1)
    s1 = send(1, every, 5, side)
    received(d0)
    s2 = send(2, every, 6, side)
    work((1, 2))
    yield s1, s2
    received(s1, s2)
    work((5, 6))
    yield fu, fd
    received(fu)
    s30 = send(3, h0, 7, side)
    received(fd)
    s31 = send(3, h1, 7, side)
    yield s30, s31
    received(s30, s31)
    work((3, 7))
    sent(copies)


A, B = pl.ds(0, 80), pl.ds(80, 48)
A0, A1 = pl.ds(0, 48), pl.ds(48, 32)
B0, B1 = pl.ds(80, 16), pl.ds(96, 32)
SCATTER_SCRATCH = (
    pltpu.VMEM((8, ROWS, WIDE), BF16),
    pltpu.VMEM((4, 48, WIDE), BF16),
    pltpu.VMEM((48, WIDE), BF16),
    pltpu.VMEM((2, 48, WIDE), BF16),
    pltpu.VMEM((2, 80, WIDE), BF16),
    pltpu.VMEM((2, 2, 80, WIDE), BF16),
    pltpu.VMEM((80, WIDE), BF16),
)


def add_rows(target, slot, rows, *others):
    value = target[slot, rows].astype(F32)
    for other in others:
        value = value + other.astype(F32)
    target[slot, rows] = value.astype(BF16)


def scatter(links, bufs, compute, total):
    sums, from_z, b_far, b_near, a_far, a_near, a_z = bufs
    up, down, across = links.to(y=1), links.to(y=3), links.to(z=2)
    copies = []

    def send(src, dst, where):
        copies.append(links.start(src, dst, where))
        return copies[-1]

    def far_a(o):
        half = o // 4
        return (
            send(sums.at[o + 3, A0], a_far.at[half, pl.ds(0, 48)], up),
            send(sums.at[o + 3, A1], a_far.at[half, pl.ds(48, 32)], down),
        )

    def near_a(o, far):
        half = o // 4
        received(far[0])
        add_rows(sums, o + 2, A0, a_far[half, 0:48])
        one = send(sums.at[o + 2, A], a_near.at[half, 0], up)
        received(far[1])
        add_rows(sums, o + 1, A1, a_far[half, 48:80])
        return one, send(sums.at[o + 1, A], a_near.at[half, 1], down)

    def cross_b(j):
        return send(sums.at[4 + j, B], from_z.at[j], across)

    compute((7, 3))
    z3 = cross_b(3)
    far_other = far_a(4)
    far_own = far_a(0)
    yield ()
    compute((5, 1))
    z1 = cross_b(1)
    yield ()
    compute((6, 2))
    z2 = cross_b(2)
    yield far_other
    near_other = near_a(4, far_other)
    compute((4, 0))
    z0 = cross_b(0)
    yield (z3,)
    received(z3)
    add_rows(sums, 3, B, from_z[3])
    far_b = (
        send(sums.at[3, B0], b_far.at[pl.ds(0, 16)], up),
        send(sums.at[3, B1], b_far.at[pl.ds(16, 32)], down),
    )
    yield far_own
    near_own = near_a(0, far_own)
    yield z1, z2
    received(z2)
    add_rows(sums, 2, B, from_z[2])
    received(z1)
    add_rows(sums, 1, B, from_z[1])
    yield far_b
    received(far_b[0])
    add_rows(sums, 2, B0, b_far[0:16])
    near_b0 = send(sums.at[2, B], b_near.at[0], up)
    received(far_b[1])
    add_rows(sums, 1, B1, b_far[16:48])
    near_b1 = send(sums.at[1, B], b_near.at[1], down)
    yield near_other
    received(*near_other)
    add_rows(sums, 4, A, a_near[1, 0], a_near[1, 1])
    z_a = send(sums.at[4, A], a_z, across)
    yield z0, near_b0, near_b1
    received(z0, near_b0, near_b1)
    total[80:128] = (
        sums[0, B].astype(F32)
        + from_z[0].astype(F32)
        + b_near[0].astype(F32)
        + b_near[1].astype(F32)
    )
    yield (z_a, *near_own)
    received(*near_own)
    received(z_a)
    total[0:80] = (
        sums[0, A].astype(F32)
        + a_near[0, 0].astype(F32)
        + a_near[0, 1].astype(F32)
        + a_z[...].astype(F32)
    )
    sent(copies)


NEAR_SCRATCH = (
    pltpu.VMEM((8, ROWS, WIDE), BF16),
    pltpu.VMEM((4, ROWS, WIDE), BF16),
    pltpu.VMEM((ROWS, WIDE), BF16),
    pltpu.VMEM((2, ROWS, WIDE), BF16),
)


def scatter_near(links, bufs, compute, total):
    sums, from_side, far, near = bufs
    up, down, side = links.to(y=1), links.to(y=3), links.to(sibling=True)
    copies = []

    def send(src, dst, where):
        copies.append(links.start(src, dst, where))
        return copies[-1]

    compute((7, 3))
    s3 = Once(send(sums.at[7], from_side.at[3], side))
    compute((5, 6))
    s12 = Once(send(sums.at[5], from_side.at[1], side), send(sums.at[6], from_side.at[2], side))
    compute((1, 2))
    later = []

    def last():
        compute((4, 0))
        later.append(Once(send(sums.at[4], from_side.at[0], side)))

    def task(first, rows):
        every = pl.ds(first, rows)
        h0, h1 = pl.ds(first, rows // 2), pl.ds(first + rows // 2, rows // 2)
        yield (s3,)
        received(s3)
        add_rows(sums, 3, every, from_side[3, every])
        fu = send(sums.at[3, h0], far.at[h0], up)
        fd = send(sums.at[3, h1], far.at[h1], down)
        received(s12)
        add_rows(sums, 2, every, from_side[2, every])
        nu1 = send(sums.at[2, h1], near.at[0, h1], up)
        add_rows(sums, 1, every, from_side[1, every])
        nd0 = send(sums.at[1, h0], near.at[1, h0], down)
        if not later:
            last()
        yield fu, fd
        received(fu)
        add_rows(sums, 2, h0, far[h0])
        nu0 = send(sums.at[2, h0], near.at[0, h0], up)
        received(fd)
        add_rows(sums, 1, h1, far[h1])
        nd1 = send(sums.at[1, h1], near.at[1, h1], down)
        yield nu1, nd0, nu0, nd1
        received(later[0], nu1, nd0, nu0, nd1)
        total[every] = (
            sums[0, every].astype(F32)
            + from_side[0, every].astype(F32)
            + near[0, every].astype(F32)
            + near[1, every].astype(F32)
        )

    return task, copies


Y0, Y1 = pl.ds(0, 2), pl.ds(2, 2)
GU = pl.ds(0, 2)


def across_y(links, piece, own, local):
    copies = []
    for step in (2, 1, 3):
        there = lax.rem(links.y + step, 4)
        copies.append(links.start(piece(there), own(), links.to(y=step)))
    keep = Local(piece(links.y), own(), local)
    return Once(keep, *copies), copies


def ring_gather(links, arrived, at, first, second):
    up, down = first
    right, left = second
    copies = []

    def send(ref, where):
        copies.append(links.start(ref, ref, where))
        return copies[-1]

    def both(a):
        return send(at(a, 0), right), send(at(a, 0), left)

    def onward(a):
        return [send(at(a, 3, Y0), right), send(at(a, 1, Y1), left)]

    yield (arrived,)
    received(arrived)
    u, d = send(at(0, 0), up), send(at(0, 0), down)
    near = [both(0)]
    yield u, d
    received(u)
    fu = send(at(3, 0, Y0), up)
    received(d)
    fd = send(at(1, 0, Y1), down)
    near.append(both(3))
    near.append(both(1))
    yield near[0]
    received(*near[0])
    far = onward(0)
    yield fu, fd
    received(fu, fd)
    near.append(both(2))
    for i, a in enumerate((3, 1, 2)):
        yield near[1 + i]
        received(*near[1 + i])
        far += onward(a)
    yield far
    received(*far)
    sent(copies)


Z_FIRST = (0, 2)


def spread(links, piece, w, local):
    along_x = (links.to(x=1), links.to(x=3))
    along_z = (links.to(z=1), links.to(z=3))
    every = pl.ds(0, 4)

    def place(k, z, x, y):
        z_hi, z_lo = links.z_at(z)
        return w.at[k, z_hi, y, z_lo, links.part(x)]

    def own():
        return w.at[:, links.z_hi, links.y, links.z_lo, links.part(0)]

    arrived, copies = across_y(links, lambda y: piece.at[y], own, local)

    def one(k, z_first):
        if z_first:
            yield from ring_gather(links, arrived, lambda a, b, y=every: place(k, a, b, y), along_z, along_x)
        else:
            yield from ring_gather(links, arrived, lambda a, b, y=every: place(k, b, a, y), along_x, along_z)
        if k == 0:
            sent(copies)

    return tuple(one(k, k in Z_FIRST) for k in range(3))


def ring_scratch(*block):
    return [pltpu.VMEM(block, BF16), pltpu.VMEM((2, *block), BF16)]


REDUCE_SCRATCH = (
    pltpu.VMEM((3, 4, 2, 2, FF, 128), BF16),
    *ring_scratch(4, 2, 2, PART, 128), *ring_scratch(4, PART, 128),
    *ring_scratch(4, 2, 2, PART, 128), *ring_scratch(4, PART, 128),
    *ring_scratch(4, FF, 128), *ring_scratch(4, PART, 128),
)


def accumulate(count, target, *others):
    def step(i, carry):
        ref = target(i)
        value = ref[...].astype(F32)
        for other in others:
            value = value + other(i)[...].astype(F32)
        ref[...] = value.astype(BF16)
        return carry

    lax.fori_loop(0, count, step, 0)


def ring_reduce(links, at, blocks, ring, far, near, devices):
    up, down = devices
    copies = []
    every = pl.ds(0, 4)

    def send(src, dst, where):
        copies.append(links.start(src, dst, where))
        return copies[-1]

    half = ring // 2
    fu, fd = send(at(2, Y0), far.at[Y0], up), send(at(2, Y1), far.at[Y1], down)
    nu, nd = send(at(1, Y1), near.at[0, Y1], up), send(at(3, Y0), near.at[1, Y0], down)
    yield fu, fd
    received(fu)
    accumulate(half, lambda i: blocks(at(1, every), i), lambda i: blocks(far, i))
    mu = send(at(1, Y0), near.at[0, Y0], up)
    received(fd)
    accumulate(half, lambda i: blocks(at(3, every), i + half), lambda i: blocks(far, i + half))
    md = send(at(3, Y1), near.at[1, Y1], down)
    yield nu, nd, mu, md
    received(nu, nd, mu, md)
    accumulate(
        ring, lambda i: blocks(at(0, every), i), lambda i: blocks(near.at[0], i), lambda i: blocks(near.at[1], i)
    )
    sent(copies)


def reduce(links, bufs, make, shard):
    g = bufs[0]
    along_x = (links.to(x=1), links.to(x=3))
    along_z = (links.to(z=1), links.to(z=3))
    made = [Mark(), Mark()]

    def one(k, x_first):
        far, near, far2, near2 = bufs[1 + 4 * k : 5 + 4 * k]
        z_hi, z_lo = links.z_at(0)

        def along_z_at(a, y):
            hi, lo = links.z_at(a)
            return g.at[k, y, hi, lo]

        def along_x_at(a, y):
            return g.at[k, y, :, :, links.part(a)]

        def rest_z(a, y):
            hi, lo = links.z_at(a)
            return g.at[k, y, hi, lo, links.part(0)]

        def rest_x(a, y):
            return g.at[k, y, z_hi, z_lo, links.part(a)]

        def four(ref, i):
            return ref.at[i // 4, lax.rem(i // 2, 2), lax.rem(i, 2)]

        def plain(ref, i):
            return ref.at[i]

        if k:
            yield (made[k - 1],)
        yield from make(k)
        if k < 2:
            made[k].done = True
        if x_first:
            yield from ring_reduce(links, along_x_at, four, 16, far, near, along_x)
            yield from ring_reduce(links, rest_z, plain, 4, far2, near2, along_z)
        else:
            yield from ring_reduce(links, along_z_at, plain, 4, far, near, along_z)
            yield from ring_reduce(links, rest_x, plain, 4, far2, near2, along_x)
        shard[k] = g[k, :, z_hi, z_lo, links.part(0)]

    return one(0, True), one(1, True), one(2, False)


def regather(links, at, half, x_first):
    xp, xm, side = links.to(x=1), links.to(x=3), links.to(sibling=True)
    beside = links.beside()
    copies, sides = [], []

    def send(ref, where):
        copies.append(links.start(ref, ref, where))
        return copies[-1]

    def share(ref):
        sides.append(send(ref, side))

    near = [(send(at(0, 0), xp), send(at(0, 0), xm))]
    z = [(0, send(at(0, 0), beside))]
    share(at(0, 0))
    far = []
    if not x_first:
        yield (z[0][1],)
        received(z[0][1])
        near.append((send(at(1, 0), xp), send(at(1, 0), xm)))
        share(at(1, 0))
    for i in range(len(near)):
        yield near[i]
        received(near[i][0])
        far_up = send(half(at(i, 3), 0), xp)
        received(near[i][1])
        far.append((far_up, send(half(at(i, 1), 1), xm)))
        for x in (3, 1):
            if x_first:
                z.append((x, send(at(0, x), beside)))
            share(at(i, x))
    for i in range(len(near)):
        yield far[i]
        received(*far[i])
        if x_first:
            z.append((2, send(at(0, 2), beside)))
        share(at(i, 2))
    if x_first:
        for x, copy in z:
            yield (copy,)
            received(copy)
            share(at(1, x))
    yield sides
    received(*sides)
    sent(copies)


def collect(links, shard, out, local):
    def own():
        return out.at[:, links.y, links.core, links.z_lo, links.part(0)]

    arrived, copies = across_y(links, lambda y: shard.at[:, y], own, local)

    def task(matrices, x_first):
        yield (arrived,)
        received(arrived)

        def at(z, x):
            return out.at[matrices, :, links.core, lax.rem(links.z_lo + z, 2), links.part(x)]

        def half(ref, i):
            return ref.at[:, pl.ds(2 * i, 2)]

        yield from regather(links, at, half, x_first)
        if x_first:
            sent(copies)

    return task(GU, False), task(pl.ds(2, 1), True)


def share_scratch(rows, lanes):
    return [
        pltpu.VMEM((2, 2, 4, rows, lanes), BF16),
        pltpu.VMEM((2, 4, rows, lanes), BF16),
        pltpu.VMEM((2, rows, lanes), BF16),
        pltpu.VMEM((2, 2, rows, lanes), BF16),
        pltpu.VMEM((rows, lanes), BF16),
    ]


SHARE_X_FIRST = (False, False, False)


def share(links, bufs, out, x_first):
    q, from_side, far, near, from_z = bufs
    xp, xm, side = links.to(x=1), links.to(x=3), links.to(sibling=True)
    beside = links.beside()
    core, z_lo = links.core, links.z_lo
    count = q.shape[3]
    copies = []

    def send(src, dst, where):
        copies.append(links.start(src, dst, where))
        return copies[-1]

    def there(x):
        return lax.rem(links.x + x, 4)

    def rows(ref):
        return lambda i: ref.at[pl.ds(pl.multiple_of(i * 64, 64), 64)]

    def add(target, *others):
        accumulate(count // 64, rows(target), *(rows(other) for other in others))

    s = send(q.at[1 - core], from_side, side)
    yield (s,)
    received(s)
    for x in (2, 1, 3, 0):
        for z in range(2):
            add(q.at[core, z, there(x)], from_side.at[z, there(x)])
        if x == 2:
            fu, fd = send(q.at[core, 0, there(2)], far.at[0], xp), send(q.at[core, 1, there(2)], far.at[1], xm)
    nu = send(q.at[core, 1, there(1)], near.at[0, 1], xp)
    nd = send(q.at[core, 0, there(3)], near.at[1, 0], xm)
    yield fu, fd
    received(fu)
    add(q.at[core, 0, there(1)], far.at[0])
    mu = send(q.at[core, 0, there(1)], near.at[0, 0], xp)
    received(fd)
    add(q.at[core, 1, there(3)], far.at[1])
    md = send(q.at[core, 1, there(3)], near.at[1, 1], xm)
    yield nu, nd, mu, md
    received(nu, nd, mu, md)
    for z in range(2):
        add(q.at[core, z, there(0)], near.at[0, z], near.at[1, z])
    b = send(q.at[core, 1 - z_lo, there(0)], from_z, beside)
    yield (b,)
    received(b)

    def finish(i, carry):
        at = pl.ds(pl.multiple_of(i * 64, 64), 64)
        value = q[core, z_lo, links.x, at].astype(F32) + from_z[at].astype(F32)
        out[core, z_lo, links.x, at] = value.astype(BF16)
        return carry

    lax.fori_loop(0, count // 64, finish, 0)

    def at(z, x):
        return out.at[core, lax.rem(z_lo + z, 2), there(x)]

    def half(ref, i):
        return ref.at[pl.ds(count // 2 * i, count // 2)]

    yield from regather(links, at, half, x_first)
    sent(copies)


def agree(links, vec, bufs):
    y, x = links.y, links.x
    copies = []
    steps = (
        links.to(sibling=True),
        links.to(y=1 + 2 * lax.rem(y, 2)),
        links.to(y=2),
        links.to(z=2),
        links.to(x=1 + 2 * lax.rem(x, 2)),
        links.to(x=2),
        links.beside(),
    )
    held, got = bufs
    held[0] = vec[...]
    for i, where in enumerate(steps):
        copies.append(links.start(held.at[i], got.at[i], where))
        yield (copies[-1],)
        received(copies[-1])
        if i < len(steps) - 1:
            held[i + 1] = held[i] + got[i]
        else:
            vec[...] = held[i] + got[i]
    sent(copies)


def dot(a, b):
    return jnp.dot(a, b, preferred_element_type=F32)


def dot_t(a, b):
    return lax.dot_general(a, b, (((1,), (1,)), ((), ())), preferred_element_type=F32)


def dot_rows(a, b):
    return lax.dot_general(a, b, (((0,), (0,)), ((), ())), preferred_element_type=F32)


def pair_of(ref, pair):
    return jnp.concatenate([ref[pair[0]], ref[pair[1]]], axis=0)


def by_chunks(body, first=0, rows=ROWS):
    def step(i, carry):
        body(pl.ds(pl.multiple_of(first + i * 16, 16), 16))
        return carry

    lax.fori_loop(0, rows // 16, step, 0)


def norm_parts(row_total):
    center = row_total - jnp.mean(row_total, axis=-1, keepdims=True)
    spread = jnp.mean(center * center, axis=-1, keepdims=True)
    inverse = lax.rsqrt(spread + norm_eps)
    return center * inverse, inverse


def norm_backward(grad_result, unit, inverse, gain):
    grad_unit = grad_result * gain
    return inverse * (
        grad_unit
        - jnp.mean(grad_unit, axis=-1, keepdims=True)
        - unit * jnp.mean(grad_unit * unit, axis=-1, keepdims=True)
    )


def rows8(values):
    return values[0:8] + values[8:16]


VMEM = pl.BlockSpec(memory_space=pltpu.VMEM)
HBM = pl.BlockSpec(memory_space=pl.ANY)
SMEM = pl.BlockSpec(memory_space=pltpu.SMEM)
KINDS = {"v": VMEM, "s": SMEM, "h": HBM}


def call(body, name, ident, outs, operands, spaces, scratch, copies, flops=0):
    sems = [pltpu.SemaphoreType.DMA((copies,)), pltpu.SemaphoreType.DMA((copies,))]
    return pl.pallas_call(
        body,
        name=name,
        out_shape=tuple(jax.ShapeDtypeStruct(s, d) for s, d, _ in outs),
        in_specs=[KINDS[k] for k in spaces],
        out_specs=tuple(KINDS[k] for _, _, k in outs),
        scratch_shapes=[*scratch, *sems],
        compiler_params=pltpu.CompilerParams(
            collective_id=ident, has_side_effects=True, vmem_limit_bytes=VMEM_BYTES
        ),
        cost_estimate=pl.CostEstimate(flops=flops, bytes_accessed=20_000_000, transcendentals=0),
    )(*operands)


FRONT = (1, 2, 3, 0, 0, 1, 1, 2, 0, 2, 0, 3, 3, 1, 1, 1, 0, 2, 2, 2, 0, 3, 3, 3, 0, 0, 0, 2, 1, 0, 0, 3, 0, 1, 0, 3, 2, 0, 0, 0, 0)
FEED = (1, 1, 0, 0, 1, 0, 1, 1, 0, 0, 1, 1, 0, 1, 0, 0, 1, 0)
FEED_BACK = (1, 2, 2, 1, 3, 3, 3, 1, 4, 4, 4, 1, 2, 0, 1, 1, 1, 0, 4, 3, 1, 1, 0, 1, 4, 0, 2, 0, 0, 0, 2, 3, 4, 2, 0, 0, 3, 4, 0, 3)
INPUT = (3, 2, 6, 1, 0, 2, 6, 3, 1, 6, 3, 4, 4, 3, 4, 1, 1, 1, 2, 0, 0, 4, 1, 3, 6, 3, 5, 5, 3, 2, 3, 5, 4, 6, 1, 0, 0, 1, 3, 5, 2, 3, 3, 2, 6, 3, 4, 0, 5, 6, 2, 2, 3, 4, 4, 2, 5, 2, 0, 4, 3, 4, 5, 5, 4, 3, 5, 5, 4, 5, 5, 3)


def piece_kernel(place_ref, *refs):
    out_ref = refs[8]
    for y in range(4):
        chunk = (y * 2 + place_ref[0]) * 4 + place_ref[1]
        row = lax.broadcasted_iota(jnp.int32, (PART, 128), 0) + chunk * PART
        inside = row < place_ref[3]
        both = refs[y][...].astype(F32)
        out_ref[y, 0] = jnp.where(inside, both[:, 0], 0.0).astype(BF16)
        out_ref[y, 1] = jnp.where(inside, both[:, 1], 0.0).astype(BF16)
        out_ref[y, 2] = jnp.where(inside, refs[4 + y][...].astype(F32), 0.0).astype(BF16)


def piece_of(gate_up, down, place):
    def chunk(y, place):
        return (y * 2 + place[0]) * 4 + place[1]

    return pl.pallas_call(
        piece_kernel,
        name="piece",
        grid_spec=pltpu.PrefetchScalarGridSpec(
            num_scalar_prefetch=1,
            grid=(1,),
            in_specs=[
                *(pl.BlockSpec((PART, 2, 128), lambda i, p, y=y: (chunk(y, p), 0, p[2])) for y in range(4)),
                *(pl.BlockSpec((PART, 128), lambda i, p, y=y: (chunk(y, p), p[2])) for y in range(4)),
            ],
            out_specs=pl.BlockSpec((4, 3, PART, 128), lambda i, p: (0, 0, 0, 0)),
        ),
        out_shape=jax.ShapeDtypeStruct((4, 3, PART, 128), BF16),
    )(place, *[gate_up] * 4, *[down] * 4)


def front_kernel(
    prefix_ref, x_ref, w_ref, cos_ref, sin_ref, w_out_ref, gain_ref, bias_ref, piece_ref,
    tokens_out, q_ref, k_ref, v_ref, heads_ref, lse_ref, normed_ref, unit_ref, inverse_ref, w_all_ref,
    all_ref, total, local, out_sem, *rest,
):
    bufs, (send, recv) = rest[:7], rest[7:]
    links = Links(send, recv)
    all_ref[0] = x_ref[...]
    to = links.to
    links.barrier(to(y=1), to(y=3), to(z=2), to(y=2), to(x=1), to(x=3), to(z=1), to(z=3))

    def project(pair):
        rows = pair_of(all_ref, pair)
        for part, out in enumerate((q_ref, k_ref, v_ref)):
            result = dot(rows, w_ref[part])
            for i, slot in enumerate(pair):
                at = pl.ds(links.first_row(slot), ROWS)
                piece = result[i * ROWS : (i + 1) * ROWS]
                if part == 2:
                    out[at] = piece.astype(BF16)
                    continue
                cosine, sine = cos_ref[at], sin_ref[at]
                for head in range(2):
                    lanes = slice(head * 128, head * 128 + 128)
                    turned = piece[:, lanes] * cosine + pltpu.roll(piece[:, lanes], 64, 1) * sine
                    if part == 0:
                        turned = turned * HEAD_DIM**-0.5
                    out[at, lanes] = turned.astype(BF16)

    def attend(first, block):
        at = pl.ds(first, block)
        for head in range(2):
            lanes = slice(head * 128, head * 128 + 128)
            scores = dot_t(k_ref[:, lanes], q_ref[at, lanes])
            key = lax.broadcasted_iota(jnp.int32, scores.shape, 0)
            limit = lax.broadcasted_iota(jnp.int32, (1, block), 1) + first
            limit = jnp.maximum(limit, prefix_ref[0] - 1)
            scores = jnp.where(key <= limit, scores, -1e30)
            peak = jnp.max(scores, axis=0, keepdims=True)
            exponent = jnp.exp(scores - peak)
            row_total = jnp.sum(exponent, axis=0, keepdims=True)
            weights = (exponent * (1.0 / row_total)).astype(BF16)
            heads_ref[at, lanes] = dot_rows(weights, v_ref[:, lanes]).astype(BF16)
            lse_ref[head, :, at] = peak + jnp.log(row_total)

    def compute(pair):
        step = (0, 3, 1, 2)[pair[1]]
        attend(pl.multiple_of(lax.rem(links.y + step, 4) * 2 * ROWS, 2 * ROWS), 2 * ROWS)
        rows = jnp.concatenate([heads_ref[pl.ds(links.first_row(s), ROWS)] for s in pair], axis=0)
        result = dot(rows, w_out_ref[...]).astype(BF16)
        for i, slot in enumerate(pair):
            bufs[0][slot] = result[i * ROWS : (i + 1) * ROWS]

    def finish(at):
        unit, inverse = norm_parts(deep_alpha * x_ref[at].astype(F32) + total[at])
        unit_ref[at] = unit
        inverse_ref[at] = jnp.broadcast_to(inverse, (16, 128))
        normed_ref[at] = unit * gain_ref[...] + bias_ref[...]

    written = pltpu.make_async_copy(all_ref, tokens_out, out_sem)

    def chain():
        yield from gather(links, all_ref, project)
        written.start()
        yield from scatter(links, bufs, compute, total)
        by_chunks(finish)

    together(FRONT, chain(), *spread(links, piece_ref, w_all_ref, local))
    written.wait()


class Loads:
    def __init__(self):
        self.copies = []

    def start(self, src, dst, sem):
        copy = pltpu.make_async_copy(src, dst, sem)
        copy.start()
        self.copies.append(copy)

    def wait(self):
        while self.copies:
            self.copies.pop().wait()


def load_weights(w_hbm, w, sem, parts):
    loads = Loads()
    for k in range(parts):
        for i in range(16):
            src = w_hbm.at[k, lax.rem(i // 2, 2), i // 4, lax.rem(i, 2)]
            loads.start(src, w.at[k, pl.ds(0, FF), pl.ds(i * 128, 128)], sem.at[k, i])
    for k in range(parts):
        w[k, FF:COLS] = jnp.zeros((COLS - FF, WIDE), BF16)
    return loads


def feed_kernel(
    clusters_ref, normed_ref, cot_ref, w_hbm, gain_ref, bias_ref,
    out_ref, all_out, gz_all_out, act_out, gz_ref, vec_ref,
    w, all_ref, gz_all_ref, act_ref, gelu_ref, slope, total, w_sem, out_sem, *rest,
):
    bufs, (send, recv) = rest[:4], rest[4:]
    links = Links(send, recv)

    def to_low(at):
        all_ref[0, at] = normed_ref[at].astype(BF16)

    by_chunks(to_low)
    load_w = load_weights(w_hbm, w, w_sem, 3)
    links.barrier(links.to(y=1), links.to(y=3), links.to(sibling=True))
    written = Loads()

    def forward(pair):
        load_w.wait()
        rows = pair_of(all_ref, pair)
        for c in range(0, COLS, 256):
            cols = slice(c, c + 256)
            gate = dot_t(rows, w[0, cols])
            up = dot_t(rows, w[1, cols])
            bell = 0.5 + 0.5 * lax.erf(gate * np.float32(np.sqrt(0.5)))
            gelu = gate * bell
            turn = bell + gate * (jnp.exp(-0.5 * gate * gate) * np.float32(1.0 / np.sqrt(2.0 * np.pi)))
            hidden = (gelu * up).astype(BF16)
            turn = turn * up
            for i, slot in enumerate(pair):
                part = slice(i * ROWS, (i + 1) * ROWS)
                gelu_ref[slot, :, cols] = gelu[part]
                slope[slot, :, cols] = turn[part]
                act_ref[slot, :, 2 * COLS + c : 2 * COLS + c + 256] = hidden[part]

    alone(gather_near(links, all_ref, forward))
    written.start(all_ref, all_out, out_sem.at[8])

    def compute(pair):
        rows = jnp.concatenate([act_ref[slot, :, 2 * COLS :] for slot in pair], axis=0)
        for d in range(0, WIDE, 512):
            result = dot(rows, w[2, :, d : d + 512]).astype(BF16)
            for i, slot in enumerate(pair):
                bufs[0][slot, :, d : d + 512] = result[i * ROWS : (i + 1) * ROWS]

    vec_ref[...] = jnp.zeros_like(vec_ref)
    own, same = clusters_ref[lax.axis_index("dp")], np.float32(0.0)
    for i in range(clusters_ref.shape[0]):
        same = same + jnp.where(clusters_ref[i] == own, np.float32(1.0), np.float32(0.0))
    seq_weight = 1.0 / jnp.full((1, WIDE), same, F32)

    def finish(at):
        unit, inverse = norm_parts(deep_alpha * normed_ref[at] + total[at])
        out_ref[at] = (unit * gain_ref[...] + bias_ref[...]).astype(BF16)
        grad = cot_ref[at].astype(F32) * seq_weight
        grad_z = norm_backward(grad, unit, inverse, gain_ref[...])
        gz_ref[at] = grad_z
        gz_all_ref[0, at] = grad_z.astype(BF16)
        vec_ref[0] += rows8(grad * unit)
        vec_ref[1] += rows8(grad)

    def backward(pair):
        rows = pair_of(gz_all_ref, pair)
        for c in range(0, COLS, 256):
            cols = slice(c, c + 256)
            grad_hidden = dot_t(rows, w[2, cols])
            for i, slot in enumerate(pair):
                part = grad_hidden[i * ROWS : (i + 1) * ROWS]
                act_ref[slot, :, cols] = (part * slope[slot, :, cols]).astype(BF16)
                act_ref[slot, :, COLS + c : COLS + c + 256] = (part * gelu_ref[slot, :, cols]).astype(BF16)
        for slot in pair:
            written.start(act_ref.at[slot], act_out.at[slot], out_sem.at[slot])

    task, copies = scatter_near(links, bufs, compute, total)
    whole = when_whole(backward, 2)

    def chain(first):
        yield from task(first, 64)
        by_chunks(finish, first, 64)
        yield from gather_near(links, gz_all_ref, whole, first, 64)

    together(FEED, chain(0), chain(64))
    sent(copies)
    written.start(gz_all_ref, gz_all_out, out_sem.at[9])
    written.wait()


def feed_back_kernel(
    act_hbm, gz_ref, w_hbm, normed_hbm, gz_all_hbm, unit_ref, inverse_ref, gain_ref, w_out_ref,
    gz1_ref, all_out, grad_heads_ref, vec_ref, shard_ref,
    act_ref, rows_ref, all_ref, w, total, w_sem, sem, *rest,
):
    bufs, more, (send, recv) = rest[:4], rest[4:17], rest[17:]
    links = Links(send, recv)
    load_act, load_rows = Loads(), Loads()
    load_act.start(act_hbm, act_ref, sem.at[0])
    load_w = load_weights(w_hbm, w, w_sem, 2)
    load_rows.start(normed_hbm, rows_ref, sem.at[1])
    to = links.to
    links.barrier(
        to(y=1), to(y=3), to(z=2), to(x=1), to(x=3), to(z=1), to(z=3), to(sibling=True)
    )
    load_act.wait()
    load_w.wait()

    def compute(pair):
        rows = jnp.concatenate([act_ref[slot, :, : 2 * COLS] for slot in pair], axis=0)
        for d in range(0, WIDE, 512):
            cols = slice(d, d + 512)
            result = dot(rows[:, :COLS], w[0, :, cols]) + dot(rows[:, COLS:], w[1, :, cols])
            result = result.astype(BF16)
            for i, slot in enumerate(pair):
                bufs[0][slot, :, cols] = result[i * ROWS : (i + 1) * ROWS]

    def finish(at):
        grad = deep_alpha * gz_ref[at] + total[at]
        unit = unit_ref[at]
        grad_z = norm_backward(grad, unit, inverse_ref[at][:, 0:1], gain_ref[...])
        gz1_ref[at] = grad_z
        all_ref[0, at] = grad_z.astype(BF16)
        vec_ref[0] += rows8(grad * unit)
        vec_ref[1] += rows8(grad)

    def work(pair):
        result = dot_t(pair_of(all_ref, pair), w_out_ref[...]).astype(BF16)
        for i, slot in enumerate(pair):
            grad_heads_ref[pl.ds(links.first_row(slot), ROWS)] = result[i * ROWS : (i + 1) * ROWS]

    written = Loads()

    vec_ref[...] = jnp.zeros_like(vec_ref)
    task, copies = scatter_near(links, bufs, compute, total)
    whole = when_whole(work, 2)

    def chain(first):
        yield from task(first, 64)
        by_chunks(finish, first, 64)
        yield from gather(links, all_ref, whole, first, 64)

    g = more[0]

    def make(k):
        load_rows.wait()
        for c in range(0, COLS, 256):
            left = act_ref[:, :, k * COLS + c : k * COLS + c + 256].reshape(LEN, 256)
            height = min(256, FF - c)
            for d in range(0, WIDE, 512):
                right = rows_ref[:, :, d : d + 512].reshape(LEN, 512)
                result = dot_rows(left, right)[:height].astype(BF16)
                for i in range(4):
                    at = d // 128 + i
                    g[k, at // 4, at // 2 % 2, at % 2, c : c + height] = result[:, i * 128 : i * 128 + 128]
            if k == 1 and c == 512:
                load_rows.start(gz_all_hbm, rows_ref, sem.at[2])
            if c < 512:
                yield ()

    together(FEED_BACK, chain(0), chain(64), *reduce(links, more, make, shard_ref))
    sent(copies)
    written.start(all_ref, all_out, sem.at[3])
    written.wait()


def input_kernel(
    prefix_ref, q_ref, k_ref, v_ref, g_ref, lse_ref, cos_ref, sin_ref,
    w_hbm, gz1_ref, tokens_hbm, heads_ref, gz_all_hbm, shard_ref, attn_vec_ref, feed_vec_ref,
    out_ref, one_ref, two_ref, whole_ref, own_ref, feed_ref,
    total, vec_ref, w_ref, tokens_ref, gz_all_ref, grads, heads, key_sum, value_sum, held, got, local, sem, *rest,
):
    bufs, more, (send, recv) = rest[:7], rest[7:22], rest[22:]
    links = Links(send, recv)
    to = links.to
    load_gz, load_tokens, load_w = Loads(), Loads(), Loads()
    load_gz.start(gz_all_hbm, gz_all_ref, sem.at[2])
    load_tokens.start(tokens_hbm, tokens_ref, sem.at[1])
    load_w.start(w_hbm, w_ref, sem.at[0])
    links.barrier(
        to(y=1), to(y=2), to(y=3), to(z=2), to(x=1), to(x=2), to(x=3), to(sibling=True), links.beside()
    )
    for i, ref in enumerate((attn_vec_ref, feed_vec_ref)):
        for j in range(2):
            vec_ref[2 * i + j : 2 * i + j + 1] = jnp.sum(ref[j], axis=0, keepdims=True)
    vec_ref[4:8] = jnp.zeros((4, WIDE), F32)
    block = 512
    ready = [Mark(), Mark(), Mark()]

    def attend_back(head):
        lanes = slice(head * 128, head * 128 + 128)

        def keep(part, first, value):
            for i in range(value.shape[0] // ROWS):
                seq = first // ROWS + i
                d = lax.rem(seq // 2 + 4 - links.y, 4)
                slot = 2 * d - d * (d - 1) // 2 - d * (d - 1) * (d - 2) // 3
                slot = slot + 4 * lax.rem(links.z_hi + seq, 2)
                at = head * 384 + part * 128
                grads[slot, :, at : at + 128] = value[i * ROWS : (i + 1) * ROWS].astype(BF16)

        for first in range(0, LEN, block):
            at = slice(first, first + block)
            query, grad = q_ref[at, lanes], g_ref[at, lanes]
            scores = dot_t(k_ref[:, lanes], query)
            key = lax.broadcasted_iota(jnp.int32, scores.shape, 0)
            limit = lax.broadcasted_iota(jnp.int32, (1, block), 1) + first
            limit = jnp.maximum(limit, prefix_ref[0] - 1)
            weights = jnp.where(key <= limit, jnp.exp(scores - lse_ref[head, :, at]), 0.0)
            grad_weights = dot_t(v_ref[:, lanes], grad)
            inner = jnp.sum(weights * grad_weights, axis=0, keepdims=True)
            grad_scores = (weights * (grad_weights - inner)).astype(BF16)
            turned = dot_rows(grad_scores, k_ref[:, lanes]) * HEAD_DIM**-0.5
            keep(0, first, turned * cos_ref[at] - pltpu.roll(turned, 64, 1) * sin_ref[at])
            grad_key = dot(grad_scores, query)
            grad_value = dot(weights.astype(BF16), grad)
            if first == 0:
                key_sum[...] = grad_key
                value_sum[...] = grad_value
            else:
                key_sum[...] += grad_key
                value_sum[...] += grad_value
            yield ()
        turned = key_sum[...]
        keep(1, 0, turned * cos_ref[...] - pltpu.roll(turned, 64, 1) * sin_ref[...])
        keep(2, 0, value_sum[...])

    def compute(pair):
        load_w.wait()
        rows = pair_of(grads, pair)
        result = 0.0
        for part in range(3):
            for head in range(2):
                at = head * 384 + part * 128
                result = result + dot_t(rows[:, at : at + 128], w_ref[part, :, head * 128 : head * 128 + 128])
        result = result.astype(BF16)
        for i, slot in enumerate(pair):
            bufs[0][slot] = result[i * ROWS : (i + 1) * ROWS]

    def finish(at):
        value = deep_alpha * gz1_ref[at] + total[at]
        for lane in range(WIDE // 128):
            out_ref[at, lane] = value[:, lane * 128 : lane * 128 + 128]

    def chain():
        yield (ready[2],)
        for head in range(2):
            yield from attend_back(head)
            ready[head].done = True
            if head == 0:
                yield ()
        yield from scatter(links, bufs, compute, total)
        by_chunks(finish)

    def qkv(head):
        flat = more[5 * head]
        yield (ready[head],)
        load_tokens.wait()
        right = grads[:, :, head * 384 : head * 384 + 384].reshape(LEN, 384)
        for d in range(8):
            left = tokens_ref[:, :, d * 256 : d * 256 + 256].reshape(LEN, 256)
            result = dot_rows(left, right).astype(BF16)
            for part in range(3):
                for i in range(2):
                    row = part * WIDE + d * 256 + i * 128
                    chunk, at = row // 384, row % 384
                    flat[chunk // 8, chunk // 4 % 2, chunk % 4, at : at + 128] = result[
                        i * 128 : i * 128 + 128, part * 128 : part * 128 + 128
                    ]
            if d == 3:
                yield ()

    def first_shared():
        for slot in range(8):
            heads[slot] = heads_ref[pl.ds(links.first_row(slot), ROWS)]
        load_gz.wait()
        left = heads[...].reshape(LEN, 256)
        for d in range(0, WIDE, 512):
            result = dot_rows(left, gz_all_ref[:, :, d : d + 512].reshape(LEN, 512)).astype(BF16)
            for i in range(4):
                lane = d // 128 + i
                for j in range(2):
                    chunk = lane // 2 * 2 + j
                    more[10][chunk // 8, chunk // 4 % 2, chunk % 4, :, lane % 2 * 128 : lane % 2 * 128 + 128] = result[
                        j * 128 : j * 128 + 128, i * 128 : i * 128 + 128
                    ]
        ready[2].done = True
        yield from share(links, more[10:15], whole_ref, SHARE_X_FIRST[2])

    def shared(head):
        yield from qkv(head)
        yield from share(links, more[5 * head : 5 * head + 5], (one_ref, two_ref)[head], SHARE_X_FIRST[head])

    together(
        INPUT,
        *collect(links, shard_ref, feed_ref, local),
        first_shared(),
        chain(),
        shared(0),
        shared(1),
        agree(links, vec_ref, (held, got)),
    )
    own_ref[...] = vec_ref[:, pl.ds(pl.multiple_of(lax.axis_index("seq") * 256, 256), 256)]


def outputs_kernel(
    feed_ref, one_ref, two_ref, out_ref, vec_ref, output_ref, input_ref,
    gate_up_ref, down_ref, grad_qkv_ref, grad_out_ref, v0_ref, v1_ref, v2_ref, v3_ref, output_out, input_out,
):
    for z in range(2):
        lanes = slice(z * 128, z * 128 + 128)
        gate_up_ref[:, 0, lanes] = feed_ref[0, 0, 0, z].astype(F32)
        gate_up_ref[:, 1, lanes] = feed_ref[1, 0, 0, z].astype(F32)
        down_ref[:, lanes] = feed_ref[2, 0, 0, z].astype(F32)
    grad_qkv_ref[:, 0:128] = one_ref[...].astype(F32)
    grad_qkv_ref[:, 128:256] = two_ref[...].astype(F32)
    grad_out_ref[...] = out_ref[...].astype(F32)
    for i, ref in enumerate((v0_ref, v1_ref, v2_ref, v3_ref)):
        ref[...] = vec_ref[i : i + 1]
    output_out[...] = output_ref[...]
    input_out[...] = input_ref[...]


def outputs(feed, one, two, out, vec, output, input_grad, total):
    half = FF // 2
    vec_part = pl.BlockSpec((1, 256), lambda i: (0, 0))
    output_part = pl.BlockSpec((ROWS // 8, WIDE), lambda i: (i // 2, 0))
    input_part = pl.BlockSpec((ROWS // 16, WIDE // 128, 128), lambda i: (i, 0, 0))
    return pl.pallas_call(
        outputs_kernel,
        name="outputs",
        grid=(16,),
        in_specs=[
            pl.BlockSpec((3, 1, 1, 2, half, 128), lambda i: (0, i // 4, i // 2 % 2, 0, i % 2, 0)),
            pl.BlockSpec((384, 128), lambda i: (i, 0)),
            pl.BlockSpec((384, 128), lambda i: (i, 0)),
            pl.BlockSpec((128, 256), lambda i: (i, 0)),
            pl.BlockSpec((8, 256), lambda i: (0, 0)),
            output_part,
            input_part,
        ],
        out_specs=(
            pl.BlockSpec((half, 2, 256), lambda i: (i, 0, 0)),
            pl.BlockSpec((half, 256), lambda i: (i, 0)),
            pl.BlockSpec((384, 256), lambda i: (i, 0)),
            pl.BlockSpec((128, 256), lambda i: (i % 2, i // 2)),
            vec_part, vec_part, vec_part, vec_part,
            output_part,
            input_part,
        ),
        out_shape=(
            jax.ShapeDtypeStruct((total, 2, 256), F32),
            jax.ShapeDtypeStruct((total, 256), F32),
            jax.ShapeDtypeStruct((6144, 256), F32),
            jax.ShapeDtypeStruct((256, WIDE), F32),
            *(jax.ShapeDtypeStruct((1, 256), F32) for _ in range(4)),
            jax.ShapeDtypeStruct(output.shape, BF16),
            jax.ShapeDtypeStruct(input_grad.shape, F32),
        ),
        compiler_params=pltpu.CompilerParams(vmem_limit_bytes=VMEM_BYTES),
    )(feed, one, two, out, vec, output, input_grad)


def on_device(
    tokens, cotangent, w_qkv, w_out, w_gate_up, w_down,
    attn_gain, attn_bias, ffn_gain, ffn_bias, prefix_len, clusters,
):
    x = tokens.reshape(ROWS, WIDE)
    cot = cotangent.reshape(ROWS, WIDE)
    dp = lax.axis_index("dp")
    cosine, sine = (jnp.asarray(t) for t in rotary_tables(LEN, HEAD_DIM))
    row = lambda v: v.reshape(1, WIDE)
    ff_total = w_down.shape[1]
    place = jnp.stack([dp % 2, dp // 2 % 4, dp // 8, jnp.int32(ff_total)]).astype(jnp.int32)
    piece = piece_of(w_gate_up.transpose(2, 1, 0), w_down.T, place)
    w_in = w_qkv.transpose(1, 0, 2)
    low, full = BF16, F32
    blocks = (8, ROWS, WIDE)
    one = pltpu.SemaphoreType.DMA
    some = lambda *n: pltpu.SemaphoreType.DMA(n)
    rows_f32 = pltpu.VMEM((ROWS, WIDE), F32)
    blocks_low = pltpu.VMEM(blocks, BF16)

    tokens_all, q, k, v, heads_out, lse, normed, unit_one, inverse_one, w_all = call(
        front_kernel, "front", 0,
        [
            (blocks, low, "h"), *[((LEN, 256), low, "v")] * 4, ((2, 1, LEN), full, "v"),
            ((ROWS, WIDE), full, "v"), ((ROWS, WIDE), full, "v"), ((ROWS, 128), full, "v"),
            ((3, 2, 4, 2, FF, 128), low, "h"),
        ],
        (prefix_len, x, w_in, cosine, sine, w_out, row(attn_gain), row(attn_bias), piece), "svvvvvvvv",
        (blocks_low, rows_f32, one, one, *SCATTER_SCRATCH), 94, 2 * LEN * WIDE * 1024,
    )
    output, normed_all, gz_all, act, grad_z2, ffn_vec = call(
        feed_kernel, "feed", 2,
        [
            ((ROWS, WIDE), low, "v"), (blocks, low, "h"), (blocks, low, "h"),
            ((8, ROWS, 3 * COLS), low, "h"), ((ROWS, WIDE), full, "v"), ((2, 8, WIDE), full, "v"),
        ],
        (clusters, normed, cot, w_all, row(ffn_gain), row(ffn_bias)), "svvhvv",
        (
            pltpu.VMEM((3, COLS, WIDE), BF16), blocks_low, blocks_low,
            pltpu.VMEM((8, ROWS, 3 * COLS), BF16), pltpu.VMEM((8, ROWS, COLS), F32),
            pltpu.VMEM((8, ROWS, COLS), F32), rows_f32, some(3, 16), some(10), *NEAR_SCRATCH,
        ),
        60, 2 * LEN * WIDE * COLS * 4,
    )
    grad_z1, gz1_all, grad_heads, attn_vec, shard = call(
        feed_back_kernel, "feed_back", 3,
        [
            ((ROWS, WIDE), full, "v"), (blocks, low, "h"), ((LEN, 256), low, "v"),
            ((2, 8, WIDE), full, "v"), ((3, 4, PART, 128), low, "v"),
        ],
        (act, grad_z2, w_all, normed_all, gz_all, unit_one, inverse_one, row(attn_gain), w_out),
        "hvhhhvvvv",
        (
            pltpu.VMEM((8, ROWS, 3 * COLS), BF16), blocks_low, blocks_low,
            pltpu.VMEM((2, COLS, WIDE), BF16), rows_f32, some(2, 16), some(4),
            *NEAR_SCRATCH, *REDUCE_SCRATCH,
        ),
        80, 2 * LEN * WIDE * COLS * 5,
    )
    steps = pltpu.VMEM((7, 8, WIDE), F32)
    head_sum = pltpu.VMEM((LEN, 128), F32)
    input_grad, one, two, out_whole, vec, ffn_whole = call(
        input_kernel, "input", 4,
        [
            ((ROWS, WIDE // 128, 128), full, "v"), ((2, 2, 4, 384, 128), low, "v"),
            ((2, 2, 4, 384, 128), low, "v"), ((2, 2, 4, 128, 256), low, "v"), ((8, 256), full, "v"),
            ((3, 4, 2, 2, FF, 128), low, "h"),
        ],
        (
            prefix_len, q, k, v, grad_heads, lse, cosine, sine,
            w_in, grad_z1, tokens_all, heads_out, gz1_all, shard, attn_vec, ffn_vec,
        ),
        "svvvvvvvhvhvhvvv",
        (
            rows_f32, pltpu.VMEM((8, WIDE), F32), pltpu.VMEM((3, WIDE, 256), BF16), blocks_low, blocks_low,
            pltpu.VMEM((8, ROWS, 768), BF16), pltpu.VMEM((8, ROWS, 256), BF16),
            head_sum, head_sum, steps, steps, pltpu.SemaphoreType.DMA, some(3),
            *SCATTER_SCRATCH, *share_scratch(384, 128), *share_scratch(384, 128), *share_scratch(128, 256),
        ),
        140, 2 * LEN * WIDE * 768,
    )
    grad_gate_up, grad_down, grad_qkv, grad_out, *vecs, output, input_grad = outputs(
        ffn_whole, one.reshape(6144, 128), two.reshape(6144, 128), out_whole.reshape(2048, 256),
        vec, output, input_grad, ff_total,
    )
    return (
        output.reshape(tokens.shape),
        input_grad.reshape(tokens.shape),
        grad_qkv.reshape(3, WIDE, 256).transpose(1, 0, 2),
        grad_out,
        grad_gate_up.transpose(2, 1, 0),
        grad_down.T,
        *(v.reshape(256) for v in vecs),
    )


def solution(mesh):
    return jax.shard_map(
        on_device,
        mesh=mesh,
        in_specs=(
            P("seq", "dp", None), P("seq", "dp", None), P(None, None, "seq"), P("seq", None),
            P("seq", None, None), P("seq", None), P(), P(), P(), P(), P("dp"), P(),
        ),
        out_specs=(
            P("seq", "dp", None), P("seq", "dp", None), P(None, None, "seq"), P("seq", None),
            P("seq", None, None), P("seq", None), P("seq"), P("seq"), P("seq"), P("seq"),
        ),
        check_vma=False,
    )
```

```python
import functools

import jax
import jax.numpy as jnp
import numpy as np
from jax import lax
from jax.experimental import pallas as pl
from jax.experimental.pallas import tpu as pltpu
from jax.sharding import PartitionSpec as P

MESH = pl.DeviceIdType.MESH
F32, BF16 = jnp.float32, jnp.bfloat16
HEAD_DIM = 128
ROWS = 128
WIDE = 2048
COLS = 768
LEN = 1024
VMEM_BYTES = 60 * 1024 * 1024
deep_alpha = 48.0**0.25
norm_eps = 1e-05
rotary_base = 10000.0


def rotary_tables(length, head_width):
    half_width = head_width // 2
    position = np.arange(length, dtype=np.float64)
    inverse = rotary_base ** (-np.arange(half_width, dtype=np.float64) * 2.0 / head_width)
    angles = position[:, None] * inverse[None, :]
    cosine_table = np.cos(angles)
    sine_table = np.sin(angles)
    return (
        np.concatenate([cosine_table, cosine_table], axis=1).astype(np.float32),
        np.concatenate([-sine_table, sine_table], axis=1).astype(np.float32),
    )


FF = 704
PART = 176


class Links:
    def __init__(self, send, recv):
        self.send, self.recv, self.count = send, recv, 0
        dp, seq = lax.axis_index("dp"), lax.axis_index("seq")
        y, z_hi = seq // 2, lax.rem(seq, 2)
        z_lo, x, core = dp // 8, lax.rem(dp // 2, 4), lax.rem(dp, 2)
        self.y, self.z_hi, self.z_lo, self.x, self.core = y, z_hi, z_lo, x, core
        self.z = z_hi * 2 + z_lo

    def to(self, x=0, y=0, z=0, sibling=False):
        z_hi, z_lo = self.z_at(z)
        x, y = lax.rem(self.x + x, 4), lax.rem(self.y + y, 4)
        core = 1 - self.core if sibling else self.core
        return (z_lo * 8 + x * 2 + core, y * 2 + z_hi)

    def beside(self):
        return (lax.rem(lax.axis_index("dp") + 8, 16), lax.axis_index("seq"))

    def z_at(self, offset):
        z = lax.rem(self.z + offset, 4)
        return z // 2, lax.rem(z, 2)

    def part(self, offset):
        return pl.ds(pl.multiple_of(lax.rem(self.x + offset, 4) * PART, 16), PART)

    def barrier(self, *where):
        gate = pltpu.get_barrier_semaphore()
        for device in where:
            pl.semaphore_signal(gate, inc=1, device_id=device, device_id_type=MESH)
        pl.semaphore_wait(gate, len(where))

    def start(self, src, dst, where):
        assert self.count < self.send.shape[0]
        copy = pltpu.make_async_remote_copy(
            src_ref=src,
            dst_ref=dst,
            send_sem=self.send.at[self.count],
            recv_sem=self.recv.at[self.count],
            device_id=where,
            device_id_type=MESH,
        )
        self.count += 1
        copy.start()
        return copy

    def first_row(self, slot):
        step = (0, 3, 1, 2)[slot % 4]
        half = self.z_hi if slot < 4 else 1 - self.z_hi
        return pl.multiple_of((lax.rem(self.y + step, 4) * 2 + half) * ROWS, ROWS)


class Once:
    def __init__(self, *copies):
        self.copies = list(copies)

    def wait_recv(self):
        while self.copies:
            self.copies.pop().wait_recv()


class Mark:
    done = False


class Local:
    def __init__(self, src, dst, sem):
        self.copy = pltpu.make_async_copy(src, dst, sem)
        self.copy.start()

    def wait_recv(self):
        self.copy.wait()


def together(order, *tasks):
    tasks = list(tasks)
    for task in tasks:
        next(task)
    left = len(tasks)
    for which in order:
        try:
            next(tasks[which])
        except StopIteration:
            left -= 1
    assert left == 0


def alone(task):
    for _ in task:
        pass


def received(*copies):
    for copy in copies:
        copy.wait_recv()


def sent(copies):
    for copy in copies:
        copy.wait_send()


def gather(links, buf, work, first=0, rows=ROWS):
    up, down, across = links.to(y=1), links.to(y=3), links.to(z=2)
    h0, h1 = pl.ds(first, rows // 2), pl.ds(first + rows // 2, rows // 2)
    copies = []

    def send(slot, at, dst, where):
        copies.append(links.start(buf.at[slot, at], buf.at[dst, at], where))
        return copies[-1]

    u0, d1 = send(0, h0, 1, up), send(0, h1, 2, down)
    z0, z1 = send(0, h0, 4, across), send(0, h1, 4, across)
    u1, d0 = send(0, h1, 1, up), send(0, h0, 2, down)
    yield u0, d1
    received(u0)
    fu = send(1, h0, 3, up)
    received(d1)
    fd = send(2, h1, 3, down)
    yield z0, z1
    received(z0)
    pu0 = send(4, h0, 5, up)
    received(z1)
    pd1 = send(4, h1, 6, down)
    pu1, pd0 = send(4, h1, 5, up), send(4, h0, 6, down)
    yield u1, d0
    received(u1, d0)
    work((0, 1))
    yield fu, fd
    received(fu, fd)
    work((2, 3))
    yield pu0, pd1
    received(pu0)
    gu = send(5, h0, 7, up)
    received(pd1)
    gd = send(6, h1, 7, down)
    yield pu1, pd0
    received(pu1, pd0)
    work((4, 5))
    yield gu, gd
    received(gu, gd)
    work((6, 7))
    sent(copies)


def when_whole(work, times):
    seen = {}

    def count(pair):
        seen[pair] = seen.get(pair, 0) + 1
        if seen[pair] == times:
            work(pair)

    return count


def gather_near(links, buf, work, first=0, rows=ROWS):
    up, down, side = links.to(y=1), links.to(y=3), links.to(sibling=True)
    every = pl.ds(first, rows)
    h0, h1 = pl.ds(first, rows // 2), pl.ds(first + rows // 2, rows // 2)
    copies = []

    def send(slot, at, dst, where):
        copies.append(links.start(buf.at[slot, at], buf.at[dst, at], where))
        return copies[-1]

    u0, d1 = send(0, h0, 1, up), send(0, h1, 2, down)
    u1, d0 = send(0, h1, 1, up), send(0, h0, 2, down)
    s0 = send(0, every, 4, side)
    yield (s0,)
    received(s0)
    work((0, 4))
    yield u0, d1
    received(u0)
    fu = send(1, h0, 3, up)
    received(d1)
    fd = send(2, h1, 3, down)
    yield u1, d0
    received(u1)
    s1 = send(1, every, 5, side)
    received(d0)
    s2 = send(2, every, 6, side)
    work((1, 2))
    yield s1, s2
    received(s1, s2)
    work((5, 6))
    yield fu, fd
    received(fu)
    s30 = send(3, h0, 7, side)
    received(fd)
    s31 = send(3, h1, 7, side)
    yield s30, s31
    received(s30, s31)
    work((3, 7))
    sent(copies)


A, B = pl.ds(0, 80), pl.ds(80, 48)
A0, A1 = pl.ds(0, 48), pl.ds(48, 32)
B0, B1 = pl.ds(80, 16), pl.ds(96, 32)
SCATTER_SCRATCH = (
    pltpu.VMEM((8, ROWS, WIDE), BF16),
    pltpu.VMEM((4, 48, WIDE), BF16),
    pltpu.VMEM((48, WIDE), BF16),
    pltpu.VMEM((2, 48, WIDE), BF16),
    pltpu.VMEM((2, 80, WIDE), BF16),
    pltpu.VMEM((2, 2, 80, WIDE), BF16),
    pltpu.VMEM((80, WIDE), BF16),
)


def add_rows(target, slot, rows, *others):
    value = target[slot, rows].astype(F32)
    for other in others:
        value = value + other.astype(F32)
    target[slot, rows] = value.astype(BF16)


def scatter(links, bufs, compute, total):
    sums, from_z, b_far, b_near, a_far, a_near, a_z = bufs
    up, down, across = links.to(y=1), links.to(y=3), links.to(z=2)
    copies = []

    def send(src, dst, where):
        copies.append(links.start(src, dst, where))
        return copies[-1]

    def far_a(o):
        half = o // 4
        return (
            send(sums.at[o + 3, A0], a_far.at[half, pl.ds(0, 48)], up),
            send(sums.at[o + 3, A1], a_far.at[half, pl.ds(48, 32)], down),
        )

    def near_a(o, far):
        half = o // 4
        received(far[0])
        add_rows(sums, o + 2, A0, a_far[half, 0:48])
        one = send(sums.at[o + 2, A], a_near.at[half, 0], up)
        received(far[1])
        add_rows(sums, o + 1, A1, a_far[half, 48:80])
        return one, send(sums.at[o + 1, A], a_near.at[half, 1], down)

    def cross_b(j):
        return send(sums.at[4 + j, B], from_z.at[j], across)

    compute((7, 3))
    z3 = cross_b(3)
    far_other = far_a(4)
    far_own = far_a(0)
    yield ()
    compute((5, 1))
    z1 = cross_b(1)
    yield ()
    compute((6, 2))
    z2 = cross_b(2)
    yield far_other
    near_other = near_a(4, far_other)
    compute((4, 0))
    z0 = cross_b(0)
    yield (z3,)
    received(z3)
    add_rows(sums, 3, B, from_z[3])
    far_b = (
        send(sums.at[3, B0], b_far.at[pl.ds(0, 16)], up),
        send(sums.at[3, B1], b_far.at[pl.ds(16, 32)], down),
    )
    yield far_own
    near_own = near_a(0, far_own)
    yield z1, z2
    received(z2)
    add_rows(sums, 2, B, from_z[2])
    received(z1)
    add_rows(sums, 1, B, from_z[1])
    yield far_b
    received(far_b[0])
    add_rows(sums, 2, B0, b_far[0:16])
    near_b0 = send(sums.at[2, B], b_near.at[0], up)
    received(far_b[1])
    add_rows(sums, 1, B1, b_far[16:48])
    near_b1 = send(sums.at[1, B], b_near.at[1], down)
    yield near_other
    received(*near_other)
    add_rows(sums, 4, A, a_near[1, 0], a_near[1, 1])
    z_a = send(sums.at[4, A], a_z, across)
    yield z0, near_b0, near_b1
    received(z0, near_b0, near_b1)
    total[80:128] = (
        sums[0, B].astype(F32)
        + from_z[0].astype(F32)
        + b_near[0].astype(F32)
        + b_near[1].astype(F32)
    )
    yield (z_a, *near_own)
    received(*near_own)
    received(z_a)
    total[0:80] = (
        sums[0, A].astype(F32)
        + a_near[0, 0].astype(F32)
        + a_near[0, 1].astype(F32)
        + a_z[...].astype(F32)
    )
    sent(copies)


NEAR_SCRATCH = (
    pltpu.VMEM((8, ROWS, WIDE), BF16),
    pltpu.VMEM((4, ROWS, WIDE), BF16),
    pltpu.VMEM((ROWS, WIDE), BF16),
    pltpu.VMEM((2, ROWS, WIDE), BF16),
)


def scatter_near(links, bufs, compute, total):
    sums, from_side, far, near = bufs
    up, down, side = links.to(y=1), links.to(y=3), links.to(sibling=True)
    copies = []

    def send(src, dst, where):
        copies.append(links.start(src, dst, where))
        return copies[-1]

    compute((7, 3))
    s3 = Once(send(sums.at[7], from_side.at[3], side))
    compute((5, 6))
    s12 = Once(send(sums.at[5], from_side.at[1], side), send(sums.at[6], from_side.at[2], side))
    compute((1, 2))
    later = []

    def last():
        compute((4, 0))
        later.append(Once(send(sums.at[4], from_side.at[0], side)))

    def task(first, rows):
        every = pl.ds(first, rows)
        h0, h1 = pl.ds(first, rows // 2), pl.ds(first + rows // 2, rows // 2)
        yield (s3,)
        received(s3)
        add_rows(sums, 3, every, from_side[3, every])
        fu = send(sums.at[3, h0], far.at[h0], up)
        fd = send(sums.at[3, h1], far.at[h1], down)
        received(s12)
        add_rows(sums, 2, every, from_side[2, every])
        nu1 = send(sums.at[2, h1], near.at[0, h1], up)
        add_rows(sums, 1, every, from_side[1, every])
        nd0 = send(sums.at[1, h0], near.at[1, h0], down)
        if not later:
            last()
        yield fu, fd
        received(fu)
        add_rows(sums, 2, h0, far[h0])
        nu0 = send(sums.at[2, h0], near.at[0, h0], up)
        received(fd)
        add_rows(sums, 1, h1, far[h1])
        nd1 = send(sums.at[1, h1], near.at[1, h1], down)
        yield nu1, nd0, nu0, nd1
        received(later[0], nu1, nd0, nu0, nd1)
        total[every] = (
            sums[0, every].astype(F32)
            + from_side[0, every].astype(F32)
            + near[0, every].astype(F32)
            + near[1, every].astype(F32)
        )

    return task, copies


Y0, Y1 = pl.ds(0, 2), pl.ds(2, 2)
GU = pl.ds(0, 2)


def across_y(links, piece, own, local):
    copies = []
    for step in (2, 1, 3):
        there = lax.rem(links.y + step, 4)
        copies.append(links.start(piece(there), own(), links.to(y=step)))
    keep = Local(piece(links.y), own(), local)
    return Once(keep, *copies), copies


def ring_gather(links, arrived, at, first, second):
    up, down = first
    right, left = second
    copies = []

    def send(ref, where):
        copies.append(links.start(ref, ref, where))
        return copies[-1]

    def both(a):
        return send(at(a, 0), right), send(at(a, 0), left)

    def onward(a):
        return [send(at(a, 3, Y0), right), send(at(a, 1, Y1), left)]

    yield (arrived,)
    received(arrived)
    u, d = send(at(0, 0), up), send(at(0, 0), down)
    near = [both(0)]
    yield u, d
    received(u)
    fu = send(at(3, 0, Y0), up)
    received(d)
    fd = send(at(1, 0, Y1), down)
    near.append(both(3))
    near.append(both(1))
    yield near[0]
    received(*near[0])
    far = onward(0)
    yield fu, fd
    received(fu, fd)
    near.append(both(2))
    for i, a in enumerate((3, 1, 2)):
        yield near[1 + i]
        received(*near[1 + i])
        far += onward(a)
    yield far
    received(*far)
    sent(copies)


Z_FIRST = (0, 2)


def spread(links, piece, w, local):
    along_x = (links.to(x=1), links.to(x=3))
    along_z = (links.to(z=1), links.to(z=3))
    every = pl.ds(0, 4)

    def place(k, z, x, y):
        z_hi, z_lo = links.z_at(z)
        return w.at[k, z_hi, y, z_lo, links.part(x)]

    def own():
        return w.at[:, links.z_hi, links.y, links.z_lo, links.part(0)]

    arrived, copies = across_y(links, lambda y: piece.at[y], own, local)

    def one(k, z_first):
        if z_first:
            yield from ring_gather(links, arrived, lambda a, b, y=every: place(k, a, b, y), along_z, along_x)
        else:
            yield from ring_gather(links, arrived, lambda a, b, y=every: place(k, b, a, y), along_x, along_z)
        if k == 0:
            sent(copies)

    return tuple(one(k, k in Z_FIRST) for k in range(3))


def ring_scratch(*block):
    return [pltpu.VMEM(block, BF16), pltpu.VMEM((2, *block), BF16)]


REDUCE_SCRATCH = (
    pltpu.VMEM((3, 4, 2, 2, FF, 128), BF16),
    *ring_scratch(4, 2, 2, PART, 128), *ring_scratch(4, PART, 128),
    *ring_scratch(4, 2, 2, PART, 128), *ring_scratch(4, PART, 128),
    *ring_scratch(4, FF, 128), *ring_scratch(4, PART, 128),
)


def accumulate(count, target, *others):
    def step(i, carry):
        ref = target(i)
        value = ref[...].astype(F32)
        for other in others:
            value = value + other(i)[...].astype(F32)
        ref[...] = value.astype(BF16)
        return carry

    lax.fori_loop(0, count, step, 0)


def ring_reduce(links, at, blocks, ring, far, near, devices):
    up, down = devices
    copies = []
    every = pl.ds(0, 4)

    def send(src, dst, where):
        copies.append(links.start(src, dst, where))
        return copies[-1]

    half = ring // 2
    fu, fd = send(at(2, Y0), far.at[Y0], up), send(at(2, Y1), far.at[Y1], down)
    nu, nd = send(at(1, Y1), near.at[0, Y1], up), send(at(3, Y0), near.at[1, Y0], down)
    yield fu, fd
    received(fu)
    accumulate(half, lambda i: blocks(at(1, every), i), lambda i: blocks(far, i))
    mu = send(at(1, Y0), near.at[0, Y0], up)
    received(fd)
    accumulate(half, lambda i: blocks(at(3, every), i + half), lambda i: blocks(far, i + half))
    md = send(at(3, Y1), near.at[1, Y1], down)
    yield nu, nd, mu, md
    received(nu, nd, mu, md)
    accumulate(
        ring, lambda i: blocks(at(0, every), i), lambda i: blocks(near.at[0], i), lambda i: blocks(near.at[1], i)
    )
    sent(copies)


def reduce(links, bufs, make, shard):
    g = bufs[0]
    along_x = (links.to(x=1), links.to(x=3))
    along_z = (links.to(z=1), links.to(z=3))
    made = [Mark(), Mark()]

    def one(k, x_first):
        far, near, far2, near2 = bufs[1 + 4 * k : 5 + 4 * k]
        z_hi, z_lo = links.z_at(0)

        def along_z_at(a, y):
            hi, lo = links.z_at(a)
            return g.at[k, y, hi, lo]

        def along_x_at(a, y):
            return g.at[k, y, :, :, links.part(a)]

        def rest_z(a, y):
            hi, lo = links.z_at(a)
            return g.at[k, y, hi, lo, links.part(0)]

        def rest_x(a, y):
            return g.at[k, y, z_hi, z_lo, links.part(a)]

        def four(ref, i):
            return ref.at[i // 4, lax.rem(i // 2, 2), lax.rem(i, 2)]

        def plain(ref, i):
            return ref.at[i]

        if k:
            yield (made[k - 1],)
        yield from make(k)
        if k < 2:
            made[k].done = True
        if x_first:
            yield from ring_reduce(links, along_x_at, four, 16, far, near, along_x)
            yield from ring_reduce(links, rest_z, plain, 4, far2, near2, along_z)
        else:
            yield from ring_reduce(links, along_z_at, plain, 4, far, near, along_z)
            yield from ring_reduce(links, rest_x, plain, 4, far2, near2, along_x)
        shard[k] = g[k, :, z_hi, z_lo, links.part(0)]

    return one(0, True), one(1, True), one(2, False)


def regather(links, at, half, x_first):
    xp, xm, side = links.to(x=1), links.to(x=3), links.to(sibling=True)
    beside = links.beside()
    copies, sides = [], []

    def send(ref, where):
        copies.append(links.start(ref, ref, where))
        return copies[-1]

    def share(ref):
        sides.append(send(ref, side))

    near = [(send(at(0, 0), xp), send(at(0, 0), xm))]
    z = [(0, send(at(0, 0), beside))]
    share(at(0, 0))
    far = []
    if not x_first:
        yield (z[0][1],)
        received(z[0][1])
        near.append((send(at(1, 0), xp), send(at(1, 0), xm)))
        share(at(1, 0))
    for i in range(len(near)):
        yield near[i]
        received(near[i][0])
        far_up = send(half(at(i, 3), 0), xp)
        received(near[i][1])
        far.append((far_up, send(half(at(i, 1), 1), xm)))
        for x in (3, 1):
            if x_first:
                z.append((x, send(at(0, x), beside)))
            share(at(i, x))
    for i in range(len(near)):
        yield far[i]
        received(*far[i])
        if x_first:
            z.append((2, send(at(0, 2), beside)))
        share(at(i, 2))
    if x_first:
        for x, copy in z:
            yield (copy,)
            received(copy)
            share(at(1, x))
    yield sides
    received(*sides)
    sent(copies)


def collect(links, shard, out, local):
    def own():
        return out.at[:, links.y, links.core, links.z_lo, links.part(0)]

    arrived, copies = across_y(links, lambda y: shard.at[:, y], own, local)

    def task(matrices, x_first):
        yield (arrived,)
        received(arrived)

        def at(z, x):
            return out.at[matrices, :, links.core, lax.rem(links.z_lo + z, 2), links.part(x)]

        def half(ref, i):
            return ref.at[:, pl.ds(2 * i, 2)]

        yield from regather(links, at, half, x_first)
        if x_first:
            sent(copies)

    return task(GU, False), task(pl.ds(2, 1), True)


def share_scratch(rows, lanes):
    return [
        pltpu.VMEM((2, 2, 4, rows, lanes), BF16),
        pltpu.VMEM((2, 4, rows, lanes), BF16),
        pltpu.VMEM((2, rows, lanes), BF16),
        pltpu.VMEM((2, 2, rows, lanes), BF16),
        pltpu.VMEM((rows, lanes), BF16),
    ]


SHARE_X_FIRST = (False, False, False)


def share(links, bufs, out, x_first):
    q, from_side, far, near, from_z = bufs
    xp, xm, side = links.to(x=1), links.to(x=3), links.to(sibling=True)
    beside = links.beside()
    core, z_lo = links.core, links.z_lo
    count = q.shape[3]
    copies = []

    def send(src, dst, where):
        copies.append(links.start(src, dst, where))
        return copies[-1]

    def there(x):
        return lax.rem(links.x + x, 4)

    def rows(ref):
        return lambda i: ref.at[pl.ds(pl.multiple_of(i * 64, 64), 64)]

    def add(target, *others):
        accumulate(count // 64, rows(target), *(rows(other) for other in others))

    s = send(q.at[1 - core], from_side, side)
    yield (s,)
    received(s)
    for x in (2, 1, 3, 0):
        for z in range(2):
            add(q.at[core, z, there(x)], from_side.at[z, there(x)])
        if x == 2:
            fu, fd = send(q.at[core, 0, there(2)], far.at[0], xp), send(q.at[core, 1, there(2)], far.at[1], xm)
    nu = send(q.at[core, 1, there(1)], near.at[0, 1], xp)
    nd = send(q.at[core, 0, there(3)], near.at[1, 0], xm)
    yield fu, fd
    received(fu)
    add(q.at[core, 0, there(1)], far.at[0])
    mu = send(q.at[core, 0, there(1)], near.at[0, 0], xp)
    received(fd)
    add(q.at[core, 1, there(3)], far.at[1])
    md = send(q.at[core, 1, there(3)], near.at[1, 1], xm)
    yield nu, nd, mu, md
    received(nu, nd, mu, md)
    for z in range(2):
        add(q.at[core, z, there(0)], near.at[0, z], near.at[1, z])
    b = send(q.at[core, 1 - z_lo, there(0)], from_z, beside)
    yield (b,)
    received(b)

    def finish(i, carry):
        at = pl.ds(pl.multiple_of(i * 64, 64), 64)
        value = q[core, z_lo, links.x, at].astype(F32) + from_z[at].astype(F32)
        out[core, z_lo, links.x, at] = value.astype(BF16)
        return carry

    lax.fori_loop(0, count // 64, finish, 0)

    def at(z, x):
        return out.at[core, lax.rem(z_lo + z, 2), there(x)]

    def half(ref, i):
        return ref.at[pl.ds(count // 2 * i, count // 2)]

    yield from regather(links, at, half, x_first)
    sent(copies)


def agree(links, vec, bufs):
    y, x = links.y, links.x
    copies = []
    steps = (
        links.to(sibling=True),
        links.to(y=1 + 2 * lax.rem(y, 2)),
        links.to(y=2),
        links.to(z=2),
        links.to(x=1 + 2 * lax.rem(x, 2)),
        links.to(x=2),
        links.beside(),
    )
    held, got = bufs
    held[0] = vec[...]
    for i, where in enumerate(steps):
        copies.append(links.start(held.at[i], got.at[i], where))
        yield (copies[-1],)
        received(copies[-1])
        if i < len(steps) - 1:
            held[i + 1] = held[i] + got[i]
        else:
            vec[...] = held[i] + got[i]
    sent(copies)


def dot(a, b):
    return jnp.dot(a, b, preferred_element_type=F32)


def dot_t(a, b):
    return lax.dot_general(a, b, (((1,), (1,)), ((), ())), preferred_element_type=F32)


def dot_rows(a, b):
    return lax.dot_general(a, b, (((0,), (0,)), ((), ())), preferred_element_type=F32)


def pair_of(ref, pair):
    return jnp.concatenate([ref[pair[0]], ref[pair[1]]], axis=0)


def by_chunks(body, first=0, rows=ROWS):
    def step(i, carry):
        body(pl.ds(pl.multiple_of(first + i * 16, 16), 16))
        return carry

    lax.fori_loop(0, rows // 16, step, 0)


def norm_parts(row_total):
    center = row_total - jnp.mean(row_total, axis=-1, keepdims=True)
    spread = jnp.mean(center * center, axis=-1, keepdims=True)
    inverse = lax.rsqrt(spread + norm_eps)
    return center * inverse, inverse


def norm_backward(grad_result, unit, inverse, gain):
    grad_unit = grad_result * gain
    return inverse * (
        grad_unit
        - jnp.mean(grad_unit, axis=-1, keepdims=True)
        - unit * jnp.mean(grad_unit * unit, axis=-1, keepdims=True)
    )


def rows8(values):
    return values[0:8] + values[8:16]


VMEM = pl.BlockSpec(memory_space=pltpu.VMEM)
HBM = pl.BlockSpec(memory_space=pl.ANY)
SMEM = pl.BlockSpec(memory_space=pltpu.SMEM)
KINDS = {"v": VMEM, "s": SMEM, "h": HBM}


def call(body, name, ident, outs, operands, spaces, scratch, copies, flops=0):
    sems = [pltpu.SemaphoreType.DMA((copies,)), pltpu.SemaphoreType.DMA((copies,))]
    return pl.pallas_call(
        body,
        name=name,
        out_shape=tuple(jax.ShapeDtypeStruct(s, d) for s, d, _ in outs),
        in_specs=[KINDS[k] for k in spaces],
        out_specs=tuple(KINDS[k] for _, _, k in outs),
        scratch_shapes=[*scratch, *sems],
        compiler_params=pltpu.CompilerParams(
            collective_id=ident, has_side_effects=True, vmem_limit_bytes=VMEM_BYTES
        ),
        cost_estimate=pl.CostEstimate(flops=flops, bytes_accessed=20_000_000, transcendentals=0),
    )(*operands)


FRONT = (1, 2, 0, 0, 3, 0, 1, 1, 2, 2, 0, 1, 1, 3, 0, 1, 3, 0, 2, 2, 1, 2, 0, 0, 0, 0, 0, 2, 1, 0, 3, 3, 3, 0, 0, 0, 2, 3, 3, 0, 0)
FEED = (0, 0, 1, 1, 0, 0, 1, 0, 1, 0, 0, 1, 1, 0, 1, 1, 0, 1)
FEED_BACK = (0, 2, 2, 0, 3, 3, 3, 0, 4, 4, 4, 0, 2, 1, 0, 0, 0, 1, 4, 3, 0, 0, 1, 0, 4, 1, 2, 1, 1, 1, 2, 3, 4, 2, 1, 3, 4, 1, 1, 3)
INPUT = (3, 2, 1, 0, 6, 3, 2, 3, 4, 4, 6, 1, 3, 4, 0, 0, 3, 6, 4, 2, 3, 5, 5, 1, 1, 1, 2, 1, 0, 3, 5, 0, 1, 3, 4, 2, 6, 1, 3, 2, 3, 3, 0, 5, 0, 4, 2, 3, 6, 2, 5, 4, 4, 2, 3, 5, 4, 4, 2, 3, 6, 5, 5, 4, 4, 3, 5, 5, 5, 3, 5, 6)


def piece_kernel(place_ref, *refs):
    out_ref = refs[8]
    for y in range(4):
        chunk = (y * 2 + place_ref[0]) * 4 + place_ref[1]
        row = lax.broadcasted_iota(jnp.int32, (PART, 128), 0) + chunk * PART
        inside = row < place_ref[3]
        both = refs[y][...].astype(F32)
        out_ref[y, 0] = jnp.where(inside, both[:, 0], 0.0).astype(BF16)
        out_ref[y, 1] = jnp.where(inside, both[:, 1], 0.0).astype(BF16)
        out_ref[y, 2] = jnp.where(inside, refs[4 + y][...].astype(F32), 0.0).astype(BF16)


def piece_of(gate_up, down, place):
    def chunk(y, place):
        return (y * 2 + place[0]) * 4 + place[1]

    return pl.pallas_call(
        piece_kernel,
        name="piece",
        grid_spec=pltpu.PrefetchScalarGridSpec(
            num_scalar_prefetch=1,
            grid=(1,),
            in_specs=[
                *(pl.BlockSpec((PART, 2, 128), lambda i, p, y=y: (chunk(y, p), 0, p[2])) for y in range(4)),
                *(pl.BlockSpec((PART, 128), lambda i, p, y=y: (chunk(y, p), p[2])) for y in range(4)),
            ],
            out_specs=pl.BlockSpec((4, 3, PART, 128), lambda i, p: (0, 0, 0, 0)),
        ),
        out_shape=jax.ShapeDtypeStruct((4, 3, PART, 128), BF16),
    )(place, *[gate_up] * 4, *[down] * 4)


def front_kernel(
    prefix_ref, x_ref, w_hbm, cos_hbm, sin_hbm, w_out_hbm, gain_ref, bias_ref, piece_ref,
    tokens_out, q_out, k_out, v_out, heads_out, lse_ref, normed_ref, unit_ref, inverse_ref, w_all_ref,
    all_ref, total, w_ref, cos_ref, sin_ref, w_out_ref, q_ref, k_ref, v_ref, heads_ref, local, sem, *rest,
):
    bufs, (send, recv) = rest[:7], rest[7:]
    links = Links(send, recv)
    loads, load_out, written = Loads(), Loads(), Loads()
    for i, (src, dst) in enumerate(((w_hbm, w_ref), (cos_hbm, cos_ref), (sin_hbm, sin_ref))):
        loads.start(src, dst, sem.at[i])
    load_out.start(w_out_hbm, w_out_ref, sem.at[3])
    all_ref[0] = x_ref[...]
    to = links.to
    links.barrier(to(y=1), to(y=3), to(z=2), to(y=2), to(x=1), to(x=3), to(z=1), to(z=3))

    def project(pair):
        loads.wait()
        rows = pair_of(all_ref, pair)
        for part, out in enumerate((q_ref, k_ref, v_ref)):
            result = dot(rows, w_ref[part])
            for i, slot in enumerate(pair):
                at = pl.ds(links.first_row(slot), ROWS)
                piece = result[i * ROWS : (i + 1) * ROWS]
                if part == 2:
                    out[at] = piece.astype(BF16)
                    continue
                cosine, sine = cos_ref[at], sin_ref[at]
                for head in range(2):
                    lanes = slice(head * 128, head * 128 + 128)
                    turned = piece[:, lanes] * cosine + pltpu.roll(piece[:, lanes], 64, 1) * sine
                    if part == 0:
                        turned = turned * HEAD_DIM**-0.5
                    out[at, lanes] = turned.astype(BF16)

    def attend(first, block):
        at = pl.ds(first, block)
        for head in range(2):
            lanes = slice(head * 128, head * 128 + 128)
            scores = dot_t(k_ref[:, lanes], q_ref[at, lanes])
            key = lax.broadcasted_iota(jnp.int32, scores.shape, 0)
            limit = lax.broadcasted_iota(jnp.int32, (1, block), 1) + first
            limit = jnp.maximum(limit, prefix_ref[0] - 1)
            scores = jnp.where(key <= limit, scores, -1e30)
            peak = jnp.max(scores, axis=0, keepdims=True)
            exponent = jnp.exp(scores - peak)
            row_total = jnp.sum(exponent, axis=0, keepdims=True)
            weights = (exponent * (1.0 / row_total)).astype(BF16)
            heads_ref[at, lanes] = dot_rows(weights, v_ref[:, lanes]).astype(BF16)
            lse_ref[head, :, at] = peak + jnp.log(row_total)

    def compute(pair):
        step = (0, 3, 1, 2)[pair[1]]
        attend(pl.multiple_of(lax.rem(links.y + step, 4) * 2 * ROWS, 2 * ROWS), 2 * ROWS)
        load_out.wait()
        rows = jnp.concatenate([heads_ref[pl.ds(links.first_row(s), ROWS)] for s in pair], axis=0)
        result = dot(rows, w_out_ref[...]).astype(BF16)
        for i, slot in enumerate(pair):
            bufs[0][slot] = result[i * ROWS : (i + 1) * ROWS]

    def finish(at):
        unit, inverse = norm_parts(deep_alpha * x_ref[at].astype(F32) + total[at])
        unit_ref[at] = unit
        inverse_ref[at] = jnp.broadcast_to(inverse, (16, 128))
        normed_ref[at] = unit * gain_ref[...] + bias_ref[...]

    def chain():
        yield from gather(links, all_ref, project)
        for i, (src, dst) in enumerate(((all_ref, tokens_out), (q_ref, q_out), (k_ref, k_out), (v_ref, v_out))):
            written.start(src, dst, sem.at[4 + i])
        yield from scatter(links, bufs, compute, total)
        written.start(heads_ref, heads_out, sem.at[8])
        by_chunks(finish)

    together(FRONT, chain(), *spread(links, piece_ref, w_all_ref, local))
    written.wait()


class Loads:
    def __init__(self):
        self.copies = []

    def start(self, src, dst, sem):
        copy = pltpu.make_async_copy(src, dst, sem)
        copy.start()
        self.copies.append(copy)

    def wait(self):
        while self.copies:
            self.copies.pop().wait()


def load_weights(w_hbm, w, sem, parts):
    loads = Loads()
    for k in range(parts):
        for i in range(16):
            src = w_hbm.at[k, lax.rem(i // 2, 2), i // 4, lax.rem(i, 2)]
            loads.start(src, w.at[k, pl.ds(0, FF), pl.ds(i * 128, 128)], sem.at[k, i])
    for k in range(parts):
        w[k, FF:COLS] = jnp.zeros((COLS - FF, WIDE), BF16)
    return loads


def feed_kernel(
    clusters_ref, normed_ref, cot_ref, w_hbm, gain_ref, bias_ref,
    out_ref, all_out, gz_all_out, act_out, gz_ref, vec_ref,
    w, all_ref, gz_all_ref, act_ref, gelu_ref, slope, total, w_sem, out_sem, *rest,
):
    bufs, (send, recv) = rest[:4], rest[4:]
    links = Links(send, recv)

    def to_low(at):
        all_ref[0, at] = normed_ref[at].astype(BF16)

    by_chunks(to_low)
    load_w = load_weights(w_hbm, w, w_sem, 3)
    links.barrier(links.to(y=1), links.to(y=3), links.to(sibling=True))
    written = Loads()

    def forward(pair):
        load_w.wait()
        rows = pair_of(all_ref, pair)
        for c in range(0, COLS, 256):
            cols = slice(c, c + 256)
            gate = dot_t(rows, w[0, cols])
            up = dot_t(rows, w[1, cols])
            bell = 0.5 + 0.5 * lax.erf(gate * np.float32(np.sqrt(0.5)))
            gelu = gate * bell
            turn = bell + gate * (jnp.exp(-0.5 * gate * gate) * np.float32(1.0 / np.sqrt(2.0 * np.pi)))
            hidden = (gelu * up).astype(BF16)
            turn = turn * up
            for i, slot in enumerate(pair):
                part = slice(i * ROWS, (i + 1) * ROWS)
                gelu_ref[slot, :, cols] = gelu[part]
                slope[slot, :, cols] = turn[part]
                act_ref[slot, :, 2 * COLS + c : 2 * COLS + c + 256] = hidden[part]

    alone(gather_near(links, all_ref, forward))
    written.start(all_ref, all_out, out_sem.at[8])

    def compute(pair):
        rows = jnp.concatenate([act_ref[slot, :, 2 * COLS :] for slot in pair], axis=0)
        for d in range(0, WIDE, 512):
            result = dot(rows, w[2, :, d : d + 512]).astype(BF16)
            for i, slot in enumerate(pair):
                bufs[0][slot, :, d : d + 512] = result[i * ROWS : (i + 1) * ROWS]

    vec_ref[...] = jnp.zeros_like(vec_ref)
    own, same = clusters_ref[lax.axis_index("dp")], np.float32(0.0)
    for i in range(clusters_ref.shape[0]):
        same = same + jnp.where(clusters_ref[i] == own, np.float32(1.0), np.float32(0.0))
    seq_weight = 1.0 / jnp.full((1, WIDE), same, F32)

    def finish(at):
        unit, inverse = norm_parts(deep_alpha * normed_ref[at] + total[at])
        out_ref[at] = (unit * gain_ref[...] + bias_ref[...]).astype(BF16)
        grad = cot_ref[at].astype(F32) * seq_weight
        grad_z = norm_backward(grad, unit, inverse, gain_ref[...])
        gz_ref[at] = grad_z
        gz_all_ref[0, at] = grad_z.astype(BF16)
        vec_ref[0] += rows8(grad * unit)
        vec_ref[1] += rows8(grad)

    def backward(pair):
        rows = pair_of(gz_all_ref, pair)
        for c in range(0, COLS, 256):
            cols = slice(c, c + 256)
            grad_hidden = dot_t(rows, w[2, cols])
            for i, slot in enumerate(pair):
                part = grad_hidden[i * ROWS : (i + 1) * ROWS]
                act_ref[slot, :, cols] = (part * slope[slot, :, cols]).astype(BF16)
                act_ref[slot, :, COLS + c : COLS + c + 256] = (part * gelu_ref[slot, :, cols]).astype(BF16)
        for slot in pair:
            written.start(act_ref.at[slot], act_out.at[slot], out_sem.at[slot])

    task, copies = scatter_near(links, bufs, compute, total)
    whole = when_whole(backward, 2)

    def chain(first):
        yield from task(first, 64)
        by_chunks(finish, first, 64)
        yield from gather_near(links, gz_all_ref, whole, first, 64)

    together(FEED, chain(0), chain(64))
    sent(copies)
    written.start(gz_all_ref, gz_all_out, out_sem.at[9])
    written.wait()


def feed_back_kernel(
    act_hbm, gz_hbm, w_hbm, normed_hbm, gz_all_hbm, unit_hbm, inverse_ref, gain_ref, w_out_hbm,
    gz1_ref, all_out, grad_heads_ref, vec_ref, shard_ref,
    gz_ref, unit_ref, w_out_ref, act_ref, rows_ref, all_ref, w, total, w_sem, sem, *rest,
):
    bufs, more, (send, recv) = rest[:4], rest[4:17], rest[17:]
    links = Links(send, recv)
    load_act, load_rows = Loads(), Loads()
    load_w = load_weights(w_hbm, w, w_sem, 2)
    load_act.start(act_hbm, act_ref, sem.at[0])
    to = links.to
    links.barrier(
        to(y=1), to(y=3), to(z=2), to(x=1), to(x=3), to(z=1), to(z=3), to(sibling=True)
    )
    load_act.wait()
    load_w.wait()
    load_rows.start(normed_hbm, rows_ref, sem.at[1])
    load_late = Loads()
    for i, (src, dst) in enumerate(((gz_hbm, gz_ref), (unit_hbm, unit_ref), (w_out_hbm, w_out_ref))):
        load_late.start(src, dst, sem.at[4 + i])

    def compute(pair):
        rows = jnp.concatenate([act_ref[slot, :, : 2 * COLS] for slot in pair], axis=0)
        for d in range(0, WIDE, 512):
            cols = slice(d, d + 512)
            result = dot(rows[:, :COLS], w[0, :, cols]) + dot(rows[:, COLS:], w[1, :, cols])
            result = result.astype(BF16)
            for i, slot in enumerate(pair):
                bufs[0][slot, :, cols] = result[i * ROWS : (i + 1) * ROWS]

    def finish(at):
        grad = deep_alpha * gz_ref[at] + total[at]
        unit = unit_ref[at]
        grad_z = norm_backward(grad, unit, inverse_ref[at][:, 0:1], gain_ref[...])
        gz1_ref[at] = grad_z
        all_ref[0, at] = grad_z.astype(BF16)
        vec_ref[0] += rows8(grad * unit)
        vec_ref[1] += rows8(grad)

    def work(pair):
        result = dot_t(pair_of(all_ref, pair), w_out_ref[...]).astype(BF16)
        for i, slot in enumerate(pair):
            grad_heads_ref[pl.ds(links.first_row(slot), ROWS)] = result[i * ROWS : (i + 1) * ROWS]

    written = Loads()

    vec_ref[...] = jnp.zeros_like(vec_ref)
    task, copies = scatter_near(links, bufs, compute, total)
    whole = when_whole(work, 2)

    def chain(first):
        yield from task(first, 64)
        load_late.wait()
        by_chunks(finish, first, 64)
        yield from gather(links, all_ref, whole, first, 64)

    g = more[0]

    def make(k):
        load_rows.wait()
        for c in range(0, COLS, 256):
            left = act_ref[:, :, k * COLS + c : k * COLS + c + 256].reshape(LEN, 256)
            height = min(256, FF - c)
            for d in range(0, WIDE, 512):
                right = rows_ref[:, :, d : d + 512].reshape(LEN, 512)
                result = dot_rows(left, right)[:height].astype(BF16)
                for i in range(4):
                    at = d // 128 + i
                    g[k, at // 4, at // 2 % 2, at % 2, c : c + height] = result[:, i * 128 : i * 128 + 128]
            if k == 1 and c == 512:
                load_rows.start(gz_all_hbm, rows_ref, sem.at[2])
            if c < 512:
                yield ()

    together(FEED_BACK, chain(0), chain(64), *reduce(links, more, make, shard_ref))
    sent(copies)
    written.start(all_ref, all_out, sem.at[3])
    written.wait()


def input_kernel(
    prefix_ref, q_ref, k_ref, v_ref, g_ref, lse_ref, cos_ref, sin_ref,
    w_hbm, gz1_ref, tokens_hbm, heads_ref, gz_all_hbm, shard_ref, attn_vec_ref, feed_vec_ref,
    out_ref, one_out, two_out, whole_out, own_ref, feed_ref,
    one_ref, two_ref, whole_ref, out_sem, total, vec_ref, w_ref, tokens_ref, gz_all_ref, grads, heads, key_sum, value_sum, held, got, local, sem, *rest,
):
    bufs, more, (send, recv) = rest[:7], rest[7:22], rest[22:]
    links = Links(send, recv)
    to = links.to
    load_gz, load_tokens, load_w, written = Loads(), Loads(), Loads(), Loads()
    load_gz.start(gz_all_hbm, gz_all_ref, sem.at[2])
    load_tokens.start(tokens_hbm, tokens_ref, sem.at[1])
    load_w.start(w_hbm, w_ref, sem.at[0])
    links.barrier(
        to(y=1), to(y=2), to(y=3), to(z=2), to(x=1), to(x=2), to(x=3), to(sibling=True), links.beside()
    )
    for i, ref in enumerate((attn_vec_ref, feed_vec_ref)):
        for j in range(2):
            vec_ref[2 * i + j : 2 * i + j + 1] = jnp.sum(ref[j], axis=0, keepdims=True)
    vec_ref[4:8] = jnp.zeros((4, WIDE), F32)
    block = 512
    ready = [Mark(), Mark(), Mark()]

    def attend_back(head):
        lanes = slice(head * 128, head * 128 + 128)

        def keep(part, first, value):
            for i in range(value.shape[0] // ROWS):
                seq = first // ROWS + i
                d = lax.rem(seq // 2 + 4 - links.y, 4)
                slot = 2 * d - d * (d - 1) // 2 - d * (d - 1) * (d - 2) // 3
                slot = slot + 4 * lax.rem(links.z_hi + seq, 2)
                at = head * 384 + part * 128
                grads[slot, :, at : at + 128] = value[i * ROWS : (i + 1) * ROWS].astype(BF16)

        for first in range(0, LEN, block):
            at = slice(first, first + block)
            query, grad = q_ref[at, lanes], g_ref[at, lanes]
            scores = dot_t(k_ref[:, lanes], query)
            key = lax.broadcasted_iota(jnp.int32, scores.shape, 0)
            limit = lax.broadcasted_iota(jnp.int32, (1, block), 1) + first
            limit = jnp.maximum(limit, prefix_ref[0] - 1)
            weights = jnp.where(key <= limit, jnp.exp(scores - lse_ref[head, :, at]), 0.0)
            grad_weights = dot_t(v_ref[:, lanes], grad)
            inner = jnp.sum(weights * grad_weights, axis=0, keepdims=True)
            grad_scores = (weights * (grad_weights - inner)).astype(BF16)
            turned = dot_rows(grad_scores, k_ref[:, lanes]) * HEAD_DIM**-0.5
            keep(0, first, turned * cos_ref[at] - pltpu.roll(turned, 64, 1) * sin_ref[at])
            grad_key = dot(grad_scores, query)
            grad_value = dot(weights.astype(BF16), grad)
            if first == 0:
                key_sum[...] = grad_key
                value_sum[...] = grad_value
            else:
                key_sum[...] += grad_key
                value_sum[...] += grad_value
            yield ()
        turned = key_sum[...]
        keep(1, 0, turned * cos_ref[...] - pltpu.roll(turned, 64, 1) * sin_ref[...])
        keep(2, 0, value_sum[...])

    def compute(pair):
        load_w.wait()
        rows = pair_of(grads, pair)
        result = 0.0
        for part in range(3):
            for head in range(2):
                at = head * 384 + part * 128
                result = result + dot_t(rows[:, at : at + 128], w_ref[part, :, head * 128 : head * 128 + 128])
        result = result.astype(BF16)
        for i, slot in enumerate(pair):
            bufs[0][slot] = result[i * ROWS : (i + 1) * ROWS]

    def finish(at):
        value = deep_alpha * gz1_ref[at] + total[at]
        for lane in range(WIDE // 128):
            out_ref[at, lane] = value[:, lane * 128 : lane * 128 + 128]

    def chain():
        yield (ready[2],)
        for head in range(2):
            yield from attend_back(head)
            ready[head].done = True
            if head == 0:
                yield ()
        yield from scatter(links, bufs, compute, total)
        by_chunks(finish)

    def qkv(head):
        flat = more[5 * head]
        yield (ready[head],)
        load_tokens.wait()
        right = grads[:, :, head * 384 : head * 384 + 384].reshape(LEN, 384)
        for d in range(8):
            left = tokens_ref[:, :, d * 256 : d * 256 + 256].reshape(LEN, 256)
            result = dot_rows(left, right).astype(BF16)
            for part in range(3):
                for i in range(2):
                    row = part * WIDE + d * 256 + i * 128
                    chunk, at = row // 384, row % 384
                    flat[chunk // 8, chunk // 4 % 2, chunk % 4, at : at + 128] = result[
                        i * 128 : i * 128 + 128, part * 128 : part * 128 + 128
                    ]
            if d == 3:
                yield ()

    def first_shared():
        for slot in range(8):
            heads[slot] = heads_ref[pl.ds(links.first_row(slot), ROWS)]
        load_gz.wait()
        left = heads[...].reshape(LEN, 256)
        for d in range(0, WIDE, 512):
            result = dot_rows(left, gz_all_ref[:, :, d : d + 512].reshape(LEN, 512)).astype(BF16)
            for i in range(4):
                lane = d // 128 + i
                for j in range(2):
                    chunk = lane // 2 * 2 + j
                    more[10][chunk // 8, chunk // 4 % 2, chunk % 4, :, lane % 2 * 128 : lane % 2 * 128 + 128] = result[
                        j * 128 : j * 128 + 128, i * 128 : i * 128 + 128
                    ]
        ready[2].done = True
        yield from share(links, more[10:15], whole_ref, SHARE_X_FIRST[2])
        written.start(whole_ref, whole_out, out_sem.at[2])

    def shared(head):
        yield from qkv(head)
        result, result_out = ((one_ref, one_out), (two_ref, two_out))[head]
        yield from share(links, more[5 * head : 5 * head + 5], result, SHARE_X_FIRST[head])
        written.start(result, result_out, out_sem.at[head])

    together(
        INPUT,
        *collect(links, shard_ref, feed_ref, local),
        first_shared(),
        chain(),
        shared(0),
        shared(1),
        agree(links, vec_ref, (held, got)),
    )
    written.wait()
    own_ref[...] = vec_ref[:, pl.ds(pl.multiple_of(lax.axis_index("seq") * 256, 256), 256)]


def outputs_kernel(
    feed_hbm, one_hbm, two_hbm, out_hbm, vec_ref, output_hbm, input_hbm,
    gate_up_hbm, down_hbm, grad_qkv_hbm, grad_out_hbm, v0_ref, v1_ref, v2_ref, v3_ref, output_out, input_out,
    feed, one, two, out, output, input_grad, gate_up, down, grad_qkv, grad_out, load_sem, store_sem,
):
    def load(i, src, dst):
        copy = pltpu.make_async_copy(src, dst, load_sem.at[i])
        copy.start()
        return copy

    stores = []

    def store(src, dst):
        stores.append(pltpu.make_async_copy(src, dst, store_sem.at[len(stores)]))
        stores[-1].start()

    chunks = []
    for k in (2, 0, 1):
        for i in range(8):
            at = (k, i // 2, i % 2)
            chunks.append((at, load(len(chunks), feed_hbm.at[at], feed.at[at])))
    rest = [load(24, one_hbm, one), load(25, two_hbm, two), load(26, out_hbm, out)]
    passed = [(load(27, output_hbm, output), output, output_out), (load(28, input_hbm, input_grad), input_grad, input_out)]
    for i, ref in enumerate((v0_ref, v1_ref, v2_ref, v3_ref)):
        ref[...] = vec_ref[i : i + 1]
    total = down.shape[0]
    for (k, y, core), copy in chunks[:8]:
        copy.wait()
        first = (2 * y + core) * FF
        last = min(first + FF, total)
        for z in range(2):
            down[first:last, z * 128 : z * 128 + 128] = feed[k, y, core, z, : last - first].astype(F32)
    store(down, down_hbm)
    for (_, gate), ((_, y, core), up) in zip(chunks[8:16], chunks[16:]):
        gate.wait()
        up.wait()
        first = (2 * y + core) * FF
        last = min(first + FF, total)
        rows = slice(0, last - first)
        for z in range(2):
            lanes = slice(z * 128, z * 128 + 128)
            gate_up[first:last, 0, lanes] = feed[0, y, core, z, rows].astype(F32)
            gate_up[first:last, 1, lanes] = feed[1, y, core, z, rows].astype(F32)
        at = pl.ds(first, last - first)
        store(gate_up.at[at], gate_up_hbm.at[at])
    for copy, src, dst in passed:
        copy.wait()
        store(src, dst)
    for copy in rest:
        copy.wait()
    for i in range(4):
        at = pl.ds(i * 1536, 1536)
        grad_qkv[at, 0:128] = one[at].astype(F32)
        grad_qkv[at, 128:256] = two[at].astype(F32)
        store(grad_qkv.at[at], grad_qkv_hbm.at[at])
    for i in range(8):
        grad_out[:, i * 256 : i * 256 + 256] = out[i * 256 : i * 256 + 256].astype(F32)
    store(grad_out, grad_out_hbm)
    for copy in stores:
        copy.wait()


def outputs(feed, one, two, out, vec, output, input_grad, total):
    shapes = [((total, 2, 256), F32), ((total, 256), F32), ((6144, 256), F32), ((256, WIDE), F32)]
    return pl.pallas_call(
        outputs_kernel,
        name="outputs",
        in_specs=[HBM, HBM, HBM, HBM, VMEM, HBM, HBM],
        out_specs=(HBM, HBM, HBM, HBM, VMEM, VMEM, VMEM, VMEM, HBM, HBM),
        out_shape=(
            *(jax.ShapeDtypeStruct(s, d) for s, d in shapes),
            *(jax.ShapeDtypeStruct((1, 256), F32) for _ in range(4)),
            jax.ShapeDtypeStruct(output.shape, BF16),
            jax.ShapeDtypeStruct(input_grad.shape, F32),
        ),
        scratch_shapes=[
            *(pltpu.VMEM(v.shape, v.dtype) for v in (feed, one, two, out, output, input_grad)),
            *(pltpu.VMEM(s, d) for s, d in shapes),
            pltpu.SemaphoreType.DMA((29,)),
            pltpu.SemaphoreType.DMA((16,)),
        ],
        compiler_params=pltpu.CompilerParams(vmem_limit_bytes=VMEM_BYTES),
    )(feed, one, two, out, vec, output, input_grad)


def on_device(
    tokens, cotangent, w_qkv, w_out, w_gate_up, w_down,
    attn_gain, attn_bias, ffn_gain, ffn_bias, prefix_len, clusters,
):
    x = tokens.reshape(ROWS, WIDE)
    cot = cotangent.reshape(ROWS, WIDE)
    dp = lax.axis_index("dp")
    cosine, sine = (jnp.asarray(t) for t in rotary_tables(LEN, HEAD_DIM))
    row = lambda v: v.reshape(1, WIDE)
    ff_total = w_down.shape[1]
    place = jnp.stack([dp % 2, dp // 2 % 4, dp // 8, jnp.int32(ff_total)]).astype(jnp.int32)
    piece = piece_of(w_gate_up.transpose(2, 1, 0), w_down.T, place)
    w_in = w_qkv.transpose(1, 0, 2)
    low, full = BF16, F32
    blocks = (8, ROWS, WIDE)
    one = pltpu.SemaphoreType.DMA
    some = lambda *n: pltpu.SemaphoreType.DMA(n)
    rows_f32 = pltpu.VMEM((ROWS, WIDE), F32)
    blocks_low = pltpu.VMEM(blocks, BF16)
    head_sum = pltpu.VMEM((LEN, 128), F32)

    tokens_all, q, k, v, heads_out, lse, normed, unit_one, inverse_one, w_all = call(
        front_kernel, "front", 0,
        [
            (blocks, low, "h"), *[((LEN, 256), low, "h")] * 4, ((2, 1, LEN), full, "v"),
            ((ROWS, WIDE), full, "v"), ((ROWS, WIDE), full, "v"), ((ROWS, 128), full, "v"),
            ((3, 2, 4, 2, FF, 128), low, "h"),
        ],
        (prefix_len, x, w_in, cosine, sine, w_out, row(attn_gain), row(attn_bias), piece), "svhhhhvvv",
        (
            blocks_low, rows_f32, pltpu.VMEM((3, WIDE, 256), BF16), head_sum, head_sum,
            pltpu.VMEM((256, WIDE), BF16), *[pltpu.VMEM((LEN, 256), BF16)] * 4, one, some(9), *SCATTER_SCRATCH,
        ),
        94, 2 * LEN * WIDE * 1024,
    )
    output, normed_all, gz_all, act, grad_z2, ffn_vec = call(
        feed_kernel, "feed", 2,
        [
            ((ROWS, WIDE), low, "v"), (blocks, low, "h"), (blocks, low, "h"),
            ((8, ROWS, 3 * COLS), low, "h"), ((ROWS, WIDE), full, "v"), ((2, 8, WIDE), full, "v"),
        ],
        (clusters, normed, cot, w_all, row(ffn_gain), row(ffn_bias)), "svvhvv",
        (
            pltpu.VMEM((3, COLS, WIDE), BF16), blocks_low, blocks_low,
            pltpu.VMEM((8, ROWS, 3 * COLS), BF16), pltpu.VMEM((8, ROWS, COLS), F32),
            pltpu.VMEM((8, ROWS, COLS), F32), rows_f32, some(3, 16), some(10), *NEAR_SCRATCH,
        ),
        60, 2 * LEN * WIDE * COLS * 4,
    )
    grad_z1, gz1_all, grad_heads, attn_vec, shard = call(
        feed_back_kernel, "feed_back", 3,
        [
            ((ROWS, WIDE), full, "v"), (blocks, low, "h"), ((LEN, 256), low, "v"),
            ((2, 8, WIDE), full, "v"), ((3, 4, PART, 128), low, "v"),
        ],
        (act, grad_z2, w_all, normed_all, gz_all, unit_one, inverse_one, row(attn_gain), w_out),
        "hhhhhhvvh",
        (
            rows_f32, rows_f32, pltpu.VMEM((256, WIDE), BF16), pltpu.VMEM((8, ROWS, 3 * COLS), BF16), blocks_low, blocks_low,
            pltpu.VMEM((2, COLS, WIDE), BF16), rows_f32, some(2, 16), some(7),
            *NEAR_SCRATCH, *REDUCE_SCRATCH,
        ),
        80, 2 * LEN * WIDE * COLS * 5,
    )
    steps = pltpu.VMEM((7, 8, WIDE), F32)
    input_grad, one, two, out_whole, vec, ffn_whole = call(
        input_kernel, "input", 4,
        [
            ((ROWS, WIDE // 128, 128), full, "v"), ((2, 2, 4, 384, 128), low, "h"),
            ((2, 2, 4, 384, 128), low, "h"), ((2, 2, 4, 128, 256), low, "h"), ((8, 256), full, "v"),
            ((3, 4, 2, 2, FF, 128), low, "h"),
        ],
        (
            prefix_len, q, k, v, grad_heads, lse, cosine, sine,
            w_in, grad_z1, tokens_all, heads_out, gz1_all, shard, attn_vec, ffn_vec,
        ),
        "svvvvvvvhvhvhvvv",
        (
            pltpu.VMEM((2, 2, 4, 384, 128), BF16), pltpu.VMEM((2, 2, 4, 384, 128), BF16),
            pltpu.VMEM((2, 2, 4, 128, 256), BF16), some(3),
            rows_f32, pltpu.VMEM((8, WIDE), F32), pltpu.VMEM((3, WIDE, 256), BF16), blocks_low, blocks_low,
            pltpu.VMEM((8, ROWS, 768), BF16), pltpu.VMEM((8, ROWS, 256), BF16),
            head_sum, head_sum, steps, steps, pltpu.SemaphoreType.DMA, some(3),
            *SCATTER_SCRATCH, *share_scratch(384, 128), *share_scratch(384, 128), *share_scratch(128, 256),
        ),
        140, 2 * LEN * WIDE * 768,
    )
    grad_gate_up, grad_down, grad_qkv, grad_out, *vecs, output, input_grad = outputs(
        ffn_whole, one.reshape(6144, 128), two.reshape(6144, 128), out_whole.reshape(2048, 256),
        vec, output, input_grad, ff_total,
    )
    return (
        output.reshape(tokens.shape),
        input_grad.reshape(tokens.shape),
        grad_qkv.reshape(3, WIDE, 256).transpose(1, 0, 2),
        grad_out,
        grad_gate_up.transpose(2, 1, 0),
        grad_down.T,
        *(v.reshape(256) for v in vecs),
    )


def solution(mesh):
    return jax.shard_map(
        on_device,
        mesh=mesh,
        in_specs=(
            P("seq", "dp", None), P("seq", "dp", None), P(None, None, "seq"), P("seq", None),
            P("seq", None, None), P("seq", None), P(), P(), P(), P(), P("dp"), P(),
        ),
        out_specs=(
            P("seq", "dp", None), P("seq", "dp", None), P(None, None, "seq"), P("seq", None),
            P("seq", None, None), P("seq", None), P("seq"), P("seq"), P("seq"), P("seq"),
        ),
        check_vma=False,
    )
```

```python
import functools

import jax
import jax.numpy as jnp
import numpy as np
from jax import lax
from jax.experimental import pallas as pl
from jax.experimental.pallas import tpu as pltpu
from jax.sharding import PartitionSpec as P

MESH = pl.DeviceIdType.MESH
F32, BF16 = jnp.float32, jnp.bfloat16
HEAD_DIM = 128
ROWS = 128
WIDE = 2048
COLS = 768
LEN = 1024
VMEM_BYTES = 60 * 1024 * 1024
deep_alpha = 48.0**0.25
norm_eps = 1e-05
rotary_base = 10000.0


def rotary_tables(length, head_width):
    half_width = head_width // 2
    position = np.arange(length, dtype=np.float64)
    inverse = rotary_base ** (-np.arange(half_width, dtype=np.float64) * 2.0 / head_width)
    angles = position[:, None] * inverse[None, :]
    cosine_table = np.cos(angles)
    sine_table = np.sin(angles)
    return (
        np.concatenate([cosine_table, cosine_table], axis=1).astype(np.float32),
        np.concatenate([-sine_table, sine_table], axis=1).astype(np.float32),
    )


FF = 704
PART = 176


class Links:
    def __init__(self, send, recv):
        self.send, self.recv, self.count = send, recv, 0
        dp, seq = lax.axis_index("dp"), lax.axis_index("seq")
        y, z_hi = seq // 2, lax.rem(seq, 2)
        z_lo, x, core = dp // 8, lax.rem(dp // 2, 4), lax.rem(dp, 2)
        self.y, self.z_hi, self.z_lo, self.x, self.core = y, z_hi, z_lo, x, core
        self.z = z_hi * 2 + z_lo

    def to(self, x=0, y=0, z=0, sibling=False):
        z_hi, z_lo = self.z_at(z)
        x, y = lax.rem(self.x + x, 4), lax.rem(self.y + y, 4)
        core = 1 - self.core if sibling else self.core
        return (z_lo * 8 + x * 2 + core, y * 2 + z_hi)

    def beside(self):
        return (lax.rem(lax.axis_index("dp") + 8, 16), lax.axis_index("seq"))

    def z_at(self, offset):
        z = lax.rem(self.z + offset, 4)
        return z // 2, lax.rem(z, 2)

    def part(self, offset):
        return pl.ds(pl.multiple_of(lax.rem(self.x + offset, 4) * PART, 16), PART)

    def barrier(self, *where):
        gate = pltpu.get_barrier_semaphore()
        for device in where:
            pl.semaphore_signal(gate, inc=1, device_id=device, device_id_type=MESH)
        pl.semaphore_wait(gate, len(where))

    def start(self, src, dst, where):
        assert self.count < self.send.shape[0]
        copy = pltpu.make_async_remote_copy(
            src_ref=src,
            dst_ref=dst,
            send_sem=self.send.at[self.count],
            recv_sem=self.recv.at[self.count],
            device_id=where,
            device_id_type=MESH,
        )
        self.count += 1
        copy.start()
        return copy

    def first_row(self, slot):
        step = (0, 3, 1, 2)[slot % 4]
        half = self.z_hi if slot < 4 else 1 - self.z_hi
        return pl.multiple_of((lax.rem(self.y + step, 4) * 2 + half) * ROWS, ROWS)


class Once:
    def __init__(self, *copies):
        self.copies = list(copies)

    def wait_recv(self):
        while self.copies:
            self.copies.pop().wait_recv()


class Mark:
    done = False


class Local:
    def __init__(self, src, dst, sem):
        self.copy = pltpu.make_async_copy(src, dst, sem)
        self.copy.start()

    def wait_recv(self):
        self.copy.wait()


def together(order, *tasks):
    tasks = list(tasks)
    for task in tasks:
        next(task)
    left = len(tasks)
    for which in order:
        try:
            next(tasks[which])
        except StopIteration:
            left -= 1
    assert left == 0


def alone(task):
    for _ in task:
        pass


def received(*copies):
    for copy in copies:
        copy.wait_recv()


def sent(copies):
    for copy in copies:
        copy.wait_send()


def gather(links, buf, work, first=0, rows=ROWS):
    up, down, across = links.to(y=1), links.to(y=3), links.to(z=2)
    h0, h1 = pl.ds(first, rows // 2), pl.ds(first + rows // 2, rows // 2)
    copies = []

    def send(slot, at, dst, where):
        copies.append(links.start(buf.at[slot, at], buf.at[dst, at], where))
        return copies[-1]

    u0, d1 = send(0, h0, 1, up), send(0, h1, 2, down)
    z0, z1 = send(0, h0, 4, across), send(0, h1, 4, across)
    u1, d0 = send(0, h1, 1, up), send(0, h0, 2, down)
    yield u0, d1
    received(u0)
    fu = send(1, h0, 3, up)
    received(d1)
    fd = send(2, h1, 3, down)
    yield z0, z1
    received(z0)
    pu0 = send(4, h0, 5, up)
    received(z1)
    pd1 = send(4, h1, 6, down)
    pu1, pd0 = send(4, h1, 5, up), send(4, h0, 6, down)
    yield u1, d0
    received(u1, d0)
    work((0, 1))
    yield fu, fd
    received(fu, fd)
    work((2, 3))
    yield pu0, pd1
    received(pu0)
    gu = send(5, h0, 7, up)
    received(pd1)
    gd = send(6, h1, 7, down)
    yield pu1, pd0
    received(pu1, pd0)
    work((4, 5))
    yield gu, gd
    received(gu, gd)
    work((6, 7))
    sent(copies)


def when_whole(work, times):
    seen = {}

    def count(pair):
        seen[pair] = seen.get(pair, 0) + 1
        if seen[pair] == times:
            work(pair)

    return count


def gather_near(links, buf, work, first=0, rows=ROWS):
    up, down, side = links.to(y=1), links.to(y=3), links.to(sibling=True)
    every = pl.ds(first, rows)
    h0, h1 = pl.ds(first, rows // 2), pl.ds(first + rows // 2, rows // 2)
    copies = []

    def send(slot, at, dst, where):
        copies.append(links.start(buf.at[slot, at], buf.at[dst, at], where))
        return copies[-1]

    u0, d1 = send(0, h0, 1, up), send(0, h1, 2, down)
    u1, d0 = send(0, h1, 1, up), send(0, h0, 2, down)
    s0 = send(0, every, 4, side)
    yield (s0,)
    received(s0)
    work((0, 4))
    yield u0, d1
    received(u0)
    fu = send(1, h0, 3, up)
    received(d1)
    fd = send(2, h1, 3, down)
    yield u1, d0
    received(u1)
    s1 = send(1, every, 5, side)
    received(d0)
    s2 = send(2, every, 6, side)
    work((1, 2))
    yield s1, s2
    received(s1, s2)
    work((5, 6))
    yield fu, fd
    received(fu)
    s30 = send(3, h0, 7, side)
    received(fd)
    s31 = send(3, h1, 7, side)
    yield s30, s31
    received(s30, s31)
    work((3, 7))
    sent(copies)


A, B = pl.ds(0, 80), pl.ds(80, 48)
A0, A1 = pl.ds(0, 48), pl.ds(48, 32)
B0, B1 = pl.ds(80, 16), pl.ds(96, 32)
SCATTER_SCRATCH = (
    pltpu.VMEM((8, ROWS, WIDE), BF16),
    pltpu.VMEM((4, 48, WIDE), BF16),
    pltpu.VMEM((48, WIDE), BF16),
    pltpu.VMEM((2, 48, WIDE), BF16),
    pltpu.VMEM((2, 80, WIDE), BF16),
    pltpu.VMEM((2, 2, 80, WIDE), BF16),
    pltpu.VMEM((80, WIDE), BF16),
)


def add_rows(target, slot, rows, *others):
    value = target[slot, rows].astype(F32)
    for other in others:
        value = value + other.astype(F32)
    target[slot, rows] = value.astype(BF16)


def scatter(links, bufs, compute, total):
    sums, from_z, b_far, b_near, a_far, a_near, a_z = bufs
    up, down, across = links.to(y=1), links.to(y=3), links.to(z=2)
    copies = []

    def send(src, dst, where):
        copies.append(links.start(src, dst, where))
        return copies[-1]

    def far_a(o):
        half = o // 4
        return (
            send(sums.at[o + 3, A0], a_far.at[half, pl.ds(0, 48)], up),
            send(sums.at[o + 3, A1], a_far.at[half, pl.ds(48, 32)], down),
        )

    def near_a(o, far):
        half = o // 4
        received(far[0])
        add_rows(sums, o + 2, A0, a_far[half, 0:48])
        one = send(sums.at[o + 2, A], a_near.at[half, 0], up)
        received(far[1])
        add_rows(sums, o + 1, A1, a_far[half, 48:80])
        return one, send(sums.at[o + 1, A], a_near.at[half, 1], down)

    def cross_b(j):
        return send(sums.at[4 + j, B], from_z.at[j], across)

    compute((7, 3))
    z3 = cross_b(3)
    far_other = far_a(4)
    far_own = far_a(0)
    yield ()
    compute((5, 1))
    z1 = cross_b(1)
    yield ()
    compute((6, 2))
    z2 = cross_b(2)
    yield far_other
    near_other = near_a(4, far_other)
    compute((4, 0))
    z0 = cross_b(0)
    yield (z3,)
    received(z3)
    add_rows(sums, 3, B, from_z[3])
    far_b = (
        send(sums.at[3, B0], b_far.at[pl.ds(0, 16)], up),
        send(sums.at[3, B1], b_far.at[pl.ds(16, 32)], down),
    )
    yield far_own
    near_own = near_a(0, far_own)
    yield z1, z2
    received(z2)
    add_rows(sums, 2, B, from_z[2])
    received(z1)
    add_rows(sums, 1, B, from_z[1])
    yield far_b
    received(far_b[0])
    add_rows(sums, 2, B0, b_far[0:16])
    near_b0 = send(sums.at[2, B], b_near.at[0], up)
    received(far_b[1])
    add_rows(sums, 1, B1, b_far[16:48])
    near_b1 = send(sums.at[1, B], b_near.at[1], down)
    yield near_other
    received(*near_other)
    add_rows(sums, 4, A, a_near[1, 0], a_near[1, 1])
    z_a = send(sums.at[4, A], a_z, across)
    yield z0, near_b0, near_b1
    received(z0, near_b0, near_b1)
    total[80:128] = (
        sums[0, B].astype(F32)
        + from_z[0].astype(F32)
        + b_near[0].astype(F32)
        + b_near[1].astype(F32)
    )
    yield (z_a, *near_own)
    received(*near_own)
    received(z_a)
    total[0:80] = (
        sums[0, A].astype(F32)
        + a_near[0, 0].astype(F32)
        + a_near[0, 1].astype(F32)
        + a_z[...].astype(F32)
    )
    sent(copies)


NEAR_SCRATCH = (
    pltpu.VMEM((8, ROWS, WIDE), BF16),
    pltpu.VMEM((4, ROWS, WIDE), BF16),
    pltpu.VMEM((ROWS, WIDE), BF16),
    pltpu.VMEM((2, ROWS, WIDE), BF16),
)


def scatter_near(links, bufs, compute, total):
    sums, from_side, far, near = bufs
    up, down, side = links.to(y=1), links.to(y=3), links.to(sibling=True)
    copies = []

    def send(src, dst, where):
        copies.append(links.start(src, dst, where))
        return copies[-1]

    compute((7, 3))
    s3 = Once(send(sums.at[7], from_side.at[3], side))
    compute((5, 6))
    s12 = Once(send(sums.at[5], from_side.at[1], side), send(sums.at[6], from_side.at[2], side))
    compute((1, 2))
    later = []

    def last():
        compute((4, 0))
        later.append(Once(send(sums.at[4], from_side.at[0], side)))

    def task(first, rows):
        every = pl.ds(first, rows)
        h0, h1 = pl.ds(first, rows // 2), pl.ds(first + rows // 2, rows // 2)
        yield (s3,)
        received(s3)
        add_rows(sums, 3, every, from_side[3, every])
        fu = send(sums.at[3, h0], far.at[h0], up)
        fd = send(sums.at[3, h1], far.at[h1], down)
        received(s12)
        add_rows(sums, 2, every, from_side[2, every])
        nu1 = send(sums.at[2, h1], near.at[0, h1], up)
        add_rows(sums, 1, every, from_side[1, every])
        nd0 = send(sums.at[1, h0], near.at[1, h0], down)
        if not later:
            last()
        yield fu, fd
        received(fu)
        add_rows(sums, 2, h0, far[h0])
        nu0 = send(sums.at[2, h0], near.at[0, h0], up)
        received(fd)
        add_rows(sums, 1, h1, far[h1])
        nd1 = send(sums.at[1, h1], near.at[1, h1], down)
        yield nu1, nd0, nu0, nd1
        received(later[0], nu1, nd0, nu0, nd1)
        total[every] = (
            sums[0, every].astype(F32)
            + from_side[0, every].astype(F32)
            + near[0, every].astype(F32)
            + near[1, every].astype(F32)
        )

    return task, copies


Y0, Y1 = pl.ds(0, 2), pl.ds(2, 2)
GU = pl.ds(0, 2)


def across_y(links, piece, own, local):
    copies = []
    for step in (2, 1, 3):
        there = lax.rem(links.y + step, 4)
        copies.append(links.start(piece(there), own(), links.to(y=step)))
    keep = Local(piece(links.y), own(), local)
    return Once(keep, *copies), copies


def ring_gather(links, arrived, at, first, second):
    up, down = first
    right, left = second
    copies = []

    def send(ref, where):
        copies.append(links.start(ref, ref, where))
        return copies[-1]

    def both(a):
        return send(at(a, 0), right), send(at(a, 0), left)

    def onward(a):
        return [send(at(a, 3, Y0), right), send(at(a, 1, Y1), left)]

    yield (arrived,)
    received(arrived)
    u, d = send(at(0, 0), up), send(at(0, 0), down)
    near = [both(0)]
    yield u, d
    received(u)
    fu = send(at(3, 0, Y0), up)
    received(d)
    fd = send(at(1, 0, Y1), down)
    near.append(both(3))
    near.append(both(1))
    yield near[0]
    received(*near[0])
    far = onward(0)
    yield fu, fd
    received(fu, fd)
    near.append(both(2))
    for i, a in enumerate((3, 1, 2)):
        yield near[1 + i]
        received(*near[1 + i])
        far += onward(a)
    yield far
    received(*far)
    sent(copies)


Z_FIRST = (0, 2)


def spread(links, piece, w, local):
    along_x = (links.to(x=1), links.to(x=3))
    along_z = (links.to(z=1), links.to(z=3))
    every = pl.ds(0, 4)

    def place(k, z, x, y):
        z_hi, z_lo = links.z_at(z)
        return w.at[k, z_hi, y, z_lo, links.part(x)]

    def own():
        return w.at[:, links.z_hi, links.y, links.z_lo, links.part(0)]

    arrived, copies = across_y(links, lambda y: piece.at[y], own, local)

    def one(k, z_first):
        if z_first:
            yield from ring_gather(links, arrived, lambda a, b, y=every: place(k, a, b, y), along_z, along_x)
        else:
            yield from ring_gather(links, arrived, lambda a, b, y=every: place(k, b, a, y), along_x, along_z)
        if k == 0:
            sent(copies)

    return tuple(one(k, k in Z_FIRST) for k in range(3))


def ring_scratch(*block):
    return [pltpu.VMEM(block, BF16), pltpu.VMEM((2, *block), BF16)]


REDUCE_SCRATCH = (
    pltpu.VMEM((3, 4, 2, 2, FF, 128), BF16),
    *ring_scratch(4, 2, 2, PART, 128), *ring_scratch(4, PART, 128),
    *ring_scratch(4, 2, 2, PART, 128), *ring_scratch(4, PART, 128),
    *ring_scratch(4, FF, 128), *ring_scratch(4, PART, 128),
)


def accumulate(count, target, *others):
    def step(i, carry):
        ref = target(i)
        value = ref[...].astype(F32)
        for other in others:
            value = value + other(i)[...].astype(F32)
        ref[...] = value.astype(BF16)
        return carry

    lax.fori_loop(0, count, step, 0)


def ring_reduce(links, at, blocks, ring, far, near, devices):
    up, down = devices
    copies = []
    every = pl.ds(0, 4)

    def send(src, dst, where):
        copies.append(links.start(src, dst, where))
        return copies[-1]

    half = ring // 2
    fu, fd = send(at(2, Y0), far.at[Y0], up), send(at(2, Y1), far.at[Y1], down)
    nu, nd = send(at(1, Y1), near.at[0, Y1], up), send(at(3, Y0), near.at[1, Y0], down)
    yield fu, fd
    received(fu)
    accumulate(half, lambda i: blocks(at(1, every), i), lambda i: blocks(far, i))
    mu = send(at(1, Y0), near.at[0, Y0], up)
    received(fd)
    accumulate(half, lambda i: blocks(at(3, every), i + half), lambda i: blocks(far, i + half))
    md = send(at(3, Y1), near.at[1, Y1], down)
    yield nu, nd, mu, md
    received(nu, nd, mu, md)
    accumulate(
        ring, lambda i: blocks(at(0, every), i), lambda i: blocks(near.at[0], i), lambda i: blocks(near.at[1], i)
    )
    sent(copies)


def reduce(links, bufs, make, shard):
    g = bufs[0]
    along_x = (links.to(x=1), links.to(x=3))
    along_z = (links.to(z=1), links.to(z=3))
    made = [Mark(), Mark()]

    def one(k, x_first):
        far, near, far2, near2 = bufs[1 + 4 * k : 5 + 4 * k]
        z_hi, z_lo = links.z_at(0)

        def along_z_at(a, y):
            hi, lo = links.z_at(a)
            return g.at[k, y, hi, lo]

        def along_x_at(a, y):
            return g.at[k, y, :, :, links.part(a)]

        def rest_z(a, y):
            hi, lo = links.z_at(a)
            return g.at[k, y, hi, lo, links.part(0)]

        def rest_x(a, y):
            return g.at[k, y, z_hi, z_lo, links.part(a)]

        def four(ref, i):
            return ref.at[i // 4, lax.rem(i // 2, 2), lax.rem(i, 2)]

        def plain(ref, i):
            return ref.at[i]

        if k:
            yield (made[k - 1],)
        yield from make(k)
        if k < 2:
            made[k].done = True
        if x_first:
            yield from ring_reduce(links, along_x_at, four, 16, far, near, along_x)
            yield from ring_reduce(links, rest_z, plain, 4, far2, near2, along_z)
        else:
            yield from ring_reduce(links, along_z_at, plain, 4, far, near, along_z)
            yield from ring_reduce(links, rest_x, plain, 4, far2, near2, along_x)
        shard[k] = g[k, :, z_hi, z_lo, links.part(0)]

    return one(0, True), one(1, True), one(2, False)


def regather(links, at, half, x_first):
    xp, xm, side = links.to(x=1), links.to(x=3), links.to(sibling=True)
    beside = links.beside()
    copies, sides = [], []

    def send(ref, where):
        copies.append(links.start(ref, ref, where))
        return copies[-1]

    def share(ref):
        sides.append(send(ref, side))

    near = [(send(at(0, 0), xp), send(at(0, 0), xm))]
    z = [(0, send(at(0, 0), beside))]
    share(at(0, 0))
    far = []
    if not x_first:
        yield (z[0][1],)
        received(z[0][1])
        near.append((send(at(1, 0), xp), send(at(1, 0), xm)))
        share(at(1, 0))
    for i in range(len(near)):
        yield near[i]
        received(near[i][0])
        far_up = send(half(at(i, 3), 0), xp)
        received(near[i][1])
        far.append((far_up, send(half(at(i, 1), 1), xm)))
        for x in (3, 1):
            if x_first:
                z.append((x, send(at(0, x), beside)))
            share(at(i, x))
    for i in range(len(near)):
        yield far[i]
        received(*far[i])
        if x_first:
            z.append((2, send(at(0, 2), beside)))
        share(at(i, 2))
    if x_first:
        for x, copy in z:
            yield (copy,)
            received(copy)
            share(at(1, x))
    yield sides
    received(*sides)
    sent(copies)


def collect(links, shard, out, local):
    def own():
        return out.at[:, links.y, links.core, links.z_lo, links.part(0)]

    arrived, copies = across_y(links, lambda y: shard.at[:, y], own, local)

    def task(matrices, x_first):
        yield (arrived,)
        received(arrived)

        def at(z, x):
            return out.at[matrices, :, links.core, lax.rem(links.z_lo + z, 2), links.part(x)]

        def half(ref, i):
            return ref.at[:, pl.ds(2 * i, 2)]

        yield from regather(links, at, half, x_first)
        if x_first:
            sent(copies)

    return task(GU, False), task(pl.ds(2, 1), True)


def share_scratch(rows, lanes):
    return [
        pltpu.VMEM((2, 2, 4, rows, lanes), BF16),
        pltpu.VMEM((2, 4, rows, lanes), BF16),
        pltpu.VMEM((2, rows, lanes), BF16),
        pltpu.VMEM((2, 2, rows, lanes), BF16),
        pltpu.VMEM((rows, lanes), BF16),
    ]


SHARE_X_FIRST = (False, False, False)


def share(links, bufs, out, x_first):
    q, from_side, far, near, from_z = bufs
    xp, xm, side = links.to(x=1), links.to(x=3), links.to(sibling=True)
    beside = links.beside()
    core, z_lo = links.core, links.z_lo
    count = q.shape[3]
    copies = []

    def send(src, dst, where):
        copies.append(links.start(src, dst, where))
        return copies[-1]

    def there(x):
        return lax.rem(links.x + x, 4)

    def rows(ref):
        return lambda i: ref.at[pl.ds(pl.multiple_of(i * 64, 64), 64)]

    def add(target, *others):
        accumulate(count // 64, rows(target), *(rows(other) for other in others))

    s = send(q.at[1 - core], from_side, side)
    yield (s,)
    received(s)
    for x in (2, 1, 3, 0):
        for z in range(2):
            add(q.at[core, z, there(x)], from_side.at[z, there(x)])
        if x == 2:
            fu, fd = send(q.at[core, 0, there(2)], far.at[0], xp), send(q.at[core, 1, there(2)], far.at[1], xm)
    nu = send(q.at[core, 1, there(1)], near.at[0, 1], xp)
    nd = send(q.at[core, 0, there(3)], near.at[1, 0], xm)
    yield fu, fd
    received(fu)
    add(q.at[core, 0, there(1)], far.at[0])
    mu = send(q.at[core, 0, there(1)], near.at[0, 0], xp)
    received(fd)
    add(q.at[core, 1, there(3)], far.at[1])
    md = send(q.at[core, 1, there(3)], near.at[1, 1], xm)
    yield nu, nd, mu, md
    received(nu, nd, mu, md)
    for z in range(2):
        add(q.at[core, z, there(0)], near.at[0, z], near.at[1, z])
    b = send(q.at[core, 1 - z_lo, there(0)], from_z, beside)
    yield (b,)
    received(b)

    def finish(i, carry):
        at = pl.ds(pl.multiple_of(i * 64, 64), 64)
        value = q[core, z_lo, links.x, at].astype(F32) + from_z[at].astype(F32)
        out[core, z_lo, links.x, at] = value.astype(BF16)
        return carry

    lax.fori_loop(0, count // 64, finish, 0)

    def at(z, x):
        return out.at[core, lax.rem(z_lo + z, 2), there(x)]

    def half(ref, i):
        return ref.at[pl.ds(count // 2 * i, count // 2)]

    yield from regather(links, at, half, x_first)
    sent(copies)


def agree(links, vec, bufs):
    y, x = links.y, links.x
    copies = []
    steps = (
        links.to(sibling=True),
        links.to(y=1 + 2 * lax.rem(y, 2)),
        links.to(y=2),
        links.to(z=2),
        links.to(x=1 + 2 * lax.rem(x, 2)),
        links.to(x=2),
        links.beside(),
    )
    held, got = bufs
    held[0] = vec[...]
    for i, where in enumerate(steps):
        copies.append(links.start(held.at[i], got.at[i], where))
        yield (copies[-1],)
        received(copies[-1])
        if i < len(steps) - 1:
            held[i + 1] = held[i] + got[i]
        else:
            vec[...] = held[i] + got[i]
    sent(copies)


def dot(a, b):
    return jnp.dot(a, b, preferred_element_type=F32)


def dot_t(a, b):
    return lax.dot_general(a, b, (((1,), (1,)), ((), ())), preferred_element_type=F32)


def dot_rows(a, b):
    return lax.dot_general(a, b, (((0,), (0,)), ((), ())), preferred_element_type=F32)


def pair_of(ref, pair):
    return jnp.concatenate([ref[pair[0]], ref[pair[1]]], axis=0)


def by_chunks(body, first=0, rows=ROWS):
    def step(i, carry):
        body(pl.ds(pl.multiple_of(first + i * 16, 16), 16))
        return carry

    lax.fori_loop(0, rows // 16, step, 0)


def norm_parts(row_total):
    center = row_total - jnp.mean(row_total, axis=-1, keepdims=True)
    spread = jnp.mean(center * center, axis=-1, keepdims=True)
    inverse = lax.rsqrt(spread + norm_eps)
    return center * inverse, inverse


def norm_backward(grad_result, unit, inverse, gain):
    grad_unit = grad_result * gain
    return inverse * (
        grad_unit
        - jnp.mean(grad_unit, axis=-1, keepdims=True)
        - unit * jnp.mean(grad_unit * unit, axis=-1, keepdims=True)
    )


def rows8(values):
    return values[0:8] + values[8:16]


VMEM = pl.BlockSpec(memory_space=pltpu.VMEM)
HBM = pl.BlockSpec(memory_space=pl.ANY)
SMEM = pl.BlockSpec(memory_space=pltpu.SMEM)
KINDS = {"v": VMEM, "s": SMEM, "h": HBM}


def call(body, name, ident, outs, operands, spaces, scratch, copies, flops=0):
    sems = [pltpu.SemaphoreType.DMA((copies,)), pltpu.SemaphoreType.DMA((copies,))]
    return pl.pallas_call(
        body,
        name=name,
        out_shape=tuple(jax.ShapeDtypeStruct(s, d) for s, d, _ in outs),
        in_specs=[KINDS[k] for k in spaces],
        out_specs=tuple(KINDS[k] for _, _, k in outs),
        scratch_shapes=[*scratch, *sems],
        compiler_params=pltpu.CompilerParams(
            collective_id=ident, has_side_effects=True, vmem_limit_bytes=VMEM_BYTES
        ),
        cost_estimate=pl.CostEstimate(flops=flops, bytes_accessed=20_000_000, transcendentals=0),
    )(*operands)


FRONT = (1, 2, 0, 0, 3, 0, 1, 1, 2, 2, 0, 1, 1, 3, 0, 1, 3, 0, 2, 2, 1, 2, 0, 0, 0, 0, 0, 2, 1, 0, 3, 3, 3, 0, 0, 0, 2, 3, 3, 0, 0)
FEED = (0, 0, 1, 1, 0, 0, 1, 0, 1, 0, 0, 1, 1, 0, 1, 1, 0, 1)
FEED_BACK = (0, 2, 2, 0, 3, 3, 3, 0, 4, 4, 4, 0, 2, 1, 0, 0, 0, 1, 4, 3, 0, 0, 1, 0, 4, 1, 2, 1, 1, 1, 2, 3, 4, 2, 1, 3, 4, 1, 1, 3)
INPUT = (3, 2, 1, 0, 6, 3, 2, 3, 4, 4, 6, 1, 3, 4, 0, 0, 3, 6, 4, 2, 3, 5, 5, 1, 1, 1, 2, 1, 0, 3, 5, 0, 1, 3, 4, 2, 6, 1, 3, 2, 3, 3, 0, 5, 0, 4, 2, 3, 6, 2, 5, 4, 4, 2, 3, 5, 4, 4, 2, 3, 6, 5, 5, 4, 4, 3, 5, 5, 5, 3, 5, 6)


def piece_kernel(place_ref, *refs):
    out_ref = refs[8]
    for y in range(4):
        chunk = (y * 2 + place_ref[0]) * 4 + place_ref[1]
        row = lax.broadcasted_iota(jnp.int32, (PART, 128), 0) + chunk * PART
        inside = row < place_ref[3]
        both = refs[y][...].astype(F32)
        out_ref[y, 0] = jnp.where(inside, both[:, 0], 0.0).astype(BF16)
        out_ref[y, 1] = jnp.where(inside, both[:, 1], 0.0).astype(BF16)
        out_ref[y, 2] = jnp.where(inside, refs[4 + y][...].astype(F32), 0.0).astype(BF16)


def piece_of(gate_up, down, place):
    def chunk(y, place):
        return (y * 2 + place[0]) * 4 + place[1]

    return pl.pallas_call(
        piece_kernel,
        name="piece",
        grid_spec=pltpu.PrefetchScalarGridSpec(
            num_scalar_prefetch=1,
            grid=(1,),
            in_specs=[
                *(pl.BlockSpec((PART, 2, 128), lambda i, p, y=y: (chunk(y, p), 0, p[2])) for y in range(4)),
                *(pl.BlockSpec((PART, 128), lambda i, p, y=y: (chunk(y, p), p[2])) for y in range(4)),
            ],
            out_specs=pl.BlockSpec((4, 3, PART, 128), lambda i, p: (0, 0, 0, 0)),
        ),
        out_shape=jax.ShapeDtypeStruct((4, 3, PART, 128), BF16),
    )(place, *[gate_up] * 4, *[down] * 4)


def front_kernel(
    prefix_ref, x_ref, w_hbm, cos_hbm, sin_hbm, w_out_hbm, gain_ref, bias_ref, piece_ref,
    tokens_out, q_out, k_out, v_out, heads_out, lse_ref, normed_ref, unit_ref, inverse_ref, w_all_ref,
    all_ref, total, w_ref, cos_ref, sin_ref, w_out_ref, q_ref, k_ref, v_ref, heads_ref, local, sem, *rest,
):
    bufs, (send, recv) = rest[:7], rest[7:]
    links = Links(send, recv)
    loads, load_out, written = Loads(), Loads(), Loads()
    for i, (src, dst) in enumerate(((w_hbm, w_ref), (cos_hbm, cos_ref), (sin_hbm, sin_ref))):
        loads.start(src, dst, sem.at[i])
    load_out.start(w_out_hbm, w_out_ref, sem.at[3])
    all_ref[0] = x_ref[...]
    to = links.to
    links.barrier(to(y=1), to(y=3), to(z=2), to(y=2), to(x=1), to(x=3), to(z=1), to(z=3))

    def project(pair):
        loads.wait()
        rows = pair_of(all_ref, pair)
        for part, out in enumerate((q_ref, k_ref, v_ref)):
            result = dot(rows, w_ref[part])
            for i, slot in enumerate(pair):
                at = pl.ds(links.first_row(slot), ROWS)
                piece = result[i * ROWS : (i + 1) * ROWS]
                if part == 2:
                    out[at] = piece.astype(BF16)
                    continue
                cosine, sine = cos_ref[at], sin_ref[at]
                for head in range(2):
                    lanes = slice(head * 128, head * 128 + 128)
                    turned = piece[:, lanes] * cosine + pltpu.roll(piece[:, lanes], 64, 1) * sine
                    if part == 0:
                        turned = turned * HEAD_DIM**-0.5
                    out[at, lanes] = turned.astype(BF16)

    def attend(first, block):
        at = pl.ds(first, block)
        for head in range(2):
            lanes = slice(head * 128, head * 128 + 128)
            scores = dot_t(k_ref[:, lanes], q_ref[at, lanes])
            key = lax.broadcasted_iota(jnp.int32, scores.shape, 0)
            limit = lax.broadcasted_iota(jnp.int32, (1, block), 1) + first
            limit = jnp.maximum(limit, prefix_ref[0] - 1)
            scores = jnp.where(key <= limit, scores, -1e30)
            peak = jnp.max(scores, axis=0, keepdims=True)
            exponent = jnp.exp(scores - peak)
            row_total = jnp.sum(exponent, axis=0, keepdims=True)
            weights = (exponent * (1.0 / row_total)).astype(BF16)
            heads_ref[at, lanes] = dot_rows(weights, v_ref[:, lanes]).astype(BF16)
            lse_ref[head, :, at] = peak + jnp.log(row_total)

    def compute(pair):
        step = (0, 3, 1, 2)[pair[1]]
        attend(pl.multiple_of(lax.rem(links.y + step, 4) * 2 * ROWS, 2 * ROWS), 2 * ROWS)
        load_out.wait()
        rows = jnp.concatenate([heads_ref[pl.ds(links.first_row(s), ROWS)] for s in pair], axis=0)
        result = dot(rows, w_out_ref[...]).astype(BF16)
        for i, slot in enumerate(pair):
            bufs[0][slot] = result[i * ROWS : (i + 1) * ROWS]

    def finish(at):
        unit, inverse = norm_parts(deep_alpha * x_ref[at].astype(F32) + total[at])
        unit_ref[at] = unit
        inverse_ref[at] = jnp.broadcast_to(inverse, (16, 128))
        normed_ref[at] = unit * gain_ref[...] + bias_ref[...]

    def chain():
        yield from gather(links, all_ref, project)
        for i, (src, dst) in enumerate(((all_ref, tokens_out), (q_ref, q_out), (k_ref, k_out), (v_ref, v_out))):
            written.start(src, dst, sem.at[4 + i])
        yield from scatter(links, bufs, compute, total)
        written.start(heads_ref, heads_out, sem.at[8])
        by_chunks(finish)

    together(FRONT, chain(), *spread(links, piece_ref, w_all_ref, local))
    written.wait()


class Loads:
    def __init__(self):
        self.copies = []

    def start(self, src, dst, sem):
        copy = pltpu.make_async_copy(src, dst, sem)
        copy.start()
        self.copies.append(copy)

    def wait(self):
        while self.copies:
            self.copies.pop().wait()


def load_weights(w_hbm, w, sem, parts):
    loads = Loads()
    for k in range(parts):
        for i in range(16):
            src = w_hbm.at[k, lax.rem(i // 2, 2), i // 4, lax.rem(i, 2)]
            loads.start(src, w.at[k, pl.ds(0, FF), pl.ds(i * 128, 128)], sem.at[k, i])
    for k in range(parts):
        w[k, FF:COLS] = jnp.zeros((COLS - FF, WIDE), BF16)
    return loads


def feed_kernel(
    clusters_ref, normed_ref, cot_ref, w_hbm, gain_ref, bias_ref,
    out_ref, all_out, gz_all_out, act_out, gz_ref, vec_ref,
    w, all_ref, gz_all_ref, act_ref, gelu_ref, slope, total, w_sem, out_sem, *rest,
):
    bufs, (send, recv) = rest[:4], rest[4:]
    links = Links(send, recv)

    def to_low(at):
        all_ref[0, at] = normed_ref[at].astype(BF16)

    by_chunks(to_low)
    load_w = load_weights(w_hbm, w, w_sem, 3)
    links.barrier(links.to(y=1), links.to(y=3), links.to(sibling=True))
    written = Loads()

    def forward(pair):
        load_w.wait()
        rows = pair_of(all_ref, pair)
        for c in range(0, COLS, 256):
            cols = slice(c, c + 256)
            gate = dot_t(rows, w[0, cols])
            up = dot_t(rows, w[1, cols])
            bell = 0.5 + 0.5 * lax.erf(gate * np.float32(np.sqrt(0.5)))
            gelu = gate * bell
            turn = bell + gate * (jnp.exp(-0.5 * gate * gate) * np.float32(1.0 / np.sqrt(2.0 * np.pi)))
            hidden = (gelu * up).astype(BF16)
            turn = turn * up
            for i, slot in enumerate(pair):
                part = slice(i * ROWS, (i + 1) * ROWS)
                gelu_ref[slot, :, cols] = gelu[part]
                slope[slot, :, cols] = turn[part]
                act_ref[slot, :, 2 * COLS + c : 2 * COLS + c + 256] = hidden[part]

    alone(gather_near(links, all_ref, forward))
    written.start(all_ref, all_out, out_sem.at[8])

    def compute(pair):
        rows = jnp.concatenate([act_ref[slot, :, 2 * COLS :] for slot in pair], axis=0)
        for d in range(0, WIDE, 512):
            result = dot(rows, w[2, :, d : d + 512]).astype(BF16)
            for i, slot in enumerate(pair):
                bufs[0][slot, :, d : d + 512] = result[i * ROWS : (i + 1) * ROWS]

    vec_ref[...] = jnp.zeros_like(vec_ref)
    own, same = clusters_ref[lax.axis_index("dp")], np.float32(0.0)
    for i in range(clusters_ref.shape[0]):
        same = same + jnp.where(clusters_ref[i] == own, np.float32(1.0), np.float32(0.0))
    seq_weight = 1.0 / jnp.full((1, WIDE), same, F32)

    def finish(at):
        unit, inverse = norm_parts(deep_alpha * normed_ref[at] + total[at])
        out_ref[at] = (unit * gain_ref[...] + bias_ref[...]).astype(BF16)
        grad = cot_ref[at].astype(F32) * seq_weight
        grad_z = norm_backward(grad, unit, inverse, gain_ref[...])
        gz_ref[at] = grad_z
        gz_all_ref[0, at] = grad_z.astype(BF16)
        vec_ref[0] += rows8(grad * unit)
        vec_ref[1] += rows8(grad)

    def backward(pair):
        rows = pair_of(gz_all_ref, pair)
        for c in range(0, COLS, 256):
            cols = slice(c, c + 256)
            grad_hidden = dot_t(rows, w[2, cols])
            for i, slot in enumerate(pair):
                part = grad_hidden[i * ROWS : (i + 1) * ROWS]
                act_ref[slot, :, cols] = (part * slope[slot, :, cols]).astype(BF16)
                act_ref[slot, :, COLS + c : COLS + c + 256] = (part * gelu_ref[slot, :, cols]).astype(BF16)
        for slot in pair:
            written.start(act_ref.at[slot], act_out.at[slot], out_sem.at[slot])

    task, copies = scatter_near(links, bufs, compute, total)
    whole = when_whole(backward, 2)

    def chain(first):
        yield from task(first, 64)
        by_chunks(finish, first, 64)
        yield from gather_near(links, gz_all_ref, whole, first, 64)

    together(FEED, chain(0), chain(64))
    sent(copies)
    written.start(gz_all_ref, gz_all_out, out_sem.at[9])
    written.wait()


def feed_back_kernel(
    act_hbm, gz_hbm, w_hbm, normed_hbm, gz_all_hbm, unit_hbm, inverse_ref, gain_ref, w_out_hbm,
    gz1_ref, all_out, grad_heads_ref, vec_ref, shard_ref,
    gz_ref, unit_ref, w_out_ref, act_ref, rows_ref, all_ref, w, total, w_sem, sem, *rest,
):
    bufs, more, (send, recv) = rest[:4], rest[4:17], rest[17:]
    links = Links(send, recv)
    load_act, load_rows = Loads(), Loads()
    load_w = load_weights(w_hbm, w, w_sem, 2)
    load_act.start(act_hbm, act_ref, sem.at[0])
    to = links.to
    links.barrier(
        to(y=1), to(y=3), to(z=2), to(x=1), to(x=3), to(z=1), to(z=3), to(sibling=True)
    )
    load_act.wait()
    load_w.wait()
    load_rows.start(normed_hbm, rows_ref, sem.at[1])
    load_late = Loads()
    for i, (src, dst) in enumerate(((gz_hbm, gz_ref), (unit_hbm, unit_ref), (w_out_hbm, w_out_ref))):
        load_late.start(src, dst, sem.at[4 + i])

    def compute(pair):
        rows = jnp.concatenate([act_ref[slot, :, : 2 * COLS] for slot in pair], axis=0)
        for d in range(0, WIDE, 512):
            cols = slice(d, d + 512)
            result = dot(rows[:, :COLS], w[0, :, cols]) + dot(rows[:, COLS:], w[1, :, cols])
            result = result.astype(BF16)
            for i, slot in enumerate(pair):
                bufs[0][slot, :, cols] = result[i * ROWS : (i + 1) * ROWS]

    def finish(at):
        grad = deep_alpha * gz_ref[at] + total[at]
        unit = unit_ref[at]
        grad_z = norm_backward(grad, unit, inverse_ref[at][:, 0:1], gain_ref[...])
        gz1_ref[at] = grad_z
        all_ref[0, at] = grad_z.astype(BF16)
        vec_ref[0] += rows8(grad * unit)
        vec_ref[1] += rows8(grad)

    def work(pair):
        result = dot_t(pair_of(all_ref, pair), w_out_ref[...]).astype(BF16)
        for i, slot in enumerate(pair):
            grad_heads_ref[pl.ds(links.first_row(slot), ROWS)] = result[i * ROWS : (i + 1) * ROWS]

    written = Loads()

    vec_ref[...] = jnp.zeros_like(vec_ref)
    task, copies = scatter_near(links, bufs, compute, total)
    whole = when_whole(work, 2)

    def chain(first):
        yield from task(first, 64)
        load_late.wait()
        by_chunks(finish, first, 64)
        yield from gather(links, all_ref, whole, first, 64)

    g = more[0]

    def make(k):
        load_rows.wait()
        for c in range(0, COLS, 256):
            left = act_ref[:, :, k * COLS + c : k * COLS + c + 256].reshape(LEN, 256)
            height = min(256, FF - c)
            for d in range(0, WIDE, 512):
                right = rows_ref[:, :, d : d + 512].reshape(LEN, 512)
                result = dot_rows(left, right)[:height].astype(BF16)
                for i in range(4):
                    at = d // 128 + i
                    g[k, at // 4, at // 2 % 2, at % 2, c : c + height] = result[:, i * 128 : i * 128 + 128]
            if k == 1 and c == 512:
                load_rows.start(gz_all_hbm, rows_ref, sem.at[2])
            if c < 512:
                yield ()

    together(FEED_BACK, chain(0), chain(64), *reduce(links, more, make, shard_ref))
    sent(copies)
    written.start(all_ref, all_out, sem.at[3])
    written.wait()


def input_kernel(
    prefix_ref, q_ref, k_ref, v_ref, g_ref, lse_ref, cos_ref, sin_ref,
    w_hbm, gz1_ref, tokens_hbm, heads_ref, gz_all_hbm, shard_ref, attn_vec_ref, feed_vec_ref,
    out_ref, one_out, two_out, whole_out, own_ref, feed_ref,
    one_ref, two_ref, whole_ref, out_sem, total, vec_ref, w_ref, tokens_ref, gz_all_ref, grads, heads, key_sum, value_sum, held, got, local, sem, *rest,
):
    bufs, more, (send, recv) = rest[:7], rest[7:22], rest[22:]
    links = Links(send, recv)
    to = links.to
    load_gz, load_tokens, load_w, written = Loads(), Loads(), Loads(), Loads()
    load_gz.start(gz_all_hbm, gz_all_ref, sem.at[2])
    load_tokens.start(tokens_hbm, tokens_ref, sem.at[1])
    load_w.start(w_hbm, w_ref, sem.at[0])
    links.barrier(
        to(y=1), to(y=2), to(y=3), to(z=2), to(x=1), to(x=2), to(x=3), to(sibling=True), links.beside()
    )
    for i, ref in enumerate((attn_vec_ref, feed_vec_ref)):
        for j in range(2):
            vec_ref[2 * i + j : 2 * i + j + 1] = jnp.sum(ref[j], axis=0, keepdims=True)
    vec_ref[4:8] = jnp.zeros((4, WIDE), F32)
    block = 512
    ready = [Mark(), Mark(), Mark()]

    def attend_back(head):
        lanes = slice(head * 128, head * 128 + 128)

        def keep(part, first, value):
            for i in range(value.shape[0] // ROWS):
                seq = first // ROWS + i
                d = lax.rem(seq // 2 + 4 - links.y, 4)
                slot = 2 * d - d * (d - 1) // 2 - d * (d - 1) * (d - 2) // 3
                slot = slot + 4 * lax.rem(links.z_hi + seq, 2)
                at = head * 384 + part * 128
                grads[slot, :, at : at + 128] = value[i * ROWS : (i + 1) * ROWS].astype(BF16)

        for first in range(0, LEN, block):
            at = slice(first, first + block)
            query, grad = q_ref[at, lanes], g_ref[at, lanes]
            scores = dot_t(k_ref[:, lanes], query)
            key = lax.broadcasted_iota(jnp.int32, scores.shape, 0)
            limit = lax.broadcasted_iota(jnp.int32, (1, block), 1) + first
            limit = jnp.maximum(limit, prefix_ref[0] - 1)
            weights = jnp.where(key <= limit, jnp.exp(scores - lse_ref[head, :, at]), 0.0)
            grad_weights = dot_t(v_ref[:, lanes], grad)
            inner = jnp.sum(weights * grad_weights, axis=0, keepdims=True)
            grad_scores = (weights * (grad_weights - inner)).astype(BF16)
            turned = dot_rows(grad_scores, k_ref[:, lanes]) * HEAD_DIM**-0.5
            keep(0, first, turned * cos_ref[at] - pltpu.roll(turned, 64, 1) * sin_ref[at])
            grad_key = dot(grad_scores, query)
            grad_value = dot(weights.astype(BF16), grad)
            if first == 0:
                key_sum[...] = grad_key
                value_sum[...] = grad_value
            else:
                key_sum[...] += grad_key
                value_sum[...] += grad_value
            yield ()
        turned = key_sum[...]
        keep(1, 0, turned * cos_ref[...] - pltpu.roll(turned, 64, 1) * sin_ref[...])
        keep(2, 0, value_sum[...])

    def compute(pair):
        load_w.wait()
        rows = pair_of(grads, pair)
        result = 0.0
        for part in range(3):
            for head in range(2):
                at = head * 384 + part * 128
                result = result + dot_t(rows[:, at : at + 128], w_ref[part, :, head * 128 : head * 128 + 128])
        result = result.astype(BF16)
        for i, slot in enumerate(pair):
            bufs[0][slot] = result[i * ROWS : (i + 1) * ROWS]

    def finish(at):
        value = deep_alpha * gz1_ref[at] + total[at]
        for lane in range(WIDE // 128):
            out_ref[at, lane] = value[:, lane * 128 : lane * 128 + 128]

    def chain():
        yield (ready[2],)
        for head in range(2):
            yield from attend_back(head)
            ready[head].done = True
            if head == 0:
                yield ()
        yield from scatter(links, bufs, compute, total)
        by_chunks(finish)

    def qkv(head):
        flat = more[5 * head]
        yield (ready[head],)
        load_tokens.wait()
        right = grads[:, :, head * 384 : head * 384 + 384].reshape(LEN, 384)
        for d in range(8):
            left = tokens_ref[:, :, d * 256 : d * 256 + 256].reshape(LEN, 256)
            result = dot_rows(left, right).astype(BF16)
            for part in range(3):
                for i in range(2):
                    row = part * WIDE + d * 256 + i * 128
                    chunk, at = row // 384, row % 384
                    flat[chunk // 8, chunk // 4 % 2, chunk % 4, at : at + 128] = result[
                        i * 128 : i * 128 + 128, part * 128 : part * 128 + 128
                    ]
            if d == 3:
                yield ()

    def first_shared():
        for slot in range(8):
            heads[slot] = heads_ref[pl.ds(links.first_row(slot), ROWS)]
        load_gz.wait()
        left = heads[...].reshape(LEN, 256)
        for d in range(0, WIDE, 512):
            result = dot_rows(left, gz_all_ref[:, :, d : d + 512].reshape(LEN, 512)).astype(BF16)
            for i in range(4):
                lane = d // 128 + i
                for j in range(2):
                    chunk = lane // 2 * 2 + j
                    more[10][chunk // 8, chunk // 4 % 2, chunk % 4, :, lane % 2 * 128 : lane % 2 * 128 + 128] = result[
                        j * 128 : j * 128 + 128, i * 128 : i * 128 + 128
                    ]
        ready[2].done = True
        yield from share(links, more[10:15], whole_ref, SHARE_X_FIRST[2])
        written.start(whole_ref, whole_out, out_sem.at[2])

    def shared(head):
        yield from qkv(head)
        result, result_out = ((one_ref, one_out), (two_ref, two_out))[head]
        yield from share(links, more[5 * head : 5 * head + 5], result, SHARE_X_FIRST[head])
        written.start(result, result_out, out_sem.at[head])

    together(
        INPUT,
        *collect(links, shard_ref, feed_ref, local),
        first_shared(),
        chain(),
        shared(0),
        shared(1),
        agree(links, vec_ref, (held, got)),
    )
    written.wait()
    own_ref[...] = vec_ref[:, pl.ds(pl.multiple_of(lax.axis_index("seq") * 256, 256), 256)]


def down_kernel(feed_ref, down_ref):
    for z in range(2):
        down_ref[:, z * 128 : z * 128 + 128] = feed_ref[0, 0, 0, z].astype(F32)


def outputs_kernel(
    feed_hbm, one_hbm, two_hbm, out_hbm, vec_ref, output_hbm, input_hbm,
    gate_up_hbm, grad_qkv_hbm, grad_out_hbm, v0_ref, v1_ref, v2_ref, v3_ref, output_out, input_out,
    feed, one, two, out, output, input_grad, gate_up, grad_qkv, grad_out, load_sem, store_sem,
):
    def load(i, src, dst):
        copy = pltpu.make_async_copy(src, dst, load_sem.at[i])
        copy.start()
        return copy

    stores = []

    def store(src, dst):
        stores.append(pltpu.make_async_copy(src, dst, store_sem.at[len(stores)]))
        stores[-1].start()

    chunks = []
    for k in range(2):
        for i in range(8):
            at = (k, i // 2, i % 2)
            chunks.append((at, load(len(chunks), feed_hbm.at[at], feed.at[at])))
    rest = [load(16, one_hbm, one), load(17, two_hbm, two), load(18, out_hbm, out)]
    passed = [(load(19, output_hbm, output), output, output_out), (load(20, input_hbm, input_grad), input_grad, input_out)]
    for i, ref in enumerate((v0_ref, v1_ref, v2_ref, v3_ref)):
        ref[...] = vec_ref[i : i + 1]
    total = gate_up_hbm.shape[0]
    for (_, gate), ((_, y, core), up) in zip(chunks[:8], chunks[8:]):
        gate.wait()
        up.wait()
        first = (2 * y + core) * FF
        for z in range(2):
            lanes = slice(z * 128, z * 128 + 128)
            gate_up[first : first + FF, 0, lanes] = feed[0, y, core, z].astype(F32)
            gate_up[first : first + FF, 1, lanes] = feed[1, y, core, z].astype(F32)
        at = pl.ds(first, min(FF, total - first))
        store(gate_up.at[at], gate_up_hbm.at[at])
    for copy, src, dst in passed:
        copy.wait()
        store(src, dst)
    for copy in rest:
        copy.wait()
    for i in range(4):
        at = pl.ds(i * 1536, 1536)
        grad_qkv[at, 0:128] = one[at].astype(F32)
        grad_qkv[at, 128:256] = two[at].astype(F32)
        store(grad_qkv.at[at], grad_qkv_hbm.at[at])
    for i in range(8):
        grad_out[:, i * 256 : i * 256 + 256] = out[i * 256 : i * 256 + 256].astype(F32)
    store(grad_out, grad_out_hbm)
    for copy in stores:
        copy.wait()


def outputs(feed, one, two, out, vec, output, input_grad, total):
    shapes = [((total, 2, 256), F32), ((6144, 256), F32), ((256, WIDE), F32)]
    grad_down = pl.pallas_call(
        down_kernel,
        name="down",
        grid=(8,),
        in_specs=[pl.BlockSpec((1, 1, 1, 2, FF, 128), lambda i: (2, i // 2, i % 2, 0, 0, 0))],
        out_specs=pl.BlockSpec((FF, 256), lambda i: (i, 0)),
        out_shape=jax.ShapeDtypeStruct((total, 256), F32),
        compiler_params=pltpu.CompilerParams(vmem_limit_bytes=VMEM_BYTES),
    )(feed)
    rest = pl.pallas_call(
        outputs_kernel,
        name="outputs",
        in_specs=[HBM, HBM, HBM, HBM, VMEM, HBM, HBM],
        out_specs=(HBM, HBM, HBM, VMEM, VMEM, VMEM, VMEM, HBM, HBM),
        out_shape=(
            *(jax.ShapeDtypeStruct(s, d) for s, d in shapes),
            *(jax.ShapeDtypeStruct((1, 256), F32) for _ in range(4)),
            jax.ShapeDtypeStruct(output.shape, BF16),
            jax.ShapeDtypeStruct(input_grad.shape, F32),
        ),
        scratch_shapes=[
            pltpu.VMEM((2, *feed.shape[1:]), BF16),
            *(pltpu.VMEM(v.shape, v.dtype) for v in (one, two, out, output, input_grad)),
            pltpu.VMEM((8 * FF, 2, 256), F32),
            *(pltpu.VMEM(s, d) for s, d in shapes[1:]),
            pltpu.SemaphoreType.DMA((21,)),
            pltpu.SemaphoreType.DMA((16,)),
        ],
        compiler_params=pltpu.CompilerParams(vmem_limit_bytes=VMEM_BYTES),
    )(feed, one, two, out, vec, output, input_grad)
    return (rest[0], grad_down, *rest[1:])


def on_device(
    tokens, cotangent, w_qkv, w_out, w_gate_up, w_down,
    attn_gain, attn_bias, ffn_gain, ffn_bias, prefix_len, clusters,
):
    x = tokens.reshape(ROWS, WIDE)
    cot = cotangent.reshape(ROWS, WIDE)
    dp = lax.axis_index("dp")
    cosine, sine = (jnp.asarray(t) for t in rotary_tables(LEN, HEAD_DIM))
    row = lambda v: v.reshape(1, WIDE)
    ff_total = w_down.shape[1]
    place = jnp.stack([dp % 2, dp // 2 % 4, dp // 8, jnp.int32(ff_total)]).astype(jnp.int32)
    piece = piece_of(w_gate_up.transpose(2, 1, 0), w_down.T, place)
    w_in = w_qkv.transpose(1, 0, 2)
    low, full = BF16, F32
    blocks = (8, ROWS, WIDE)
    one = pltpu.SemaphoreType.DMA
    some = lambda *n: pltpu.SemaphoreType.DMA(n)
    rows_f32 = pltpu.VMEM((ROWS, WIDE), F32)
    blocks_low = pltpu.VMEM(blocks, BF16)
    head_sum = pltpu.VMEM((LEN, 128), F32)

    tokens_all, q, k, v, heads_out, lse, normed, unit_one, inverse_one, w_all = call(
        front_kernel, "front", 0,
        [
            (blocks, low, "h"), *[((LEN, 256), low, "h")] * 4, ((2, 1, LEN), full, "v"),
            ((ROWS, WIDE), full, "v"), ((ROWS, WIDE), full, "v"), ((ROWS, 128), full, "v"),
            ((3, 2, 4, 2, FF, 128), low, "h"),
        ],
        (prefix_len, x, w_in, cosine, sine, w_out, row(attn_gain), row(attn_bias), piece), "svhhhhvvv",
        (
            blocks_low, rows_f32, pltpu.VMEM((3, WIDE, 256), BF16), head_sum, head_sum,
            pltpu.VMEM((256, WIDE), BF16), *[pltpu.VMEM((LEN, 256), BF16)] * 4, one, some(9), *SCATTER_SCRATCH,
        ),
        94, 2 * LEN * WIDE * 1024,
    )
    output, normed_all, gz_all, act, grad_z2, ffn_vec = call(
        feed_kernel, "feed", 2,
        [
            ((ROWS, WIDE), low, "v"), (blocks, low, "h"), (blocks, low, "h"),
            ((8, ROWS, 3 * COLS), low, "h"), ((ROWS, WIDE), full, "v"), ((2, 8, WIDE), full, "v"),
        ],
        (clusters, normed, cot, w_all, row(ffn_gain), row(ffn_bias)), "svvhvv",
        (
            pltpu.VMEM((3, COLS, WIDE), BF16), blocks_low, blocks_low,
            pltpu.VMEM((8, ROWS, 3 * COLS), BF16), pltpu.VMEM((8, ROWS, COLS), F32),
            pltpu.VMEM((8, ROWS, COLS), F32), rows_f32, some(3, 16), some(10), *NEAR_SCRATCH,
        ),
        60, 2 * LEN * WIDE * COLS * 4,
    )
    grad_z1, gz1_all, grad_heads, attn_vec, shard = call(
        feed_back_kernel, "feed_back", 3,
        [
            ((ROWS, WIDE), full, "v"), (blocks, low, "h"), ((LEN, 256), low, "v"),
            ((2, 8, WIDE), full, "v"), ((3, 4, PART, 128), low, "v"),
        ],
        (act, grad_z2, w_all, normed_all, gz_all, unit_one, inverse_one, row(attn_gain), w_out),
        "hhhhhhvvh",
        (
            rows_f32, rows_f32, pltpu.VMEM((256, WIDE), BF16), pltpu.VMEM((8, ROWS, 3 * COLS), BF16), blocks_low, blocks_low,
            pltpu.VMEM((2, COLS, WIDE), BF16), rows_f32, some(2, 16), some(7),
            *NEAR_SCRATCH, *REDUCE_SCRATCH,
        ),
        80, 2 * LEN * WIDE * COLS * 5,
    )
    steps = pltpu.VMEM((7, 8, WIDE), F32)
    input_grad, one, two, out_whole, vec, ffn_whole = call(
        input_kernel, "input", 4,
        [
            ((ROWS, WIDE // 128, 128), full, "v"), ((2, 2, 4, 384, 128), low, "h"),
            ((2, 2, 4, 384, 128), low, "h"), ((2, 2, 4, 128, 256), low, "h"), ((8, 256), full, "v"),
            ((3, 4, 2, 2, FF, 128), low, "h"),
        ],
        (
            prefix_len, q, k, v, grad_heads, lse, cosine, sine,
            w_in, grad_z1, tokens_all, heads_out, gz1_all, shard, attn_vec, ffn_vec,
        ),
        "svvvvvvvhvhvhvvv",
        (
            pltpu.VMEM((2, 2, 4, 384, 128), BF16), pltpu.VMEM((2, 2, 4, 384, 128), BF16),
            pltpu.VMEM((2, 2, 4, 128, 256), BF16), some(3),
            rows_f32, pltpu.VMEM((8, WIDE), F32), pltpu.VMEM((3, WIDE, 256), BF16), blocks_low, blocks_low,
            pltpu.VMEM((8, ROWS, 768), BF16), pltpu.VMEM((8, ROWS, 256), BF16),
            head_sum, head_sum, steps, steps, pltpu.SemaphoreType.DMA, some(3),
            *SCATTER_SCRATCH, *share_scratch(384, 128), *share_scratch(384, 128), *share_scratch(128, 256),
        ),
        140, 2 * LEN * WIDE * 768,
    )
    grad_gate_up, grad_down, grad_qkv, grad_out, *vecs, output, input_grad = outputs(
        ffn_whole, one.reshape(6144, 128), two.reshape(6144, 128), out_whole.reshape(2048, 256),
        vec, output, input_grad, ff_total,
    )
    return (
        output.reshape(tokens.shape),
        input_grad.reshape(tokens.shape),
        grad_qkv.reshape(3, WIDE, 256).transpose(1, 0, 2),
        grad_out,
        grad_gate_up.transpose(2, 1, 0),
        grad_down.T,
        *(v.reshape(256) for v in vecs),
    )


def solution(mesh):
    return jax.shard_map(
        on_device,
        mesh=mesh,
        in_specs=(
            P("seq", "dp", None), P("seq", "dp", None), P(None, None, "seq"), P("seq", None),
            P("seq", None, None), P("seq", None), P(), P(), P(), P(), P("dp"), P(),
        ),
        out_specs=(
            P("seq", "dp", None), P("seq", "dp", None), P(None, None, "seq"), P("seq", None),
            P("seq", None, None), P("seq", None), P("seq"), P("seq"), P("seq"), P("seq"),
        ),
        check_vma=False,
    )
```
